32 devices in a mesh: src: 4 (over z), tgt: 8 (over y, x, core).
Axes of the slice: x: 2, y: 2, z: 4, core: 2. Of those that a mesh axis runs over, the one named last changes fastest.
Arguments:
- coupling: bfloat16 [2048, 4096], P('src', 'tgt'), may hold values from 0.25 to 4
- src_pcs: bfloat16 [50, 2048], P(None, 'src'), may hold values from -24 to 24
- tgt_pcs: bfloat16 [50, 4096], P(None, 'tgt'), may hold values from -24 to 24
- src_mass: float32 [2048], P('src'), may hold values from 0.25 to 4
- tgt_mass: float32 [4096], P('tgt'), may hold values from 0.25 to 4
Outputs:
- log_coupling: float32 [2048, 4096], P('src', 'tgt')
- row_potential: float32 [2048], P('src')
- col_potential: float32 [4096], P('tgt')
The draws below stay inside these ranges and needn't reach their ends.
All inputs are finite; a program needn't handle non-finite values.
Results may differ from the reference program's by a relative error of at most 0.0019.
Values sent between devices are 32-bit elements; how exact they have to be, the bound alone decides.
No kernel may reach another device: no remote copies, remote signals or barrier semaphores. Data moves between devices by JAX's collectives and lax.ppermute only.
A program may use at most 64 MiB of HBM per device.

```python
import math
import jax
import jax.numpy as jnp
from jax import lax

PCS = 50
ITERS = 4
NS = 2048
NT = 4096


def pc_field(key, cells):
    entry_key, scale_key = jax.random.split(key)
    leading = 2.0
    entries = jax.random.truncated_normal(entry_key, -4.0, 4.0, (PCS, cells), jnp.float32)
    components = leading * 0.1 ** (jnp.arange(PCS, dtype=jnp.float32) / (PCS - 1))
    cell_scale = jnp.exp(jax.random.uniform(scale_key, (cells,), jnp.float32, jnp.log(0.3), jnp.log(3.0)))
    return (entries * components[:, None] * cell_scale[None, :]).astype(jnp.bfloat16)


def draw_src_pcs(key, part):
    return pc_field(jax.random.fold_in(key, 11), NS)


def draw_tgt_pcs(key, part):
    return pc_field(jax.random.fold_in(key, 23), NT)


def block_levels(own_key, extent, cuts, smallest, high):
    def one(position, shards_of):
        heights = jax.random.uniform(jax.random.fold_in(jax.random.fold_in(own_key, 6), position), (shards_of,), jnp.float32, smallest / len(cuts), high / len(cuts))
        return jnp.repeat(jnp.exp(heights), extent[position] // shards_of).reshape((-1,) + (1,) * (len(extent) - position - 1))

    loudness = one(*cuts[0])
    for cut in cuts[1:]:
        loudness = loudness * one(*cut)
    return loudness


def setup_inputs(seed: int = 0) -> dict:
    splits = jax.random.split(jax.random.key(seed), 6)
    return {
        "coupling": jnp.clip(jnp.exp(math.log(4.0) - 2.7725887 * jax.random.uniform(splits[0], (NS, NT), jnp.float32) ** block_levels(splits[0], (NS, NT), ((0, 4), (1, 8)), -0.2, 0.2)), 0.25, 4.0).astype(jnp.bfloat16),
        "src_pcs": draw_src_pcs(jax.random.fold_in(splits[5], 71), 0),
        "tgt_pcs": draw_tgt_pcs(jax.random.fold_in(splits[5], 71), 0),
        "src_mass": jnp.clip(jnp.exp(math.log(4.0) - 2.7725887 * jax.random.uniform(splits[3], (NS,), jnp.float32) ** block_levels(splits[3], (NS,), ((0, 4),), -0.2, 0.2)), 0.25, 4.0),
        "tgt_mass": jnp.clip(jnp.exp(math.log(4.0) - 2.7725887 * jax.random.uniform(splits[4], (NT,), jnp.float32) ** block_levels(splits[4], (NT,), ((0, 8),), -0.2, 0.2)), 0.25, 4.0),
    }


eps_reg = 0.5
marg_power = 1.0 / (1.0 + eps_reg)
tiny_eps = 1e-06

def reference(coupling, src_pcs, tgt_pcs, src_mass, tgt_mass):
    exact = lax.Precision.HIGHEST
    panel = jnp.dot(src_pcs, coupling, preferred_element_type=jnp.float32)
    moment = jnp.dot(panel, tgt_pcs.astype(jnp.float32).T, precision=exact) * (NS * NT) ** (-0.5)
    normed = moment / jnp.sqrt(jnp.mean(moment * moment) + tiny_eps)
    weighted = jnp.dot(normed, tgt_pcs.astype(jnp.float32), precision=exact)
    scores = jnp.dot(src_pcs.astype(jnp.float32).T, weighted, precision=exact) * (2.0 / (eps_reg * PCS))
    log_src = jnp.log(src_mass)
    log_tgt = jnp.log(tgt_mass)
    col_potential = jnp.zeros((NT,), jnp.float32)
    row_potential = jnp.zeros((NS,), jnp.float32)
    for iteration in range(ITERS):
        shifted = scores + col_potential[None, :]
        highest = lax.optimization_barrier(jnp.max(shifted, axis=1))
        summed_exp = lax.optimization_barrier(jnp.sum(jnp.exp(shifted - highest[:, None]), axis=1))
        row_potential = marg_power * (log_src - (highest + jnp.log(summed_exp) - jnp.log(jnp.float32(NT))))
        shifted = scores + row_potential[:, None]
        highest = lax.optimization_barrier(jnp.max(shifted, axis=0))
        summed_exp = lax.optimization_barrier(jnp.sum(jnp.exp(shifted - highest[None, :]), axis=0))
        col_potential = marg_power * (log_tgt - (highest + jnp.log(summed_exp) - jnp.log(jnp.float32(NS))))
    log_coupling = scores + row_potential[:, None] + col_potential[None, :]
    return (log_coupling, row_potential, col_potential)
```

```python
import functools

import jax
import jax.numpy as jnp
from jax import lax
from jax.sharding import PartitionSpec as P

PCS = 50
ITERS = 4


eps_reg = 0.5
marg_power = 1.0 / (1.0 + eps_reg)
tiny_eps = 1e-06

RADIX = 8


def exchange(value, axis, low, span):
    size = lax.axis_size(axis)
    out = [value]
    for j in range(1, span):
        perm = [(i, i ^ (low * j)) for i in range(size)]
        out.append(lax.ppermute(value, axis, perm))
    return out


def tree(values, combine):
    while len(values) > 1:
        values = [combine(values[i], values[i + 1]) for i in range(0, len(values), 2)]
    return values[0]


def stages(axis):
    size = lax.axis_size(axis)
    low = 1
    while low < size:
        span = min(RADIX, size // low)
        yield low, span
        low *= span


def all_sum(value, axis):
    for low, span in stages(axis):
        value = tree(exchange(value, axis, low, span), jnp.add)
    return value


def all_logsum(value, axis):
    for low, span in stages(axis):
        parts = exchange(value, axis, low, span)
        highest = tree(parts, jnp.maximum)
        total = tree([jnp.exp(part - highest) for part in parts], jnp.add)
        value = highest + jnp.log(total)
    return value


def all_blocks(value, axis):
    blocks = [value]
    for low, span in stages(axis):
        fresh = [exchange(block, axis, low, span) for block in blocks]
        blocks = [fresh[b][j] for j in range(span) for b in range(len(blocks))]
    return blocks


def shards(coupling, src_pcs, tgt_pcs, src_mass, tgt_mass):
    exact = lax.Precision.HIGHEST
    total_rows = coupling.shape[0] * lax.axis_size("src")
    total_cols = coupling.shape[1] * lax.axis_size("tgt")
    src_float = src_pcs.astype(jnp.float32)
    tgt_float = tgt_pcs.astype(jnp.float32)
    packed = jnp.concatenate([src_float, src_mass[None, :]], axis=0)
    src_blocks = all_blocks(packed, "src")
    block_panel = jnp.dot(src_pcs, coupling, preferred_element_type=jnp.float32)
    block_moment = jnp.dot(block_panel, tgt_float.T, precision=exact)
    moment = all_sum(all_sum(block_moment, "tgt"), "src")
    moment = moment * (total_rows * total_cols) ** (-0.5)
    normed = moment / jnp.sqrt(jnp.mean(moment * moment) + tiny_eps)
    weighted = jnp.dot(normed, tgt_float, precision=exact) * (2.0 / (eps_reg * PCS))
    everything = jnp.concatenate(src_blocks, axis=1)
    src_all = everything[:PCS]
    log_src = jnp.log(everything[PCS]) + jnp.log(jnp.float32(total_cols))
    log_tgt = jnp.log(tgt_mass) + jnp.log(jnp.float32(total_rows))
    scores = jnp.dot(src_all.T, weighted, precision=exact)
    col_potential = jnp.zeros((coupling.shape[1],), jnp.float32)
    blocks = len(src_blocks)
    rows = coupling.shape[0]
    for iteration in range(ITERS):
        shifted = scores + col_potential[None, :]
        highest = jnp.max(shifted, axis=1)
        summed = jnp.sum(jnp.exp(shifted - highest[:, None]), axis=1)
        row_potential = marg_power * (log_src - all_logsum(highest + jnp.log(summed), "tgt"))
        shifted = (scores + row_potential[:, None]).reshape(blocks, rows, -1)
        highest = jnp.max(shifted, axis=(0, 1))
        sums = jnp.sum(jnp.exp(shifted - highest[None, None, :]), axis=1)
        summed = tree([sums[b] for b in range(blocks)], jnp.add)
        col_potential = marg_power * (log_tgt - (highest + jnp.log(summed)))
    row_potential = row_potential[:rows]
    log_coupling = scores[:rows] + row_potential[:, None] + col_potential[None, :]
    return (log_coupling, row_potential, col_potential)


def solution(mesh):
    in_specs = (P("src", "tgt"), P(None, "src"), P(None, "tgt"), P("src"), P("tgt"))
    out_specs = (P("src", "tgt"), P("src"), P("tgt"))
    return jax.shard_map(shards, mesh=mesh, in_specs=in_specs, out_specs=out_specs, check_vma=False)
```

```python
import functools

import jax
import jax.numpy as jnp
from jax import lax
from jax.sharding import PartitionSpec as P

PCS = 50
ITERS = 4


eps_reg = 0.5
marg_power = 1.0 / (1.0 + eps_reg)
tiny_eps = 1e-06

RADIX = 2


def exchange(value, axis, low, span):
    size = lax.axis_size(axis)
    out = [value]
    for j in range(1, span):
        perm = [(i, i ^ (low * j)) for i in range(size)]
        out.append(lax.ppermute(value, axis, perm))
    return out


def tree(values, combine):
    while len(values) > 1:
        values = [combine(values[i], values[i + 1]) for i in range(0, len(values), 2)]
    return values[0]


def stages(axis):
    size = lax.axis_size(axis)
    low = 1
    while low < size:
        span = min(RADIX, size // low)
        yield low, span
        low *= span


def all_sum(value, axis):
    for low, span in stages(axis):
        value = tree(exchange(value, axis, low, span), jnp.add)
    return value


def all_logsum(value, axis):
    for low, span in stages(axis):
        parts = exchange(value, axis, low, span)
        highest = tree(parts, jnp.maximum)
        total = tree([jnp.exp(part - highest) for part in parts], jnp.add)
        value = highest + jnp.log(total)
    return value


def all_blocks(value, axis):
    blocks = [value]
    for j in range(1, lax.axis_size(axis)):
        perm = [(i, i ^ j) for i in range(lax.axis_size(axis))]
        blocks.append(lax.ppermute(value, axis, perm))
    return blocks


def shards(coupling, src_pcs, tgt_pcs, src_mass, tgt_mass):
    exact = lax.Precision.HIGHEST
    total_rows = coupling.shape[0] * lax.axis_size("src")
    total_cols = coupling.shape[1] * lax.axis_size("tgt")
    src_float = src_pcs.astype(jnp.float32)
    tgt_float = tgt_pcs.astype(jnp.float32)
    packed = jnp.concatenate([src_float, src_mass[None, :]], axis=0)
    half = packed.shape[1] // 2
    odd = lax.axis_index("tgt") % 2
    mine = lax.dynamic_slice_in_dim(packed, odd * half, half, axis=1)
    near = jnp.concatenate(all_blocks(mine, "src"), axis=0)
    far = lax.ppermute(near, "tgt", [(i, i ^ 1) for i in range(lax.axis_size("tgt"))])
    block_panel = jnp.dot(src_pcs, coupling, preferred_element_type=jnp.float32)
    block_moment = jnp.dot(block_panel, tgt_float.T, precision=exact)
    moment = all_sum(block_moment, "tgt")
    moment, near, far = lax.optimization_barrier((moment, near, far))
    moment = all_sum(moment, "src")
    moment = moment * (total_rows * total_cols) ** (-0.5)
    normed = moment / jnp.sqrt(jnp.mean(moment * moment) + tiny_eps)
    weighted = jnp.dot(normed, tgt_float, precision=exact) * (2.0 / (eps_reg * PCS))
    left = jnp.where(odd == 0, near, far)
    right = jnp.where(odd == 0, far, near)
    blocks = lax.axis_size("src")
    both = jnp.concatenate([left, right], axis=1).reshape(blocks, PCS + 1, -1)
    everything = jnp.concatenate([both[b] for b in range(blocks)], axis=1)
    src_all = everything[:PCS]
    log_src = jnp.log(everything[PCS]) + jnp.log(jnp.float32(total_cols))
    log_tgt = jnp.log(tgt_mass) + jnp.log(jnp.float32(total_rows))
    scores = jnp.dot(src_all.T, weighted, precision=exact)
    col_potential = jnp.zeros((coupling.shape[1],), jnp.float32)
    rows = coupling.shape[0]
    for iteration in range(ITERS):
        shifted = scores + col_potential[None, :]
        highest = jnp.max(shifted, axis=1)
        summed = jnp.sum(jnp.exp(shifted - highest[:, None]), axis=1)
        row_potential = marg_power * (log_src - all_logsum(highest + jnp.log(summed), "tgt"))
        shifted = (scores + row_potential[:, None]).reshape(blocks, rows, -1)
        highest = jnp.max(shifted, axis=(0, 1))
        sums = jnp.sum(jnp.exp(shifted - highest[None, None, :]), axis=1)
        summed = tree([sums[b] for b in range(blocks)], jnp.add)
        col_potential = marg_power * (log_tgt - (highest + jnp.log(summed)))
    row_potential = row_potential[:rows]
    log_coupling = scores[:rows] + row_potential[:, None] + col_potential[None, :]
    return (log_coupling, row_potential, col_potential)


def solution(mesh):
    in_specs = (P("src", "tgt"), P(None, "src"), P(None, "tgt"), P("src"), P("tgt"))
    out_specs = (P("src", "tgt"), P("src"), P("tgt"))
    return jax.shard_map(shards, mesh=mesh, in_specs=in_specs, out_specs=out_specs, check_vma=False)
```

```python
import functools
import math

import jax
import jax.numpy as jnp
from jax import lax
from jax.experimental import pallas as pl
from jax.experimental.pallas import tpu as pltpu
from jax.sharding import PartitionSpec as P

ITERS = 4

eps_reg = 0.5
marg_power = 1.0 / (1.0 + eps_reg)
tiny_eps = 1e-06

LANES = 128
DEPTH = 64
LN2 = math.log(2.0)
SCORES_BYTES = 1 << 24
VMEM = pl.BlockSpec(memory_space=pltpu.VMEM)


def params(mib):
    return pltpu.CompilerParams(vmem_limit_bytes=mib << 20)


def tree(values, combine):
    values = list(values)
    while len(values) > 1:
        paired = [combine(values[i], values[i + 1]) for i in range(0, len(values) - 1, 2)]
        values = paired + ([values[-1]] if len(values) % 2 else [])
    return values[0]


def pieces(value):
    high = value.astype(jnp.bfloat16)
    rest = value - high.astype(jnp.float32)
    middle = rest.astype(jnp.bfloat16)
    low = (rest - middle.astype(jnp.float32)).astype(jnp.bfloat16)
    return high, middle, low


def padded(value):
    return jnp.concatenate(
        [value, jnp.zeros((DEPTH - value.shape[0], value.shape[1]), value.dtype)], axis=0
    )


def pack_kernel(src_ref, tgt_ref, src_mass_ref, tgt_mass_ref, half_ref, whole_ref):
    pcs = src_ref.shape[0]
    half = half_ref.shape[1]
    odd = lax.rem(lax.axis_index("tgt"), 2)
    below = jnp.zeros((half_ref.shape[0] - pcs - 1, 2 * half), jnp.float32)
    src = jnp.concatenate(
        [src_ref[...].astype(jnp.float32), jnp.log2(src_mass_ref[...]), below], axis=0
    )
    half_ref[...] = jnp.where(odd == 0, src[:, :half], src[:, half:])
    below = jnp.zeros((half_ref.shape[0] - pcs - 1, tgt_ref.shape[1]), jnp.float32)
    whole_ref[...] = jnp.concatenate(
        [tgt_ref[...].astype(jnp.float32), jnp.log2(tgt_mass_ref[...]), below], axis=0
    )


def moment_kernel(coupling_ref, src_ref, tgt_ref, out_ref):
    src = padded(src_ref[...].astype(jnp.float32)).astype(jnp.bfloat16)
    tgt = padded(tgt_ref[...].astype(jnp.float32)).astype(jnp.bfloat16)
    twice = jnp.concatenate([src, src], axis=0)
    panel = jnp.dot(twice, coupling_ref[...], preferred_element_type=jnp.float32)
    moment = sum(
        lax.dot_general(tgt, part, (((1,), (1,)), ((), ())), preferred_element_type=jnp.float32)
        for part in pieces(panel)
    )
    lane = lax.broadcasted_iota(jnp.int32, (DEPTH // 2, LANES), 1)
    out_ref[...] = jnp.where(lane < DEPTH, moment[: DEPTH // 2], moment[DEPTH // 2 :])


def start_kernel(pcs, entries, merged, *refs):
    moment_ref, near_ref, far_ref = refs[:3]
    tgt_refs = refs[3 : 3 + merged]
    scores_ref, sums_ref, log_src_ref, log_tgt_ref, src_all, weights = refs[3 + merged :]
    blocks = moment_ref.shape[0]
    packed_rows = near_ref.shape[0] // blocks
    half = near_ref.shape[1]
    width = tgt_refs[0].shape[1]
    z = lax.axis_index("src")
    t = lax.axis_index("tgt")
    odd = lax.rem(t, 2)
    total_rows = 2 * half * blocks
    total_cols = width * lax.axis_size("tgt")

    packed = tree([moment_ref[b] for b in range(blocks)], jnp.add) * entries ** (-0.5)
    spread = jnp.sqrt(jnp.sum(packed * packed) * (1.0 / (pcs * pcs)) + tiny_eps)
    packed = packed / spread * (2.0 / (eps_reg * pcs) / LN2)
    turned = pltpu.roll(packed, DEPTH, axis=1)
    left = lax.broadcasted_iota(jnp.int32, packed.shape, 1) < DEPTH
    normed = jnp.concatenate(
        [jnp.where(left, packed, turned), jnp.where(left, turned, packed)], axis=0
    )
    normed = jnp.concatenate([normed, normed], axis=1)

    for b in range(blocks):
        place = jnp.bitwise_xor(z, b)
        for ref, side in ((near_ref, odd), (far_ref, 1 - odd)):
            block = ref[pl.ds(b * packed_rows, packed_rows), :]
            lanes = pl.ds(pl.multiple_of((place * 2 + side) * half, half), half)
            log_src_ref[:, lanes] = marg_power * (block[pcs : pcs + 1] + math.log2(total_cols))
            block = padded(block).astype(jnp.bfloat16)
            for copy in range(4):
                src_all[pl.ds(copy * DEPTH, DEPTH), lanes] = block

    parts = pieces(normed)
    first = lax.broadcasted_iota(jnp.int32, (width, LANES), 1) < DEPTH
    mine = lax.rem(lax.div(t, 2), merged)
    for b in range(merged):
        base = pl.multiple_of(jnp.bitwise_xor(mine, b) * width, width)
        turned = padded(tgt_refs[b][...]).T
        log_tgt_ref[pl.ds(base, width), :] = jnp.broadcast_to(
            marg_power * (turned[:, pcs : pcs + 1] + math.log2(total_rows)), (width, LANES)
        )
        turned = turned.astype(jnp.bfloat16)
        weighted = sum(jnp.dot(turned, part, preferred_element_type=jnp.float32) for part in parts)
        high, middle, low = pieces(weighted)
        weights[pl.ds(base, width), :LANES] = jnp.where(first, high[:, :LANES], middle[:, :LANES])
        weights[pl.ds(base, width), LANES:] = jnp.where(
            first, low[:, LANES:], jnp.zeros((width, LANES), jnp.bfloat16)
        )

    chunk, rows = 512, 256
    for left_lane in range(0, total_rows, chunk):
        lanes = pl.ds(left_lane, chunk)

        def step(i, carry, lanes=lanes):
            base = pl.multiple_of(i * rows, rows)
            block = jnp.dot(
                weights[pl.ds(base, rows), :], src_all[:, lanes], preferred_element_type=jnp.float32
            )
            scores_ref[pl.ds(base, rows), lanes] = block
            fresh = []
            for j in range(chunk // LANES):
                highest, summed = carry[j]
                terms = [block[g : g + 8, j * LANES : (j + 1) * LANES] for g in range(0, rows, 8)]
                fresh.append(running(highest, summed, terms))
            return tuple(fresh)

        carry = lax.fori_loop(0, scores_ref.shape[0] // rows, step, (unset(),) * (chunk // LANES))
        for j, state in enumerate(carry):
            sums_ref[:, pl.ds(left_lane + j * LANES, LANES)] = down(*state)


def unset():
    return (jnp.full((8, LANES), -jnp.inf, jnp.float32), jnp.zeros((8, LANES), jnp.float32))


def running(highest, summed, terms):
    fresh = jnp.maximum(highest, tree(terms, jnp.maximum))
    total = tree([jnp.exp2(term - fresh) for term in terms], jnp.add)
    return fresh, summed * jnp.exp2(highest - fresh) + total


def down(highest, summed):
    top = jnp.max(highest, axis=0, keepdims=True)
    return top + jnp.log2(jnp.sum(summed * jnp.exp2(highest - top), axis=0, keepdims=True))


def logsum(one, other):
    top = jnp.maximum(one, other)
    return top + jnp.log2(jnp.exp2(one - top) + jnp.exp2(other - top))


def row_values(log_src_ref, sums_ref, more_ref):
    return log_src_ref[...] - marg_power * logsum(sums_ref[...], more_ref[...])


def columns(scores_ref, rows_ref, log_tgt_ref, high_ref, sum_ref, base, count):
    tiles = scores_ref.shape[1] // LANES
    span = min(16, tiles)
    group = 4

    def scan(i, carry):
        for u in range(group):
            low = pl.multiple_of((i * group + u) * 8, 8)
            state = None
            for start in range(0, tiles, span):
                terms = [
                    scores_ref[pl.ds(pl.multiple_of(base + low, 8), 8), pl.ds(j * LANES, LANES)]
                    + rows_ref[:, pl.ds(j * LANES, LANES)]
                    for j in range(start, start + span)
                ]
                if state is None:
                    highest = tree(terms, jnp.maximum)
                    state = highest, tree([jnp.exp2(term - highest) for term in terms], jnp.add)
                else:
                    state = running(*state, terms)
            high_ref[pl.ds(low, 8), :], sum_ref[pl.ds(low, 8), :] = state
        return carry

    lax.fori_loop(0, count // (8 * group), scan, 0)
    part = 128

    def finish(i, carry):
        low = pl.multiple_of(i * part, part)
        highest = high_ref[pl.ds(low, part), :]
        top = jnp.max(highest, axis=1, keepdims=True)
        total = jnp.sum(sum_ref[pl.ds(low, part), :] * jnp.exp2(highest - top), axis=1, keepdims=True)
        high_ref[pl.ds(low, part), :] = log_tgt_ref[
            pl.ds(pl.multiple_of(base + low, part), part), :
        ] - marg_power * (top + jnp.log2(total))
        return carry

    lax.fori_loop(0, count // part, finish, 0)


def middle_kernel(scores_ref, sums_ref, more_ref, log_src_ref, log_tgt_ref, out_ref, rows_ref, high_ref, sum_ref):
    rows_ref[...] = jnp.broadcast_to(row_values(log_src_ref, sums_ref, more_ref), rows_ref.shape)
    cols, total = scores_ref.shape
    columns(scores_ref, rows_ref, log_tgt_ref, high_ref, sum_ref, 0, cols)
    beside, deep = 8, 16
    for start in range(0, total // LANES, beside):

        def step(i, carry, start=start):
            fresh = []
            base = i * (8 * deep)
            lows = [pl.multiple_of(base + 8 * g, 8) for g in range(deep)]
            potentials = [high_ref[pl.ds(low, 8), :] for low in lows]
            for j in range(beside):
                lanes = pl.ds((start + j) * LANES, LANES)
                terms = [scores_ref[pl.ds(low, 8), lanes] + c for low, c in zip(lows, potentials)]
                fresh.append(running(*carry[j], terms))
            return tuple(fresh)

        carry = lax.fori_loop(0, cols // (8 * deep), step, (unset(),) * beside)
        for j, state in enumerate(carry):
            out_ref[:, pl.ds((start + j) * LANES, LANES)] = down(*state)


def last_kernel(merged, scores_ref, sums_ref, more_ref, log_src_ref, log_tgt_ref, out_ref, row_ref, col_ref, rows_ref, high_ref, sum_ref):
    own_rows, own_cols = out_ref.shape
    rows = row_values(log_src_ref, sums_ref, more_ref)
    rows_ref[...] = jnp.broadcast_to(rows, rows_ref.shape)
    base = pl.multiple_of(lax.rem(lax.div(lax.axis_index("tgt"), 2), merged) * own_cols, own_cols)
    lanes = pl.ds(pl.multiple_of(lax.axis_index("src") * own_rows, own_rows), own_rows)
    columns(scores_ref, rows_ref, log_tgt_ref, high_ref, sum_ref, base, own_cols)
    row_ref[...] = rows_ref[0:1, lanes] * LN2
    col_ref[...] = high_ref[...].T[0:1, :] * LN2
    block = scores_ref[pl.ds(base, own_cols), lanes] + rows_ref[0:1, lanes] + high_ref[:, 0:1]
    out_ref[...] = (block * LN2).T


def swap(value, axis, offset):
    return lax.ppermute(value, axis, [(i, i ^ offset) for i in range(lax.axis_size(axis))])


def everyone(value, axis):
    size = lax.axis_size(axis)
    copies = jnp.broadcast_to(value[None], (size, *value.shape))
    return lax.all_to_all(copies, axis, 0, 0)


def shards(coupling, src_pcs, tgt_pcs, src_mass, tgt_mass):
    f32 = jnp.float32
    pcs = src_pcs.shape[0]
    rows, cols = coupling.shape
    src_size, tgt_size = lax.axis_size("src"), lax.axis_size("tgt")
    total_rows, total_cols = rows * src_size, cols * tgt_size
    merged = 1
    while 2 * merged * 2 <= tgt_size and 2 * merged * cols * total_rows * 4 <= SCORES_BYTES:
        merged *= 2
    wide = merged * cols
    packed_rows = -(-(pcs + 1) // 8) * 8

    half, whole = pl.pallas_call(
        pack_kernel,
        out_shape=(
            jax.ShapeDtypeStruct((packed_rows, rows // 2), f32),
            jax.ShapeDtypeStruct((packed_rows, cols), f32),
        ),
        in_specs=[VMEM] * 4,
        out_specs=(VMEM, VMEM),
        compiler_params=params(8),
    )(src_pcs, tgt_pcs, src_mass.reshape(1, -1), tgt_mass.reshape(1, -1))
    moment = pl.pallas_call(
        moment_kernel,
        out_shape=jax.ShapeDtypeStruct((DEPTH // 2, LANES), f32),
        in_specs=[VMEM] * 3,
        out_specs=VMEM,
        compiler_params=params(8),
    )(coupling, src_pcs, tgt_pcs)

    near = jnp.concatenate([half] + [swap(half, "src", b) for b in range(1, src_size)], axis=0)
    targets = [whole] + [swap(whole, "tgt", 2 * b) for b in range(1, merged)]
    moment = jnp.sum(everyone(moment, "tgt"), axis=0)
    moments = everyone(moment, "src")
    far = swap(near, "tgt", 1)

    scores, sums, log_src, log_tgt = pl.pallas_call(
        functools.partial(start_kernel, pcs, total_rows * total_cols, merged),
        out_shape=(
            jax.ShapeDtypeStruct((wide, total_rows), f32),
            jax.ShapeDtypeStruct((1, total_rows), f32),
            jax.ShapeDtypeStruct((1, total_rows), f32),
            jax.ShapeDtypeStruct((wide, LANES), f32),
        ),
        in_specs=[VMEM] * (3 + merged),
        out_specs=(VMEM,) * 4,
        scratch_shapes=[
            pltpu.VMEM((4 * DEPTH, total_rows), jnp.bfloat16),
            pltpu.VMEM((wide, 4 * DEPTH), jnp.bfloat16),
        ],
        compiler_params=params(16),
    )(moments, near, far, *targets)

    def both(value):
        offset = 2 * merged
        while offset < tgt_size:
            value = logsum(value, swap(value, "tgt", offset))
            offset *= 2
        return value, swap(value, "tgt", 1)

    for iteration in range(ITERS - 1):
        sums = pl.pallas_call(
            middle_kernel,
            out_shape=jax.ShapeDtypeStruct((1, total_rows), f32),
            in_specs=[VMEM] * 5,
            out_specs=VMEM,
            scratch_shapes=[
                pltpu.VMEM((8, total_rows), f32),
                pltpu.VMEM((wide, LANES), f32),
                pltpu.VMEM((wide, LANES), f32),
            ],
            compiler_params=params(12),
        )(scores, *both(sums), log_src, log_tgt)

    log_coupling, row_potential, col_potential = pl.pallas_call(
        functools.partial(last_kernel, merged),
        out_shape=(
            jax.ShapeDtypeStruct((rows, cols), f32),
            jax.ShapeDtypeStruct((1, rows), f32),
            jax.ShapeDtypeStruct((1, cols), f32),
        ),
        in_specs=[VMEM] * 5,
        out_specs=(VMEM,) * 3,
        scratch_shapes=[
            pltpu.VMEM((8, total_rows), f32),
            pltpu.VMEM((cols, LANES), f32),
            pltpu.VMEM((cols, LANES), f32),
        ],
        compiler_params=params(12),
    )(scores, *both(sums), log_src, log_tgt)
    return log_coupling, row_potential.reshape(-1), col_potential.reshape(-1)


def solution(mesh):
    in_specs = (P("src", "tgt"), P(None, "src"), P(None, "tgt"), P("src"), P("tgt"))
    out_specs = (P("src", "tgt"), P("src"), P("tgt"))
    return jax.shard_map(shards, mesh=mesh, in_specs=in_specs, out_specs=out_specs, check_vma=False)
```

```python
import functools
import math

import jax
import jax.numpy as jnp
from jax import lax
from jax.experimental import pallas as pl
from jax.experimental.pallas import tpu as pltpu
from jax.sharding import PartitionSpec as P

ITERS = 4

eps_reg = 0.5
marg_power = 1.0 / (1.0 + eps_reg)
tiny_eps = 1e-06

LANES = 128
DEPTH = 64
LN2 = math.log(2.0)
SCORES_BYTES = 1 << 24
VMEM = pl.BlockSpec(memory_space=pltpu.VMEM)


def params(mib):
    return pltpu.CompilerParams(vmem_limit_bytes=mib << 20)


def tree(values, combine):
    values = list(values)
    while len(values) > 1:
        paired = [combine(values[i], values[i + 1]) for i in range(0, len(values) - 1, 2)]
        values = paired + ([values[-1]] if len(values) % 2 else [])
    return values[0]


def pieces(value):
    high = value.astype(jnp.bfloat16)
    rest = value - high.astype(jnp.float32)
    middle = rest.astype(jnp.bfloat16)
    low = (rest - middle.astype(jnp.float32)).astype(jnp.bfloat16)
    return high, middle, low


def padded(value):
    return jnp.concatenate(
        [value, jnp.zeros((DEPTH - value.shape[0], value.shape[1]), value.dtype)], axis=0
    )


def front_kernel(*refs):
    sources, (half_ref, whole_ref, moment_ref), local, sems = refs[:5], refs[5:8], refs[8:13], refs[13]
    copies = [pltpu.make_async_copy(a, b, sems.at[i]) for i, (a, b) in enumerate(zip(sources, local))]
    for copy in copies:
        copy.start()
    coupling_ref, src_ref, tgt_ref, src_mass_ref, tgt_mass_ref = local
    pcs = src_ref.shape[0]
    half = half_ref.shape[1]
    odd = lax.rem(lax.axis_index("tgt"), 2)
    for copy in copies[1:]:
        copy.wait()
    src = src_ref[...].astype(jnp.float32)
    tgt = tgt_ref[...].astype(jnp.float32)
    below = jnp.zeros((half_ref.shape[0] - pcs - 1, 2 * half), jnp.float32)
    joined = jnp.concatenate([src, jnp.log2(src_mass_ref[...]), below], axis=0)
    half_ref[...] = jnp.where(odd == 0, joined[:, :half], joined[:, half:])
    below = jnp.zeros((half_ref.shape[0] - pcs - 1, tgt.shape[1]), jnp.float32)
    whole_ref[...] = jnp.concatenate([tgt, jnp.log2(tgt_mass_ref[...]), below], axis=0)
    src = padded(src).astype(jnp.bfloat16)
    tgt = padded(tgt).astype(jnp.bfloat16)
    twice = jnp.concatenate([src, src], axis=0)
    copies[0].wait()
    panel = jnp.dot(twice, coupling_ref[...], preferred_element_type=jnp.float32)
    moment = sum(
        lax.dot_general(tgt, part, (((1,), (1,)), ((), ())), preferred_element_type=jnp.float32)
        for part in pieces(panel)
    )
    lane = lax.broadcasted_iota(jnp.int32, (DEPTH // 2, LANES), 1)
    moment_ref[...] = jnp.where(lane < DEPTH, moment[: DEPTH // 2], moment[DEPTH // 2 :])


def start_kernel(pcs, entries, merged, blocks, *refs):
    near_ref, far_ref = refs[:2]
    tgt_refs = refs[2 : 2 + merged.bit_length()]
    moment_refs = refs[2 + merged.bit_length() : -6]
    scores_ref, sums_ref, log_src_ref, log_tgt_ref, src_all, weights = refs[-6:]
    packed_rows = near_ref.shape[0] // blocks
    half = near_ref.shape[1]
    width = tgt_refs[0].shape[1]
    targets = [ref.at[pl.ds(i, packed_rows), :] for ref in tgt_refs for i in range(0, ref.shape[0], packed_rows)]
    z = lax.axis_index("src")
    t = lax.axis_index("tgt")
    odd = lax.rem(t, 2)
    total_rows = 2 * half * blocks
    total_cols = width * lax.axis_size("tgt")

    packed = tree([ref[...] for ref in moment_refs], jnp.add) * entries ** (-0.5)
    spread = jnp.sqrt(jnp.sum(packed * packed) * (1.0 / (pcs * pcs)) + tiny_eps)
    packed = packed / spread * (2.0 / (eps_reg * pcs) / LN2)
    turned = pltpu.roll(packed, DEPTH, axis=1)
    left = lax.broadcasted_iota(jnp.int32, packed.shape, 1) < DEPTH
    normed = jnp.concatenate(
        [jnp.where(left, packed, turned), jnp.where(left, turned, packed)], axis=0
    )
    normed = jnp.concatenate([normed, normed], axis=1)

    for b in range(blocks):
        place = jnp.bitwise_xor(z, b)
        for ref, side in ((near_ref, odd), (far_ref, 1 - odd)):
            block = ref[pl.ds(b * packed_rows, packed_rows), :]
            lanes = pl.ds(pl.multiple_of((place * 2 + side) * half, half), half)
            log_src_ref[:, lanes] = marg_power * (block[pcs : pcs + 1] + math.log2(total_cols))
            block = padded(block).astype(jnp.bfloat16)
            for copy in range(4):
                src_all[pl.ds(copy * DEPTH, DEPTH), lanes] = block

    parts = pieces(normed)
    first = lax.broadcasted_iota(jnp.int32, (width, LANES), 1) < DEPTH
    mine = lax.rem(lax.div(t, 2), merged)
    for b in range(merged):
        base = pl.multiple_of(jnp.bitwise_xor(mine, b) * width, width)
        turned = padded(targets[b][...]).T
        log_tgt_ref[pl.ds(base, width), :] = jnp.broadcast_to(
            marg_power * (turned[:, pcs : pcs + 1] + math.log2(total_rows)), (width, LANES)
        )
        turned = turned.astype(jnp.bfloat16)
        weighted = sum(jnp.dot(turned, part, preferred_element_type=jnp.float32) for part in parts)
        high, middle, low = pieces(weighted)
        weights[pl.ds(base, width), :LANES] = jnp.where(first, high[:, :LANES], middle[:, :LANES])
        weights[pl.ds(base, width), LANES:] = jnp.where(
            first, low[:, LANES:], jnp.zeros((width, LANES), jnp.bfloat16)
        )

    chunk, rows = 512, 256
    for left_lane in range(0, total_rows, chunk):
        lanes = pl.ds(left_lane, chunk)

        def step(i, carry, lanes=lanes):
            base = pl.multiple_of(i * rows, rows)
            block = jnp.dot(
                weights[pl.ds(base, rows), :], src_all[:, lanes], preferred_element_type=jnp.float32
            )
            scores_ref[pl.ds(base, rows), lanes] = block
            fresh = []
            for j in range(chunk // LANES):
                highest, summed = carry[j]
                terms = [block[g : g + 8, j * LANES : (j + 1) * LANES] for g in range(0, rows, 8)]
                fresh.append(running(highest, summed, terms))
            return tuple(fresh)

        carry = lax.fori_loop(0, scores_ref.shape[0] // rows, step, (unset(),) * (chunk // LANES))
        for j, state in enumerate(carry):
            sums_ref[:, pl.ds(left_lane + j * LANES, LANES)] = down(*state)


def unset():
    return (jnp.full((8, LANES), -jnp.inf, jnp.float32), jnp.zeros((8, LANES), jnp.float32))


def running(highest, summed, terms):
    fresh = jnp.maximum(highest, tree(terms, jnp.maximum))
    total = tree([jnp.exp2(term - fresh) for term in terms], jnp.add)
    return fresh, summed * jnp.exp2(highest - fresh) + total


def down(highest, summed):
    top = jnp.max(highest, axis=0, keepdims=True)
    return top + jnp.log2(jnp.sum(summed * jnp.exp2(highest - top), axis=0, keepdims=True))


def logsum(one, other):
    top = jnp.maximum(one, other)
    return top + jnp.log2(jnp.exp2(one - top) + jnp.exp2(other - top))


def row_values(log_src_ref, sums_ref, more_ref):
    return log_src_ref[...] - marg_power * logsum(sums_ref[...], more_ref[...])


def columns(scores_ref, rows_ref, log_tgt_ref, high_ref, sum_ref, base, count):
    tiles = scores_ref.shape[1] // LANES
    span = min(16, tiles)
    unroll = 4

    groups = count // 8

    def load(g, start):
        low = pl.multiple_of(base + jnp.minimum(g, groups - 1) * 8, 8)
        return [
            scores_ref[pl.ds(low, 8), pl.ds(j * LANES, LANES)] + rows_ref[:, pl.ds(j * LANES, LANES)]
            for j in range(start, start + span)
        ]

    def scan(i, carry):
        terms, highest = carry
        for u in range(unroll):
            g = i * unroll + u
            state = None
            for start in range(0, tiles, span):
                last = start + span == tiles
                ahead = load(g + 1, 0) if last else load(g, start + span)
                ahead_highest = tree(ahead, jnp.maximum)
                if state is None:
                    state = highest, tree([jnp.exp2(term - highest) for term in terms], jnp.add)
                else:
                    state = running(*state, terms)
                terms, highest = ahead, ahead_highest
            low = pl.multiple_of(g * 8, 8)
            high_ref[pl.ds(low, 8), :], sum_ref[pl.ds(low, 8), :] = state
        return tuple(terms), highest

    terms = load(0, 0)
    lax.fori_loop(0, groups // unroll, scan, (tuple(terms), tree(terms, jnp.maximum)))
    part = 128

    def finish(i, carry):
        low = pl.multiple_of(i * part, part)
        highest = high_ref[pl.ds(low, part), :]
        top = jnp.max(highest, axis=1, keepdims=True)
        total = jnp.sum(sum_ref[pl.ds(low, part), :] * jnp.exp2(highest - top), axis=1, keepdims=True)
        high_ref[pl.ds(low, part), :] = log_tgt_ref[
            pl.ds(pl.multiple_of(base + low, part), part), :
        ] - marg_power * (top + jnp.log2(total))
        return carry

    lax.fori_loop(0, count // part, finish, 0)


def middle_kernel(scores_ref, sums_ref, more_ref, log_src_ref, log_tgt_ref, out_ref, rows_ref, high_ref, sum_ref):
    rows_ref[...] = jnp.broadcast_to(row_values(log_src_ref, sums_ref, more_ref), rows_ref.shape)
    cols, total = scores_ref.shape
    columns(scores_ref, rows_ref, log_tgt_ref, high_ref, sum_ref, 0, cols)
    beside, deep = 8, 8
    for start in range(0, total // LANES, beside):

        def step(i, carry, start=start):
            fresh = []
            base = i * (8 * deep)
            lows = [pl.multiple_of(base + 8 * g, 8) for g in range(deep)]
            potentials = [high_ref[pl.ds(low, 8), :] for low in lows]

            def load(j):
                lanes = pl.ds((start + j) * LANES, LANES)
                terms = [scores_ref[pl.ds(low, 8), lanes] + c for low, c in zip(lows, potentials)]
                return terms, jnp.maximum(carry[j][0], tree(terms, jnp.maximum))

            ahead = load(0)
            for j in range(beside):
                terms, highest = ahead
                if j + 1 < beside:
                    ahead = load(j + 1)
                total = tree([jnp.exp2(term - highest) for term in terms], jnp.add)
                fresh.append((highest, carry[j][1] * jnp.exp2(carry[j][0] - highest) + total))
            return tuple(fresh)

        carry = lax.fori_loop(0, cols // (8 * deep), step, (unset(),) * beside)
        for j, state in enumerate(carry):
            out_ref[:, pl.ds((start + j) * LANES, LANES)] = down(*state)


def last_kernel(merged, scores_ref, sums_ref, more_ref, log_src_ref, log_tgt_ref, out_ref, row_ref, col_ref, rows_ref, high_ref, sum_ref):
    own_rows, own_cols = out_ref.shape
    rows = row_values(log_src_ref, sums_ref, more_ref)
    rows_ref[...] = jnp.broadcast_to(rows, rows_ref.shape)
    base = pl.multiple_of(lax.rem(lax.div(lax.axis_index("tgt"), 2), merged) * own_cols, own_cols)
    lanes = pl.ds(pl.multiple_of(lax.axis_index("src") * own_rows, own_rows), own_rows)
    columns(scores_ref, rows_ref, log_tgt_ref, high_ref, sum_ref, base, own_cols)
    row_ref[...] = rows_ref[0:1, lanes] * LN2
    col_ref[...] = high_ref[...].T[0:1, :] * LN2
    block = scores_ref[pl.ds(base, own_cols), lanes] + rows_ref[0:1, lanes] + high_ref[:, 0:1]
    out_ref[...] = (block * LN2).T


def swap(value, axis, offset):
    return lax.ppermute(value, axis, [(i, i ^ offset) for i in range(lax.axis_size(axis))])


def staged_parts(value, axis, low, width):
    size = lax.axis_size(axis)
    terms = [value]
    while low < size:
        span = min(width, size // low)
        value = tree(terms, jnp.add)
        terms = [value] + [swap(value, axis, low * j) for j in range(1, span)]
        low *= span
    return terms


def more(held, axis, low, goal):
    unit = held[0].shape[0]
    while sum(part.shape[0] for part in held) < goal * unit:
        known = held[0] if len(held) == 1 else jnp.concatenate(held, axis=0)
        held.append(swap(known, axis, low * known.shape[0] // unit))


def shards(coupling, src_pcs, tgt_pcs, src_mass, tgt_mass):
    f32 = jnp.float32
    pcs = src_pcs.shape[0]
    rows, cols = coupling.shape
    src_size, tgt_size = lax.axis_size("src"), lax.axis_size("tgt")
    total_rows, total_cols = rows * src_size, cols * tgt_size
    merged = 1
    while 2 * merged * 2 <= tgt_size and 2 * merged * cols * total_rows * 4 <= SCORES_BYTES:
        merged *= 2
    wide = merged * cols
    packed_rows = -(-(pcs + 1) // 8) * 8

    arguments = (coupling, src_pcs, tgt_pcs, src_mass.reshape(1, -1), tgt_mass.reshape(1, -1))
    half, whole, moment = pl.pallas_call(
        front_kernel,
        out_shape=(
            jax.ShapeDtypeStruct((packed_rows, rows // 2), f32),
            jax.ShapeDtypeStruct((packed_rows, cols), f32),
            jax.ShapeDtypeStruct((DEPTH // 2, LANES), f32),
        ),
        in_specs=[pl.BlockSpec(memory_space=pltpu.HBM)] * 5,
        out_specs=(VMEM,) * 3,
        scratch_shapes=[pltpu.VMEM(a.shape, a.dtype) for a in arguments]
        + [pltpu.SemaphoreType.DMA((5,))],
        compiler_params=params(60),
    )(*arguments)

    moment = moment + swap(moment, "tgt", 1)
    half, whole, moment = lax.optimization_barrier((half, whole, moment))
    parts = staged_parts(moment, "tgt", 2, 4)
    sources, targets = [half], [whole]
    more(sources, "src", 1, 2)
    more(targets, "tgt", 2, min(2, merged))
    parts, sources, targets = lax.optimization_barrier((parts, sources, targets))
    moments = staged_parts(tree(parts, jnp.add), "src", 1, 4)
    more(sources, "src", 1, src_size)
    more(targets, "tgt", 2, merged)
    sources, moments = lax.optimization_barrier((sources, moments))
    near = jnp.concatenate(sources, axis=0)
    far = swap(near, "tgt", 1)

    scores, sums, log_src, log_tgt = pl.pallas_call(
        functools.partial(start_kernel, pcs, total_rows * total_cols, merged, src_size),
        out_shape=(
            jax.ShapeDtypeStruct((wide, total_rows), f32),
            jax.ShapeDtypeStruct((1, total_rows), f32),
            jax.ShapeDtypeStruct((1, total_rows), f32),
            jax.ShapeDtypeStruct((wide, LANES), f32),
        ),
        in_specs=[VMEM] * (2 + len(targets) + len(moments)),
        out_specs=(VMEM,) * 4,
        scratch_shapes=[
            pltpu.VMEM((4 * DEPTH, total_rows), jnp.bfloat16),
            pltpu.VMEM((wide, 4 * DEPTH), jnp.bfloat16),
        ],
        compiler_params=params(16),
    )(near, far, *targets, *moments)

    def both(value):
        offset = 2 * merged
        while offset < tgt_size:
            value = logsum(value, swap(value, "tgt", offset))
            offset *= 2
        return value, swap(value, "tgt", 1)

    for iteration in range(ITERS - 1):
        sums = pl.pallas_call(
            middle_kernel,
            out_shape=jax.ShapeDtypeStruct((1, total_rows), f32),
            in_specs=[VMEM] * 5,
            out_specs=VMEM,
            scratch_shapes=[
                pltpu.VMEM((8, total_rows), f32),
                pltpu.VMEM((wide, LANES), f32),
                pltpu.VMEM((wide, LANES), f32),
            ],
            compiler_params=params(12),
        )(scores, *both(sums), log_src, log_tgt)

    log_coupling, row_potential, col_potential = pl.pallas_call(
        functools.partial(last_kernel, merged),
        out_shape=(
            jax.ShapeDtypeStruct((rows, cols), f32),
            jax.ShapeDtypeStruct((1, rows), f32),
            jax.ShapeDtypeStruct((1, cols), f32),
        ),
        in_specs=[VMEM] * 5,
        out_specs=(VMEM,) * 3,
        scratch_shapes=[
            pltpu.VMEM((8, total_rows), f32),
            pltpu.VMEM((cols, LANES), f32),
            pltpu.VMEM((cols, LANES), f32),
        ],
        compiler_params=params(12),
    )(scores, *both(sums), log_src, log_tgt)
    return log_coupling, row_potential.reshape(-1), col_potential.reshape(-1)


def solution(mesh):
    in_specs = (P("src", "tgt"), P(None, "src"), P(None, "tgt"), P("src"), P("tgt"))
    out_specs = (P("src", "tgt"), P("src"), P("tgt"))
    return jax.shard_map(shards, mesh=mesh, in_specs=in_specs, out_specs=out_specs, check_vma=False)
```

```python
import functools
import math

import jax
import jax.numpy as jnp
from jax import lax
from jax.experimental import pallas as pl
from jax.experimental.pallas import tpu as pltpu
from jax.sharding import PartitionSpec as P

ITERS = 4

eps_reg = 0.5
marg_power = 1.0 / (1.0 + eps_reg)
tiny_eps = 1e-06

LANES = 128
DEPTH = 64
SCORES_BYTES = 1 << 24
VMEM = pl.BlockSpec(memory_space=pltpu.VMEM)


def params(mib):
    return pltpu.CompilerParams(vmem_limit_bytes=mib << 20)


def tree(values, combine):
    values = list(values)
    while len(values) > 1:
        paired = [combine(values[i], values[i + 1]) for i in range(0, len(values) - 1, 2)]
        values = paired + ([values[-1]] if len(values) % 2 else [])
    return values[0]


def pieces(value):
    high = value.astype(jnp.bfloat16)
    rest = value - high.astype(jnp.float32)
    middle = rest.astype(jnp.bfloat16)
    low = (rest - middle.astype(jnp.float32)).astype(jnp.bfloat16)
    return high, middle, low


def padded(value):
    return jnp.concatenate(
        [value, jnp.zeros((DEPTH - value.shape[0], value.shape[1]), value.dtype)], axis=0
    )


def front_kernel(*refs):
    sources, (half_ref, whole_ref, moment_ref), local, sems = refs[:5], refs[5:8], refs[8:13], refs[13]
    copies = [pltpu.make_async_copy(a, b, sems.at[i]) for i, (a, b) in enumerate(zip(sources, local))]
    for copy in copies:
        copy.start()
    coupling_ref, src_ref, tgt_ref, src_mass_ref, tgt_mass_ref = local
    pcs = src_ref.shape[0]
    half = half_ref.shape[1]
    odd = lax.rem(lax.axis_index("tgt"), 2)
    for copy in copies[1:]:
        copy.wait()
    src = src_ref[...].astype(jnp.float32)
    tgt = tgt_ref[...].astype(jnp.float32)
    below = jnp.zeros((half_ref.shape[0] - pcs - 1, 2 * half), jnp.float32)
    joined = jnp.concatenate([src, jnp.log(src_mass_ref[...]), below], axis=0)
    half_ref[...] = jnp.where(odd == 0, joined[:, :half], joined[:, half:])
    below = jnp.zeros((half_ref.shape[0] - pcs - 1, tgt.shape[1]), jnp.float32)
    whole_ref[...] = jnp.concatenate([tgt, jnp.log(tgt_mass_ref[...]), below], axis=0)
    src = padded(src).astype(jnp.bfloat16)
    tgt = padded(tgt).astype(jnp.bfloat16)
    twice = jnp.concatenate([src, src], axis=0)
    copies[0].wait()
    panel = jnp.dot(twice, coupling_ref[...], preferred_element_type=jnp.float32)
    moment = sum(
        lax.dot_general(tgt, part, (((1,), (1,)), ((), ())), preferred_element_type=jnp.float32)
        for part in pieces(panel)
    )
    lane = lax.broadcasted_iota(jnp.int32, (DEPTH // 2, LANES), 1)
    moment_ref[...] = jnp.where(lane < DEPTH, moment[: DEPTH // 2], moment[DEPTH // 2 :])


def start_kernel(pcs, entries, merged, blocks, *refs):
    near_ref, far_ref = refs[:2]
    tgt_refs = refs[2 : 2 + merged.bit_length()]
    moment_refs = refs[2 + merged.bit_length() : -6]
    scores_ref, sums_ref, log_src_ref, log_tgt_ref, src_all, weights = refs[-6:]
    packed_rows = near_ref.shape[0] // blocks
    half = near_ref.shape[1]
    width = tgt_refs[0].shape[1]
    targets = [ref.at[pl.ds(i, packed_rows), :] for ref in tgt_refs for i in range(0, ref.shape[0], packed_rows)]
    z = lax.axis_index("src")
    t = lax.axis_index("tgt")
    odd = lax.rem(t, 2)
    total_rows = 2 * half * blocks
    total_cols = width * lax.axis_size("tgt")

    packed = tree([ref[...] for ref in moment_refs], jnp.add) * entries ** (-0.5)
    spread = jnp.sqrt(jnp.sum(packed * packed) * (1.0 / (pcs * pcs)) + tiny_eps)
    packed = packed / spread * (2.0 / (eps_reg * pcs))
    turned = pltpu.roll(packed, DEPTH, axis=1)
    left = lax.broadcasted_iota(jnp.int32, packed.shape, 1) < DEPTH
    normed = jnp.concatenate(
        [jnp.where(left, packed, turned), jnp.where(left, turned, packed)], axis=0
    )
    normed = jnp.concatenate([normed, normed], axis=1)

    for b in range(blocks):
        place = jnp.bitwise_xor(z, b)
        for ref, side in ((near_ref, odd), (far_ref, 1 - odd)):
            block = ref[pl.ds(b * packed_rows, packed_rows), :]
            lanes = pl.ds(pl.multiple_of((place * 2 + side) * half, half), half)
            log_src_ref[:, lanes] = marg_power * (block[pcs : pcs + 1] + math.log(total_cols))
            block = padded(block).astype(jnp.bfloat16)
            for copy in range(4):
                src_all[pl.ds(copy * DEPTH, DEPTH), lanes] = block

    parts = pieces(normed)
    first = lax.broadcasted_iota(jnp.int32, (width, LANES), 1) < DEPTH
    mine = lax.rem(lax.div(t, 2), merged)
    for b in range(merged):
        base = pl.multiple_of(jnp.bitwise_xor(mine, b) * width, width)
        turned = padded(targets[b][...]).T
        log_tgt_ref[pl.ds(base, width), :] = jnp.broadcast_to(
            marg_power * (turned[:, pcs : pcs + 1] + math.log(total_rows)), (width, LANES)
        )
        turned = turned.astype(jnp.bfloat16)
        weighted = sum(jnp.dot(turned, part, preferred_element_type=jnp.float32) for part in parts)
        high, middle, low = pieces(weighted)
        weights[pl.ds(base, width), :LANES] = jnp.where(first, high[:, :LANES], middle[:, :LANES])
        weights[pl.ds(base, width), LANES:] = jnp.where(
            first, low[:, LANES:], jnp.zeros((width, LANES), jnp.bfloat16)
        )

    chunk, rows = 512, 256
    for left_lane in range(0, total_rows, chunk):
        lanes = pl.ds(left_lane, chunk)

        def step(i, carry, lanes=lanes):
            base = pl.multiple_of(i * rows, rows)
            block = jnp.dot(
                weights[pl.ds(base, rows), :], src_all[:, lanes], preferred_element_type=jnp.float32
            )
            scores_ref[pl.ds(base, rows), lanes] = block
            fresh = []
            for j in range(chunk // LANES):
                highest, summed = carry[j]
                terms = [block[g : g + 8, j * LANES : (j + 1) * LANES] for g in range(0, rows, 8)]
                fresh.append(running(highest, summed, terms))
            return tuple(fresh)

        carry = lax.fori_loop(0, scores_ref.shape[0] // rows, step, (unset(),) * (chunk // LANES))
        for j, state in enumerate(carry):
            sums_ref[:, pl.ds(left_lane + j * LANES, LANES)] = down(*state)


def unset():
    return (jnp.full((8, LANES), -jnp.inf, jnp.float32), jnp.zeros((8, LANES), jnp.float32))


def running(highest, summed, terms):
    fresh = jnp.maximum(highest, tree(terms, jnp.maximum))
    total = tree([jnp.exp(term - fresh) for term in terms], jnp.add)
    return fresh, summed * jnp.exp(highest - fresh) + total


def down(highest, summed):
    top = jnp.max(highest, axis=0, keepdims=True)
    return top + jnp.log(jnp.sum(summed * jnp.exp(highest - top), axis=0, keepdims=True))


def logsum(one, other):
    top = jnp.maximum(one, other)
    return top + jnp.log(jnp.exp(one - top) + jnp.exp(other - top))


def row_values(log_src_ref, sums_ref, more_ref):
    return log_src_ref[...] - marg_power * logsum(sums_ref[...], more_ref[...])


def columns(scores_ref, rows_ref, log_tgt_ref, high_ref, sum_ref, base, count):
    tiles = scores_ref.shape[1] // LANES
    span = min(16, tiles)
    unroll = 4

    groups = count // 8

    def load(g, start):
        low = pl.multiple_of(base + jnp.minimum(g, groups - 1) * 8, 8)
        return [
            scores_ref[pl.ds(low, 8), pl.ds(j * LANES, LANES)] + rows_ref[:, pl.ds(j * LANES, LANES)]
            for j in range(start, start + span)
        ]

    def scan(i, carry):
        terms, highest = carry
        for u in range(unroll):
            g = i * unroll + u
            state = None
            for start in range(0, tiles, span):
                last = start + span == tiles
                ahead = load(g + 1, 0) if last else load(g, start + span)
                ahead_highest = tree(ahead, jnp.maximum)
                if state is None:
                    state = highest, tree([jnp.exp(term - highest) for term in terms], jnp.add)
                else:
                    state = running(*state, terms)
                terms, highest = ahead, ahead_highest
            low = pl.multiple_of(g * 8, 8)
            high_ref[pl.ds(low, 8), :], sum_ref[pl.ds(low, 8), :] = state
        return tuple(terms), highest

    terms = load(0, 0)
    lax.fori_loop(0, groups // unroll, scan, (tuple(terms), tree(terms, jnp.maximum)))
    part = 128

    def finish(i, carry):
        low = pl.multiple_of(i * part, part)
        highest = high_ref[pl.ds(low, part), :]
        top = jnp.max(highest, axis=1, keepdims=True)
        total = jnp.sum(sum_ref[pl.ds(low, part), :] * jnp.exp(highest - top), axis=1, keepdims=True)
        high_ref[pl.ds(low, part), :] = log_tgt_ref[
            pl.ds(pl.multiple_of(base + low, part), part), :
        ] - marg_power * (top + jnp.log(total))
        return carry

    lax.fori_loop(0, count // part, finish, 0)


def middle_kernel(scores_ref, sums_ref, more_ref, log_src_ref, log_tgt_ref, out_ref, rows_ref, high_ref, sum_ref):
    rows_ref[...] = jnp.broadcast_to(row_values(log_src_ref, sums_ref, more_ref), rows_ref.shape)
    cols, total = scores_ref.shape
    columns(scores_ref, rows_ref, log_tgt_ref, high_ref, sum_ref, 0, cols)
    beside, deep = 8, 8
    for start in range(0, total // LANES, beside):

        def step(i, carry, start=start):
            fresh = []
            base = i * (8 * deep)
            lows = [pl.multiple_of(base + 8 * g, 8) for g in range(deep)]
            potentials = [high_ref[pl.ds(low, 8), :] for low in lows]

            def load(j):
                lanes = pl.ds((start + j) * LANES, LANES)
                terms = [scores_ref[pl.ds(low, 8), lanes] + c for low, c in zip(lows, potentials)]
                return terms, jnp.maximum(carry[j][0], tree(terms, jnp.maximum))

            ahead = load(0)
            for j in range(beside):
                terms, highest = ahead
                if j + 1 < beside:
                    ahead = load(j + 1)
                total = tree([jnp.exp(term - highest) for term in terms], jnp.add)
                fresh.append((highest, carry[j][1] * jnp.exp(carry[j][0] - highest) + total))
            return tuple(fresh)

        carry = lax.fori_loop(0, cols // (8 * deep), step, (unset(),) * beside)
        for j, state in enumerate(carry):
            out_ref[:, pl.ds((start + j) * LANES, LANES)] = down(*state)


def last_kernel(merged, scores_ref, sums_ref, more_ref, log_src_ref, log_tgt_ref, out_ref, row_ref, col_ref, rows_ref, high_ref, sum_ref):
    own_rows, own_cols = out_ref.shape
    rows = row_values(log_src_ref, sums_ref, more_ref)
    rows_ref[...] = jnp.broadcast_to(rows, rows_ref.shape)
    base = pl.multiple_of(lax.rem(lax.div(lax.axis_index("tgt"), 2), merged) * own_cols, own_cols)
    lanes = pl.ds(pl.multiple_of(lax.axis_index("src") * own_rows, own_rows), own_rows)
    columns(scores_ref, rows_ref, log_tgt_ref, high_ref, sum_ref, base, own_cols)
    row_ref[...] = rows_ref[0:1, lanes]
    col_ref[...] = high_ref[...].T[0:1, :]
    block = scores_ref[pl.ds(base, own_cols), lanes] + rows_ref[0:1, lanes] + high_ref[:, 0:1]
    out_ref[...] = block.T


def swap(value, axis, offset):
    return lax.ppermute(value, axis, [(i, i ^ offset) for i in range(lax.axis_size(axis))])


def staged_parts(value, axis, low, width):
    size = lax.axis_size(axis)
    terms = [value]
    while low < size:
        span = min(width, size // low)
        value = tree(terms, jnp.add)
        terms = [value] + [swap(value, axis, low * j) for j in range(1, span)]
        low *= span
    return terms


def more(held, axis, low, goal):
    unit = held[0].shape[0]
    while sum(part.shape[0] for part in held) < goal * unit:
        known = held[0] if len(held) == 1 else jnp.concatenate(held, axis=0)
        held.append(swap(known, axis, low * known.shape[0] // unit))


def shards(coupling, src_pcs, tgt_pcs, src_mass, tgt_mass):
    f32 = jnp.float32
    pcs = src_pcs.shape[0]
    rows, cols = coupling.shape
    src_size, tgt_size = lax.axis_size("src"), lax.axis_size("tgt")
    total_rows, total_cols = rows * src_size, cols * tgt_size
    merged = 1
    while 2 * merged * 2 <= tgt_size and 2 * merged * cols * total_rows * 4 <= SCORES_BYTES:
        merged *= 2
    wide = merged * cols
    packed_rows = -(-(pcs + 1) // 8) * 8

    arguments = (coupling, src_pcs, tgt_pcs, src_mass.reshape(1, -1), tgt_mass.reshape(1, -1))
    half, whole, moment = pl.pallas_call(
        front_kernel,
        out_shape=(
            jax.ShapeDtypeStruct((packed_rows, rows // 2), f32),
            jax.ShapeDtypeStruct((packed_rows, cols), f32),
            jax.ShapeDtypeStruct((DEPTH // 2, LANES), f32),
        ),
        in_specs=[pl.BlockSpec(memory_space=pltpu.HBM)] * 5,
        out_specs=(VMEM,) * 3,
        scratch_shapes=[pltpu.VMEM(a.shape, a.dtype) for a in arguments]
        + [pltpu.SemaphoreType.DMA((5,))],
        compiler_params=params(60),
    )(*arguments)

    moment = moment + swap(moment, "tgt", 1)
    half, whole, moment = lax.optimization_barrier((half, whole, moment))
    parts = staged_parts(moment, "tgt", 2, 4)
    sources, targets = [half], [whole]
    more(sources, "src", 1, 2)
    more(targets, "tgt", 2, min(2, merged))
    parts, sources, targets = lax.optimization_barrier((parts, sources, targets))
    moments = staged_parts(tree(parts, jnp.add), "src", 1, 4)
    more(sources, "src", 1, src_size)
    more(targets, "tgt", 2, merged)
    sources, moments = lax.optimization_barrier((sources, moments))
    near = jnp.concatenate(sources, axis=0)
    far = swap(near, "tgt", 1)

    scores, sums, log_src, log_tgt = pl.pallas_call(
        functools.partial(start_kernel, pcs, total_rows * total_cols, merged, src_size),
        out_shape=(
            jax.ShapeDtypeStruct((wide, total_rows), f32),
            jax.ShapeDtypeStruct((1, total_rows), f32),
            jax.ShapeDtypeStruct((1, total_rows), f32),
            jax.ShapeDtypeStruct((wide, LANES), f32),
        ),
        in_specs=[VMEM] * (2 + len(targets) + len(moments)),
        out_specs=(VMEM,) * 4,
        scratch_shapes=[
            pltpu.VMEM((4 * DEPTH, total_rows), jnp.bfloat16),
            pltpu.VMEM((wide, 4 * DEPTH), jnp.bfloat16),
        ],
        compiler_params=params(16),
    )(near, far, *targets, *moments)

    def both(value):
        offset = 2 * merged
        while offset < tgt_size:
            value = logsum(value, swap(value, "tgt", offset))
            offset *= 2
        return value, swap(value, "tgt", 1)

    for iteration in range(ITERS - 1):
        sums = pl.pallas_call(
            middle_kernel,
            out_shape=jax.ShapeDtypeStruct((1, total_rows), f32),
            in_specs=[VMEM] * 5,
            out_specs=VMEM,
            scratch_shapes=[
                pltpu.VMEM((8, total_rows), f32),
                pltpu.VMEM((wide, LANES), f32),
                pltpu.VMEM((wide, LANES), f32),
            ],
            compiler_params=params(12),
        )(scores, *both(sums), log_src, log_tgt)

    log_coupling, row_potential, col_potential = pl.pallas_call(
        functools.partial(last_kernel, merged),
        out_shape=(
            jax.ShapeDtypeStruct((rows, cols), f32),
            jax.ShapeDtypeStruct((1, rows), f32),
            jax.ShapeDtypeStruct((1, cols), f32),
        ),
        in_specs=[VMEM] * 5,
        out_specs=(VMEM,) * 3,
        scratch_shapes=[
            pltpu.VMEM((8, total_rows), f32),
            pltpu.VMEM((cols, LANES), f32),
            pltpu.VMEM((cols, LANES), f32),
        ],
        compiler_params=params(12),
    )(scores, *both(sums), log_src, log_tgt)
    return log_coupling, row_potential.reshape(-1), col_potential.reshape(-1)


def solution(mesh):
    in_specs = (P("src", "tgt"), P(None, "src"), P(None, "tgt"), P("src"), P("tgt"))
    out_specs = (P("src", "tgt"), P("src"), P("tgt"))
    return jax.shard_map(shards, mesh=mesh, in_specs=in_specs, out_specs=out_specs, check_vma=False)
```

```python
import functools
import math

import jax
import jax.numpy as jnp
from jax import lax
from jax.experimental import pallas as pl
from jax.experimental.pallas import tpu as pltpu
from jax.sharding import PartitionSpec as P

ITERS = 4

eps_reg = 0.5
marg_power = 1.0 / (1.0 + eps_reg)
tiny_eps = 1e-06

LANES = 128
DEPTH = 64
LN2 = math.log(2.0)
SCORES_BYTES = 1 << 24
LIFT = 57.0
SPAN = 150.0
VMEM = pl.BlockSpec(memory_space=pltpu.VMEM)


def params(mib):
    return pltpu.CompilerParams(vmem_limit_bytes=mib << 20)


def tree(values, combine):
    values = list(values)
    while len(values) > 1:
        paired = [combine(values[i], values[i + 1]) for i in range(0, len(values) - 1, 2)]
        values = paired + ([values[-1]] if len(values) % 2 else [])
    return values[0]


def pieces(value):
    high = value.astype(jnp.bfloat16)
    rest = value - high.astype(jnp.float32)
    middle = rest.astype(jnp.bfloat16)
    low = (rest - middle.astype(jnp.float32)).astype(jnp.bfloat16)
    return high, middle, low


def padded(value):
    return jnp.concatenate(
        [value, jnp.zeros((DEPTH - value.shape[0], value.shape[1]), value.dtype)], axis=0
    )


def front_kernel(*refs):
    sources, (half_ref, whole_ref, moment_ref), local, sems = refs[:5], refs[5:8], refs[8:13], refs[13]
    copies = [pltpu.make_async_copy(a, b, sems.at[i]) for i, (a, b) in enumerate(zip(sources, local))]
    for copy in copies:
        copy.start()
    coupling_ref, src_ref, tgt_ref, src_mass_ref, tgt_mass_ref = local
    pcs = src_ref.shape[0]
    half = half_ref.shape[1]
    odd = lax.rem(lax.axis_index("tgt"), 2)
    for copy in copies[1:]:
        copy.wait()
    src = src_ref[...].astype(jnp.float32)
    tgt = tgt_ref[...].astype(jnp.float32)
    below = jnp.zeros((half_ref.shape[0] - pcs - 1, 2 * half), jnp.float32)
    joined = jnp.concatenate([src, jnp.log2(src_mass_ref[...]), below], axis=0)
    half_ref[...] = jnp.where(odd == 0, joined[:, :half], joined[:, half:])
    below = jnp.zeros((half_ref.shape[0] - pcs - 1, tgt.shape[1]), jnp.float32)
    whole_ref[...] = jnp.concatenate([tgt, jnp.log2(tgt_mass_ref[...]), below], axis=0)
    src = padded(src).astype(jnp.bfloat16)
    tgt = padded(tgt).astype(jnp.bfloat16)
    twice = jnp.concatenate([src, src], axis=0)
    copies[0].wait()
    panel = jnp.dot(twice, coupling_ref[...], preferred_element_type=jnp.float32)
    moment = sum(
        lax.dot_general(tgt, part, (((1,), (1,)), ((), ())), preferred_element_type=jnp.float32)
        for part in pieces(panel)
    )
    lane = lax.broadcasted_iota(jnp.int32, (DEPTH // 2, LANES), 1)
    moment_ref[...] = jnp.where(lane < DEPTH, moment[: DEPTH // 2], moment[DEPTH // 2 :])


def start_kernel(pcs, entries, merged, blocks, *refs):
    near_ref, far_ref = refs[:2]
    tgt_refs = refs[2 : 2 + merged.bit_length()]
    moment_refs = refs[2 + merged.bit_length() : -7]
    scores_ref, sums_ref, log_src_ref, log_tgt_ref, src_all, weights, top_ref = refs[-7:]
    packed_rows = near_ref.shape[0] // blocks
    half = near_ref.shape[1]
    width = tgt_refs[0].shape[1]
    targets = [ref.at[pl.ds(i, packed_rows), :] for ref in tgt_refs for i in range(0, ref.shape[0], packed_rows)]
    z = lax.axis_index("src")
    t = lax.axis_index("tgt")
    odd = lax.rem(t, 2)
    total_rows = 2 * half * blocks
    total_cols = width * lax.axis_size("tgt")

    packed = tree([ref[...] for ref in moment_refs], jnp.add) * entries ** (-0.5)
    spread = jnp.sqrt(jnp.sum(packed * packed) * (1.0 / (pcs * pcs)) + tiny_eps)
    packed = packed / spread * (2.0 / (eps_reg * pcs) / LN2)
    turned = pltpu.roll(packed, DEPTH, axis=1)
    left = lax.broadcasted_iota(jnp.int32, packed.shape, 1) < DEPTH
    normed = jnp.concatenate(
        [jnp.where(left, packed, turned), jnp.where(left, turned, packed)], axis=0
    )
    normed = jnp.concatenate([normed, normed], axis=1)

    for b in range(blocks):
        place = jnp.bitwise_xor(z, b)
        for ref, side in ((near_ref, odd), (far_ref, 1 - odd)):
            block = ref[pl.ds(b * packed_rows, packed_rows), :]
            lanes = pl.ds(pl.multiple_of((place * 2 + side) * half, half), half)
            log_src_ref[:, lanes] = marg_power * (block[pcs : pcs + 1] + math.log2(total_cols))
            block = padded(block).astype(jnp.bfloat16)
            for copy in range(4):
                src_all[pl.ds(copy * DEPTH, DEPTH), lanes] = block

    parts = pieces(normed)
    first = lax.broadcasted_iota(jnp.int32, (width, LANES), 1) < DEPTH
    mine = lax.rem(lax.div(t, 2), merged)
    for b in range(merged):
        base = pl.multiple_of(jnp.bitwise_xor(mine, b) * width, width)
        turned = padded(targets[b][...]).T
        log_tgt_ref[pl.ds(base, width), :] = jnp.broadcast_to(
            marg_power * (turned[:, pcs : pcs + 1] + math.log2(total_rows)), (width, LANES)
        )
        turned = turned.astype(jnp.bfloat16)
        weighted = sum(jnp.dot(turned, part, preferred_element_type=jnp.float32) for part in parts)
        high, middle, low = pieces(weighted)
        weights[pl.ds(base, width), :LANES] = jnp.where(first, high[:, :LANES], middle[:, :LANES])
        weights[pl.ds(base, width), LANES:] = jnp.where(
            first, low[:, LANES:], jnp.zeros((width, LANES), jnp.bfloat16)
        )

    chunk, rows = 512, 256
    for left_lane in range(0, total_rows, chunk):
        lanes = pl.ds(left_lane, chunk)

        def step(i, carry, lanes=lanes):
            base = pl.multiple_of(i * rows, rows)
            block = jnp.dot(
                weights[pl.ds(base, rows), :], src_all[:, lanes], preferred_element_type=jnp.float32
            )
            scores_ref[pl.ds(base, rows), lanes] = block
            return jnp.maximum(carry, jnp.max(block.reshape(rows // 8, 8, chunk), axis=0))

        unset = jnp.full((8, chunk), -jnp.inf, jnp.float32)
        top_ref[:, lanes] = lax.fori_loop(0, scores_ref.shape[0] // rows, step, unset) - LIFT
    rows_exp(scores_ref, None, top_ref, sums_ref, None)


def down(highest, summed):
    top = jnp.max(highest, axis=0, keepdims=True)
    return top + jnp.log2(jnp.sum(summed * jnp.exp2(highest - top), axis=0, keepdims=True))


def logsum(one, other):
    top = jnp.maximum(one, other)
    return top + jnp.log2(jnp.exp2(one - top) + jnp.exp2(other - top))


def row_values(log_src_ref, sums_ref, more_ref):
    return log_src_ref[...] - marg_power * logsum(sums_ref[...], more_ref[...])


def streamed(terms, combine):
    held = []
    for term in terms:
        if len(held) < 2:
            held.append(term)
        else:
            held = [held[1], combine(held[0], term)]
    return tree(held, combine)


def lane_tiles(ref):
    return [pl.ds(j, LANES) for j in range(0, ref.shape[1], LANES)]


def halves(low):
    low = pl.multiple_of(low, 16)
    return pl.ds(low, 16), [pl.ds(low, 8), pl.ds(pl.multiple_of(low + 8, 8), 8)]


def columns_exp(scores_ref, rows_ref, top_ref, sum_ref, base, count, keep_ref):
    tiles = lane_tiles(scores_ref)

    def highest(i, carry):
        for u in range(4):
            low = pl.multiple_of((i * 4 + u) * 8, 8)
            at = pl.ds(pl.multiple_of(base + low, 8), 8)
            terms = (scores_ref[at, lanes] + rows_ref[:, lanes] for lanes in tiles)
            top_ref[pl.ds(low, 8), :] = streamed(terms, jnp.maximum) - LIFT
        return carry

    def total(i, carry):
        for u in range(2):
            _, places = halves((i * 2 + u) * 16)
            at, sources = halves(base + (i * 2 + u) * 16)
            tops = [top_ref[place, :] for place in places]
            sums = [jnp.zeros((8, LANES), jnp.float32)] * 2
            for lanes in tiles:
                row = rows_ref[:, lanes]
                parts = [jnp.exp2(scores_ref[src, lanes] + row - top) for src, top in zip(sources, tops)]
                if keep_ref is not None:
                    keep_ref[at, lanes] = jnp.concatenate(parts, axis=0).astype(keep_ref.dtype)
                sums = [a + b for a, b in zip(sums, parts)]
            for place, value in zip(places, sums):
                sum_ref[place, :] = value
        return carry

    lax.fori_loop(0, count // 32, highest, 0)
    lax.fori_loop(0, count // 32, total, 0)


def columns_product(keep_ref, kept_top_ref, factor_ref, shift, top_ref, sum_ref, base, count):
    tiles = lane_tiles(keep_ref)

    def total(i, carry):
        for u in range(2):
            whole, _ = halves((i * 2 + u) * 16)
            at, _ = halves(base + (i * 2 + u) * 16)
            sums = [jnp.zeros((8, LANES), jnp.float32)] * 2
            for lanes in tiles:
                kept = keep_ref[at, lanes].astype(jnp.float32)
                factor = factor_ref[:, lanes]
                sums = [sums[0] + kept[:8] * factor, sums[1] + kept[8:] * factor]
            sum_ref[whole, :] = jnp.concatenate(sums, axis=0)
            top_ref[whole, :] = kept_top_ref[at, :] + (shift - LIFT)
        return carry

    lax.fori_loop(0, count // 32, total, 0)


def columns_finish(top_ref, sum_ref, log_tgt_ref, cols_ref, base, count):
    part = 128

    def finish(i, carry):
        low = pl.multiple_of(i * part, part)
        at = pl.ds(pl.multiple_of(base + low, part), part)
        tops = top_ref[pl.ds(low, part), :]
        top = jnp.max(tops, axis=1, keepdims=True)
        total = jnp.sum(sum_ref[pl.ds(low, part), :] * jnp.exp2(tops - top), axis=1, keepdims=True)
        cols_ref[pl.ds(low, part), :] = log_tgt_ref[at, :] - marg_power * (top + jnp.log2(total))
        return carry

    lax.fori_loop(0, count // part, finish, 0)


BESIDE, DEEP = 8, 4


def over_tiles(count, width, body, first, done):
    for start in range(0, width, BESIDE * LANES):
        tiles = [pl.ds(start + j * LANES, LANES) for j in range(BESIDE)]

        def step(i, carry, tiles=tiles):
            carry = list(carry)
            for g in range(DEEP):
                body(*halves((i * DEEP + g) * 16), tiles, carry)
            return tuple(carry)

        state = lax.fori_loop(0, count // (16 * DEEP), step, tuple(first for _ in tiles))
        for lanes, value in zip(tiles, state):
            done(lanes, value)


def rows_highest(scores_ref, cols_ref, top_ref):
    def body(at, places, tiles, carry):
        for place in places:
            potential = cols_ref[place, :]
            for j, lanes in enumerate(tiles):
                carry[j] = jnp.maximum(carry[j], scores_ref[place, lanes] + potential)

    def done(lanes, value):
        top_ref[:, lanes] = value - LIFT

    over_tiles(*scores_ref.shape, body, jnp.full((8, LANES), -jnp.inf, jnp.float32), done)


def rows_exp(scores_ref, cols_ref, top_ref, out_ref, keep_ref):
    def body(at, places, tiles, carry):
        if cols_ref is not None:
            potentials = [cols_ref[place, :] for place in places]
        for j, lanes in enumerate(tiles):
            top = top_ref[:, lanes]
            terms = [scores_ref[place, lanes] for place in places]
            if cols_ref is not None:
                terms = [term + potential for term, potential in zip(terms, potentials)]
            parts = [jnp.exp2(term - top) for term in terms]
            if keep_ref is not None:
                keep_ref[at, lanes] = jnp.concatenate(parts, axis=0).astype(keep_ref.dtype)
            carry[j] = carry[j] + (parts[0] + parts[1])

    def done(lanes, value):
        out_ref[:, lanes] = down(top_ref[:, lanes], value)

    over_tiles(*scores_ref.shape, body, jnp.zeros((8, LANES), jnp.float32), done)


def rows_product(keep_ref, kept_top_ref, factor_ref, shift, out_ref):
    def body(at, places, tiles, carry):
        factors = [factor_ref[place, :] for place in places]
        for j, lanes in enumerate(tiles):
            kept = keep_ref[at, lanes].astype(jnp.float32)
            carry[j] = carry[j] + (kept[:8] * factors[0] + kept[8:] * factors[1])

    def done(lanes, value):
        out_ref[:, lanes] = down(kept_top_ref[:, lanes] + (shift - LIFT), value)

    over_tiles(*keep_ref.shape, body, jnp.zeros((8, LANES), jnp.float32), done)


def columns_either(rows, args, kept, rows_ref, top_ref, sum_ref, base, count):
    scores_ref, log_tgt_ref = args
    keep_ref, kept_top_ref, kept_rows_ref = kept
    change = rows - kept_rows_ref[...]
    shift = jnp.max(change)
    near = shift - jnp.min(change) <= SPAN

    @pl.when(near)
    def _():
        rows_ref[...] = jnp.broadcast_to(jnp.exp2(change - (shift - LIFT)), rows_ref.shape)
        columns_product(keep_ref, kept_top_ref, rows_ref, shift, top_ref, sum_ref, base, count)

    @pl.when(jnp.logical_not(near))
    def _():
        rows_ref[...] = jnp.broadcast_to(rows, rows_ref.shape)
        columns_exp(scores_ref, rows_ref, top_ref, sum_ref, base, count, None)


def rows_either(scores_ref, cols_ref, kept, factor_ref, top_ref, out_ref):
    keep_ref, kept_top_ref, kept_cols_ref = kept
    change = cols_ref[...] - kept_cols_ref[...]
    shift = jnp.max(change)
    near = shift - jnp.min(change) <= SPAN

    @pl.when(near)
    def _():
        factor_ref[...] = jnp.exp2(cols_ref[...] - kept_cols_ref[...] - (shift - LIFT))
        rows_product(keep_ref, kept_top_ref, factor_ref, shift, out_ref)

    @pl.when(jnp.logical_not(near))
    def _():
        rows_highest(scores_ref, cols_ref, top_ref)
        rows_exp(scores_ref, cols_ref, top_ref, out_ref, None)


def first_kernel(scores_ref, sums_ref, more_ref, log_src_ref, log_tgt_ref, out_ref, keep_ref, top_ref, cols_ref, rows_ref, high_ref, sum_ref):
    rows_ref[...] = jnp.broadcast_to(row_values(log_src_ref, sums_ref, more_ref), rows_ref.shape)
    count = scores_ref.shape[0]
    columns_exp(scores_ref, rows_ref, high_ref, sum_ref, 0, count, None)
    columns_finish(high_ref, sum_ref, log_tgt_ref, cols_ref, 0, count)
    rows_highest(scores_ref, cols_ref, top_ref)
    rows_exp(scores_ref, cols_ref, top_ref, out_ref, keep_ref)


def second_kernel(scores_ref, sums_ref, more_ref, log_src_ref, log_tgt_ref, *refs):
    kept, (out_ref, keep_ref, high_ref, base_ref) = refs[:3], refs[3:7]
    rows_ref, cols_ref, sum_ref, top_ref = refs[7:]
    base_ref[...] = row_values(log_src_ref, sums_ref, more_ref)
    rows_ref[...] = jnp.broadcast_to(base_ref[...], rows_ref.shape)
    count = scores_ref.shape[0]
    columns_exp(scores_ref, rows_ref, high_ref, sum_ref, 0, count, keep_ref)
    columns_finish(high_ref, sum_ref, log_tgt_ref, cols_ref, 0, count)
    rows_either(scores_ref, cols_ref, kept, sum_ref, top_ref, out_ref)


def later_kernel(scores_ref, sums_ref, more_ref, log_src_ref, log_tgt_ref, *refs):
    kept, kept_columns, out_ref = refs[:3], refs[3:6], refs[6]
    rows_ref, cols_ref, high_ref, sum_ref, top_ref = refs[7:]
    rows = row_values(log_src_ref, sums_ref, more_ref)
    count = scores_ref.shape[0]
    columns_either(rows, (scores_ref, log_tgt_ref), kept_columns, rows_ref, high_ref, sum_ref, 0, count)
    columns_finish(high_ref, sum_ref, log_tgt_ref, cols_ref, 0, count)
    rows_either(scores_ref, cols_ref, kept, sum_ref, top_ref, out_ref)


def last_kernel(merged, scores_ref, sums_ref, more_ref, log_src_ref, log_tgt_ref, *refs):
    kept_columns, (out_ref, row_ref, col_ref) = refs[:3], refs[3:6]
    rows_ref, values_ref, cols_ref, high_ref, sum_ref = refs[6:]
    own_rows, own_cols = out_ref.shape
    rows = row_values(log_src_ref, sums_ref, more_ref)
    values_ref[...] = rows
    base = pl.multiple_of(lax.rem(lax.div(lax.axis_index("tgt"), 2), merged) * own_cols, own_cols)
    lanes = pl.ds(pl.multiple_of(lax.axis_index("src") * own_rows, own_rows), own_rows)
    columns_either(rows, (scores_ref, log_tgt_ref), kept_columns, rows_ref, high_ref, sum_ref, base, own_cols)
    columns_finish(high_ref, sum_ref, log_tgt_ref, cols_ref, base, own_cols)
    row_ref[...] = values_ref[:, lanes] * LN2
    col_ref[...] = cols_ref[...].T[0:1, :] * LN2
    block = scores_ref[pl.ds(base, own_cols), lanes] + values_ref[:, lanes] + cols_ref[:, 0:1]
    out_ref[...] = (block * LN2).T


def swap(value, axis, offset):
    return lax.ppermute(value, axis, [(i, i ^ offset) for i in range(lax.axis_size(axis))])


def staged_parts(value, axis, low, width):
    size = lax.axis_size(axis)
    terms = [value]
    while low < size:
        span = min(width, size // low)
        value = tree(terms, jnp.add)
        terms = [value] + [swap(value, axis, low * j) for j in range(1, span)]
        low *= span
    return terms


def more(held, axis, low, goal):
    unit = held[0].shape[0]
    while sum(part.shape[0] for part in held) < goal * unit:
        known = held[0] if len(held) == 1 else jnp.concatenate(held, axis=0)
        held.append(swap(known, axis, low * known.shape[0] // unit))


def shards(coupling, src_pcs, tgt_pcs, src_mass, tgt_mass):
    f32 = jnp.float32
    pcs = src_pcs.shape[0]
    rows, cols = coupling.shape
    src_size, tgt_size = lax.axis_size("src"), lax.axis_size("tgt")
    total_rows, total_cols = rows * src_size, cols * tgt_size
    merged = 1
    while 2 * merged * 2 <= tgt_size and 2 * merged * cols * total_rows * 4 <= SCORES_BYTES:
        merged *= 2
    wide = merged * cols
    packed_rows = -(-(pcs + 1) // 8) * 8

    arguments = (coupling, src_pcs, tgt_pcs, src_mass.reshape(1, -1), tgt_mass.reshape(1, -1))
    half, whole, moment = pl.pallas_call(
        front_kernel,
        out_shape=(
            jax.ShapeDtypeStruct((packed_rows, rows // 2), f32),
            jax.ShapeDtypeStruct((packed_rows, cols), f32),
            jax.ShapeDtypeStruct((DEPTH // 2, LANES), f32),
        ),
        in_specs=[pl.BlockSpec(memory_space=pltpu.HBM)] * 5,
        out_specs=(VMEM,) * 3,
        scratch_shapes=[pltpu.VMEM(a.shape, a.dtype) for a in arguments]
        + [pltpu.SemaphoreType.DMA((5,))],
        compiler_params=params(60),
    )(*arguments)

    moment = moment + swap(moment, "tgt", 1)
    half, whole, moment = lax.optimization_barrier((half, whole, moment))
    parts = staged_parts(moment, "tgt", 2, 4)
    sources, targets = [half], [whole]
    more(sources, "src", 1, 2)
    more(targets, "tgt", 2, min(2, merged))
    parts, sources, targets = lax.optimization_barrier((parts, sources, targets))
    moments = staged_parts(tree(parts, jnp.add), "src", 1, 4)
    more(sources, "src", 1, src_size)
    more(targets, "tgt", 2, merged)
    sources, moments = lax.optimization_barrier((sources, moments))
    near = jnp.concatenate(sources, axis=0)
    far = swap(near, "tgt", 1)

    scores, sums, log_src, log_tgt = pl.pallas_call(
        functools.partial(start_kernel, pcs, total_rows * total_cols, merged, src_size),
        out_shape=(
            jax.ShapeDtypeStruct((wide, total_rows), f32),
            jax.ShapeDtypeStruct((1, total_rows), f32),
            jax.ShapeDtypeStruct((1, total_rows), f32),
            jax.ShapeDtypeStruct((wide, LANES), f32),
        ),
        in_specs=[VMEM] * (2 + len(targets) + len(moments)),
        out_specs=(VMEM,) * 4,
        scratch_shapes=[
            pltpu.VMEM((4 * DEPTH, total_rows), jnp.bfloat16),
            pltpu.VMEM((wide, 4 * DEPTH), jnp.bfloat16),
            pltpu.VMEM((8, total_rows), f32),
        ],
        compiler_params=params(16),
    )(near, far, *targets, *moments)

    def both(value):
        offset = 2 * merged
        while offset < tgt_size:
            value = logsum(value, swap(value, "tgt", offset))
            offset *= 2
        return value, swap(value, "tgt", 1)

    bf16, block = jnp.bfloat16, (wide, total_rows)

    def call(kernel, sums, extra, outs, scratch):
        return pl.pallas_call(
            kernel,
            out_shape=tuple(jax.ShapeDtypeStruct(shape, bf16 if shape == block else f32) for shape in outs),
            in_specs=[VMEM] * (5 + len(extra)),
            out_specs=(VMEM,) * len(outs),
            scratch_shapes=[pltpu.VMEM(shape, f32) for shape in scratch],
            compiler_params=params(10),
        )(scores, *both(sums), log_src, log_tgt, *extra)

    line, lines, pads = (1, total_rows), (8, total_rows), (wide, LANES)
    sums, *kept_rows = call(
        first_kernel, sums, (), (line, block, lines, pads), (lines, pads, pads)
    )
    sums, *kept_columns = call(
        second_kernel, sums, kept_rows, (line, block, pads, line), (lines, pads, pads, lines)
    )
    for iteration in range(ITERS - 3):
        (sums,) = call(
            later_kernel, sums, (*kept_rows, *kept_columns), (line,), (lines, pads, pads, pads, lines)
        )
    pads = (cols, LANES)
    log_coupling, row_potential, col_potential = call(
        functools.partial(last_kernel, merged), sums, kept_columns,
        ((rows, cols), (1, rows), (1, cols)), (lines, line, pads, pads, pads),
    )
    return log_coupling, row_potential.reshape(-1), col_potential.reshape(-1)


def solution(mesh):
    in_specs = (P("src", "tgt"), P(None, "src"), P(None, "tgt"), P("src"), P("tgt"))
    out_specs = (P("src", "tgt"), P("src"), P("tgt"))
    return jax.shard_map(shards, mesh=mesh, in_specs=in_specs, out_specs=out_specs, check_vma=False)
```

```python
import functools
import math

import jax
import jax.numpy as jnp
from jax import lax
from jax.experimental import pallas as pl
from jax.experimental.pallas import tpu as pltpu
from jax.sharding import PartitionSpec as P

ITERS = 4

eps_reg = 0.5
marg_power = 1.0 / (1.0 + eps_reg)
tiny_eps = 1e-06

LANES = 128
DEPTH = 64
LN2 = math.log(2.0)
SCORES_BYTES = 1 << 24
LIFT = 57.0
SPAN = 150.0
VMEM = pl.BlockSpec(memory_space=pltpu.VMEM)


def params(mib):
    return pltpu.CompilerParams(vmem_limit_bytes=mib << 20)


def tree(values, combine):
    values = list(values)
    while len(values) > 1:
        paired = [combine(values[i], values[i + 1]) for i in range(0, len(values) - 1, 2)]
        values = paired + ([values[-1]] if len(values) % 2 else [])
    return values[0]


def pieces(value):
    high = value.astype(jnp.bfloat16)
    rest = value - high.astype(jnp.float32)
    middle = rest.astype(jnp.bfloat16)
    low = (rest - middle.astype(jnp.float32)).astype(jnp.bfloat16)
    return high, middle, low


def padded(value):
    return jnp.concatenate(
        [value, jnp.zeros((DEPTH - value.shape[0], value.shape[1]), value.dtype)], axis=0
    )


def front_kernel(*refs):
    sources, (half_ref, whole_ref, moment_ref), local, sems = refs[:5], refs[5:8], refs[8:13], refs[13]
    copies = [pltpu.make_async_copy(a, b, sems.at[i]) for i, (a, b) in enumerate(zip(sources, local))]
    for copy in copies:
        copy.start()
    coupling_ref, src_ref, tgt_ref, src_mass_ref, tgt_mass_ref = local
    pcs = src_ref.shape[0]
    half = half_ref.shape[1]
    odd = lax.rem(lax.axis_index("tgt"), 2)
    for copy in copies[1:]:
        copy.wait()
    src = src_ref[...].astype(jnp.float32)
    tgt = tgt_ref[...].astype(jnp.float32)
    below = jnp.zeros((half_ref.shape[0] - pcs - 1, 2 * half), jnp.float32)
    joined = jnp.concatenate([src, jnp.log2(src_mass_ref[...]), below], axis=0)
    half_ref[...] = jnp.where(odd == 0, joined[:, :half], joined[:, half:])
    below = jnp.zeros((half_ref.shape[0] - pcs - 1, tgt.shape[1]), jnp.float32)
    whole_ref[...] = jnp.concatenate([tgt, jnp.log2(tgt_mass_ref[...]), below], axis=0)
    src = padded(src).astype(jnp.bfloat16)
    tgt = padded(tgt).astype(jnp.bfloat16)
    twice = jnp.concatenate([src, src], axis=0)
    copies[0].wait()
    panel = jnp.dot(twice, coupling_ref[...], preferred_element_type=jnp.float32)
    moment = sum(
        lax.dot_general(tgt, part, (((1,), (1,)), ((), ())), preferred_element_type=jnp.float32)
        for part in pieces(panel)
    )
    lane = lax.broadcasted_iota(jnp.int32, (DEPTH // 2, LANES), 1)
    moment_ref[...] = jnp.where(lane < DEPTH, moment[: DEPTH // 2], moment[DEPTH // 2 :])


def start_kernel(pcs, entries, merged, blocks, *refs):
    near_ref, far_ref = refs[:2]
    tgt_refs = refs[2 : 2 + merged.bit_length()]
    moment_refs = refs[2 + merged.bit_length() : -7]
    scores_ref, sums_ref, log_src_ref, log_tgt_ref, src_all, weights, top_ref = refs[-7:]
    packed_rows = near_ref.shape[0] // blocks
    half = near_ref.shape[1]
    width = tgt_refs[0].shape[1]
    targets = [ref.at[pl.ds(i, packed_rows), :] for ref in tgt_refs for i in range(0, ref.shape[0], packed_rows)]
    z = lax.axis_index("src")
    t = lax.axis_index("tgt")
    odd = lax.rem(t, 2)
    total_rows = 2 * half * blocks
    total_cols = width * lax.axis_size("tgt")

    packed = tree([ref[...] for ref in moment_refs], jnp.add) * entries ** (-0.5)
    spread = jnp.sqrt(jnp.sum(packed * packed) * (1.0 / (pcs * pcs)) + tiny_eps)
    packed = packed / spread * (2.0 / (eps_reg * pcs) / LN2)
    turned = pltpu.roll(packed, DEPTH, axis=1)
    left = lax.broadcasted_iota(jnp.int32, packed.shape, 1) < DEPTH
    normed = jnp.concatenate(
        [jnp.where(left, packed, turned), jnp.where(left, turned, packed)], axis=0
    )
    normed = jnp.concatenate([normed, normed], axis=1)

    for b in range(blocks):
        place = jnp.bitwise_xor(z, b)
        for ref, side in ((near_ref, odd), (far_ref, 1 - odd)):
            block = ref[pl.ds(b * packed_rows, packed_rows), :]
            lanes = pl.ds(pl.multiple_of((place * 2 + side) * half, half), half)
            log_src_ref[:, lanes] = marg_power * (block[pcs : pcs + 1] + math.log2(total_cols))
            block = padded(block).astype(jnp.bfloat16)
            for copy in range(4):
                src_all[pl.ds(copy * DEPTH, DEPTH), lanes] = block

    parts = pieces(normed)
    first = lax.broadcasted_iota(jnp.int32, (width, LANES), 1) < DEPTH
    mine = lax.rem(lax.div(t, 2), merged)
    for b in range(merged):
        base = pl.multiple_of(jnp.bitwise_xor(mine, b) * width, width)
        turned = padded(targets[b][...]).T
        log_tgt_ref[pl.ds(base, width), :] = jnp.broadcast_to(
            marg_power * (turned[:, pcs : pcs + 1] + math.log2(total_rows)), (width, LANES)
        )
        turned = turned.astype(jnp.bfloat16)
        weighted = sum(jnp.dot(turned, part, preferred_element_type=jnp.float32) for part in parts)
        high, middle, low = pieces(weighted)
        weights[pl.ds(base, width), :LANES] = jnp.where(first, high[:, :LANES], middle[:, :LANES])
        weights[pl.ds(base, width), LANES:] = jnp.where(
            first, low[:, LANES:], jnp.zeros((width, LANES), jnp.bfloat16)
        )

    chunk, rows = 512, 256
    for left_lane in range(0, total_rows, chunk):
        lanes = pl.ds(left_lane, chunk)

        def step(i, carry, lanes=lanes):
            base = pl.multiple_of(i * rows, rows)
            block = jnp.dot(
                weights[pl.ds(base, rows), :], src_all[:, lanes], preferred_element_type=jnp.float32
            )
            scores_ref[pl.ds(base, rows), lanes] = block
            return jnp.maximum(carry, jnp.max(block.reshape(rows // 8, 8, chunk), axis=0))

        unset = jnp.full((8, chunk), -jnp.inf, jnp.float32)
        top_ref[:, lanes] = lax.fori_loop(0, scores_ref.shape[0] // rows, step, unset) - LIFT
    rows_exp(scores_ref, None, top_ref, sums_ref, None)


def down(highest, summed):
    top = jnp.max(highest, axis=0, keepdims=True)
    return top + jnp.log2(jnp.sum(summed * jnp.exp2(highest - top), axis=0, keepdims=True))


def logsum(one, other):
    top = jnp.maximum(one, other)
    return top + jnp.log2(jnp.exp2(one - top) + jnp.exp2(other - top))


def row_values(log_src_ref, sums_ref, more_ref):
    return log_src_ref[...] - marg_power * logsum(sums_ref[...], more_ref[...])


def streamed(terms, combine):
    held = []
    for term in terms:
        if len(held) < 2:
            held.append(term)
        else:
            held = [held[1], combine(held[0], term)]
    return tree(held, combine)


def lane_tiles(ref):
    return [pl.ds(j, LANES) for j in range(0, ref.shape[1], LANES)]


def halves(low):
    low = pl.multiple_of(low, 16)
    return pl.ds(low, 16), [pl.ds(low, 8), pl.ds(pl.multiple_of(low + 8, 8), 8)]


def columns_exp(scores_ref, rows_ref, top_ref, sum_ref, base, count, keep_ref):
    tiles = lane_tiles(scores_ref)

    def highest(i, carry):
        for u in range(4):
            low = pl.multiple_of((i * 4 + u) * 8, 8)
            at = pl.ds(pl.multiple_of(base + low, 8), 8)
            terms = (scores_ref[at, lanes] + rows_ref[:, lanes] for lanes in tiles)
            top_ref[pl.ds(low, 8), :] = streamed(terms, jnp.maximum) - LIFT
        return carry

    def total(i, carry):
        for u in range(2):
            _, places = halves((i * 2 + u) * 16)
            at, sources = halves(base + (i * 2 + u) * 16)
            tops = [top_ref[place, :] for place in places]
            sums = [jnp.zeros((8, LANES), jnp.float32)] * 2
            for lanes in tiles:
                row = rows_ref[:, lanes]
                parts = [jnp.exp2(scores_ref[src, lanes] + row - top) for src, top in zip(sources, tops)]
                if keep_ref is not None:
                    keep_ref[at, lanes] = jnp.concatenate(parts, axis=0).astype(keep_ref.dtype)
                sums = [a + b for a, b in zip(sums, parts)]
            for place, value in zip(places, sums):
                sum_ref[place, :] = value
        return carry

    lax.fori_loop(0, count // 32, highest, 0)
    lax.fori_loop(0, count // 32, total, 0)


def columns_product(keep_ref, kept_top_ref, factor_ref, shift, top_ref, sum_ref, base, count):
    tiles = lane_tiles(keep_ref)

    def total(i, carry):
        for u in range(2):
            whole, _ = halves((i * 2 + u) * 16)
            at, _ = halves(base + (i * 2 + u) * 16)
            sums = [jnp.zeros((8, LANES), jnp.float32)] * 2
            for lanes in tiles:
                kept = keep_ref[at, lanes].astype(jnp.float32)
                factor = factor_ref[:, lanes]
                sums = [sums[0] + kept[:8] * factor, sums[1] + kept[8:] * factor]
            sum_ref[whole, :] = jnp.concatenate(sums, axis=0)
            top_ref[whole, :] = kept_top_ref[at, :] + (shift - LIFT)
        return carry

    lax.fori_loop(0, count // 32, total, 0)


def columns_finish(top_ref, sum_ref, log_tgt_ref, cols_ref, base, count):
    part = min(count, 1024)
    for low in range(0, count, part):
        here = pl.ds(low, part)
        tops = top_ref[here, :]
        top = jnp.max(tops, axis=1, keepdims=True)
        total = jnp.sum(sum_ref[here, :] * jnp.exp2(tops - top), axis=1, keepdims=True)
        at = pl.ds(pl.multiple_of(base + low, part), part)
        cols_ref[here, :] = log_tgt_ref[at, :] - marg_power * (top + jnp.log2(total))


BESIDE, DEEP = 8, 4


def over_tiles(count, width, body, first, done):
    for start in range(0, width, BESIDE * LANES):
        tiles = [pl.ds(start + j * LANES, LANES) for j in range(BESIDE)]

        def step(i, carry, tiles=tiles):
            carry = list(carry)
            for g in range(DEEP):
                body(*halves((i * DEEP + g) * 16), tiles, carry)
            return tuple(carry)

        state = lax.fori_loop(0, count // (16 * DEEP), step, tuple(first for _ in tiles))
        for lanes, value in zip(tiles, state):
            done(lanes, value)


def rows_highest(scores_ref, cols_ref, top_ref):
    def body(at, places, tiles, carry):
        for place in places:
            potential = cols_ref[place, :]
            for j, lanes in enumerate(tiles):
                carry[j] = jnp.maximum(carry[j], scores_ref[place, lanes] + potential)

    def done(lanes, value):
        top_ref[:, lanes] = value - LIFT

    over_tiles(*scores_ref.shape, body, jnp.full((8, LANES), -jnp.inf, jnp.float32), done)


def rows_exp(scores_ref, cols_ref, top_ref, out_ref, keep_ref):
    def body(at, places, tiles, carry):
        if cols_ref is not None:
            potentials = [cols_ref[place, :] for place in places]
        for j, lanes in enumerate(tiles):
            top = top_ref[:, lanes]
            terms = [scores_ref[place, lanes] for place in places]
            if cols_ref is not None:
                terms = [term + potential for term, potential in zip(terms, potentials)]
            parts = [jnp.exp2(term - top) for term in terms]
            if keep_ref is not None:
                keep_ref[at, lanes] = jnp.concatenate(parts, axis=0).astype(keep_ref.dtype)
            carry[j] = carry[j] + (parts[0] + parts[1])

    def done(lanes, value):
        out_ref[:, lanes] = down(top_ref[:, lanes], value)

    over_tiles(*scores_ref.shape, body, jnp.zeros((8, LANES), jnp.float32), done)


def rows_product(keep_ref, kept_top_ref, factor_ref, shift, out_ref):
    def body(at, places, tiles, carry):
        factors = [factor_ref[place, :] for place in places]
        for j, lanes in enumerate(tiles):
            kept = keep_ref[at, lanes].astype(jnp.float32)
            carry[j] = carry[j] + (kept[:8] * factors[0] + kept[8:] * factors[1])

    def done(lanes, value):
        out_ref[:, lanes] = down(kept_top_ref[:, lanes] + (shift - LIFT), value)

    over_tiles(*keep_ref.shape, body, jnp.zeros((8, LANES), jnp.float32), done)


def columns_either(rows, args, kept, rows_ref, top_ref, sum_ref, base, count):
    scores_ref, log_tgt_ref = args
    keep_ref, kept_top_ref, kept_rows_ref = kept
    change = rows - kept_rows_ref[...]
    shift = jnp.max(change)
    near = shift - jnp.min(change) <= SPAN

    @pl.when(near)
    def _():
        rows_ref[...] = jnp.broadcast_to(jnp.exp2(change - (shift - LIFT)), rows_ref.shape)
        columns_product(keep_ref, kept_top_ref, rows_ref, shift, top_ref, sum_ref, base, count)

    @pl.when(jnp.logical_not(near))
    def _():
        rows_ref[...] = jnp.broadcast_to(rows, rows_ref.shape)
        columns_exp(scores_ref, rows_ref, top_ref, sum_ref, base, count, None)


def rows_either(scores_ref, cols_ref, kept, factor_ref, top_ref, out_ref):
    keep_ref, kept_top_ref, kept_cols_ref = kept
    change = cols_ref[...] - kept_cols_ref[...]
    shift = jnp.max(change)
    near = shift - jnp.min(change) <= SPAN

    @pl.when(near)
    def _():
        factor_ref[...] = jnp.exp2(cols_ref[...] - kept_cols_ref[...] - (shift - LIFT))
        rows_product(keep_ref, kept_top_ref, factor_ref, shift, out_ref)

    @pl.when(jnp.logical_not(near))
    def _():
        rows_highest(scores_ref, cols_ref, top_ref)
        rows_exp(scores_ref, cols_ref, top_ref, out_ref, None)


def first_kernel(scores_ref, sums_ref, more_ref, log_src_ref, log_tgt_ref, out_ref, keep_ref, top_ref, cols_ref, rows_ref, high_ref, sum_ref):
    rows_ref[...] = jnp.broadcast_to(row_values(log_src_ref, sums_ref, more_ref), rows_ref.shape)
    count = scores_ref.shape[0]
    columns_exp(scores_ref, rows_ref, high_ref, sum_ref, 0, count, None)
    columns_finish(high_ref, sum_ref, log_tgt_ref, cols_ref, 0, count)
    rows_highest(scores_ref, cols_ref, top_ref)
    rows_exp(scores_ref, cols_ref, top_ref, out_ref, keep_ref)


def second_kernel(scores_ref, sums_ref, more_ref, log_src_ref, log_tgt_ref, *refs):
    kept, (out_ref, keep_ref, high_ref, base_ref) = refs[:3], refs[3:7]
    rows_ref, cols_ref, sum_ref, top_ref = refs[7:]
    base_ref[...] = row_values(log_src_ref, sums_ref, more_ref)
    rows_ref[...] = jnp.broadcast_to(base_ref[...], rows_ref.shape)
    count = scores_ref.shape[0]
    columns_exp(scores_ref, rows_ref, high_ref, sum_ref, 0, count, keep_ref)
    columns_finish(high_ref, sum_ref, log_tgt_ref, cols_ref, 0, count)
    rows_either(scores_ref, cols_ref, kept, sum_ref, top_ref, out_ref)


def later_kernel(scores_ref, sums_ref, more_ref, log_src_ref, log_tgt_ref, *refs):
    kept, kept_columns, out_ref = refs[:3], refs[3:6], refs[6]
    rows_ref, cols_ref, high_ref, sum_ref, top_ref = refs[7:]
    rows = row_values(log_src_ref, sums_ref, more_ref)
    count = scores_ref.shape[0]
    columns_either(rows, (scores_ref, log_tgt_ref), kept_columns, rows_ref, high_ref, sum_ref, 0, count)
    columns_finish(high_ref, sum_ref, log_tgt_ref, cols_ref, 0, count)
    rows_either(scores_ref, cols_ref, kept, sum_ref, top_ref, out_ref)


def last_kernel(merged, scores_ref, sums_ref, more_ref, log_src_ref, log_tgt_ref, *refs):
    kept_columns, (out_ref, row_ref, col_ref) = refs[:3], refs[3:6]
    rows_ref, values_ref, cols_ref, high_ref, sum_ref = refs[6:]
    own_rows, own_cols = out_ref.shape
    rows = row_values(log_src_ref, sums_ref, more_ref)
    values_ref[...] = rows
    base = pl.multiple_of(lax.rem(lax.div(lax.axis_index("tgt"), 2), merged) * own_cols, own_cols)
    lanes = pl.ds(pl.multiple_of(lax.axis_index("src") * own_rows, own_rows), own_rows)
    columns_either(rows, (scores_ref, log_tgt_ref), kept_columns, rows_ref, high_ref, sum_ref, base, own_cols)
    columns_finish(high_ref, sum_ref, log_tgt_ref, cols_ref, base, own_cols)
    row_ref[...] = values_ref[:, lanes] * LN2
    col_ref[...] = cols_ref[...].T[0:1, :] * LN2
    block = scores_ref[pl.ds(base, own_cols), lanes] + values_ref[:, lanes] + cols_ref[:, 0:1]
    out_ref[...] = (block * LN2).T


def swap(value, axis, offset):
    return lax.ppermute(value, axis, [(i, i ^ offset) for i in range(lax.axis_size(axis))])


def staged_parts(value, axis, low, width):
    size = lax.axis_size(axis)
    terms = [value]
    while low < size:
        span = min(width, size // low)
        value = tree(terms, jnp.add)
        terms = [value] + [swap(value, axis, low * j) for j in range(1, span)]
        low *= span
    return terms


def more(held, axis, low, goal):
    unit = held[0].shape[0]
    while sum(part.shape[0] for part in held) < goal * unit:
        known = held[0] if len(held) == 1 else jnp.concatenate(held, axis=0)
        held.append(swap(known, axis, low * known.shape[0] // unit))


def shards(coupling, src_pcs, tgt_pcs, src_mass, tgt_mass):
    f32 = jnp.float32
    pcs = src_pcs.shape[0]
    rows, cols = coupling.shape
    src_size, tgt_size = lax.axis_size("src"), lax.axis_size("tgt")
    total_rows, total_cols = rows * src_size, cols * tgt_size
    merged = 1
    while 2 * merged * 2 <= tgt_size and 2 * merged * cols * total_rows * 4 <= SCORES_BYTES:
        merged *= 2
    wide = merged * cols
    packed_rows = -(-(pcs + 1) // 8) * 8

    arguments = (coupling, src_pcs, tgt_pcs, src_mass.reshape(1, -1), tgt_mass.reshape(1, -1))
    half, whole, moment = pl.pallas_call(
        front_kernel,
        out_shape=(
            pltpu.VMEM((packed_rows, rows // 2), f32),
            pltpu.VMEM((packed_rows, cols), f32),
            pltpu.VMEM((DEPTH // 2, LANES), f32),
        ),
        in_specs=[pl.BlockSpec(memory_space=pltpu.HBM)] * 5,
        out_specs=(VMEM,) * 3,
        scratch_shapes=[pltpu.VMEM(a.shape, a.dtype) for a in arguments]
        + [pltpu.SemaphoreType.DMA((5,))],
        compiler_params=params(8),
    )(*[pltpu.with_memory_space_constraint(a, pltpu.HBM) for a in arguments])

    moment = moment + swap(moment, "tgt", 1)
    half, whole, moment = lax.optimization_barrier((half, whole, moment))
    parts = staged_parts(moment, "tgt", 2, 4)
    sources, targets = [half], [whole]
    more(sources, "src", 1, 2)
    more(targets, "tgt", 2, min(2, merged))
    parts, sources, targets = lax.optimization_barrier((parts, sources, targets))
    moments = staged_parts(tree(parts, jnp.add), "src", 1, 4)
    more(sources, "src", 1, src_size)
    more(targets, "tgt", 2, merged)
    sources, moments = lax.optimization_barrier((sources, moments))
    near = jnp.concatenate(sources, axis=0)
    far = swap(near, "tgt", 1)

    scores, sums, log_src, log_tgt = pl.pallas_call(
        functools.partial(start_kernel, pcs, total_rows * total_cols, merged, src_size),
        out_shape=(
            jax.ShapeDtypeStruct((wide, total_rows), f32),
            jax.ShapeDtypeStruct((1, total_rows), f32),
            jax.ShapeDtypeStruct((1, total_rows), f32),
            jax.ShapeDtypeStruct((wide, LANES), f32),
        ),
        in_specs=[VMEM] * (2 + len(targets) + len(moments)),
        out_specs=(VMEM,) * 4,
        scratch_shapes=[
            pltpu.VMEM((4 * DEPTH, total_rows), jnp.bfloat16),
            pltpu.VMEM((wide, 4 * DEPTH), jnp.bfloat16),
            pltpu.VMEM((8, total_rows), f32),
        ],
        compiler_params=params(16),
    )(near, far, *targets, *moments)

    def both(value):
        offset = 2 * merged
        while offset < tgt_size:
            value = logsum(value, swap(value, "tgt", offset))
            offset *= 2
        return value, swap(value, "tgt", 1)

    bf16, block = jnp.bfloat16, (wide, total_rows)

    def call(kernel, sums, extra, outs, scratch):
        return pl.pallas_call(
            kernel,
            out_shape=tuple(jax.ShapeDtypeStruct(shape, bf16 if shape == block else f32) for shape in outs),
            in_specs=[VMEM] * (5 + len(extra)),
            out_specs=(VMEM,) * len(outs),
            scratch_shapes=[pltpu.VMEM(shape, f32) for shape in scratch],
            compiler_params=params(10),
        )(scores, *both(sums), log_src, log_tgt, *extra)

    line, lines, pads = (1, total_rows), (8, total_rows), (wide, LANES)
    sums, *kept_rows = call(
        first_kernel, sums, (), (line, block, lines, pads), (lines, pads, pads)
    )
    sums, *kept_columns = call(
        second_kernel, sums, kept_rows, (line, block, pads, line), (lines, pads, pads, lines)
    )
    for iteration in range(ITERS - 3):
        (sums,) = call(
            later_kernel, sums, (*kept_rows, *kept_columns), (line,), (lines, pads, pads, pads, lines)
        )
    pads = (cols, LANES)
    log_coupling, row_potential, col_potential = call(
        functools.partial(last_kernel, merged), sums, kept_columns,
        ((rows, cols), (1, rows), (1, cols)), (lines, line, pads, pads, pads),
    )
    return log_coupling, row_potential.reshape(-1), col_potential.reshape(-1)


def solution(mesh):
    in_specs = (P("src", "tgt"), P(None, "src"), P(None, "tgt"), P("src"), P("tgt"))
    out_specs = (P("src", "tgt"), P("src"), P("tgt"))
    return jax.shard_map(shards, mesh=mesh, in_specs=in_specs, out_specs=out_specs, check_vma=False)
```

```python
import functools
import math

import jax
import jax.numpy as jnp
from jax import lax
from jax.experimental import pallas as pl
from jax.experimental.pallas import tpu as pltpu
from jax.sharding import PartitionSpec as P

ITERS = 4

eps_reg = 0.5
marg_power = 1.0 / (1.0 + eps_reg)
tiny_eps = 1e-06

LANES = 128
DEPTH = 64
LN2 = math.log(2.0)
SCORES_BYTES = 1 << 24
LIFT = 57.0
SPAN = 150.0
VMEM = pl.BlockSpec(memory_space=pltpu.VMEM)


def params(mib):
    return pltpu.CompilerParams(vmem_limit_bytes=mib << 20)


def tree(values, combine):
    values = list(values)
    while len(values) > 1:
        paired = [combine(values[i], values[i + 1]) for i in range(0, len(values) - 1, 2)]
        values = paired + ([values[-1]] if len(values) % 2 else [])
    return values[0]


def pieces(value):
    high = value.astype(jnp.bfloat16)
    rest = value - high.astype(jnp.float32)
    middle = rest.astype(jnp.bfloat16)
    low = (rest - middle.astype(jnp.float32)).astype(jnp.bfloat16)
    return high, middle, low


def padded(value):
    return jnp.concatenate(
        [value, jnp.zeros((DEPTH - value.shape[0], value.shape[1]), value.dtype)], axis=0
    )


def front_kernel(*refs):
    sources, (half_ref, whole_ref, moment_ref), local, sems = refs[:5], refs[5:8], refs[8:13], refs[13]
    copies = [pltpu.make_async_copy(a, b, sems.at[i]) for i, (a, b) in enumerate(zip(sources, local))]
    for copy in copies:
        copy.start()
    coupling_ref, src_ref, tgt_ref, src_mass_ref, tgt_mass_ref = local
    pcs = src_ref.shape[0]
    half = half_ref.shape[1]
    odd = lax.rem(lax.axis_index("tgt"), 2)
    for copy in copies[1:]:
        copy.wait()
    src = src_ref[...].astype(jnp.float32)
    tgt = tgt_ref[...].astype(jnp.float32)
    below = jnp.zeros((half_ref.shape[0] - pcs - 1, 2 * half), jnp.float32)
    joined = jnp.concatenate([src, jnp.log2(src_mass_ref[...]), below], axis=0)
    half_ref[...] = jnp.where(odd == 0, joined[:, :half], joined[:, half:])
    below = jnp.zeros((half_ref.shape[0] - pcs - 1, tgt.shape[1]), jnp.float32)
    whole_ref[...] = jnp.concatenate([tgt, jnp.log2(tgt_mass_ref[...]), below], axis=0)
    src = padded(src).astype(jnp.bfloat16)
    tgt = padded(tgt).astype(jnp.bfloat16)
    twice = jnp.concatenate([src, src], axis=0)
    copies[0].wait()
    panel = jnp.dot(twice, coupling_ref[...], preferred_element_type=jnp.float32)
    moment = sum(
        lax.dot_general(tgt, part, (((1,), (1,)), ((), ())), preferred_element_type=jnp.float32)
        for part in pieces(panel)
    )
    lane = lax.broadcasted_iota(jnp.int32, (DEPTH // 2, LANES), 1)
    moment_ref[...] = jnp.where(lane < DEPTH, moment[: DEPTH // 2], moment[DEPTH // 2 :])


def start_kernel(pcs, entries, merged, blocks, *refs):
    near_ref, far_ref = refs[:2]
    tgt_refs = refs[2 : 2 + merged]
    moment_refs = refs[2 + merged : -7]
    scores_ref, sums_ref, log_src_ref, log_tgt_ref, src_all, weights, top_ref = refs[-7:]
    packed_rows = near_ref.shape[0] // blocks
    half = near_ref.shape[1]
    width = tgt_refs[0].shape[1]
    z = lax.axis_index("src")
    t = lax.axis_index("tgt")
    odd = lax.rem(t, 2)
    total_rows = 2 * half * blocks
    total_cols = width * lax.axis_size("tgt")

    packed = tree([ref[...] for ref in moment_refs], jnp.add) * entries ** (-0.5)
    spread = jnp.sqrt(jnp.sum(packed * packed) * (1.0 / (pcs * pcs)) + tiny_eps)
    packed = packed / spread * (2.0 / (eps_reg * pcs) / LN2)
    turned = pltpu.roll(packed, DEPTH, axis=1)
    left = lax.broadcasted_iota(jnp.int32, packed.shape, 1) < DEPTH
    normed = jnp.concatenate(
        [jnp.where(left, packed, turned), jnp.where(left, turned, packed)], axis=0
    )
    normed = jnp.concatenate([normed, normed], axis=1)

    for b in range(blocks):
        place = jnp.bitwise_xor(z, b)
        for ref, side in ((near_ref, odd), (far_ref, 1 - odd)):
            block = ref[pl.ds(b * packed_rows, packed_rows), :]
            lanes = pl.ds(pl.multiple_of((place * 2 + side) * half, half), half)
            log_src_ref[:, lanes] = marg_power * (block[pcs : pcs + 1] + math.log2(total_cols))
            block = padded(block).astype(jnp.bfloat16)
            for copy in range(4):
                src_all[pl.ds(copy * DEPTH, DEPTH), lanes] = block

    parts = pieces(normed)
    first = lax.broadcasted_iota(jnp.int32, (width, LANES), 1) < DEPTH
    mine = lax.rem(lax.div(t, 2), merged)
    for b in range(merged):
        base = pl.multiple_of(jnp.bitwise_xor(mine, b) * width, width)
        turned = padded(tgt_refs[b][...]).T
        log_tgt_ref[pl.ds(base, width), :] = jnp.broadcast_to(
            marg_power * (turned[:, pcs : pcs + 1] + math.log2(total_rows)), (width, LANES)
        )
        turned = turned.astype(jnp.bfloat16)
        weighted = sum(jnp.dot(turned, part, preferred_element_type=jnp.float32) for part in parts)
        high, middle, low = pieces(weighted)
        weights[pl.ds(base, width), :LANES] = jnp.where(first, high[:, :LANES], middle[:, :LANES])
        weights[pl.ds(base, width), LANES:] = jnp.where(
            first, low[:, LANES:], jnp.zeros((width, LANES), jnp.bfloat16)
        )

    chunk, rows = 256, min(1024, scores_ref.shape[0])
    across = total_rows // chunk

    def step(i, carry):
        lanes = pl.ds(pl.multiple_of(lax.rem(i, across) * chunk, chunk), chunk)
        at = pl.ds(pl.multiple_of(lax.div(i, across) * rows, rows), rows)
        scores_ref[at, lanes] = jnp.dot(
            weights[at, :], src_all[:, lanes], preferred_element_type=jnp.float32
        )
        return carry

    lax.fori_loop(0, across * (scores_ref.shape[0] // rows), step, 0)
    rows_highest(scores_ref, None, top_ref)
    rows_exp(scores_ref, None, top_ref, sums_ref, None)


def down(highest, summed):
    top = jnp.max(highest, axis=0, keepdims=True)
    return top + jnp.log2(jnp.sum(summed * jnp.exp2(highest - top), axis=0, keepdims=True))


def logsum(one, other):
    top = jnp.maximum(one, other)
    return top + jnp.log2(jnp.exp2(one - top) + jnp.exp2(other - top))


def row_values(log_src_ref, sums_ref, more_ref):
    return log_src_ref[...] - marg_power * logsum(sums_ref[...], more_ref[...])


def lane_tiles(ref):
    return [pl.ds(j, LANES) for j in range(0, ref.shape[1], LANES)]


def halves(low):
    low = pl.multiple_of(low, 16)
    return pl.ds(low, 16), [pl.ds(low, 8), pl.ds(pl.multiple_of(low + 8, 8), 8)]


def columns_exp(scores_ref, rows_ref, top_ref, sum_ref, base, count, keep_ref):
    tiles = lane_tiles(scores_ref)

    def highest(i, carry):
        places = [pl.ds(pl.multiple_of(i * 64 + g * 8, 8), 8) for g in range(8)]
        sources = [pl.ds(pl.multiple_of(base + i * 64 + g * 8, 8), 8) for g in range(8)]
        tops = [None] * 8
        for lanes in tiles:
            row = rows_ref[:, lanes]
            for g, source in enumerate(sources):
                term = scores_ref[source, lanes] + row
                tops[g] = term if tops[g] is None else jnp.maximum(tops[g], term)
        for place, top in zip(places, tops):
            top_ref[place, :] = top - LIFT
        return carry

    def total(i, carry):
        pairs = [halves(base + i * 64 + g * 16) for g in range(4)]
        places = [place for g in range(4) for place in halves(i * 64 + g * 16)[1]]
        tops = [top_ref[place, :] for place in places]
        sums = [jnp.zeros((8, LANES), jnp.float32)] * 8
        for lanes in tiles:
            row = rows_ref[:, lanes]
            for g, (at, sources) in enumerate(pairs):
                parts = []
                for h, source in enumerate(sources):
                    parts.append(jnp.exp2(scores_ref[source, lanes] + row - tops[2 * g + h]))
                    sums[2 * g + h] = sums[2 * g + h] + parts[h]
                if keep_ref is not None:
                    keep_ref[at, lanes] = jnp.concatenate(parts, axis=0).astype(keep_ref.dtype)
        for place, value in zip(places, sums):
            sum_ref[place, :] = value
        return carry

    lax.fori_loop(0, count // 64, highest, 0)
    lax.fori_loop(0, count // 64, total, 0)


def columns_product(keep_ref, kept_top_ref, factor_ref, shift, top_ref, sum_ref, base, count):
    tiles = lane_tiles(keep_ref)

    def total(i, carry):
        pairs = [halves(base + i * 64 + g * 16)[0] for g in range(4)]
        sums = [jnp.zeros((8, LANES), jnp.float32)] * 8
        for lanes in tiles:
            factor = factor_ref[:, lanes]
            for g, at in enumerate(pairs):
                kept = keep_ref[at, lanes].astype(jnp.float32)
                sums[2 * g] = sums[2 * g] + kept[:8] * factor
                sums[2 * g + 1] = sums[2 * g + 1] + kept[8:] * factor
        for g, at in enumerate(pairs):
            place, _ = halves(i * 64 + g * 16)
            sum_ref[place, :] = jnp.concatenate(sums[2 * g : 2 * g + 2], axis=0)
            top_ref[place, :] = kept_top_ref[at, :] + (shift - LIFT)
        return carry

    lax.fori_loop(0, count // 64, total, 0)


def columns_finish(top_ref, sum_ref, log_tgt_ref, cols_ref, base, count):
    part = min(count, 2048)
    for low in range(0, count, part):
        here = pl.ds(low, part)
        tops = top_ref[here, :]
        top = jnp.max(tops, axis=1, keepdims=True)
        total = jnp.sum(sum_ref[here, :] * jnp.exp2(tops - top), axis=1, keepdims=True)
        at = pl.ds(pl.multiple_of(base + low, part), part)
        cols_ref[here, :] = log_tgt_ref[at, :] - marg_power * (top + jnp.log2(total))


BESIDE, DEEP = 8, 4


def over_tiles(count, width, body, first, done):
    for start in range(0, width, BESIDE * LANES):
        tiles = [pl.ds(start + j * LANES, LANES) for j in range(BESIDE)]

        def step(i, carry, tiles=tiles):
            carry = list(carry)
            body([halves((i * DEEP + g) * 16) for g in range(DEEP)], tiles, carry)
            return tuple(carry)

        state = lax.fori_loop(0, count // (16 * DEEP), step, tuple(first for _ in tiles))
        for lanes, value in zip(tiles, state):
            done(lanes, value)


def rows_highest(scores_ref, cols_ref, top_ref):
    def body(pairs, tiles, carry):
        for _, places in pairs:
            for place in places:
                if cols_ref is not None:
                    potential = cols_ref[place, :]
                for j, lanes in enumerate(tiles):
                    term = scores_ref[place, lanes]
                    if cols_ref is not None:
                        term = term + potential
                    carry[j] = jnp.maximum(carry[j], term)

    def done(lanes, value):
        top_ref[:, lanes] = value - LIFT

    over_tiles(*scores_ref.shape, body, jnp.full((8, LANES), -jnp.inf, jnp.float32), done)


def rows_exp(scores_ref, cols_ref, top_ref, out_ref, keep_ref):
    def body(pairs, tiles, carry):
        tops = [top_ref[:, lanes] for lanes in tiles]
        for at, places in pairs:
            if cols_ref is not None:
                potentials = [cols_ref[place, :] for place in places]
            for j, lanes in enumerate(tiles):
                terms = [scores_ref[place, lanes] for place in places]
                if cols_ref is not None:
                    terms = [term + potential for term, potential in zip(terms, potentials)]
                parts = [jnp.exp2(term - tops[j]) for term in terms]
                if keep_ref is not None:
                    keep_ref[at, lanes] = jnp.concatenate(parts, axis=0).astype(keep_ref.dtype)
                carry[j] = carry[j] + (parts[0] + parts[1])

    def done(lanes, value):
        out_ref[:, lanes] = down(top_ref[:, lanes], value)

    over_tiles(*scores_ref.shape, body, jnp.zeros((8, LANES), jnp.float32), done)


def rows_product(keep_ref, kept_top_ref, factor_ref, shift, out_ref):
    def body(pairs, tiles, carry):
        for at, places in pairs:
            factors = [factor_ref[place, :] for place in places]
            for j, lanes in enumerate(tiles):
                kept = keep_ref[at, lanes].astype(jnp.float32)
                carry[j] = carry[j] + (kept[:8] * factors[0] + kept[8:] * factors[1])

    def done(lanes, value):
        out_ref[:, lanes] = down(kept_top_ref[:, lanes] + (shift - LIFT), value)

    over_tiles(*keep_ref.shape, body, jnp.zeros((8, LANES), jnp.float32), done)


def columns_either(rows, args, kept, rows_ref, top_ref, sum_ref, base, count):
    scores_ref, log_tgt_ref = args
    keep_ref, kept_top_ref, kept_rows_ref = kept
    change = rows - kept_rows_ref[...]
    shift = jnp.max(change)
    near = shift - jnp.min(change) <= SPAN

    @pl.when(near)
    def _():
        rows_ref[...] = jnp.broadcast_to(jnp.exp2(change - (shift - LIFT)), rows_ref.shape)
        columns_product(keep_ref, kept_top_ref, rows_ref, shift, top_ref, sum_ref, base, count)

    @pl.when(jnp.logical_not(near))
    def _():
        rows_ref[...] = jnp.broadcast_to(rows, rows_ref.shape)
        columns_exp(scores_ref, rows_ref, top_ref, sum_ref, base, count, None)


def rows_either(scores_ref, cols_ref, kept, factor_ref, top_ref, out_ref):
    keep_ref, kept_top_ref, kept_cols_ref = kept
    change = cols_ref[...] - kept_cols_ref[...]
    shift = jnp.max(change)
    near = shift - jnp.min(change) <= SPAN

    @pl.when(near)
    def _():
        factor_ref[...] = jnp.exp2(cols_ref[...] - kept_cols_ref[...] - (shift - LIFT))
        rows_product(keep_ref, kept_top_ref, factor_ref, shift, out_ref)

    @pl.when(jnp.logical_not(near))
    def _():
        rows_highest(scores_ref, cols_ref, top_ref)
        rows_exp(scores_ref, cols_ref, top_ref, out_ref, None)


def first_kernel(scores_ref, sums_ref, more_ref, log_src_ref, log_tgt_ref, out_ref, keep_ref, top_ref, cols_ref, rows_ref, high_ref, sum_ref):
    rows_ref[...] = jnp.broadcast_to(row_values(log_src_ref, sums_ref, more_ref), rows_ref.shape)
    count = scores_ref.shape[0]
    columns_exp(scores_ref, rows_ref, high_ref, sum_ref, 0, count, None)
    columns_finish(high_ref, sum_ref, log_tgt_ref, cols_ref, 0, count)
    rows_highest(scores_ref, cols_ref, top_ref)
    rows_exp(scores_ref, cols_ref, top_ref, out_ref, keep_ref)


def second_kernel(scores_ref, sums_ref, more_ref, log_src_ref, log_tgt_ref, *refs):
    kept, (out_ref, keep_ref, high_ref, base_ref) = refs[:3], refs[3:7]
    rows_ref, cols_ref, sum_ref, top_ref = refs[7:]
    base_ref[...] = row_values(log_src_ref, sums_ref, more_ref)
    rows_ref[...] = jnp.broadcast_to(base_ref[...], rows_ref.shape)
    count = scores_ref.shape[0]
    columns_exp(scores_ref, rows_ref, high_ref, sum_ref, 0, count, keep_ref)
    columns_finish(high_ref, sum_ref, log_tgt_ref, cols_ref, 0, count)
    rows_either(scores_ref, cols_ref, kept, sum_ref, top_ref, out_ref)


def later_kernel(scores_ref, sums_ref, more_ref, log_src_ref, log_tgt_ref, *refs):
    kept, kept_columns, out_ref = refs[:3], refs[3:6], refs[6]
    rows_ref, cols_ref, high_ref, sum_ref, top_ref = refs[7:]
    rows = row_values(log_src_ref, sums_ref, more_ref)
    count = scores_ref.shape[0]
    columns_either(rows, (scores_ref, log_tgt_ref), kept_columns, rows_ref, high_ref, sum_ref, 0, count)
    columns_finish(high_ref, sum_ref, log_tgt_ref, cols_ref, 0, count)
    rows_either(scores_ref, cols_ref, kept, sum_ref, top_ref, out_ref)


def last_kernel(merged, scores_ref, sums_ref, more_ref, log_src_ref, log_tgt_ref, *refs):
    kept_columns, (out_ref, row_ref, col_ref) = refs[:3], refs[3:6]
    rows_ref, values_ref, cols_ref, high_ref, sum_ref = refs[6:]
    own_rows, own_cols = out_ref.shape
    rows = row_values(log_src_ref, sums_ref, more_ref)
    values_ref[...] = rows
    base = pl.multiple_of(lax.rem(lax.div(lax.axis_index("tgt"), 2), merged) * own_cols, own_cols)
    lanes = pl.ds(pl.multiple_of(lax.axis_index("src") * own_rows, own_rows), own_rows)
    columns_either(rows, (scores_ref, log_tgt_ref), kept_columns, rows_ref, high_ref, sum_ref, base, own_cols)
    columns_finish(high_ref, sum_ref, log_tgt_ref, cols_ref, base, own_cols)
    row_ref[...] = values_ref[:, lanes] * LN2
    col_ref[...] = cols_ref[...].T[0:1, :] * LN2
    block = scores_ref[pl.ds(base, own_cols), lanes] + values_ref[:, lanes] + cols_ref[:, 0:1]
    out_ref[...] = (block * LN2).T


def swap(value, axis, offset):
    return lax.ppermute(value, axis, [(i, i ^ offset) for i in range(lax.axis_size(axis))])


def staged_parts(value, axis, low, width):
    size = lax.axis_size(axis)
    terms = [value]
    while low < size:
        span = min(width, size // low)
        value = tree(terms, jnp.add)
        terms = [value] + [swap(value, axis, low * j) for j in range(1, span)]
        low *= span
    return terms


def shards(coupling, src_pcs, tgt_pcs, src_mass, tgt_mass):
    f32 = jnp.float32
    pcs = src_pcs.shape[0]
    rows, cols = coupling.shape
    src_size, tgt_size = lax.axis_size("src"), lax.axis_size("tgt")
    total_rows, total_cols = rows * src_size, cols * tgt_size
    merged = 1
    while 2 * merged * 2 <= tgt_size and 2 * merged * cols * total_rows * 4 <= SCORES_BYTES:
        merged *= 2
    wide = merged * cols
    packed_rows = -(-(pcs + 1) // 8) * 8

    arguments = (coupling, src_pcs, tgt_pcs, src_mass.reshape(1, -1), tgt_mass.reshape(1, -1))
    half, whole, moment = pl.pallas_call(
        front_kernel,
        out_shape=(
            pltpu.VMEM((packed_rows, rows // 2), f32),
            pltpu.VMEM((packed_rows, cols), f32),
            pltpu.VMEM((DEPTH // 2, LANES), f32),
        ),
        in_specs=[pl.BlockSpec(memory_space=pltpu.HBM)] * 5,
        out_specs=(VMEM,) * 3,
        scratch_shapes=[pltpu.VMEM(a.shape, a.dtype) for a in arguments]
        + [pltpu.SemaphoreType.DMA((5,))],
        compiler_params=params(8),
    )(*[pltpu.with_memory_space_constraint(a, pltpu.HBM) for a in arguments])

    sources = [half] + [swap(half, "src", b) for b in range(1, src_size)]
    targets = [whole] + [swap(whole, "tgt", 2 * b) for b in range(1, min(2, merged))]
    moment = moment + swap(moment, "tgt", 1)
    moment, whole, sources, targets = lax.optimization_barrier((moment, whole, sources, targets))
    parts = staged_parts(moment, "tgt", 2, 4)
    targets += [swap(whole, "tgt", 2 * b) for b in range(2, merged)]
    parts, sources, targets = lax.optimization_barrier((parts, sources, targets))
    moments = staged_parts(tree(parts, jnp.add), "src", 1, 4)
    near = jnp.concatenate(sources, axis=0)
    far = swap(near, "tgt", 1)

    scores, sums, log_src, log_tgt = pl.pallas_call(
        functools.partial(start_kernel, pcs, total_rows * total_cols, merged, src_size),
        out_shape=(
            jax.ShapeDtypeStruct((wide, total_rows), f32),
            jax.ShapeDtypeStruct((1, total_rows), f32),
            jax.ShapeDtypeStruct((1, total_rows), f32),
            jax.ShapeDtypeStruct((wide, LANES), f32),
        ),
        in_specs=[VMEM] * (2 + len(targets) + len(moments)),
        out_specs=(VMEM,) * 4,
        scratch_shapes=[
            pltpu.VMEM((4 * DEPTH, total_rows), jnp.bfloat16),
            pltpu.VMEM((wide, 4 * DEPTH), jnp.bfloat16),
            pltpu.VMEM((8, total_rows), f32),
        ],
        compiler_params=params(16),
    )(near, far, *targets, *moments)

    def both(value):
        offset = 2 * merged
        while offset < tgt_size:
            value = logsum(value, swap(value, "tgt", offset))
            offset *= 2
        return value, swap(value, "tgt", 1)

    bf16, block = jnp.bfloat16, (wide, total_rows)

    def call(kernel, sums, extra, outs, scratch):
        return pl.pallas_call(
            kernel,
            out_shape=tuple(jax.ShapeDtypeStruct(shape, bf16 if shape == block else f32) for shape in outs),
            in_specs=[VMEM] * (5 + len(extra)),
            out_specs=(VMEM,) * len(outs),
            scratch_shapes=[pltpu.VMEM(shape, f32) for shape in scratch],
            compiler_params=params(10),
        )(scores, *both(sums), log_src, log_tgt, *extra)

    line, lines, pads = (1, total_rows), (8, total_rows), (wide, LANES)
    sums, *kept_rows = call(
        first_kernel, sums, (), (line, block, lines, pads), (lines, pads, pads)
    )
    sums, *kept_columns = call(
        second_kernel, sums, kept_rows, (line, block, pads, line), (lines, pads, pads, lines)
    )
    for iteration in range(ITERS - 3):
        (sums,) = call(
            later_kernel, sums, (*kept_rows, *kept_columns), (line,), (lines, pads, pads, pads, lines)
        )
    pads = (cols, LANES)
    log_coupling, row_potential, col_potential = call(
        functools.partial(last_kernel, merged), sums, kept_columns,
        ((rows, cols), (1, rows), (1, cols)), (lines, line, pads, pads, pads),
    )
    return log_coupling, row_potential.reshape(-1), col_potential.reshape(-1)


def solution(mesh):
    in_specs = (P("src", "tgt"), P(None, "src"), P(None, "tgt"), P("src"), P("tgt"))
    out_specs = (P("src", "tgt"), P("src"), P("tgt"))
    return jax.shard_map(shards, mesh=mesh, in_specs=in_specs, out_specs=out_specs, check_vma=False)
```

```python
import functools
import math

import jax
import jax.numpy as jnp
from jax import lax
from jax.experimental import pallas as pl
from jax.experimental.pallas import tpu as pltpu
from jax.sharding import PartitionSpec as P

ITERS = 4

eps_reg = 0.5
marg_power = 1.0 / (1.0 + eps_reg)
tiny_eps = 1e-06

LANES = 128
DEPTH = 64
LN2 = math.log(2.0)
SCORES_BYTES = 1 << 24
LIFT = 54.0
SPAN = 145.0
VMEM = pl.BlockSpec(memory_space=pltpu.VMEM)


def params(mib):
    return pltpu.CompilerParams(vmem_limit_bytes=mib << 20)


def tree(values, combine):
    values = list(values)
    while len(values) > 1:
        paired = [combine(values[i], values[i + 1]) for i in range(0, len(values) - 1, 2)]
        values = paired + ([values[-1]] if len(values) % 2 else [])
    return values[0]


def pieces(value):
    high = value.astype(jnp.bfloat16)
    rest = value - high.astype(jnp.float32)
    middle = rest.astype(jnp.bfloat16)
    low = (rest - middle.astype(jnp.float32)).astype(jnp.bfloat16)
    return high, middle, low


def padded(value):
    return jnp.concatenate(
        [value, jnp.zeros((DEPTH - value.shape[0], value.shape[1]), value.dtype)], axis=0
    )


def front_kernel(*refs):
    sources, (half_ref, whole_ref, moment_ref), local, sems = refs[:5], refs[5:8], refs[8:13], refs[13]
    copies = [pltpu.make_async_copy(a, b, sems.at[i]) for i, (a, b) in enumerate(zip(sources, local))]
    for copy in copies:
        copy.start()
    coupling_ref, src_ref, tgt_ref, src_mass_ref, tgt_mass_ref = local
    pcs = src_ref.shape[0]
    half = half_ref.shape[1]
    odd = lax.rem(lax.axis_index("tgt"), 2)
    for copy in copies[1:]:
        copy.wait()
    src = src_ref[...].astype(jnp.float32)
    tgt = tgt_ref[...].astype(jnp.float32)
    below = jnp.zeros((half_ref.shape[0] - pcs - 1, 2 * half), jnp.float32)
    joined = jnp.concatenate([src, jnp.log2(src_mass_ref[...]), below], axis=0)
    half_ref[...] = jnp.where(odd == 0, joined[:, :half], joined[:, half:])
    below = jnp.zeros((half_ref.shape[0] - pcs - 1, tgt.shape[1]), jnp.float32)
    whole_ref[...] = jnp.concatenate([tgt, jnp.log2(tgt_mass_ref[...]), below], axis=0)
    src = padded(src).astype(jnp.bfloat16)
    tgt = padded(tgt).astype(jnp.bfloat16)
    twice = jnp.concatenate([src, src], axis=0)
    copies[0].wait()
    panel = jnp.dot(twice, coupling_ref[...], preferred_element_type=jnp.float32)
    moment = sum(
        lax.dot_general(tgt, part, (((1,), (1,)), ((), ())), preferred_element_type=jnp.float32)
        for part in pieces(panel)
    )
    lane = lax.broadcasted_iota(jnp.int32, (DEPTH // 2, LANES), 1)
    moment_ref[...] = jnp.where(lane < DEPTH, moment[: DEPTH // 2], moment[DEPTH // 2 :])


def start_kernel(pcs, entries, merged, blocks, *refs):
    near_ref, far_ref = refs[:2]
    tgt_refs = refs[2 : 2 + merged.bit_length()]
    moment_refs = refs[2 + merged.bit_length() : -7]
    scores_ref, sums_ref, log_src_ref, log_tgt_ref, src_all, weights, top_ref = refs[-7:]
    packed_rows = near_ref.shape[0] // blocks
    half = near_ref.shape[1]
    width = tgt_refs[0].shape[1]
    targets = [ref.at[pl.ds(i, packed_rows), :] for ref in tgt_refs for i in range(0, ref.shape[0], packed_rows)]
    z = lax.axis_index("src")
    t = lax.axis_index("tgt")
    odd = lax.rem(t, 2)
    total_rows = 2 * half * blocks
    total_cols = width * lax.axis_size("tgt")

    packed = tree([ref[...] for ref in moment_refs], jnp.add) * entries ** (-0.5)
    spread = jnp.sqrt(jnp.sum(packed * packed) * (1.0 / (pcs * pcs)) + tiny_eps)
    packed = packed / spread * (2.0 / (eps_reg * pcs) / LN2)
    turned = pltpu.roll(packed, DEPTH, axis=1)
    left = lax.broadcasted_iota(jnp.int32, packed.shape, 1) < DEPTH
    normed = jnp.concatenate(
        [jnp.where(left, packed, turned), jnp.where(left, turned, packed)], axis=0
    )
    normed = jnp.concatenate([normed, normed], axis=1)

    for b in range(blocks):
        place = jnp.bitwise_xor(z, b)
        for ref, side in ((near_ref, odd), (far_ref, 1 - odd)):
            block = ref[pl.ds(b * packed_rows, packed_rows), :]
            lanes = pl.ds(pl.multiple_of((place * 2 + side) * half, half), half)
            log_src_ref[:, lanes] = marg_power * (block[pcs : pcs + 1] + math.log2(total_cols))
            block = padded(block).astype(jnp.bfloat16)
            for copy in range(4):
                src_all[pl.ds(copy * DEPTH, DEPTH), lanes] = block

    parts = pieces(normed)
    first = lax.broadcasted_iota(jnp.int32, (width, LANES), 1) < DEPTH
    mine = lax.rem(lax.div(t, 2), merged)
    for b in range(merged):
        base = pl.multiple_of(jnp.bitwise_xor(mine, b) * width, width)
        turned = padded(targets[b][...]).T
        log_tgt_ref[pl.ds(base, width), :] = jnp.broadcast_to(
            marg_power * (turned[:, pcs : pcs + 1] + math.log2(total_rows)), (width, LANES)
        )
        turned = turned.astype(jnp.bfloat16)
        weighted = sum(jnp.dot(turned, part, preferred_element_type=jnp.float32) for part in parts)
        high, middle, low = pieces(weighted)
        weights[pl.ds(base, width), :LANES] = jnp.where(first, high[:, :LANES], middle[:, :LANES])
        weights[pl.ds(base, width), LANES:] = jnp.where(
            first, low[:, LANES:], jnp.zeros((width, LANES), jnp.bfloat16)
        )

    chunk, rows = 1024, min(256, scores_ref.shape[0])
    across = total_rows // chunk

    def step(i, carry):
        lanes = pl.ds(pl.multiple_of(lax.rem(i, across) * chunk, chunk), chunk)
        at = pl.ds(pl.multiple_of(lax.div(i, across) * rows, rows), rows)
        scores_ref[at, lanes] = jnp.dot(
            weights[at, :], src_all[:, lanes], preferred_element_type=jnp.float32
        )
        return carry

    lax.fori_loop(0, across * (scores_ref.shape[0] // rows), step, 0)
    rows_highest(scores_ref, None, top_ref)
    rows_exp(scores_ref, None, top_ref, sums_ref, None)


def down(highest, summed):
    top = jnp.max(highest, axis=0, keepdims=True)
    return top + jnp.log2(jnp.sum(summed * jnp.exp2(highest - top), axis=0, keepdims=True))


def logsum(one, other):
    top = jnp.maximum(one, other)
    return top + jnp.log2(jnp.exp2(one - top) + jnp.exp2(other - top))


def row_values(log_src_ref, sums_ref, more_ref):
    return log_src_ref[...] - marg_power * logsum(sums_ref[...], more_ref[...])


def lane_tiles(ref):
    return [pl.ds(j, LANES) for j in range(0, ref.shape[1], LANES)]


def halves(low):
    low = pl.multiple_of(low, 16)
    return pl.ds(low, 16), [pl.ds(low, 8), pl.ds(pl.multiple_of(low + 8, 8), 8)]


def columns_exp(scores_ref, rows_ref, top_ref, sum_ref, base, count, keep_ref):
    tiles = lane_tiles(scores_ref)

    def highest(i, carry):
        places = [pl.ds(pl.multiple_of(i * 64 + g * 8, 8), 8) for g in range(8)]
        sources = [pl.ds(pl.multiple_of(base + i * 64 + g * 8, 8), 8) for g in range(8)]
        tops = [None] * 8
        for lanes in tiles:
            row = rows_ref[:, lanes]
            for g, source in enumerate(sources):
                term = scores_ref[source, lanes] + row
                tops[g] = term if tops[g] is None else jnp.maximum(tops[g], term)
        for place, top in zip(places, tops):
            top_ref[place, :] = top - LIFT
        return carry

    def total(i, carry):
        pairs = [halves(base + i * 64 + g * 16) for g in range(4)]
        places = [place for g in range(4) for place in halves(i * 64 + g * 16)[1]]
        tops = [top_ref[place, :] for place in places]
        sums = [jnp.zeros((8, LANES), jnp.float32)] * 8
        for lanes in tiles:
            row = rows_ref[:, lanes]
            for g, (at, sources) in enumerate(pairs):
                parts = []
                for h, source in enumerate(sources):
                    parts.append(jnp.exp2(scores_ref[source, lanes] + row - tops[2 * g + h]))
                    sums[2 * g + h] = sums[2 * g + h] + parts[h]
                if keep_ref is not None:
                    keep_ref[at, lanes] = jnp.concatenate(parts, axis=0).astype(keep_ref.dtype)
        for place, value in zip(places, sums):
            sum_ref[place, :] = value
        return carry

    lax.fori_loop(0, count // 64, highest, 0)
    if keep_ref is not None:
        tops = top_ref[pl.ds(0, count), :]
        top_ref[pl.ds(0, count), :] = jnp.broadcast_to(jnp.max(tops, axis=1, keepdims=True), tops.shape)
    lax.fori_loop(0, count // 64, total, 0)


def split_rows(line):
    row = lax.broadcasted_iota(jnp.int32, (16, line.shape[1]), 0)
    high, middle, low = (part.astype(jnp.float32) for part in pieces(line))
    spread = jnp.where(row == 0, high, jnp.where(row == 1, middle, jnp.where(row == 2, low, 0.0)))
    return spread.astype(jnp.bfloat16)


def columns_product(keep_ref, kept_top_ref, factor, shift, top_ref, sum_ref, base, count):
    factors = split_rows(factor)
    factors = jnp.concatenate([factors, jnp.zeros((LANES - 16, factor.shape[1]), factors.dtype)], axis=0)
    part = min(count, 512)
    for low in range(0, count, part):
        here = pl.ds(low, part)
        at = pl.ds(pl.multiple_of(base + low, part), part)
        sum_ref[here, :] = lax.dot_general(
            keep_ref[at, :], factors, (((1,), (1,)), ((), ())), preferred_element_type=jnp.float32
        )
        top_ref[here, :] = kept_top_ref[at, :] + (shift - LIFT)


def columns_finish(top_ref, sum_ref, log_tgt_ref, cols_ref, base, count):
    part = min(count, 2048)
    for low in range(0, count, part):
        here = pl.ds(low, part)
        tops = top_ref[here, :]
        top = jnp.max(tops, axis=1, keepdims=True)
        total = jnp.sum(sum_ref[here, :] * jnp.exp2(tops - top), axis=1, keepdims=True)
        at = pl.ds(pl.multiple_of(base + low, part), part)
        cols_ref[here, :] = log_tgt_ref[at, :] - marg_power * (top + jnp.log2(total))


BESIDE, DEEP = 8, 4


def over_tiles(count, width, body, first, done):
    for start in range(0, width, BESIDE * LANES):
        tiles = [pl.ds(start + j * LANES, LANES) for j in range(BESIDE)]

        def step(i, carry, tiles=tiles):
            carry = list(carry)
            body([halves((i * DEEP + g) * 16) for g in range(DEEP)], tiles, carry)
            return tuple(carry)

        state = lax.fori_loop(0, count // (16 * DEEP), step, tuple(first for _ in tiles))
        for lanes, value in zip(tiles, state):
            done(lanes, value)


def rows_highest(scores_ref, cols_ref, top_ref):
    def body(pairs, tiles, carry):
        for _, places in pairs:
            for place in places:
                if cols_ref is not None:
                    potential = cols_ref[place, :]
                for j, lanes in enumerate(tiles):
                    term = scores_ref[place, lanes]
                    if cols_ref is not None:
                        term = term + potential
                    carry[j] = jnp.maximum(carry[j], term)

    def done(lanes, value):
        top_ref[:, lanes] = jnp.broadcast_to(jnp.max(value, axis=0, keepdims=True), value.shape) - LIFT

    over_tiles(*scores_ref.shape, body, jnp.full((8, LANES), -jnp.inf, jnp.float32), done)


def rows_exp(scores_ref, cols_ref, top_ref, out_ref, keep_ref):
    def body(pairs, tiles, carry):
        tops = [top_ref[:, lanes] for lanes in tiles]
        for at, places in pairs:
            if cols_ref is not None:
                potentials = [cols_ref[place, :] for place in places]
            for j, lanes in enumerate(tiles):
                terms = [scores_ref[place, lanes] for place in places]
                if cols_ref is not None:
                    terms = [term + potential for term, potential in zip(terms, potentials)]
                parts = [jnp.exp2(term - tops[j]) for term in terms]
                if keep_ref is not None:
                    keep_ref[at, lanes] = jnp.concatenate(parts, axis=0).astype(keep_ref.dtype)
                carry[j] = carry[j] + (parts[0] + parts[1])

    def done(lanes, value):
        out_ref[:, lanes] = down(top_ref[:, lanes], value)

    over_tiles(*scores_ref.shape, body, jnp.zeros((8, LANES), jnp.float32), done)


def rows_product(keep_ref, kept_top_ref, factor, shift, out_ref):
    factors = split_rows(factor.T[0:1, :])
    chunk = 512
    for start in range(0, keep_ref.shape[1], chunk):
        lanes = pl.ds(start, chunk)
        sums = jnp.dot(factors, keep_ref[:, lanes], preferred_element_type=jnp.float32)
        out_ref[:, lanes] = (
            kept_top_ref[0:1, lanes] + (shift - LIFT) + jnp.log2(jnp.sum(sums, axis=0, keepdims=True))
        )


def columns_either(rows, args, kept, rows_ref, top_ref, sum_ref, base, count):
    scores_ref, log_tgt_ref = args
    keep_ref, kept_top_ref, kept_rows_ref = kept
    change = rows - kept_rows_ref[...]
    shift = jnp.max(change)
    near = shift - jnp.min(change) <= SPAN

    @pl.when(near)
    def _():
        factor = jnp.exp2(change - (shift - LIFT))
        columns_product(keep_ref, kept_top_ref, factor, shift, top_ref, sum_ref, base, count)

    @pl.when(jnp.logical_not(near))
    def _():
        rows_ref[...] = jnp.broadcast_to(rows, rows_ref.shape)
        columns_exp(scores_ref, rows_ref, top_ref, sum_ref, base, count, None)


def rows_either(scores_ref, cols_ref, kept, top_ref, out_ref):
    keep_ref, kept_top_ref, kept_cols_ref = kept
    change = cols_ref[...] - kept_cols_ref[...]
    shift = jnp.max(change)
    near = shift - jnp.min(change) <= SPAN

    @pl.when(near)
    def _():
        factor = jnp.exp2(cols_ref[...] - kept_cols_ref[...] - (shift - LIFT))
        rows_product(keep_ref, kept_top_ref, factor, shift, out_ref)

    @pl.when(jnp.logical_not(near))
    def _():
        rows_highest(scores_ref, cols_ref, top_ref)
        rows_exp(scores_ref, cols_ref, top_ref, out_ref, None)


def first_kernel(scores_ref, sums_ref, more_ref, log_src_ref, log_tgt_ref, out_ref, keep_ref, top_ref, cols_ref, rows_ref, high_ref, sum_ref):
    rows_ref[...] = jnp.broadcast_to(row_values(log_src_ref, sums_ref, more_ref), rows_ref.shape)
    count = scores_ref.shape[0]
    columns_exp(scores_ref, rows_ref, high_ref, sum_ref, 0, count, None)
    columns_finish(high_ref, sum_ref, log_tgt_ref, cols_ref, 0, count)
    rows_highest(scores_ref, cols_ref, top_ref)
    rows_exp(scores_ref, cols_ref, top_ref, out_ref, keep_ref)


def second_kernel(scores_ref, sums_ref, more_ref, log_src_ref, log_tgt_ref, *refs):
    kept, (out_ref, keep_ref, high_ref, base_ref) = refs[:3], refs[3:7]
    rows_ref, cols_ref, sum_ref, top_ref = refs[7:]
    base_ref[...] = row_values(log_src_ref, sums_ref, more_ref)
    rows_ref[...] = jnp.broadcast_to(base_ref[...], rows_ref.shape)
    count = scores_ref.shape[0]
    columns_exp(scores_ref, rows_ref, high_ref, sum_ref, 0, count, keep_ref)
    columns_finish(high_ref, sum_ref, log_tgt_ref, cols_ref, 0, count)
    rows_either(scores_ref, cols_ref, kept, top_ref, out_ref)


def later_kernel(scores_ref, sums_ref, more_ref, log_src_ref, log_tgt_ref, *refs):
    kept, kept_columns, out_ref = refs[:3], refs[3:6], refs[6]
    rows_ref, cols_ref, high_ref, sum_ref, top_ref = refs[7:]
    rows = row_values(log_src_ref, sums_ref, more_ref)
    count = scores_ref.shape[0]
    columns_either(rows, (scores_ref, log_tgt_ref), kept_columns, rows_ref, high_ref, sum_ref, 0, count)
    columns_finish(high_ref, sum_ref, log_tgt_ref, cols_ref, 0, count)
    rows_either(scores_ref, cols_ref, kept, top_ref, out_ref)


def last_kernel(merged, scores_ref, sums_ref, more_ref, log_src_ref, log_tgt_ref, *refs):
    kept_columns, (out_ref, row_ref, col_ref) = refs[:3], refs[3:6]
    rows_ref, values_ref, cols_ref, high_ref, sum_ref = refs[6:]
    own_rows, own_cols = out_ref.shape
    rows = row_values(log_src_ref, sums_ref, more_ref)
    values_ref[...] = rows
    base = pl.multiple_of(lax.rem(lax.div(lax.axis_index("tgt"), 2), merged) * own_cols, own_cols)
    lanes = pl.ds(pl.multiple_of(lax.axis_index("src") * own_rows, own_rows), own_rows)
    columns_either(rows, (scores_ref, log_tgt_ref), kept_columns, rows_ref, high_ref, sum_ref, base, own_cols)
    columns_finish(high_ref, sum_ref, log_tgt_ref, cols_ref, base, own_cols)
    row_ref[...] = values_ref[:, lanes] * LN2
    col_ref[...] = cols_ref[...].T[0:1, :] * LN2
    block = scores_ref[pl.ds(base, own_cols), lanes] + values_ref[:, lanes] + cols_ref[:, 0:1]
    out_ref[...] = (block * LN2).T


def swap(value, axis, offset):
    return lax.ppermute(value, axis, [(i, i ^ offset) for i in range(lax.axis_size(axis))])


def staged_parts(value, axis, low, width):
    size = lax.axis_size(axis)
    terms = [value]
    while low < size:
        span = min(width, size // low)
        value = tree(terms, jnp.add)
        terms = [value] + [swap(value, axis, low * j) for j in range(1, span)]
        low *= span
    return terms


def more(held, axis, low, goal):
    unit = held[0].shape[0]
    while sum(part.shape[0] for part in held) < goal * unit:
        known = held[0] if len(held) == 1 else jnp.concatenate(held, axis=0)
        held.append(swap(known, axis, low * known.shape[0] // unit))


def shards(coupling, src_pcs, tgt_pcs, src_mass, tgt_mass):
    f32 = jnp.float32
    pcs = src_pcs.shape[0]
    rows, cols = coupling.shape
    src_size, tgt_size = lax.axis_size("src"), lax.axis_size("tgt")
    total_rows, total_cols = rows * src_size, cols * tgt_size
    merged = 1
    while 2 * merged * 2 <= tgt_size and 2 * merged * cols * total_rows * 4 <= SCORES_BYTES:
        merged *= 2
    wide = merged * cols
    packed_rows = -(-(pcs + 1) // 8) * 8

    arguments = (coupling, src_pcs, tgt_pcs, src_mass.reshape(1, -1), tgt_mass.reshape(1, -1))
    half, whole, moment = pl.pallas_call(
        front_kernel,
        out_shape=(
            pltpu.VMEM((packed_rows, rows // 2), f32),
            pltpu.VMEM((packed_rows, cols), f32),
            pltpu.VMEM((DEPTH // 2, LANES), f32),
        ),
        in_specs=[pl.BlockSpec(memory_space=pltpu.HBM)] * 5,
        out_specs=(VMEM,) * 3,
        scratch_shapes=[pltpu.VMEM(a.shape, a.dtype) for a in arguments]
        + [pltpu.SemaphoreType.DMA((5,))],
        compiler_params=params(8),
    )(*[pltpu.with_memory_space_constraint(a, pltpu.HBM) for a in arguments])

    sources, targets = [half], [whole]
    more(sources, "src", 1, min(2, src_size))
    more(targets, "tgt", 2, min(2, merged))
    moment = moment + swap(moment, "tgt", 1)
    moment, sources, targets = lax.optimization_barrier((moment, sources, targets))
    more(sources, "src", 1, min(4, src_size))
    more(targets, "tgt", 2, merged)
    parts = staged_parts(moment, "tgt", 2, 4)
    parts, sources, targets = lax.optimization_barrier((parts, sources, targets))
    more(sources, "src", 1, src_size)
    moments = staged_parts(tree(parts, jnp.add), "src", 1, 4)
    near = jnp.concatenate(sources, axis=0)
    far = swap(near, "tgt", 1)

    scores, sums, log_src, log_tgt = pl.pallas_call(
        functools.partial(start_kernel, pcs, total_rows * total_cols, merged, src_size),
        out_shape=(
            jax.ShapeDtypeStruct((wide, total_rows), f32),
            jax.ShapeDtypeStruct((1, total_rows), f32),
            jax.ShapeDtypeStruct((1, total_rows), f32),
            jax.ShapeDtypeStruct((wide, LANES), f32),
        ),
        in_specs=[VMEM] * (2 + len(targets) + len(moments)),
        out_specs=(VMEM,) * 4,
        scratch_shapes=[
            pltpu.VMEM((4 * DEPTH, total_rows), jnp.bfloat16),
            pltpu.VMEM((wide, 4 * DEPTH), jnp.bfloat16),
            pltpu.VMEM((8, total_rows), f32),
        ],
        compiler_params=params(16),
    )(near, far, *targets, *moments)

    def both(value):
        offset = 2 * merged
        while offset < tgt_size:
            value = logsum(value, swap(value, "tgt", offset))
            offset *= 2
        return value, swap(value, "tgt", 1)

    bf16, block = jnp.bfloat16, (wide, total_rows)

    def call(kernel, sums, extra, outs, scratch):
        return pl.pallas_call(
            kernel,
            out_shape=tuple(jax.ShapeDtypeStruct(shape, bf16 if shape == block else f32) for shape in outs),
            in_specs=[VMEM] * (5 + len(extra)),
            out_specs=(VMEM,) * len(outs),
            scratch_shapes=[pltpu.VMEM(shape, f32) for shape in scratch],
            compiler_params=params(10),
        )(scores, *both(sums), log_src, log_tgt, *extra)

    line, lines, pads = (1, total_rows), (8, total_rows), (wide, LANES)
    sums, *kept_rows = call(
        first_kernel, sums, (), (line, block, lines, pads), (lines, pads, pads)
    )
    sums, *kept_columns = call(
        second_kernel, sums, kept_rows, (line, block, pads, line), (lines, pads, pads, lines)
    )
    for iteration in range(ITERS - 3):
        (sums,) = call(
            later_kernel, sums, (*kept_rows, *kept_columns), (line,), (lines, pads, pads, pads, lines)
        )
    pads = (cols, LANES)
    log_coupling, row_potential, col_potential = call(
        functools.partial(last_kernel, merged), sums, kept_columns,
        ((rows, cols), (1, rows), (1, cols)), (lines, line, pads, pads, pads),
    )
    return log_coupling, row_potential.reshape(-1), col_potential.reshape(-1)


def solution(mesh):
    in_specs = (P("src", "tgt"), P(None, "src"), P(None, "tgt"), P("src"), P("tgt"))
    out_specs = (P("src", "tgt"), P("src"), P("tgt"))
    return jax.shard_map(shards, mesh=mesh, in_specs=in_specs, out_specs=out_specs, check_vma=False)
```

```python
import functools
import math

import jax
import jax.numpy as jnp
from jax import lax
from jax.experimental import pallas as pl
from jax.experimental.pallas import tpu as pltpu
from jax.sharding import PartitionSpec as P

ITERS = 4

eps_reg = 0.5
marg_power = 1.0 / (1.0 + eps_reg)
tiny_eps = 1e-06

LANES = 128
DEPTH = 64
LN2 = math.log(2.0)
SCORES_BYTES = 1 << 24
LIFT = 54.0
SPAN = 145.0
VMEM = pl.BlockSpec(memory_space=pltpu.VMEM)


def params(mib):
    return pltpu.CompilerParams(vmem_limit_bytes=mib << 20)


def tree(values, combine):
    values = list(values)
    while len(values) > 1:
        paired = [combine(values[i], values[i + 1]) for i in range(0, len(values) - 1, 2)]
        values = paired + ([values[-1]] if len(values) % 2 else [])
    return values[0]


def pieces(value):
    high = value.astype(jnp.bfloat16)
    rest = value - high.astype(jnp.float32)
    middle = rest.astype(jnp.bfloat16)
    low = (rest - middle.astype(jnp.float32)).astype(jnp.bfloat16)
    return high, middle, low


def padded(value):
    return jnp.concatenate(
        [value, jnp.zeros((DEPTH - value.shape[0], value.shape[1]), value.dtype)], axis=0
    )


def front_kernel(*refs):
    sources, (half_ref, whole_ref, moment_ref), local, sems = refs[:5], refs[5:8], refs[8:13], refs[13]
    copies = [pltpu.make_async_copy(a, b, sems.at[i]) for i, (a, b) in enumerate(zip(sources, local))]
    for copy in copies:
        copy.start()
    coupling_ref, src_ref, tgt_ref, src_mass_ref, tgt_mass_ref = local
    pcs = src_ref.shape[0]
    half = half_ref.shape[1]
    odd = lax.rem(lax.axis_index("tgt"), 2)
    for copy in copies[1:]:
        copy.wait()
    src = src_ref[...].astype(jnp.float32)
    tgt = tgt_ref[...].astype(jnp.float32)
    below = jnp.zeros((half_ref.shape[0] - pcs - 1, 2 * half), jnp.float32)
    joined = jnp.concatenate([src, jnp.log2(src_mass_ref[...]), below], axis=0)
    half_ref[...] = jnp.where(odd == 0, joined[:, :half], joined[:, half:])
    below = jnp.zeros((half_ref.shape[0] - pcs - 1, tgt.shape[1]), jnp.float32)
    whole_ref[...] = jnp.concatenate([tgt, jnp.log2(tgt_mass_ref[...]), below], axis=0)
    src = padded(src).astype(jnp.bfloat16)
    tgt = padded(tgt).astype(jnp.bfloat16)
    twice = jnp.concatenate([src, src], axis=0)
    copies[0].wait()
    panel = jnp.dot(twice, coupling_ref[...], preferred_element_type=jnp.float32)
    moment = sum(
        lax.dot_general(tgt, part, (((1,), (1,)), ((), ())), preferred_element_type=jnp.float32)
        for part in pieces(panel)
    )
    lane = lax.broadcasted_iota(jnp.int32, (DEPTH // 2, LANES), 1)
    moment = jnp.where(lane < DEPTH, moment[: DEPTH // 2], moment[DEPTH // 2 :])
    for i in range(4):
        moment_ref[:, i * LANES : (i + 1) * LANES] = moment[i * 8 : i * 8 + 8]


def prepare_kernel(pcs, blocks, merged, near_ref, far_ref, *refs):
    tgt_refs, (src_ref, turned_ref, log_src_ref, log_tgt_ref) = refs[:merged], refs[merged:]
    packed_rows = near_ref.shape[0] // blocks
    half = near_ref.shape[1]
    width = tgt_refs[0].shape[1]
    z = lax.axis_index("src")
    t = lax.axis_index("tgt")
    odd = lax.rem(t, 2)
    total_rows = 2 * half * blocks
    total_cols = width * lax.axis_size("tgt")
    for b in range(blocks):
        place = jnp.bitwise_xor(z, b)
        for ref, side in ((near_ref, odd), (far_ref, 1 - odd)):
            block = ref[pl.ds(b * packed_rows, packed_rows), :]
            lanes = pl.ds(pl.multiple_of((place * 2 + side) * half, half), half)
            log_src_ref[:, lanes] = marg_power * (block[pcs : pcs + 1] + math.log2(total_cols))
            block = padded(block).astype(jnp.bfloat16)
            for copy in range(4):
                src_ref[pl.ds(copy * DEPTH, DEPTH), lanes] = block
    mine = lax.rem(lax.div(t, 2), merged)
    for b in range(merged):
        base = pl.multiple_of(jnp.bitwise_xor(mine, b) * width, width)
        block = padded(tgt_refs[b][:packed_rows, :])
        turned = jnp.concatenate([block, block], axis=0).T
        log_tgt_ref[pl.ds(base, width), :] = jnp.broadcast_to(
            marg_power * (turned[:, pcs : pcs + 1] + math.log2(total_rows)), (width, LANES)
        )
        turned_ref[pl.ds(base, width), :] = turned.astype(jnp.bfloat16)


def start_kernel(pcs, entries, src_all, turned_ref, *refs):
    moment_refs, (scores_ref, sums_ref, weights, top_ref) = refs[:-4], refs[-4:]
    total_rows = src_all.shape[1]
    packed = tree([ref[...] for ref in moment_refs], jnp.add) * entries ** (-0.5)
    spread = jnp.sqrt(jnp.sum(packed * packed) * (1.0 / (pcs * pcs)) + tiny_eps)
    packed = packed / spread * (2.0 / (eps_reg * pcs) / LN2)
    packed = jnp.concatenate([packed[:, i * LANES : (i + 1) * LANES] for i in range(4)], axis=0)
    turned = pltpu.roll(packed, DEPTH, axis=1)
    left = lax.broadcasted_iota(jnp.int32, packed.shape, 1) < DEPTH
    normed = jnp.concatenate(
        [jnp.where(left, packed, turned), jnp.where(left, turned, packed)], axis=0
    )
    high, middle, low = pieces(normed)
    upper = jnp.concatenate([high, middle], axis=0)
    lower = jnp.concatenate([low, jnp.zeros_like(low)], axis=0)

    width = min(512, turned_ref.shape[0])
    first = lax.broadcasted_iota(jnp.int32, (width, LANES), 1) < DEPTH
    for base in range(0, turned_ref.shape[0], width):
        at = pl.ds(base, width)
        weighted = sum(
            jnp.dot(turned_ref[at, :], part, preferred_element_type=jnp.float32)
            for part in (upper, lower)
        )
        high, middle, low = pieces(weighted)
        weights[at, :LANES] = jnp.where(first, high, middle)
        weights[at, LANES:] = jnp.where(first, low, jnp.zeros_like(low))

    chunk, rows = 1024, min(256, scores_ref.shape[0])
    across = total_rows // chunk

    def step(i, carry):
        lanes = pl.ds(pl.multiple_of(lax.rem(i, across) * chunk, chunk), chunk)
        at = pl.ds(pl.multiple_of(lax.div(i, across) * rows, rows), rows)
        scores_ref[at, lanes] = jnp.dot(
            weights[at, :], src_all[:, lanes], preferred_element_type=jnp.float32
        )
        return carry

    lax.fori_loop(0, across * (scores_ref.shape[0] // rows), step, 0)
    rows_highest(scores_ref, None, top_ref)
    rows_exp(scores_ref, None, top_ref, sums_ref, None)


def down(highest, summed):
    top = jnp.max(highest, axis=0, keepdims=True)
    return top + jnp.log2(jnp.sum(summed * jnp.exp2(highest - top), axis=0, keepdims=True))


def logsum(one, other):
    top = jnp.maximum(one, other)
    return top + jnp.log2(jnp.exp2(one - top) + jnp.exp2(other - top))


def row_values(log_src_ref, sums_ref, more_ref):
    return log_src_ref[...] - marg_power * logsum(sums_ref[...], more_ref[...])


def lane_tiles(ref):
    return [pl.ds(j, LANES) for j in range(0, ref.shape[1], LANES)]


def halves(low):
    low = pl.multiple_of(low, 16)
    return pl.ds(low, 16), [pl.ds(low, 8), pl.ds(pl.multiple_of(low + 8, 8), 8)]


def columns_exp(scores_ref, rows_ref, top_ref, sum_ref, base, count, keep_ref):
    tiles = lane_tiles(scores_ref)

    def highest(i, carry):
        places = [pl.ds(pl.multiple_of(i * 64 + g * 8, 8), 8) for g in range(8)]
        sources = [pl.ds(pl.multiple_of(base + i * 64 + g * 8, 8), 8) for g in range(8)]
        tops = [None] * 8
        for lanes in tiles:
            row = rows_ref[:, lanes]
            for g, source in enumerate(sources):
                term = scores_ref[source, lanes] + row
                tops[g] = term if tops[g] is None else jnp.maximum(tops[g], term)
        for place, top in zip(places, tops):
            top_ref[place, :] = top - LIFT
        return carry

    def total(i, carry):
        pairs = [halves(base + i * 64 + g * 16) for g in range(4)]
        places = [place for g in range(4) for place in halves(i * 64 + g * 16)[1]]
        tops = [top_ref[place, :] for place in places]
        sums = [jnp.zeros((8, LANES), jnp.float32)] * 8
        for lanes in tiles:
            row = rows_ref[:, lanes]
            for g, (at, sources) in enumerate(pairs):
                parts = []
                for h, source in enumerate(sources):
                    parts.append(jnp.exp2(scores_ref[source, lanes] + row - tops[2 * g + h]))
                    sums[2 * g + h] = sums[2 * g + h] + parts[h]
                if keep_ref is not None:
                    keep_ref[at, lanes] = jnp.concatenate(parts, axis=0).astype(keep_ref.dtype)
        for place, value in zip(places, sums):
            sum_ref[place, :] = value
        return carry

    lax.fori_loop(0, count // 64, highest, 0)
    if keep_ref is not None:
        tops = top_ref[pl.ds(0, count), :]
        top_ref[pl.ds(0, count), :] = jnp.broadcast_to(jnp.max(tops, axis=1, keepdims=True), tops.shape)
    lax.fori_loop(0, count // 64, total, 0)


def split_rows(line):
    row = lax.broadcasted_iota(jnp.int32, (16, line.shape[1]), 0)
    high, middle, low = (part.astype(jnp.float32) for part in pieces(line))
    spread = jnp.where(row == 0, high, jnp.where(row == 1, middle, jnp.where(row == 2, low, 0.0)))
    return spread.astype(jnp.bfloat16)


def columns_product(keep_ref, kept_top_ref, factor, shift, top_ref, sum_ref, base, count):
    factors = split_rows(factor)
    factors = jnp.concatenate([factors, jnp.zeros((LANES - 16, factor.shape[1]), factors.dtype)], axis=0)
    part = min(count, 512)
    for low in range(0, count, part):
        here = pl.ds(low, part)
        at = pl.ds(pl.multiple_of(base + low, part), part)
        sum_ref[here, :] = lax.dot_general(
            keep_ref[at, :], factors, (((1,), (1,)), ((), ())), preferred_element_type=jnp.float32
        )
        top_ref[here, :] = kept_top_ref[at, :] + (shift - LIFT)


def columns_finish(top_ref, sum_ref, log_tgt_ref, cols_ref, base, count):
    part = min(count, 2048)
    for low in range(0, count, part):
        here = pl.ds(low, part)
        tops = top_ref[here, :]
        top = jnp.max(tops, axis=1, keepdims=True)
        total = jnp.sum(sum_ref[here, :] * jnp.exp2(tops - top), axis=1, keepdims=True)
        at = pl.ds(pl.multiple_of(base + low, part), part)
        cols_ref[here, :] = log_tgt_ref[at, :] - marg_power * (top + jnp.log2(total))


BESIDE, DEEP = 8, 4


def over_tiles(count, width, body, first, done):
    for start in range(0, width, BESIDE * LANES):
        tiles = [pl.ds(start + j * LANES, LANES) for j in range(BESIDE)]

        def step(i, carry, tiles=tiles):
            carry = list(carry)
            body([halves((i * DEEP + g) * 16) for g in range(DEEP)], tiles, carry)
            return tuple(carry)

        state = lax.fori_loop(0, count // (16 * DEEP), step, tuple(first for _ in tiles))
        for lanes, value in zip(tiles, state):
            done(lanes, value)


def rows_highest(scores_ref, cols_ref, top_ref):
    def body(pairs, tiles, carry):
        for _, places in pairs:
            for place in places:
                if cols_ref is not None:
                    potential = cols_ref[place, :]
                for j, lanes in enumerate(tiles):
                    term = scores_ref[place, lanes]
                    if cols_ref is not None:
                        term = term + potential
                    carry[j] = jnp.maximum(carry[j], term)

    def done(lanes, value):
        top_ref[:, lanes] = jnp.broadcast_to(jnp.max(value, axis=0, keepdims=True), value.shape) - LIFT

    over_tiles(*scores_ref.shape, body, jnp.full((8, LANES), -jnp.inf, jnp.float32), done)


def rows_exp(scores_ref, cols_ref, top_ref, out_ref, keep_ref):
    def body(pairs, tiles, carry):
        tops = [top_ref[:, lanes] for lanes in tiles]
        for at, places in pairs:
            if cols_ref is not None:
                potentials = [cols_ref[place, :] for place in places]
            for j, lanes in enumerate(tiles):
                terms = [scores_ref[place, lanes] for place in places]
                if cols_ref is not None:
                    terms = [term + potential for term, potential in zip(terms, potentials)]
                parts = [jnp.exp2(term - tops[j]) for term in terms]
                if keep_ref is not None:
                    keep_ref[at, lanes] = jnp.concatenate(parts, axis=0).astype(keep_ref.dtype)
                carry[j] = carry[j] + (parts[0] + parts[1])

    def done(lanes, value):
        out_ref[:, lanes] = down(top_ref[:, lanes], value)

    over_tiles(*scores_ref.shape, body, jnp.zeros((8, LANES), jnp.float32), done)


def rows_product(keep_ref, kept_top_ref, factor, shift, out_ref):
    factors = split_rows(factor.T[0:1, :])
    chunk = 512
    for start in range(0, keep_ref.shape[1], chunk):
        lanes = pl.ds(start, chunk)
        sums = jnp.dot(factors, keep_ref[:, lanes], preferred_element_type=jnp.float32)
        out_ref[:, lanes] = (
            kept_top_ref[0:1, lanes] + (shift - LIFT) + jnp.log2(jnp.sum(sums, axis=0, keepdims=True))
        )


def columns_either(rows, args, kept, rows_ref, top_ref, sum_ref, base, count):
    scores_ref, log_tgt_ref = args
    keep_ref, kept_top_ref, kept_rows_ref = kept
    change = rows - kept_rows_ref[...]
    shift = jnp.max(change)
    near = shift - jnp.min(change) <= SPAN

    @pl.when(near)
    def _():
        factor = jnp.exp2(change - (shift - LIFT))
        columns_product(keep_ref, kept_top_ref, factor, shift, top_ref, sum_ref, base, count)

    @pl.when(jnp.logical_not(near))
    def _():
        rows_ref[...] = jnp.broadcast_to(rows, rows_ref.shape)
        columns_exp(scores_ref, rows_ref, top_ref, sum_ref, base, count, None)


def rows_either(scores_ref, cols_ref, kept, top_ref, out_ref):
    keep_ref, kept_top_ref, kept_cols_ref = kept
    change = cols_ref[...] - kept_cols_ref[...]
    shift = jnp.max(change)
    near = shift - jnp.min(change) <= SPAN

    @pl.when(near)
    def _():
        factor = jnp.exp2(cols_ref[...] - kept_cols_ref[...] - (shift - LIFT))
        rows_product(keep_ref, kept_top_ref, factor, shift, out_ref)

    @pl.when(jnp.logical_not(near))
    def _():
        rows_highest(scores_ref, cols_ref, top_ref)
        rows_exp(scores_ref, cols_ref, top_ref, out_ref, None)


def first_kernel(scores_ref, sums_ref, more_ref, log_src_ref, log_tgt_ref, out_ref, keep_ref, top_ref, cols_ref, rows_ref, high_ref, sum_ref):
    rows_ref[...] = jnp.broadcast_to(row_values(log_src_ref, sums_ref, more_ref), rows_ref.shape)
    count = scores_ref.shape[0]
    columns_exp(scores_ref, rows_ref, high_ref, sum_ref, 0, count, None)
    columns_finish(high_ref, sum_ref, log_tgt_ref, cols_ref, 0, count)
    rows_highest(scores_ref, cols_ref, top_ref)
    rows_exp(scores_ref, cols_ref, top_ref, out_ref, keep_ref)


def second_kernel(scores_ref, sums_ref, more_ref, log_src_ref, log_tgt_ref, *refs):
    kept, (out_ref, keep_ref, high_ref, base_ref) = refs[:3], refs[3:7]
    rows_ref, cols_ref, sum_ref, top_ref = refs[7:]
    base_ref[...] = row_values(log_src_ref, sums_ref, more_ref)
    rows_ref[...] = jnp.broadcast_to(base_ref[...], rows_ref.shape)
    count = scores_ref.shape[0]
    columns_exp(scores_ref, rows_ref, high_ref, sum_ref, 0, count, keep_ref)
    columns_finish(high_ref, sum_ref, log_tgt_ref, cols_ref, 0, count)
    rows_either(scores_ref, cols_ref, kept, top_ref, out_ref)


def later_kernel(scores_ref, sums_ref, more_ref, log_src_ref, log_tgt_ref, *refs):
    kept, kept_columns, out_ref = refs[:3], refs[3:6], refs[6]
    rows_ref, cols_ref, high_ref, sum_ref, top_ref = refs[7:]
    rows = row_values(log_src_ref, sums_ref, more_ref)
    count = scores_ref.shape[0]
    columns_either(rows, (scores_ref, log_tgt_ref), kept_columns, rows_ref, high_ref, sum_ref, 0, count)
    columns_finish(high_ref, sum_ref, log_tgt_ref, cols_ref, 0, count)
    rows_either(scores_ref, cols_ref, kept, top_ref, out_ref)


def last_kernel(merged, scores_ref, sums_ref, more_ref, log_src_ref, log_tgt_ref, *refs):
    kept_columns, (out_ref, row_ref, col_ref) = refs[:3], refs[3:6]
    rows_ref, values_ref, cols_ref, high_ref, sum_ref = refs[6:]
    own_rows, own_cols = out_ref.shape
    rows = row_values(log_src_ref, sums_ref, more_ref)
    values_ref[...] = rows
    base = pl.multiple_of(lax.rem(lax.div(lax.axis_index("tgt"), 2), merged) * own_cols, own_cols)
    lanes = pl.ds(pl.multiple_of(lax.axis_index("src") * own_rows, own_rows), own_rows)
    columns_either(rows, (scores_ref, log_tgt_ref), kept_columns, rows_ref, high_ref, sum_ref, base, own_cols)
    columns_finish(high_ref, sum_ref, log_tgt_ref, cols_ref, base, own_cols)
    row_ref[...] = values_ref[:, lanes] * LN2
    col_ref[...] = cols_ref[...].T[0:1, :] * LN2
    block = scores_ref[pl.ds(base, own_cols), lanes] + values_ref[:, lanes] + cols_ref[:, 0:1]
    out_ref[...] = (block * LN2).T


def swap(value, axis, offset):
    return lax.ppermute(value, axis, [(i, i ^ offset) for i in range(lax.axis_size(axis))])


def staged_parts(value, axis, low, width):
    size = lax.axis_size(axis)
    terms = [value]
    while low < size:
        span = min(width, size // low)
        value = tree(terms, jnp.add)
        terms = [value] + [swap(value, axis, low * j) for j in range(1, span)]
        low *= span
    return terms


def shards(coupling, src_pcs, tgt_pcs, src_mass, tgt_mass):
    f32 = jnp.float32
    pcs = src_pcs.shape[0]
    rows, cols = coupling.shape
    src_size, tgt_size = lax.axis_size("src"), lax.axis_size("tgt")
    total_rows, total_cols = rows * src_size, cols * tgt_size
    merged = 1
    while 2 * merged * 2 <= tgt_size and 2 * merged * cols * total_rows * 4 <= SCORES_BYTES:
        merged *= 2
    wide = merged * cols
    packed_rows = -(-(pcs + 1) // 8) * 8

    arguments = (coupling, src_pcs, tgt_pcs, src_mass.reshape(1, -1), tgt_mass.reshape(1, -1))
    half, whole, moment = pl.pallas_call(
        front_kernel,
        out_shape=(
            pltpu.VMEM((packed_rows, rows // 2), f32),
            pltpu.VMEM((packed_rows, cols), f32),
            pltpu.VMEM((8, 4 * LANES), f32),
        ),
        in_specs=[pl.BlockSpec(memory_space=pltpu.HBM)] * 5,
        out_specs=(VMEM,) * 3,
        scratch_shapes=[pltpu.VMEM(a.shape, a.dtype) for a in arguments]
        + [pltpu.SemaphoreType.DMA((5,))],
        compiler_params=params(8),
    )(*[pltpu.with_memory_space_constraint(a, pltpu.HBM) for a in arguments])

    moment = moment + swap(moment, "tgt", 1)
    half, whole, moment = lax.optimization_barrier((half, whole, moment))
    parts, targets = [moment], [whole]
    if merged > 1:
        message = jnp.concatenate([whole, moment], axis=0)
        targets += [swap(message, "tgt", 2 * b) for b in range(1, merged)]
        parts += [target[packed_rows:] for target in targets[1:]]
    sources = [half] + [swap(half, "src", b) for b in range(1, src_size)]
    parts, sources, targets = lax.optimization_barrier((parts, sources, targets))
    if 2 * merged < tgt_size:
        parts = staged_parts(tree(parts, jnp.add), "tgt", 2 * merged, 4)
    moments = staged_parts(tree(parts, jnp.add), "src", 1, 4)
    near = jnp.concatenate(sources, axis=0)
    far = swap(near, "tgt", 1)

    src_all, turned, log_src, log_tgt = pl.pallas_call(
        functools.partial(prepare_kernel, pcs, src_size, merged),
        out_shape=(
            jax.ShapeDtypeStruct((4 * DEPTH, total_rows), jnp.bfloat16),
            jax.ShapeDtypeStruct((wide, LANES), jnp.bfloat16),
            jax.ShapeDtypeStruct((1, total_rows), f32),
            jax.ShapeDtypeStruct((wide, LANES), f32),
        ),
        in_specs=[VMEM] * (2 + merged),
        out_specs=(VMEM,) * 4,
        compiler_params=params(10),
    )(near, far, *targets)
    scores, sums = pl.pallas_call(
        functools.partial(start_kernel, pcs, total_rows * total_cols),
        out_shape=(
            jax.ShapeDtypeStruct((wide, total_rows), f32),
            jax.ShapeDtypeStruct((1, total_rows), f32),
        ),
        in_specs=[VMEM] * (2 + len(moments)),
        out_specs=(VMEM,) * 2,
        scratch_shapes=[
            pltpu.VMEM((wide, 4 * DEPTH), jnp.bfloat16),
            pltpu.VMEM((8, total_rows), f32),
        ],
        compiler_params=params(14),
    )(src_all, turned, *moments)

    def both(value):
        offset = 2 * merged
        while offset < tgt_size:
            value = logsum(value, swap(value, "tgt", offset))
            offset *= 2
        return value, swap(value, "tgt", 1)

    bf16, block = jnp.bfloat16, (wide, total_rows)

    def call(kernel, sums, extra, outs, scratch):
        return pl.pallas_call(
            kernel,
            out_shape=tuple(jax.ShapeDtypeStruct(shape, bf16 if shape == block else f32) for shape in outs),
            in_specs=[VMEM] * (5 + len(extra)),
            out_specs=(VMEM,) * len(outs),
            scratch_shapes=[pltpu.VMEM(shape, f32) for shape in scratch],
            compiler_params=params(10),
        )(scores, *both(sums), log_src, log_tgt, *extra)

    line, lines, pads = (1, total_rows), (8, total_rows), (wide, LANES)
    sums, *kept_rows = call(
        first_kernel, sums, (), (line, block, lines, pads), (lines, pads, pads)
    )
    sums, *kept_columns = call(
        second_kernel, sums, kept_rows, (line, block, pads, line), (lines, pads, pads, lines)
    )
    for iteration in range(ITERS - 3):
        (sums,) = call(
            later_kernel, sums, (*kept_rows, *kept_columns), (line,), (lines, pads, pads, pads, lines)
        )
    pads = (cols, LANES)
    log_coupling, row_potential, col_potential = call(
        functools.partial(last_kernel, merged), sums, kept_columns,
        ((rows, cols), (1, rows), (1, cols)), (lines, line, pads, pads, pads),
    )
    return log_coupling, row_potential.reshape(-1), col_potential.reshape(-1)


def solution(mesh):
    in_specs = (P("src", "tgt"), P(None, "src"), P(None, "tgt"), P("src"), P("tgt"))
    out_specs = (P("src", "tgt"), P("src"), P("tgt"))
    return jax.shard_map(shards, mesh=mesh, in_specs=in_specs, out_specs=out_specs, check_vma=False)
```

```python
import functools
import math

import jax
import jax.numpy as jnp
from jax import lax
from jax.experimental import pallas as pl
from jax.experimental.pallas import tpu as pltpu
from jax.sharding import PartitionSpec as P

ITERS = 4

eps_reg = 0.5
marg_power = 1.0 / (1.0 + eps_reg)
tiny_eps = 1e-06

LANES = 128
DEPTH = 64
LN2 = math.log(2.0)
SCORES_BYTES = 1 << 24
LIFT = 54.0
SPAN = 145.0
VMEM = pl.BlockSpec(memory_space=pltpu.VMEM)


def params(mib):
    return pltpu.CompilerParams(vmem_limit_bytes=mib << 20)


def tree(values, combine):
    values = list(values)
    while len(values) > 1:
        paired = [combine(values[i], values[i + 1]) for i in range(0, len(values) - 1, 2)]
        values = paired + ([values[-1]] if len(values) % 2 else [])
    return values[0]


def pieces(value):
    high = value.astype(jnp.bfloat16)
    rest = value - high.astype(jnp.float32)
    middle = rest.astype(jnp.bfloat16)
    low = (rest - middle.astype(jnp.float32)).astype(jnp.bfloat16)
    return high, middle, low


def padded(value):
    return jnp.concatenate(
        [value, jnp.zeros((DEPTH - value.shape[0], value.shape[1]), value.dtype)], axis=0
    )


def front_kernel(*refs):
    sources, (half_ref, whole_ref, moment_ref), local, sems = refs[:5], refs[5:8], refs[8:13], refs[13]
    copies = [pltpu.make_async_copy(a, b, sems.at[i]) for i, (a, b) in enumerate(zip(sources, local))]
    for copy in copies:
        copy.start()
    coupling_ref, src_ref, tgt_ref, src_mass_ref, tgt_mass_ref = local
    pcs = src_ref.shape[0]
    half = half_ref.shape[1]
    odd = lax.rem(lax.axis_index("tgt"), 2)
    for copy in copies[1:]:
        copy.wait()
    src = src_ref[...].astype(jnp.float32)
    tgt = tgt_ref[...].astype(jnp.float32)
    below = jnp.zeros((half_ref.shape[0] - pcs - 1, 2 * half), jnp.float32)
    joined = jnp.concatenate([src, jnp.log2(src_mass_ref[...]), below], axis=0)
    half_ref[...] = jnp.where(odd == 0, joined[:, :half], joined[:, half:])
    below = jnp.zeros((half_ref.shape[0] - pcs - 1, tgt.shape[1]), jnp.float32)
    whole_ref[...] = jnp.concatenate([tgt, jnp.log2(tgt_mass_ref[...]), below], axis=0)
    src = padded(src).astype(jnp.bfloat16)
    tgt = padded(tgt).astype(jnp.bfloat16)
    twice = jnp.concatenate([src, src], axis=0)
    copies[0].wait()
    panel = jnp.dot(twice, coupling_ref[...], preferred_element_type=jnp.float32)
    moment = sum(
        lax.dot_general(tgt, part, (((1,), (1,)), ((), ())), preferred_element_type=jnp.float32)
        for part in pieces(panel)
    )
    lane = lax.broadcasted_iota(jnp.int32, (DEPTH // 2, LANES), 1)
    moment = jnp.where(lane < DEPTH, moment[: DEPTH // 2], moment[DEPTH // 2 :])
    for i in range(4):
        moment_ref[:, i * LANES : (i + 1) * LANES] = moment[i * 8 : i * 8 + 8]


def prepare_kernel(pcs, blocks, merged, near_ref, far_ref, *refs):
    tgt_refs, (src_ref, turned_ref, log_src_ref, log_tgt_ref, line_ref) = refs[:merged], refs[merged:]
    packed_rows = near_ref.shape[0] // blocks
    half = near_ref.shape[1]
    width = tgt_refs[0].shape[1]
    z = lax.axis_index("src")
    t = lax.axis_index("tgt")
    odd = lax.rem(t, 2)
    total_rows = 2 * half * blocks
    total_cols = width * lax.axis_size("tgt")
    for b in range(blocks):
        place = jnp.bitwise_xor(z, b)
        for ref, side in ((near_ref, odd), (far_ref, 1 - odd)):
            block = ref[pl.ds(b * packed_rows, packed_rows), :]
            lanes = pl.ds(pl.multiple_of((place * 2 + side) * half, half), half)
            log_src_ref[:, lanes] = marg_power * (block[pcs : pcs + 1] + math.log2(total_cols))
            block = padded(block).astype(jnp.bfloat16)
            for copy in range(4):
                src_ref[pl.ds(copy * DEPTH, DEPTH), lanes] = block
    mine = lax.rem(lax.div(t, 2), merged)
    for b in range(merged):
        base = pl.multiple_of(jnp.bitwise_xor(mine, b) * width, width)
        block = padded(tgt_refs[b][:packed_rows, :])
        line_ref[:, pl.ds(base, width)] = marg_power * (block[pcs : pcs + 1] + math.log2(total_rows))
        turned = jnp.concatenate([block, block], axis=0).T
        log_tgt_ref[pl.ds(base, width), :] = jnp.broadcast_to(
            marg_power * (turned[:, pcs : pcs + 1] + math.log2(total_rows)), (width, LANES)
        )
        turned_ref[pl.ds(base, width), :] = turned.astype(jnp.bfloat16)


def start_kernel(pcs, entries, src_all, turned_ref, *refs):
    moment_refs, (scores_ref, sums_ref, weights) = refs[:-3], refs[-3:]
    total_rows = src_all.shape[1]
    packed = tree([ref[...] for ref in moment_refs], jnp.add) * entries ** (-0.5)
    spread = jnp.sqrt(jnp.sum(packed * packed) * (1.0 / (pcs * pcs)) + tiny_eps)
    packed = packed / spread * (2.0 / (eps_reg * pcs) / LN2)
    packed = jnp.concatenate([packed[:, i * LANES : (i + 1) * LANES] for i in range(4)], axis=0)
    turned = pltpu.roll(packed, DEPTH, axis=1)
    left = lax.broadcasted_iota(jnp.int32, packed.shape, 1) < DEPTH
    normed = jnp.concatenate(
        [jnp.where(left, packed, turned), jnp.where(left, turned, packed)], axis=0
    )
    high, middle, low = pieces(normed)
    upper = jnp.concatenate([high, middle], axis=0)
    lower = jnp.concatenate([low, jnp.zeros_like(low)], axis=0)

    width = min(512, turned_ref.shape[0])
    first = lax.broadcasted_iota(jnp.int32, (width, LANES), 1) < DEPTH
    for base in range(0, turned_ref.shape[0], width):
        at = pl.ds(base, width)
        weighted = sum(
            jnp.dot(turned_ref[at, :], part, preferred_element_type=jnp.float32)
            for part in (upper, lower)
        )
        high, middle, low = pieces(weighted)
        weights[at, :LANES] = jnp.where(first, high, middle)
        weights[at, LANES:] = jnp.where(first, low, jnp.zeros_like(low))

    chunk, rows = 1024, min(256, scores_ref.shape[0])
    across = total_rows // chunk

    def step(i, carry):
        lanes = pl.ds(pl.multiple_of(lax.rem(i, across) * chunk, chunk), chunk)
        at = pl.ds(pl.multiple_of(lax.div(i, across) * rows, rows), rows)
        scores_ref[at, lanes] = jnp.dot(
            weights[at, :], src_all[:, lanes], preferred_element_type=jnp.float32
        )
        return carry

    lax.fori_loop(0, across * (scores_ref.shape[0] // rows), step, 0)
    rows_running(scores_ref, sums_ref)


def down(highest, summed):
    top = jnp.max(highest, axis=0, keepdims=True)
    return top + jnp.log2(jnp.sum(summed * jnp.exp2(highest - top), axis=0, keepdims=True))


def logsum(one, other):
    top = jnp.maximum(one, other)
    return top + jnp.log2(jnp.exp2(one - top) + jnp.exp2(other - top))


def row_values(log_src_ref, sums_ref, more_ref):
    return log_src_ref[...] - marg_power * logsum(sums_ref[...], more_ref[...])


def lane_tiles(ref):
    return [pl.ds(j, LANES) for j in range(0, ref.shape[1], LANES)]


def halves(low):
    low = pl.multiple_of(low, 16)
    return pl.ds(low, 16), [pl.ds(low, 8), pl.ds(pl.multiple_of(low + 8, 8), 8)]


def running(highest, summed, terms):
    fresh = jnp.maximum(highest, tree(terms, jnp.maximum))
    total = tree([jnp.exp2(term - fresh) for term in terms], jnp.add)
    return fresh, summed * jnp.exp2(highest - fresh) + total


def columns_running(scores_ref, rows_ref, top_ref, sum_ref, base, count):
    tiles = lane_tiles(scores_ref)
    span = min(16, len(tiles))

    def scan(i, carry):
        for u in range(4):
            low = pl.multiple_of((i * 4 + u) * 8, 8)
            at = pl.ds(pl.multiple_of(base + low, 8), 8)
            state = None
            for start in range(0, len(tiles), span):
                terms = [scores_ref[at, lanes] + rows_ref[:, lanes] for lanes in tiles[start : start + span]]
                if state is None:
                    highest = tree(terms, jnp.maximum)
                    state = highest, tree([jnp.exp2(term - highest) for term in terms], jnp.add)
                else:
                    state = running(*state, terms)
            top_ref[pl.ds(low, 8), :], sum_ref[pl.ds(low, 8), :] = state
        return carry

    lax.fori_loop(0, count // 32, scan, 0)


def rows_running(scores_ref, out_ref):
    count, total = scores_ref.shape
    beside, deep = 8, 16
    unset = (jnp.full((8, LANES), -jnp.inf, jnp.float32), jnp.zeros((8, LANES), jnp.float32))
    for start in range(0, total, beside * LANES):
        tiles = [pl.ds(start + j * LANES, LANES) for j in range(beside)]

        def step(i, carry, tiles=tiles):
            ats = [pl.ds(pl.multiple_of((i * deep + g) * 8, 8), 8) for g in range(deep)]
            return tuple(
                running(*state, [scores_ref[at, lanes] for at in ats])
                for state, lanes in zip(carry, tiles)
            )

        carry = lax.fori_loop(0, count // (8 * deep), step, (unset,) * beside)
        for lanes, state in zip(tiles, carry):
            out_ref[:, lanes] = down(*state)


def columns_exp(scores_ref, rows_ref, top_ref, sum_ref, base, count, keep_ref):
    tiles = lane_tiles(scores_ref)

    def highest(i, carry):
        places = [pl.ds(pl.multiple_of(i * 64 + g * 8, 8), 8) for g in range(8)]
        sources = [pl.ds(pl.multiple_of(base + i * 64 + g * 8, 8), 8) for g in range(8)]
        tops = [None] * 8
        for lanes in tiles:
            row = rows_ref[:, lanes]
            for g, source in enumerate(sources):
                term = scores_ref[source, lanes] + row
                tops[g] = term if tops[g] is None else jnp.maximum(tops[g], term)
        for place, top in zip(places, tops):
            top_ref[place, :] = top - LIFT
        return carry

    def total(i, carry):
        pairs = [halves(base + i * 64 + g * 16) for g in range(4)]
        places = [place for g in range(4) for place in halves(i * 64 + g * 16)[1]]
        tops = [top_ref[place, :] for place in places]
        sums = [jnp.zeros((8, LANES), jnp.float32)] * 8
        for lanes in tiles:
            row = rows_ref[:, lanes]
            for g, (at, sources) in enumerate(pairs):
                parts = []
                for h, source in enumerate(sources):
                    parts.append(jnp.exp2(scores_ref[source, lanes] + row - tops[2 * g + h]))
                    sums[2 * g + h] = sums[2 * g + h] + parts[h]
                if keep_ref is not None:
                    keep_ref[at, lanes] = jnp.concatenate(parts, axis=0).astype(keep_ref.dtype)
        for place, value in zip(places, sums):
            sum_ref[place, :] = value
        return carry

    lax.fori_loop(0, count // 64, highest, 0)
    if keep_ref is not None:
        tops = top_ref[pl.ds(0, count), :]
        top_ref[pl.ds(0, count), :] = jnp.broadcast_to(jnp.max(tops, axis=1, keepdims=True), tops.shape)
    lax.fori_loop(0, count // 64, total, 0)


def split_rows(line):
    row = lax.broadcasted_iota(jnp.int32, (16, line.shape[1]), 0)
    high, middle, low = (part.astype(jnp.float32) for part in pieces(line))
    spread = jnp.where(row == 0, high, jnp.where(row == 1, middle, jnp.where(row == 2, low, 0.0)))
    return spread.astype(jnp.bfloat16)


def split_rows(line):
    row = lax.broadcasted_iota(jnp.int32, (16, line.shape[1]), 0)
    high, middle, low = (part.astype(jnp.float32) for part in pieces(line))
    spread = jnp.where(row == 0, high, jnp.where(row == 1, middle, jnp.where(row == 2, low, 0.0)))
    return spread.astype(jnp.bfloat16)


def columns_product(keep_ref, kept_top_ref, factor, shift, log_tgt_line_ref, line_ref, base, count):
    factors = split_rows(factor)
    part = min(count, 512)
    for low in range(0, count, part):
        at = pl.ds(pl.multiple_of(base + low, part), part)
        sums = lax.dot_general(
            factors, keep_ref[at, :], (((1,), (1,)), ((), ())), preferred_element_type=jnp.float32
        )
        logs = kept_top_ref[:, at] + (shift - LIFT) + jnp.log2(jnp.sum(sums, axis=0, keepdims=True))
        line_ref[:, pl.ds(low, part)] = log_tgt_line_ref[:, at] - marg_power * logs


def columns_finish(top_ref, sum_ref, log_tgt_ref, cols_ref, base, count):
    part = min(count, 2048)
    for low in range(0, count, part):
        here = pl.ds(low, part)
        tops = top_ref[here, :]
        top = jnp.max(tops, axis=1, keepdims=True)
        total = jnp.sum(sum_ref[here, :] * jnp.exp2(tops - top), axis=1, keepdims=True)
        at = pl.ds(pl.multiple_of(base + low, part), part)
        cols_ref[here, :] = log_tgt_ref[at, :] - marg_power * (top + jnp.log2(total))


BESIDE, DEEP = 8, 4


def over_tiles(count, width, body, first, done):
    for start in range(0, width, BESIDE * LANES):
        tiles = [pl.ds(start + j * LANES, LANES) for j in range(BESIDE)]

        def step(i, carry, tiles=tiles):
            carry = list(carry)
            body([halves((i * DEEP + g) * 16) for g in range(DEEP)], tiles, carry)
            return tuple(carry)

        state = lax.fori_loop(0, count // (16 * DEEP), step, tuple(first for _ in tiles))
        for lanes, value in zip(tiles, state):
            done(lanes, value)


def rows_highest(scores_ref, cols_ref, top_ref):
    def body(pairs, tiles, carry):
        for _, places in pairs:
            for place in places:
                if cols_ref is not None:
                    potential = cols_ref[place, :]
                for j, lanes in enumerate(tiles):
                    term = scores_ref[place, lanes]
                    if cols_ref is not None:
                        term = term + potential
                    carry[j] = jnp.maximum(carry[j], term)

    def done(lanes, value):
        top_ref[:, lanes] = jnp.broadcast_to(jnp.max(value, axis=0, keepdims=True), value.shape) - LIFT

    over_tiles(*scores_ref.shape, body, jnp.full((8, LANES), -jnp.inf, jnp.float32), done)


def rows_exp(scores_ref, cols_ref, top_ref, out_ref, keep_ref):
    def body(pairs, tiles, carry):
        tops = [top_ref[:, lanes] for lanes in tiles]
        for at, places in pairs:
            if cols_ref is not None:
                potentials = [cols_ref[place, :] for place in places]
            for j, lanes in enumerate(tiles):
                terms = [scores_ref[place, lanes] for place in places]
                if cols_ref is not None:
                    terms = [term + potential for term, potential in zip(terms, potentials)]
                parts = [jnp.exp2(term - tops[j]) for term in terms]
                if keep_ref is not None:
                    keep_ref[at, lanes] = jnp.concatenate(parts, axis=0).astype(keep_ref.dtype)
                carry[j] = carry[j] + (parts[0] + parts[1])

    def done(lanes, value):
        out_ref[:, lanes] = down(top_ref[:, lanes], value)

    over_tiles(*scores_ref.shape, body, jnp.zeros((8, LANES), jnp.float32), done)


def rows_product(keep_ref, kept_top_ref, factor, shift, out_ref):
    factors = split_rows(factor)
    chunk = 512
    for start in range(0, keep_ref.shape[1], chunk):
        lanes = pl.ds(start, chunk)
        sums = jnp.dot(factors, keep_ref[:, lanes], preferred_element_type=jnp.float32)
        out_ref[:, lanes] = (
            kept_top_ref[0:1, lanes] + (shift - LIFT) + jnp.log2(jnp.sum(sums, axis=0, keepdims=True))
        )


def columns_either(rows, shared, kept, line_ref, scratch, base, count):
    scores_ref, log_tgt_ref, log_tgt_line_ref = shared
    keep_ref, kept_top_ref, kept_rows_ref = kept
    rows_ref, cols_ref, top_ref, sum_ref = scratch
    change = rows - kept_rows_ref[...]
    shift = jnp.max(change)
    near = shift - jnp.min(change) <= SPAN

    @pl.when(near)
    def _():
        factor = jnp.exp2(change - (shift - LIFT))
        columns_product(keep_ref, kept_top_ref, factor, shift, log_tgt_line_ref, line_ref, base, count)

    @pl.when(jnp.logical_not(near))
    def _():
        rows_ref[...] = jnp.broadcast_to(rows, rows_ref.shape)
        columns_running(scores_ref, rows_ref, top_ref, sum_ref, base, count)
        columns_finish(top_ref, sum_ref, log_tgt_ref, cols_ref, base, count)
        line_ref[...] = cols_ref[...].T[0:1, :]


def rows_either(scores_ref, line_ref, kept, cols_ref, row_top_ref, out_ref):
    keep_ref, kept_top_ref, kept_line_ref = kept
    change = line_ref[...] - kept_line_ref[...]
    shift = jnp.max(change)
    near = shift - jnp.min(change) <= SPAN

    @pl.when(near)
    def _():
        rows_product(keep_ref, kept_top_ref, jnp.exp2(change - (shift - LIFT)), shift, out_ref)

    @pl.when(jnp.logical_not(near))
    def _():
        cols_ref[...] = jnp.broadcast_to(line_ref[...], (LANES, line_ref.shape[1])).T
        rows_highest(scores_ref, cols_ref, row_top_ref)
        rows_exp(scores_ref, cols_ref, row_top_ref, out_ref, None)


def first_kernel(scores_ref, sums_ref, more_ref, log_src_ref, log_tgt_ref, log_tgt_line_ref, *refs):
    out_ref, keep_ref, row_top_ref, line_ref = refs[:4]
    rows_ref, cols_ref, top_ref, sum_ref = refs[4:]
    rows_ref[...] = jnp.broadcast_to(row_values(log_src_ref, sums_ref, more_ref), rows_ref.shape)
    count = scores_ref.shape[0]
    columns_running(scores_ref, rows_ref, top_ref, sum_ref, 0, count)
    columns_finish(top_ref, sum_ref, log_tgt_ref, cols_ref, 0, count)
    line_ref[...] = cols_ref[...].T[0:1, :]
    rows_highest(scores_ref, cols_ref, row_top_ref)
    rows_exp(scores_ref, cols_ref, row_top_ref, out_ref, keep_ref)


def second_kernel(scores_ref, sums_ref, more_ref, log_src_ref, log_tgt_ref, log_tgt_line_ref, *refs):
    kept, (out_ref, keep_ref, kept_top_ref, base_ref) = refs[:3], refs[3:7]
    rows_ref, cols_ref, top_ref, sum_ref, line_ref, row_top_ref = refs[7:]
    base_ref[...] = row_values(log_src_ref, sums_ref, more_ref)
    rows_ref[...] = jnp.broadcast_to(base_ref[...], rows_ref.shape)
    count = scores_ref.shape[0]
    columns_exp(scores_ref, rows_ref, top_ref, sum_ref, 0, count, keep_ref)
    columns_finish(top_ref, sum_ref, log_tgt_ref, cols_ref, 0, count)
    kept_top_ref[...] = top_ref[...].T[0:1, :]
    line_ref[...] = cols_ref[...].T[0:1, :]
    rows_either(scores_ref, line_ref, kept, cols_ref, row_top_ref, out_ref)


def later_kernel(scores_ref, sums_ref, more_ref, log_src_ref, log_tgt_ref, log_tgt_line_ref, *refs):
    kept, kept_columns, out_ref = refs[:3], refs[3:6], refs[6]
    scratch, line_ref, row_top_ref = refs[7:11], refs[11], refs[12]
    rows = row_values(log_src_ref, sums_ref, more_ref)
    shared = scores_ref, log_tgt_ref, log_tgt_line_ref
    columns_either(rows, shared, kept_columns, line_ref, scratch, 0, scores_ref.shape[0])
    rows_either(scores_ref, line_ref, kept, scratch[1], row_top_ref, out_ref)


def last_kernel(merged, scores_ref, sums_ref, more_ref, log_src_ref, log_tgt_ref, log_tgt_line_ref, *refs):
    kept_columns, (out_ref, row_ref, col_ref) = refs[:3], refs[3:6]
    scratch, line_ref, values_ref = refs[6:10], refs[10], refs[11]
    own_rows, own_cols = out_ref.shape
    rows = row_values(log_src_ref, sums_ref, more_ref)
    values_ref[...] = rows
    base = pl.multiple_of(lax.rem(lax.div(lax.axis_index("tgt"), 2), merged) * own_cols, own_cols)
    lanes = pl.ds(pl.multiple_of(lax.axis_index("src") * own_rows, own_rows), own_rows)
    shared = scores_ref, log_tgt_ref, log_tgt_line_ref
    columns_either(rows, shared, kept_columns, line_ref, scratch, base, own_cols)
    row_ref[...] = values_ref[:, lanes] * LN2
    col_ref[...] = line_ref[...] * LN2
    block = scores_ref[pl.ds(base, own_cols), lanes] + values_ref[:, lanes]
    out_ref[...] = (block.T + line_ref[...]) * LN2


def swap(value, axis, offset):
    return lax.ppermute(value, axis, [(i, i ^ offset) for i in range(lax.axis_size(axis))])


def staged_parts(value, axis, low, width):
    size = lax.axis_size(axis)
    terms = [value]
    while low < size:
        span = min(width, size // low)
        value = tree(terms, jnp.add)
        terms = [value] + [swap(value, axis, low * j) for j in range(1, span)]
        low *= span
    return terms


def shards(coupling, src_pcs, tgt_pcs, src_mass, tgt_mass):
    f32 = jnp.float32
    pcs = src_pcs.shape[0]
    rows, cols = coupling.shape
    src_size, tgt_size = lax.axis_size("src"), lax.axis_size("tgt")
    total_rows, total_cols = rows * src_size, cols * tgt_size
    merged = 1
    while 2 * merged * 2 <= tgt_size and 2 * merged * cols * total_rows * 4 <= SCORES_BYTES:
        merged *= 2
    wide = merged * cols
    packed_rows = -(-(pcs + 1) // 8) * 8

    arguments = (coupling, src_pcs, tgt_pcs, src_mass.reshape(1, -1), tgt_mass.reshape(1, -1))
    half, whole, moment = pl.pallas_call(
        front_kernel,
        out_shape=(
            pltpu.VMEM((packed_rows, rows // 2), f32),
            pltpu.VMEM((packed_rows, cols), f32),
            pltpu.VMEM((8, 4 * LANES), f32),
        ),
        in_specs=[pl.BlockSpec(memory_space=pltpu.HBM)] * 5,
        out_specs=(VMEM,) * 3,
        scratch_shapes=[pltpu.VMEM(a.shape, a.dtype) for a in arguments]
        + [pltpu.SemaphoreType.DMA((5,))],
        compiler_params=params(8),
    )(*[pltpu.with_memory_space_constraint(a, pltpu.HBM) for a in arguments])

    moment = moment + swap(moment, "tgt", 1)
    half, whole, moment = lax.optimization_barrier((half, whole, moment))
    parts, targets = [moment], [whole]
    if merged > 1:
        message = jnp.concatenate([whole, moment], axis=0)
        targets += [swap(message, "tgt", 2 * b) for b in range(1, merged)]
        parts += [target[packed_rows:] for target in targets[1:]]
    sources = [half] + [swap(half, "src", b) for b in range(1, src_size)]
    parts, sources, targets = lax.optimization_barrier((parts, sources, targets))
    if 2 * merged < tgt_size:
        parts = staged_parts(tree(parts, jnp.add), "tgt", 2 * merged, 4)
    moments = staged_parts(tree(parts, jnp.add), "src", 1, 4)
    near = jnp.concatenate(sources, axis=0)
    far = swap(near, "tgt", 1)

    src_all, turned, log_src, log_tgt, log_tgt_line = pl.pallas_call(
        functools.partial(prepare_kernel, pcs, src_size, merged),
        out_shape=(
            jax.ShapeDtypeStruct((4 * DEPTH, total_rows), jnp.bfloat16),
            jax.ShapeDtypeStruct((wide, LANES), jnp.bfloat16),
            jax.ShapeDtypeStruct((1, total_rows), f32),
            jax.ShapeDtypeStruct((wide, LANES), f32),
            jax.ShapeDtypeStruct((1, wide), f32),
        ),
        in_specs=[VMEM] * (2 + merged),
        out_specs=(VMEM,) * 5,
        compiler_params=params(10),
    )(near, far, *targets)
    scores, sums = pl.pallas_call(
        functools.partial(start_kernel, pcs, total_rows * total_cols),
        out_shape=(
            jax.ShapeDtypeStruct((wide, total_rows), f32),
            jax.ShapeDtypeStruct((1, total_rows), f32),
        ),
        in_specs=[VMEM] * (2 + len(moments)),
        out_specs=(VMEM,) * 2,
        scratch_shapes=[
            pltpu.VMEM((wide, 4 * DEPTH), jnp.bfloat16),
        ],
        compiler_params=params(14),
    )(src_all, turned, *moments)

    def both(value):
        offset = 2 * merged
        while offset < tgt_size:
            value = logsum(value, swap(value, "tgt", offset))
            offset *= 2
        return value, swap(value, "tgt", 1)

    bf16, block = jnp.bfloat16, (wide, total_rows)

    def call(kernel, sums, extra, outs, scratch):
        return pl.pallas_call(
            kernel,
            out_shape=tuple(jax.ShapeDtypeStruct(shape, bf16 if shape == block else f32) for shape in outs),
            in_specs=[VMEM] * (6 + len(extra)),
            out_specs=(VMEM,) * len(outs),
            scratch_shapes=[pltpu.VMEM(shape, f32) for shape in scratch],
            compiler_params=params(10),
        )(scores, *both(sums), log_src, log_tgt, log_tgt_line, *extra)

    line, lines, pads = (1, total_rows), (8, total_rows), (wide, LANES)
    side, columns = (1, wide), (lines, pads, pads, pads)
    sums, *kept_rows = call(first_kernel, sums, (), (line, block, lines, side), columns)
    sums, *kept_columns = call(
        second_kernel, sums, kept_rows, (line, block, side, line), (*columns, side, lines)
    )
    for iteration in range(ITERS - 3):
        (sums,) = call(
            later_kernel, sums, (*kept_rows, *kept_columns), (line,), (*columns, side, lines)
        )
    pads, side = (cols, LANES), (1, cols)
    log_coupling, row_potential, col_potential = call(
        functools.partial(last_kernel, merged), sums, kept_columns,
        ((rows, cols), (1, rows), side), (lines, pads, pads, pads, side, line),
    )
    return log_coupling, row_potential.reshape(-1), col_potential.reshape(-1)


def solution(mesh):
    in_specs = (P("src", "tgt"), P(None, "src"), P(None, "tgt"), P("src"), P("tgt"))
    out_specs = (P("src", "tgt"), P("src"), P("tgt"))
    return jax.shard_map(shards, mesh=mesh, in_specs=in_specs, out_specs=out_specs, check_vma=False)
```

```python
import functools
import math

import jax
import jax.numpy as jnp
from jax import lax
from jax.experimental import pallas as pl
from jax.experimental.pallas import tpu as pltpu
from jax.sharding import PartitionSpec as P

ITERS = 4

eps_reg = 0.5
marg_power = 1.0 / (1.0 + eps_reg)
tiny_eps = 1e-06

LANES = 128
DEPTH = 64
LN2 = math.log(2.0)
SCORES_BYTES = 1 << 24
LIFT = 54.0
SPAN = 145.0
VMEM = pl.BlockSpec(memory_space=pltpu.VMEM)


def params(mib):
    return pltpu.CompilerParams(vmem_limit_bytes=mib << 20)


def tree(values, combine):
    values = list(values)
    while len(values) > 1:
        paired = [combine(values[i], values[i + 1]) for i in range(0, len(values) - 1, 2)]
        values = paired + ([values[-1]] if len(values) % 2 else [])
    return values[0]


def pieces(value):
    high = value.astype(jnp.bfloat16)
    rest = value - high.astype(jnp.float32)
    middle = rest.astype(jnp.bfloat16)
    low = (rest - middle.astype(jnp.float32)).astype(jnp.bfloat16)
    return high, middle, low


def padded(value):
    return jnp.concatenate(
        [value, jnp.zeros((DEPTH - value.shape[0], value.shape[1]), value.dtype)], axis=0
    )


def front_kernel(*refs):
    sources, (half_ref, whole_ref, moment_ref), local, sems = refs[:5], refs[5:8], refs[8:13], refs[13]
    copies = [pltpu.make_async_copy(a, b, sems.at[i]) for i, (a, b) in enumerate(zip(sources, local))]
    for copy in copies:
        copy.start()
    coupling_ref, src_ref, tgt_ref, src_mass_ref, tgt_mass_ref = local
    pcs = src_ref.shape[0]
    half = half_ref.shape[1]
    odd = lax.rem(lax.axis_index("tgt"), 2)
    for copy in copies[1:]:
        copy.wait()
    src = src_ref[...].astype(jnp.float32)
    tgt = tgt_ref[...].astype(jnp.float32)
    below = jnp.zeros((half_ref.shape[0] - pcs - 1, 2 * half), jnp.float32)
    joined = jnp.concatenate([src, jnp.log2(src_mass_ref[...]), below], axis=0)
    half_ref[...] = jnp.where(odd == 0, joined[:, :half], joined[:, half:])
    below = jnp.zeros((half_ref.shape[0] - pcs - 1, tgt.shape[1]), jnp.float32)
    whole_ref[...] = jnp.concatenate([tgt, jnp.log2(tgt_mass_ref[...]), below], axis=0)
    src = padded(src).astype(jnp.bfloat16)
    tgt = padded(tgt).astype(jnp.bfloat16)
    twice = jnp.concatenate([src, src], axis=0)
    copies[0].wait()
    panel = jnp.dot(twice, coupling_ref[...], preferred_element_type=jnp.float32)
    moment = sum(
        lax.dot_general(tgt, part, (((1,), (1,)), ((), ())), preferred_element_type=jnp.float32)
        for part in pieces(panel)
    )
    lane = lax.broadcasted_iota(jnp.int32, (DEPTH // 2, LANES), 1)
    moment = jnp.where(lane < DEPTH, moment[: DEPTH // 2], moment[DEPTH // 2 :])
    for i in range(4):
        moment_ref[:, i * LANES : (i + 1) * LANES] = moment[i * 8 : i * 8 + 8]


def prepare_kernel(pcs, blocks, merged, near_ref, far_ref, *refs):
    tgt_refs, (src_ref, turned_ref, log_src_ref, log_tgt_ref, line_ref) = refs[:merged], refs[merged:]
    packed_rows = near_ref.shape[0] // blocks
    half = near_ref.shape[1]
    width = tgt_refs[0].shape[1]
    z = lax.axis_index("src")
    t = lax.axis_index("tgt")
    odd = lax.rem(t, 2)
    total_rows = 2 * half * blocks
    total_cols = width * lax.axis_size("tgt")
    for b in range(blocks):
        place = jnp.bitwise_xor(z, b)
        for ref, side in ((near_ref, odd), (far_ref, 1 - odd)):
            block = ref[pl.ds(b * packed_rows, packed_rows), :]
            lanes = pl.ds(pl.multiple_of((place * 2 + side) * half, half), half)
            log_src_ref[:, lanes] = marg_power * (block[pcs : pcs + 1] + math.log2(total_cols))
            block = padded(block).astype(jnp.bfloat16)
            for copy in range(4):
                src_ref[pl.ds(copy * DEPTH, DEPTH), lanes] = block
    mine = lax.rem(lax.div(t, 2), merged)
    for b in range(merged):
        base = pl.multiple_of(jnp.bitwise_xor(mine, b) * width, width)
        block = padded(tgt_refs[b][:packed_rows, :])
        line_ref[:, pl.ds(base, width)] = marg_power * (block[pcs : pcs + 1] + math.log2(total_rows))
        turned = jnp.concatenate([block, block], axis=0).T
        log_tgt_ref[pl.ds(base, width), :] = jnp.broadcast_to(
            marg_power * (turned[:, pcs : pcs + 1] + math.log2(total_rows)), (width, LANES)
        )
        turned_ref[pl.ds(base, width), :] = turned.astype(jnp.bfloat16)


def start_kernel(pcs, entries, turned_ref, *refs):
    moment_refs, weights = refs[:-1], refs[-1]
    packed = tree([ref[...] for ref in moment_refs], jnp.add) * entries ** (-0.5)
    spread = jnp.sqrt(jnp.sum(packed * packed) * (1.0 / (pcs * pcs)) + tiny_eps)
    packed = packed / spread * (2.0 / (eps_reg * pcs) / LN2)
    packed = jnp.concatenate([packed[:, i * LANES : (i + 1) * LANES] for i in range(4)], axis=0)
    turned = pltpu.roll(packed, DEPTH, axis=1)
    left = lax.broadcasted_iota(jnp.int32, packed.shape, 1) < DEPTH
    normed = jnp.concatenate(
        [jnp.where(left, packed, turned), jnp.where(left, turned, packed)], axis=0
    )
    high, middle, low = pieces(normed)
    upper = jnp.concatenate([high, middle], axis=0)
    lower = jnp.concatenate([low, jnp.zeros_like(low)], axis=0)

    width = min(512, turned_ref.shape[0])
    first = lax.broadcasted_iota(jnp.int32, (width, LANES), 1) < DEPTH
    for base in range(0, turned_ref.shape[0], width):
        at = pl.ds(base, width)
        weighted = sum(
            jnp.dot(turned_ref[at, :], part, preferred_element_type=jnp.float32)
            for part in (upper, lower)
        )
        high, middle, low = pieces(weighted)
        weights[at, :LANES] = jnp.where(first, high, middle)
        weights[at, LANES:] = jnp.where(first, low, jnp.zeros_like(low))


def down(highest, summed):
    top = jnp.max(highest, axis=0, keepdims=True)
    return top + jnp.log2(jnp.sum(summed * jnp.exp2(highest - top), axis=0, keepdims=True))


def logsum(one, other):
    top = jnp.maximum(one, other)
    return top + jnp.log2(jnp.exp2(one - top) + jnp.exp2(other - top))


def row_values(log_src_ref, sums_ref, more_ref):
    return log_src_ref[...] - marg_power * logsum(sums_ref[...], more_ref[...])


def lane_tiles(ref):
    return [pl.ds(j, LANES) for j in range(0, ref.shape[1], LANES)]


def halves(low):
    low = pl.multiple_of(low, 16)
    return pl.ds(low, 16), [pl.ds(low, 8), pl.ds(pl.multiple_of(low + 8, 8), 8)]


def running(highest, summed, terms):
    fresh = jnp.maximum(highest, tree(terms, jnp.maximum))
    total = tree([jnp.exp2(term - fresh) for term in terms], jnp.add)
    return fresh, summed * jnp.exp2(highest - fresh) + total


def columns_running(scores_ref, rows_ref, top_ref, sum_ref, base, count):
    tiles = lane_tiles(scores_ref)
    span = min(16, len(tiles))

    def scan(i, carry):
        for u in range(4):
            low = pl.multiple_of((i * 4 + u) * 8, 8)
            at = pl.ds(pl.multiple_of(base + low, 8), 8)
            state = None
            for start in range(0, len(tiles), span):
                terms = [scores_ref[at, lanes] + rows_ref[:, lanes] for lanes in tiles[start : start + span]]
                if state is None:
                    highest = tree(terms, jnp.maximum)
                    state = highest, tree([jnp.exp2(term - highest) for term in terms], jnp.add)
                else:
                    state = running(*state, terms)
            top_ref[pl.ds(low, 8), :], sum_ref[pl.ds(low, 8), :] = state
        return carry

    lax.fori_loop(0, count // 32, scan, 0)


def rows_running(scores_ref, out_ref):
    count, total = scores_ref.shape
    beside, deep = 8, 16
    unset = (jnp.full((8, LANES), -jnp.inf, jnp.float32), jnp.zeros((8, LANES), jnp.float32))
    for start in range(0, total, beside * LANES):
        tiles = [pl.ds(start + j * LANES, LANES) for j in range(beside)]

        def step(i, carry, tiles=tiles):
            ats = [pl.ds(pl.multiple_of((i * deep + g) * 8, 8), 8) for g in range(deep)]
            return tuple(
                running(*state, [scores_ref[at, lanes] for at in ats])
                for state, lanes in zip(carry, tiles)
            )

        carry = lax.fori_loop(0, count // (8 * deep), step, (unset,) * beside)
        for lanes, state in zip(tiles, carry):
            out_ref[:, lanes] = down(*state)


def columns_exp(scores_ref, rows_ref, top_ref, sum_ref, base, count, keep_ref):
    tiles = lane_tiles(scores_ref)

    def highest(i, carry):
        places = [pl.ds(pl.multiple_of(i * 64 + g * 8, 8), 8) for g in range(8)]
        sources = [pl.ds(pl.multiple_of(base + i * 64 + g * 8, 8), 8) for g in range(8)]
        tops = [None] * 8
        for lanes in tiles:
            row = rows_ref[:, lanes]
            for g, source in enumerate(sources):
                term = scores_ref[source, lanes] + row
                tops[g] = term if tops[g] is None else jnp.maximum(tops[g], term)
        for place, top in zip(places, tops):
            top_ref[place, :] = top - LIFT
        return carry

    def total(i, carry):
        pairs = [halves(base + i * 64 + g * 16) for g in range(4)]
        places = [place for g in range(4) for place in halves(i * 64 + g * 16)[1]]
        tops = [top_ref[place, :] for place in places]
        sums = [jnp.zeros((8, LANES), jnp.float32)] * 8
        for lanes in tiles:
            row = rows_ref[:, lanes]
            for g, (at, sources) in enumerate(pairs):
                parts = []
                for h, source in enumerate(sources):
                    parts.append(jnp.exp2(scores_ref[source, lanes] + row - tops[2 * g + h]))
                    sums[2 * g + h] = sums[2 * g + h] + parts[h]
                if keep_ref is not None:
                    keep_ref[at, lanes] = jnp.concatenate(parts, axis=0).astype(keep_ref.dtype)
        for place, value in zip(places, sums):
            sum_ref[place, :] = value
        return carry

    lax.fori_loop(0, count // 64, highest, 0)
    if keep_ref is not None:
        tops = top_ref[pl.ds(0, count), :]
        top_ref[pl.ds(0, count), :] = jnp.broadcast_to(jnp.max(tops, axis=1, keepdims=True), tops.shape)
    lax.fori_loop(0, count // 64, total, 0)


def split_rows(line):
    row = lax.broadcasted_iota(jnp.int32, (16, line.shape[1]), 0)
    high, middle, low = (part.astype(jnp.float32) for part in pieces(line))
    spread = jnp.where(row == 0, high, jnp.where(row == 1, middle, jnp.where(row == 2, low, 0.0)))
    return spread.astype(jnp.bfloat16)


def split_rows(line):
    row = lax.broadcasted_iota(jnp.int32, (16, line.shape[1]), 0)
    high, middle, low = (part.astype(jnp.float32) for part in pieces(line))
    spread = jnp.where(row == 0, high, jnp.where(row == 1, middle, jnp.where(row == 2, low, 0.0)))
    return spread.astype(jnp.bfloat16)


def columns_product(keep_ref, kept_top_ref, factor, shift, log_tgt_line_ref, line_ref, base, count):
    factors = split_rows(factor)
    part = min(count, 512)
    for low in range(0, count, part):
        at = pl.ds(pl.multiple_of(base + low, part), part)
        sums = lax.dot_general(
            factors, keep_ref[at, :], (((1,), (1,)), ((), ())), preferred_element_type=jnp.float32
        )
        logs = kept_top_ref[:, at] + (shift - LIFT) + jnp.log2(jnp.sum(sums, axis=0, keepdims=True))
        line_ref[:, pl.ds(low, part)] = log_tgt_line_ref[:, at] - marg_power * logs


def columns_finish(top_ref, sum_ref, log_tgt_ref, cols_ref, base, count):
    part = min(count, 2048)
    for low in range(0, count, part):
        here = pl.ds(low, part)
        tops = top_ref[here, :]
        top = jnp.max(tops, axis=1, keepdims=True)
        total = jnp.sum(sum_ref[here, :] * jnp.exp2(tops - top), axis=1, keepdims=True)
        at = pl.ds(pl.multiple_of(base + low, part), part)
        cols_ref[here, :] = log_tgt_ref[at, :] - marg_power * (top + jnp.log2(total))


BESIDE, DEEP = 8, 4


def over_tiles(count, width, body, first, done):
    for start in range(0, width, BESIDE * LANES):
        tiles = [pl.ds(start + j * LANES, LANES) for j in range(BESIDE)]

        def step(i, carry, tiles=tiles):
            carry = list(carry)
            body([halves((i * DEEP + g) * 16) for g in range(DEEP)], tiles, carry)
            return tuple(carry)

        state = lax.fori_loop(0, count // (16 * DEEP), step, tuple(first for _ in tiles))
        for lanes, value in zip(tiles, state):
            done(lanes, value)


def rows_highest(scores_ref, cols_ref, top_ref):
    def body(pairs, tiles, carry):
        for _, places in pairs:
            for place in places:
                if cols_ref is not None:
                    potential = cols_ref[place, :]
                for j, lanes in enumerate(tiles):
                    term = scores_ref[place, lanes]
                    if cols_ref is not None:
                        term = term + potential
                    carry[j] = jnp.maximum(carry[j], term)

    def done(lanes, value):
        top_ref[:, lanes] = jnp.broadcast_to(jnp.max(value, axis=0, keepdims=True), value.shape) - LIFT

    over_tiles(*scores_ref.shape, body, jnp.full((8, LANES), -jnp.inf, jnp.float32), done)


def rows_exp(scores_ref, cols_ref, top_ref, out_ref, keep_ref):
    def body(pairs, tiles, carry):
        tops = [top_ref[:, lanes] for lanes in tiles]
        for at, places in pairs:
            if cols_ref is not None:
                potentials = [cols_ref[place, :] for place in places]
            for j, lanes in enumerate(tiles):
                terms = [scores_ref[place, lanes] for place in places]
                if cols_ref is not None:
                    terms = [term + potential for term, potential in zip(terms, potentials)]
                parts = [jnp.exp2(term - tops[j]) for term in terms]
                if keep_ref is not None:
                    keep_ref[at, lanes] = jnp.concatenate(parts, axis=0).astype(keep_ref.dtype)
                carry[j] = carry[j] + (parts[0] + parts[1])

    def done(lanes, value):
        out_ref[:, lanes] = down(top_ref[:, lanes], value)

    over_tiles(*scores_ref.shape, body, jnp.zeros((8, LANES), jnp.float32), done)


def rows_product(keep_ref, kept_top_ref, factor, shift, out_ref):
    factors = split_rows(factor)
    chunk = 512
    for start in range(0, keep_ref.shape[1], chunk):
        lanes = pl.ds(start, chunk)
        sums = jnp.dot(factors, keep_ref[:, lanes], preferred_element_type=jnp.float32)
        out_ref[:, lanes] = (
            kept_top_ref[0:1, lanes] + (shift - LIFT) + jnp.log2(jnp.sum(sums, axis=0, keepdims=True))
        )


def columns_either(rows, shared, kept, line_ref, scratch, base, count):
    scores_ref, log_tgt_ref, log_tgt_line_ref = shared
    keep_ref, kept_top_ref, kept_rows_ref = kept
    rows_ref, cols_ref, top_ref, sum_ref = scratch
    change = rows - kept_rows_ref[...]
    shift = jnp.max(change)
    near = shift - jnp.min(change) <= SPAN

    @pl.when(near)
    def _():
        factor = jnp.exp2(change - (shift - LIFT))
        columns_product(keep_ref, kept_top_ref, factor, shift, log_tgt_line_ref, line_ref, base, count)

    @pl.when(jnp.logical_not(near))
    def _():
        rows_ref[...] = jnp.broadcast_to(rows, rows_ref.shape)
        columns_running(scores_ref, rows_ref, top_ref, sum_ref, base, count)
        columns_finish(top_ref, sum_ref, log_tgt_ref, cols_ref, base, count)
        line_ref[...] = cols_ref[...].T[0:1, :]


def rows_either(scores_ref, line_ref, kept, cols_ref, row_top_ref, out_ref):
    keep_ref, kept_top_ref, kept_line_ref = kept
    change = line_ref[...] - kept_line_ref[...]
    shift = jnp.max(change)
    near = shift - jnp.min(change) <= SPAN

    @pl.when(near)
    def _():
        rows_product(keep_ref, kept_top_ref, jnp.exp2(change - (shift - LIFT)), shift, out_ref)

    @pl.when(jnp.logical_not(near))
    def _():
        cols_ref[...] = jnp.broadcast_to(line_ref[...], (LANES, line_ref.shape[1])).T
        rows_highest(scores_ref, cols_ref, row_top_ref)
        rows_exp(scores_ref, cols_ref, row_top_ref, out_ref, None)


def first_kernel(scores_ref, sums_ref, more_ref, log_src_ref, log_tgt_ref, log_tgt_line_ref, *refs):
    out_ref, keep_ref, row_top_ref, line_ref = refs[:4]
    rows_ref, cols_ref, top_ref, sum_ref = refs[4:]
    rows_ref[...] = jnp.broadcast_to(row_values(log_src_ref, sums_ref, more_ref), rows_ref.shape)
    count = scores_ref.shape[0]
    columns_running(scores_ref, rows_ref, top_ref, sum_ref, 0, count)
    columns_finish(top_ref, sum_ref, log_tgt_ref, cols_ref, 0, count)
    line_ref[...] = cols_ref[...].T[0:1, :]
    rows_highest(scores_ref, cols_ref, row_top_ref)
    rows_exp(scores_ref, cols_ref, row_top_ref, out_ref, keep_ref)


def second_kernel(scores_ref, sums_ref, more_ref, log_src_ref, log_tgt_ref, log_tgt_line_ref, *refs):
    kept, (out_ref, keep_ref, kept_top_ref, base_ref) = refs[:3], refs[3:7]
    rows_ref, cols_ref, top_ref, sum_ref, line_ref, row_top_ref = refs[7:]
    base_ref[...] = row_values(log_src_ref, sums_ref, more_ref)
    rows_ref[...] = jnp.broadcast_to(base_ref[...], rows_ref.shape)
    count = scores_ref.shape[0]
    columns_exp(scores_ref, rows_ref, top_ref, sum_ref, 0, count, keep_ref)
    columns_finish(top_ref, sum_ref, log_tgt_ref, cols_ref, 0, count)
    kept_top_ref[...] = top_ref[...].T[0:1, :]
    line_ref[...] = cols_ref[...].T[0:1, :]
    rows_either(scores_ref, line_ref, kept, cols_ref, row_top_ref, out_ref)


def later_kernel(scores_ref, sums_ref, more_ref, log_src_ref, log_tgt_ref, log_tgt_line_ref, *refs):
    kept, kept_columns, out_ref = refs[:3], refs[3:6], refs[6]
    scratch, line_ref, row_top_ref = refs[7:11], refs[11], refs[12]
    rows = row_values(log_src_ref, sums_ref, more_ref)
    shared = scores_ref, log_tgt_ref, log_tgt_line_ref
    columns_either(rows, shared, kept_columns, line_ref, scratch, 0, scores_ref.shape[0])
    rows_either(scores_ref, line_ref, kept, scratch[1], row_top_ref, out_ref)


def last_kernel(merged, scores_ref, sums_ref, more_ref, log_src_ref, log_tgt_ref, log_tgt_line_ref, *refs):
    kept_columns, (out_ref, row_ref, col_ref) = refs[:3], refs[3:6]
    scratch, line_ref, values_ref = refs[6:10], refs[10], refs[11]
    own_rows, own_cols = out_ref.shape
    rows = row_values(log_src_ref, sums_ref, more_ref)
    values_ref[...] = rows
    base = pl.multiple_of(lax.rem(lax.div(lax.axis_index("tgt"), 2), merged) * own_cols, own_cols)
    lanes = pl.ds(pl.multiple_of(lax.axis_index("src") * own_rows, own_rows), own_rows)
    shared = scores_ref, log_tgt_ref, log_tgt_line_ref
    columns_either(rows, shared, kept_columns, line_ref, scratch, base, own_cols)
    row_ref[...] = values_ref[:, lanes] * LN2
    col_ref[...] = line_ref[...] * LN2
    block = scores_ref[pl.ds(base, own_cols), lanes] + values_ref[:, lanes]
    out_ref[...] = (block.T + line_ref[...]) * LN2


def swap(value, axis, offset):
    return lax.ppermute(value, axis, [(i, i ^ offset) for i in range(lax.axis_size(axis))])


def staged_parts(value, axis, low, width):
    size = lax.axis_size(axis)
    terms = [value]
    while low < size:
        span = min(width, size // low)
        value = tree(terms, jnp.add)
        terms = [value] + [swap(value, axis, low * j) for j in range(1, span)]
        low *= span
    return terms


def shards(coupling, src_pcs, tgt_pcs, src_mass, tgt_mass):
    f32 = jnp.float32
    pcs = src_pcs.shape[0]
    rows, cols = coupling.shape
    src_size, tgt_size = lax.axis_size("src"), lax.axis_size("tgt")
    total_rows, total_cols = rows * src_size, cols * tgt_size
    merged = 1
    while 2 * merged * 2 <= tgt_size and 2 * merged * cols * total_rows * 4 <= SCORES_BYTES:
        merged *= 2
    wide = merged * cols
    packed_rows = -(-(pcs + 1) // 8) * 8

    arguments = (coupling, src_pcs, tgt_pcs, src_mass.reshape(1, -1), tgt_mass.reshape(1, -1))
    half, whole, moment = pl.pallas_call(
        front_kernel,
        out_shape=(
            pltpu.VMEM((packed_rows, rows // 2), f32),
            pltpu.VMEM((packed_rows, cols), f32),
            pltpu.VMEM((8, 4 * LANES), f32),
        ),
        in_specs=[pl.BlockSpec(memory_space=pltpu.HBM)] * 5,
        out_specs=(VMEM,) * 3,
        scratch_shapes=[pltpu.VMEM(a.shape, a.dtype) for a in arguments]
        + [pltpu.SemaphoreType.DMA((5,))],
        compiler_params=params(8),
    )(*[pltpu.with_memory_space_constraint(a, pltpu.HBM) for a in arguments])

    moment = moment + swap(moment, "tgt", 1)
    half, whole, moment = lax.optimization_barrier((half, whole, moment))
    parts, targets = [moment], [whole]
    if merged > 1:
        message = jnp.concatenate([whole, moment], axis=0)
        targets += [swap(message, "tgt", 2 * b) for b in range(1, merged)]
        parts += [target[packed_rows:] for target in targets[1:]]
    sources = [half] + [swap(half, "src", b) for b in range(1, src_size)]
    parts, sources, targets = lax.optimization_barrier((parts, sources, targets))
    if 2 * merged < tgt_size:
        parts = staged_parts(tree(parts, jnp.add), "tgt", 2 * merged, 4)
    moments = staged_parts(tree(parts, jnp.add), "src", 1, 4)
    near = jnp.concatenate(sources, axis=0)
    far = swap(near, "tgt", 1)

    src_all, turned, log_src, log_tgt, log_tgt_line = pl.pallas_call(
        functools.partial(prepare_kernel, pcs, src_size, merged),
        out_shape=(
            jax.ShapeDtypeStruct((4 * DEPTH, total_rows), jnp.bfloat16),
            jax.ShapeDtypeStruct((wide, LANES), jnp.bfloat16),
            jax.ShapeDtypeStruct((1, total_rows), f32),
            jax.ShapeDtypeStruct((wide, LANES), f32),
            jax.ShapeDtypeStruct((1, wide), f32),
        ),
        in_specs=[VMEM] * (2 + merged),
        out_specs=(VMEM,) * 5,
        compiler_params=params(10),
    )(near, far, *targets)
    weights = pl.pallas_call(
        functools.partial(start_kernel, pcs, total_rows * total_cols),
        out_shape=jax.ShapeDtypeStruct((wide, 4 * DEPTH), jnp.bfloat16),
        in_specs=[VMEM] * (1 + len(moments)),
        out_specs=VMEM,
        compiler_params=params(10),
    )(turned, *moments)
    scores = jnp.dot(weights, src_all, preferred_element_type=f32)
    sums = pl.pallas_call(
        rows_running,
        out_shape=jax.ShapeDtypeStruct((1, total_rows), f32),
        in_specs=[VMEM],
        out_specs=VMEM,
        compiler_params=params(10),
    )(scores)

    def both(value):
        offset = 2 * merged
        while offset < tgt_size:
            value = logsum(value, swap(value, "tgt", offset))
            offset *= 2
        return value, swap(value, "tgt", 1)

    bf16, block = jnp.bfloat16, (wide, total_rows)

    def call(kernel, sums, extra, outs, scratch):
        return pl.pallas_call(
            kernel,
            out_shape=tuple(jax.ShapeDtypeStruct(shape, bf16 if shape == block else f32) for shape in outs),
            in_specs=[VMEM] * (6 + len(extra)),
            out_specs=(VMEM,) * len(outs),
            scratch_shapes=[pltpu.VMEM(shape, f32) for shape in scratch],
            compiler_params=params(10),
        )(scores, *both(sums), log_src, log_tgt, log_tgt_line, *extra)

    line, lines, pads = (1, total_rows), (8, total_rows), (wide, LANES)
    side, columns = (1, wide), (lines, pads, pads, pads)
    sums, *kept_rows = call(first_kernel, sums, (), (line, block, lines, side), columns)
    sums, *kept_columns = call(
        second_kernel, sums, kept_rows, (line, block, side, line), (*columns, side, lines)
    )
    for iteration in range(ITERS - 3):
        (sums,) = call(
            later_kernel, sums, (*kept_rows, *kept_columns), (line,), (*columns, side, lines)
        )
    pads, side = (cols, LANES), (1, cols)
    log_coupling, row_potential, col_potential = call(
        functools.partial(last_kernel, merged), sums, kept_columns,
        ((rows, cols), (1, rows), side), (lines, pads, pads, pads, side, line),
    )
    return log_coupling, row_potential.reshape(-1), col_potential.reshape(-1)


def solution(mesh):
    in_specs = (P("src", "tgt"), P(None, "src"), P(None, "tgt"), P("src"), P("tgt"))
    out_specs = (P("src", "tgt"), P("src"), P("tgt"))
    return jax.shard_map(shards, mesh=mesh, in_specs=in_specs, out_specs=out_specs, check_vma=False)
```

```python
import functools
import math

import jax
import jax.numpy as jnp
from jax import lax
from jax.experimental import pallas as pl
from jax.experimental.pallas import tpu as pltpu
from jax.sharding import PartitionSpec as P

ITERS = 4

eps_reg = 0.5
marg_power = 1.0 / (1.0 + eps_reg)
tiny_eps = 1e-06

LANES = 128
DEPTH = 64
LN2 = math.log(2.0)
SCORES_BYTES = 1 << 24
LIFT = 54.0
SPAN = 145.0
VMEM = pl.BlockSpec(memory_space=pltpu.VMEM)


def params(mib):
    return pltpu.CompilerParams(vmem_limit_bytes=mib << 20)


def tree(values, combine):
    values = list(values)
    while len(values) > 1:
        paired = [combine(values[i], values[i + 1]) for i in range(0, len(values) - 1, 2)]
        values = paired + ([values[-1]] if len(values) % 2 else [])
    return values[0]


def pieces(value):
    high = value.astype(jnp.bfloat16)
    rest = value - high.astype(jnp.float32)
    middle = rest.astype(jnp.bfloat16)
    low = (rest - middle.astype(jnp.float32)).astype(jnp.bfloat16)
    return high, middle, low


def padded(value):
    return jnp.concatenate(
        [value, jnp.zeros((DEPTH - value.shape[0], value.shape[1]), value.dtype)], axis=0
    )


def front_kernel(*refs):
    sources, (src_pack_ref, tgt_pack_ref, moment_ref), local, sems = refs[:5], refs[5:8], refs[8:13], refs[13]
    copies = [pltpu.make_async_copy(a, b, sems.at[i]) for i, (a, b) in enumerate(zip(sources, local))]
    for copy in copies:
        copy.start()
    coupling_ref, src_ref, tgt_ref, src_mass_ref, tgt_mass_ref = local
    pcs = src_ref.shape[0]
    for copy in copies[1:]:
        copy.wait()
    src = src_ref[...].astype(jnp.float32)
    tgt = tgt_ref[...].astype(jnp.float32)
    below = jnp.zeros((src_pack_ref.shape[0] - pcs - 1, src.shape[1]), jnp.float32)
    joined = jnp.concatenate([src, jnp.log2(src_mass_ref[...]), below], axis=0)
    src_pack_ref[...] = joined
    below = jnp.zeros((src_pack_ref.shape[0] - pcs - 1, tgt.shape[1]), jnp.float32)
    tgt_pack_ref[...] = jnp.concatenate([tgt, jnp.log2(tgt_mass_ref[...]), below], axis=0)
    src = padded(src).astype(jnp.bfloat16)
    tgt = padded(tgt).astype(jnp.bfloat16)
    twice = jnp.concatenate([src, src], axis=0)
    copies[0].wait()
    panel = jnp.dot(twice, coupling_ref[...], preferred_element_type=jnp.float32)
    moment = sum(
        lax.dot_general(tgt, part, (((1,), (1,)), ((), ())), preferred_element_type=jnp.float32)
        for part in pieces(panel)
    )
    lane = lax.broadcasted_iota(jnp.int32, (DEPTH // 2, LANES), 1)
    moment = jnp.where(lane < DEPTH, moment[: DEPTH // 2], moment[DEPTH // 2 :])
    for i in range(4):
        moment_ref[:, i * LANES : (i + 1) * LANES] = moment[i * 8 : i * 8 + 8]


def prepare_kernel(pcs, total_cols, packs_ref, tgt_packs_ref, src_ref, turned_ref, log_src_ref, log_tgt_ref, line_ref):
    blocks, _, height = packs_ref.shape
    merged, _, width = tgt_packs_ref.shape
    for b in range(blocks):
        block = packs_ref[b]
        lanes = pl.ds(b * height, height)
        log_src_ref[:, lanes] = marg_power * (block[pcs : pcs + 1] + math.log2(total_cols))
        block = padded(block).astype(jnp.bfloat16)
        for copy in range(4):
            src_ref[pl.ds(copy * DEPTH, DEPTH), lanes] = block
    for b in range(merged):
        block = padded(tgt_packs_ref[b])
        at = pl.ds(b * width, width)
        line_ref[:, at] = marg_power * (block[pcs : pcs + 1] + math.log2(blocks * height))
        turned = jnp.concatenate([block, block], axis=0).T
        log_tgt_ref[at, :] = jnp.broadcast_to(
            marg_power * (turned[:, pcs : pcs + 1] + math.log2(blocks * height)), (width, LANES)
        )
        turned_ref[at, :] = turned.astype(jnp.bfloat16)


def start_kernel(pcs, entries, turned_ref, *refs):
    moment_refs, weights = refs[:-1], refs[-1]
    packed = tree([ref[...] for ref in moment_refs], jnp.add) * entries ** (-0.5)
    spread = jnp.sqrt(jnp.sum(packed * packed) * (1.0 / (pcs * pcs)) + tiny_eps)
    packed = packed / spread * (2.0 / (eps_reg * pcs) / LN2)
    packed = jnp.concatenate([packed[:, i * LANES : (i + 1) * LANES] for i in range(4)], axis=0)
    turned = pltpu.roll(packed, DEPTH, axis=1)
    left = lax.broadcasted_iota(jnp.int32, packed.shape, 1) < DEPTH
    normed = jnp.concatenate(
        [jnp.where(left, packed, turned), jnp.where(left, turned, packed)], axis=0
    )
    high, middle, low = pieces(normed)
    upper = jnp.concatenate([high, middle], axis=0)
    lower = jnp.concatenate([low, jnp.zeros_like(low)], axis=0)

    width = min(512, turned_ref.shape[0])
    first = lax.broadcasted_iota(jnp.int32, (width, LANES), 1) < DEPTH
    for base in range(0, turned_ref.shape[0], width):
        at = pl.ds(base, width)
        weighted = sum(
            jnp.dot(turned_ref[at, :], part, preferred_element_type=jnp.float32)
            for part in (upper, lower)
        )
        high, middle, low = pieces(weighted)
        weights[at, :LANES] = jnp.where(first, high, middle)
        weights[at, LANES:] = jnp.where(first, low, jnp.zeros_like(low))


def down(highest, summed):
    top = jnp.max(highest, axis=0, keepdims=True)
    return top + jnp.log2(jnp.sum(summed * jnp.exp2(highest - top), axis=0, keepdims=True))


def logsum(one, other):
    top = jnp.maximum(one, other)
    return top + jnp.log2(jnp.exp2(one - top) + jnp.exp2(other - top))


def row_values(log_src_ref, sums_ref, more_ref):
    return log_src_ref[...] - marg_power * logsum(sums_ref[...], more_ref[...])


def lane_tiles(ref):
    return [pl.ds(j, LANES) for j in range(0, ref.shape[1], LANES)]


def halves(low):
    low = pl.multiple_of(low, 16)
    return pl.ds(low, 16), [pl.ds(low, 8), pl.ds(pl.multiple_of(low + 8, 8), 8)]


def running(highest, summed, terms):
    fresh = jnp.maximum(highest, tree(terms, jnp.maximum))
    total = tree([jnp.exp2(term - fresh) for term in terms], jnp.add)
    return fresh, summed * jnp.exp2(highest - fresh) + total


def columns_running(scores_ref, rows_ref, top_ref, sum_ref, base, count):
    tiles = lane_tiles(scores_ref)
    span = min(16, len(tiles))

    def scan(i, carry):
        for u in range(4):
            low = pl.multiple_of((i * 4 + u) * 8, 8)
            at = pl.ds(pl.multiple_of(base + low, 8), 8)
            state = None
            for start in range(0, len(tiles), span):
                terms = [scores_ref[at, lanes] + rows_ref[:, lanes] for lanes in tiles[start : start + span]]
                if state is None:
                    highest = tree(terms, jnp.maximum)
                    state = highest, tree([jnp.exp2(term - highest) for term in terms], jnp.add)
                else:
                    state = running(*state, terms)
            top_ref[pl.ds(low, 8), :], sum_ref[pl.ds(low, 8), :] = state
        return carry

    lax.fori_loop(0, count // 32, scan, 0)


def rows_running(scores_ref, out_ref):
    count, total = scores_ref.shape
    beside, deep = 8, 16
    unset = (jnp.full((8, LANES), -jnp.inf, jnp.float32), jnp.zeros((8, LANES), jnp.float32))
    for start in range(0, total, beside * LANES):
        tiles = [pl.ds(start + j * LANES, LANES) for j in range(beside)]

        def step(i, carry, tiles=tiles):
            ats = [pl.ds(pl.multiple_of((i * deep + g) * 8, 8), 8) for g in range(deep)]
            return tuple(
                running(*state, [scores_ref[at, lanes] for at in ats])
                for state, lanes in zip(carry, tiles)
            )

        carry = lax.fori_loop(0, count // (8 * deep), step, (unset,) * beside)
        for lanes, state in zip(tiles, carry):
            out_ref[:, lanes] = down(*state)


def columns_exp(scores_ref, rows_ref, top_ref, sum_ref, base, count, keep_ref):
    tiles = lane_tiles(scores_ref)

    def highest(i, carry):
        places = [pl.ds(pl.multiple_of(i * 64 + g * 8, 8), 8) for g in range(8)]
        sources = [pl.ds(pl.multiple_of(base + i * 64 + g * 8, 8), 8) for g in range(8)]
        tops = [None] * 8
        for lanes in tiles:
            row = rows_ref[:, lanes]
            for g, source in enumerate(sources):
                term = scores_ref[source, lanes] + row
                tops[g] = term if tops[g] is None else jnp.maximum(tops[g], term)
        for place, top in zip(places, tops):
            top_ref[place, :] = top - LIFT
        return carry

    def total(i, carry):
        pairs = [halves(base + i * 64 + g * 16) for g in range(4)]
        places = [place for g in range(4) for place in halves(i * 64 + g * 16)[1]]
        tops = [top_ref[place, :] for place in places]
        sums = [jnp.zeros((8, LANES), jnp.float32)] * 8
        for lanes in tiles:
            row = rows_ref[:, lanes]
            for g, (at, sources) in enumerate(pairs):
                parts = []
                for h, source in enumerate(sources):
                    parts.append(jnp.exp2(scores_ref[source, lanes] + row - tops[2 * g + h]))
                    sums[2 * g + h] = sums[2 * g + h] + parts[h]
                if keep_ref is not None:
                    keep_ref[at, lanes] = jnp.concatenate(parts, axis=0).astype(keep_ref.dtype)
        for place, value in zip(places, sums):
            sum_ref[place, :] = value
        return carry

    lax.fori_loop(0, count // 64, highest, 0)
    if keep_ref is not None:
        tops = top_ref[pl.ds(0, count), :]
        top_ref[pl.ds(0, count), :] = jnp.broadcast_to(jnp.max(tops, axis=1, keepdims=True), tops.shape)
    lax.fori_loop(0, count // 64, total, 0)


def split_rows(line):
    row = lax.broadcasted_iota(jnp.int32, (16, line.shape[1]), 0)
    high, middle, low = (part.astype(jnp.float32) for part in pieces(line))
    spread = jnp.where(row == 0, high, jnp.where(row == 1, middle, jnp.where(row == 2, low, 0.0)))
    return spread.astype(jnp.bfloat16)


def split_rows(line):
    row = lax.broadcasted_iota(jnp.int32, (16, line.shape[1]), 0)
    high, middle, low = (part.astype(jnp.float32) for part in pieces(line))
    spread = jnp.where(row == 0, high, jnp.where(row == 1, middle, jnp.where(row == 2, low, 0.0)))
    return spread.astype(jnp.bfloat16)


def columns_product(keep_ref, kept_top_ref, factor, shift, log_tgt_line_ref, line_ref, base, count):
    factors = split_rows(factor)
    part = min(count, 512)
    for low in range(0, count, part):
        at = pl.ds(pl.multiple_of(base + low, part), part)
        sums = lax.dot_general(
            factors, keep_ref[at, :], (((1,), (1,)), ((), ())), preferred_element_type=jnp.float32
        )
        logs = kept_top_ref[:, at] + (shift - LIFT) + jnp.log2(jnp.sum(sums, axis=0, keepdims=True))
        line_ref[:, pl.ds(low, part)] = log_tgt_line_ref[:, at] - marg_power * logs


def columns_finish(top_ref, sum_ref, log_tgt_ref, cols_ref, base, count):
    part = min(count, 2048)
    for low in range(0, count, part):
        here = pl.ds(low, part)
        tops = top_ref[here, :]
        top = jnp.max(tops, axis=1, keepdims=True)
        total = jnp.sum(sum_ref[here, :] * jnp.exp2(tops - top), axis=1, keepdims=True)
        at = pl.ds(pl.multiple_of(base + low, part), part)
        cols_ref[here, :] = log_tgt_ref[at, :] - marg_power * (top + jnp.log2(total))


BESIDE, DEEP = 8, 4


def over_tiles(count, width, body, first, done):
    for start in range(0, width, BESIDE * LANES):
        tiles = [pl.ds(start + j * LANES, LANES) for j in range(BESIDE)]

        def step(i, carry, tiles=tiles):
            carry = list(carry)
            body([halves((i * DEEP + g) * 16) for g in range(DEEP)], tiles, carry)
            return tuple(carry)

        state = lax.fori_loop(0, count // (16 * DEEP), step, tuple(first for _ in tiles))
        for lanes, value in zip(tiles, state):
            done(lanes, value)


def rows_highest(scores_ref, cols_ref, top_ref):
    def body(pairs, tiles, carry):
        for _, places in pairs:
            for place in places:
                if cols_ref is not None:
                    potential = cols_ref[place, :]
                for j, lanes in enumerate(tiles):
                    term = scores_ref[place, lanes]
                    if cols_ref is not None:
                        term = term + potential
                    carry[j] = jnp.maximum(carry[j], term)

    def done(lanes, value):
        top_ref[:, lanes] = jnp.broadcast_to(jnp.max(value, axis=0, keepdims=True), value.shape) - LIFT

    over_tiles(*scores_ref.shape, body, jnp.full((8, LANES), -jnp.inf, jnp.float32), done)


def rows_exp(scores_ref, cols_ref, top_ref, out_ref, keep_ref):
    def body(pairs, tiles, carry):
        tops = [top_ref[:, lanes] for lanes in tiles]
        for at, places in pairs:
            if cols_ref is not None:
                potentials = [cols_ref[place, :] for place in places]
            for j, lanes in enumerate(tiles):
                terms = [scores_ref[place, lanes] for place in places]
                if cols_ref is not None:
                    terms = [term + potential for term, potential in zip(terms, potentials)]
                parts = [jnp.exp2(term - tops[j]) for term in terms]
                if keep_ref is not None:
                    keep_ref[at, lanes] = jnp.concatenate(parts, axis=0).astype(keep_ref.dtype)
                carry[j] = carry[j] + (parts[0] + parts[1])

    def done(lanes, value):
        out_ref[:, lanes] = down(top_ref[:, lanes], value)

    over_tiles(*scores_ref.shape, body, jnp.zeros((8, LANES), jnp.float32), done)


def rows_product(keep_ref, kept_top_ref, factor, shift, out_ref):
    factors = split_rows(factor)
    chunk = 512
    for start in range(0, keep_ref.shape[1], chunk):
        lanes = pl.ds(start, chunk)
        sums = jnp.dot(factors, keep_ref[:, lanes], preferred_element_type=jnp.float32)
        out_ref[:, lanes] = (
            kept_top_ref[0:1, lanes] + (shift - LIFT) + jnp.log2(jnp.sum(sums, axis=0, keepdims=True))
        )


def columns_either(rows, shared, kept, line_ref, scratch, base, count):
    scores_ref, log_tgt_ref, log_tgt_line_ref = shared
    keep_ref, kept_top_ref, kept_rows_ref = kept
    rows_ref, cols_ref, top_ref, sum_ref = scratch
    change = rows - kept_rows_ref[...]
    shift = jnp.max(change)
    near = shift - jnp.min(change) <= SPAN

    @pl.when(near)
    def _():
        factor = jnp.exp2(change - (shift - LIFT))
        columns_product(keep_ref, kept_top_ref, factor, shift, log_tgt_line_ref, line_ref, base, count)

    @pl.when(jnp.logical_not(near))
    def _():
        rows_ref[...] = jnp.broadcast_to(rows, rows_ref.shape)
        columns_running(scores_ref, rows_ref, top_ref, sum_ref, base, count)
        columns_finish(top_ref, sum_ref, log_tgt_ref, cols_ref, base, count)
        line_ref[...] = cols_ref[...].T[0:1, :]


def rows_either(scores_ref, line_ref, kept, cols_ref, row_top_ref, out_ref):
    keep_ref, kept_top_ref, kept_line_ref = kept
    change = line_ref[...] - kept_line_ref[...]
    shift = jnp.max(change)
    near = shift - jnp.min(change) <= SPAN

    @pl.when(near)
    def _():
        rows_product(keep_ref, kept_top_ref, jnp.exp2(change - (shift - LIFT)), shift, out_ref)

    @pl.when(jnp.logical_not(near))
    def _():
        cols_ref[...] = jnp.broadcast_to(line_ref[...], (LANES, line_ref.shape[1])).T
        rows_highest(scores_ref, cols_ref, row_top_ref)
        rows_exp(scores_ref, cols_ref, row_top_ref, out_ref, None)


def first_kernel(scores_ref, sums_ref, more_ref, log_src_ref, log_tgt_ref, log_tgt_line_ref, *refs):
    out_ref, keep_ref, row_top_ref, line_ref = refs[:4]
    rows_ref, cols_ref, top_ref, sum_ref = refs[4:]
    rows_ref[...] = jnp.broadcast_to(row_values(log_src_ref, sums_ref, more_ref), rows_ref.shape)
    count = scores_ref.shape[0]
    columns_running(scores_ref, rows_ref, top_ref, sum_ref, 0, count)
    columns_finish(top_ref, sum_ref, log_tgt_ref, cols_ref, 0, count)
    line_ref[...] = cols_ref[...].T[0:1, :]
    rows_highest(scores_ref, cols_ref, row_top_ref)
    rows_exp(scores_ref, cols_ref, row_top_ref, out_ref, keep_ref)


def second_kernel(scores_ref, sums_ref, more_ref, log_src_ref, log_tgt_ref, log_tgt_line_ref, *refs):
    kept, (out_ref, keep_ref, kept_top_ref, base_ref) = refs[:3], refs[3:7]
    rows_ref, cols_ref, top_ref, sum_ref, line_ref, row_top_ref = refs[7:]
    base_ref[...] = row_values(log_src_ref, sums_ref, more_ref)
    rows_ref[...] = jnp.broadcast_to(base_ref[...], rows_ref.shape)
    count = scores_ref.shape[0]
    columns_exp(scores_ref, rows_ref, top_ref, sum_ref, 0, count, keep_ref)
    columns_finish(top_ref, sum_ref, log_tgt_ref, cols_ref, 0, count)
    kept_top_ref[...] = top_ref[...].T[0:1, :]
    line_ref[...] = cols_ref[...].T[0:1, :]
    rows_either(scores_ref, line_ref, kept, cols_ref, row_top_ref, out_ref)


def later_kernel(scores_ref, sums_ref, more_ref, log_src_ref, log_tgt_ref, log_tgt_line_ref, *refs):
    kept, kept_columns, out_ref = refs[:3], refs[3:6], refs[6]
    scratch, line_ref, row_top_ref = refs[7:11], refs[11], refs[12]
    rows = row_values(log_src_ref, sums_ref, more_ref)
    shared = scores_ref, log_tgt_ref, log_tgt_line_ref
    columns_either(rows, shared, kept_columns, line_ref, scratch, 0, scores_ref.shape[0])
    rows_either(scores_ref, line_ref, kept, scratch[1], row_top_ref, out_ref)


def last_kernel(merged, scores_ref, sums_ref, more_ref, log_src_ref, log_tgt_ref, log_tgt_line_ref, *refs):
    kept_columns, (out_ref, row_ref, col_ref) = refs[:3], refs[3:6]
    scratch, line_ref, values_ref = refs[6:10], refs[10], refs[11]
    own_rows, own_cols = out_ref.shape
    rows = row_values(log_src_ref, sums_ref, more_ref)
    values_ref[...] = rows
    base = pl.multiple_of(lax.rem(lax.div(lax.axis_index("tgt"), 2), merged) * own_cols, own_cols)
    lanes = pl.ds(pl.multiple_of(lax.axis_index("src") * own_rows, own_rows), own_rows)
    shared = scores_ref, log_tgt_ref, log_tgt_line_ref
    columns_either(rows, shared, kept_columns, line_ref, scratch, base, own_cols)
    row_ref[...] = values_ref[:, lanes] * LN2
    col_ref[...] = line_ref[...] * LN2
    block = scores_ref[pl.ds(base, own_cols), lanes] + values_ref[:, lanes]
    out_ref[...] = (block.T + line_ref[...]) * LN2


def swap(value, axis, offset):
    return lax.ppermute(value, axis, [(i, i ^ offset) for i in range(lax.axis_size(axis))])


def staged_parts(value, axis, low, width):
    size = lax.axis_size(axis)
    terms = [value]
    while low < size:
        span = min(width, size // low)
        value = tree(terms, jnp.add)
        terms = [value] + [swap(value, axis, low * j) for j in range(1, span)]
        low *= span
    return terms


def shards(coupling, src_pcs, tgt_pcs, src_mass, tgt_mass):
    f32 = jnp.float32
    pcs = src_pcs.shape[0]
    rows, cols = coupling.shape
    src_size, tgt_size = lax.axis_size("src"), lax.axis_size("tgt")
    total_rows, total_cols = rows * src_size, cols * tgt_size
    merged = 1
    while 2 * merged * 2 <= tgt_size and 2 * merged * cols * total_rows * 4 <= SCORES_BYTES:
        merged *= 2
    wide = merged * cols
    packed_rows = -(-(pcs + 1) // 8) * 8

    arguments = (coupling, src_pcs, tgt_pcs, src_mass.reshape(1, -1), tgt_mass.reshape(1, -1))
    src_pack, tgt_pack, moment = pl.pallas_call(
        front_kernel,
        out_shape=(
            pltpu.VMEM((packed_rows, rows), f32),
            pltpu.VMEM((packed_rows, cols), f32),
            pltpu.VMEM((8, 4 * LANES), f32),
        ),
        in_specs=[pl.BlockSpec(memory_space=pltpu.HBM)] * 5,
        out_specs=(VMEM,) * 3,
        scratch_shapes=[pltpu.VMEM(a.shape, a.dtype) for a in arguments]
        + [pltpu.SemaphoreType.DMA((5,))],
        compiler_params=params(8),
    )(*[pltpu.with_memory_space_constraint(a, pltpu.HBM) for a in arguments])

    src_packs = lax.all_gather(src_pack, "src")
    ring = range(0, 2 * merged, 2)
    groups = [[i + j for j in ring] for k in range(0, tgt_size, 2 * merged) for i in (k, k + 1)]
    tgt_packs = lax.all_gather(tgt_pack, "tgt", axis_index_groups=groups) if merged > 1 else tgt_pack[None]
    moment = moment + swap(moment, "tgt", 1)
    parts = staged_parts(moment, "tgt", 2, 4)
    moments = staged_parts(tree(parts, jnp.add), "src", 1, 4)

    src_all, turned, log_src, log_tgt, log_tgt_line = pl.pallas_call(
        functools.partial(prepare_kernel, pcs, total_cols),
        out_shape=(
            jax.ShapeDtypeStruct((4 * DEPTH, total_rows), jnp.bfloat16),
            jax.ShapeDtypeStruct((wide, LANES), jnp.bfloat16),
            jax.ShapeDtypeStruct((1, total_rows), f32),
            jax.ShapeDtypeStruct((wide, LANES), f32),
            jax.ShapeDtypeStruct((1, wide), f32),
        ),
        in_specs=[VMEM] * 2,
        out_specs=(VMEM,) * 5,
        compiler_params=params(10),
    )(src_packs, tgt_packs)
    weights = pl.pallas_call(
        functools.partial(start_kernel, pcs, total_rows * total_cols),
        out_shape=jax.ShapeDtypeStruct((wide, 4 * DEPTH), jnp.bfloat16),
        in_specs=[VMEM] * (1 + len(moments)),
        out_specs=VMEM,
        compiler_params=params(10),
    )(turned, *moments)
    scores = jnp.dot(weights, src_all, preferred_element_type=f32)
    sums = pl.pallas_call(
        rows_running,
        out_shape=jax.ShapeDtypeStruct((1, total_rows), f32),
        in_specs=[VMEM],
        out_specs=VMEM,
        compiler_params=params(10),
    )(scores)

    def both(value):
        offset = 2 * merged
        while offset < tgt_size:
            value = logsum(value, swap(value, "tgt", offset))
            offset *= 2
        return value, swap(value, "tgt", 1)

    bf16, block = jnp.bfloat16, (wide, total_rows)

    def call(kernel, sums, extra, outs, scratch):
        return pl.pallas_call(
            kernel,
            out_shape=tuple(jax.ShapeDtypeStruct(shape, bf16 if shape == block else f32) for shape in outs),
            in_specs=[VMEM] * (6 + len(extra)),
            out_specs=(VMEM,) * len(outs),
            scratch_shapes=[pltpu.VMEM(shape, f32) for shape in scratch],
            compiler_params=params(10),
        )(scores, *both(sums), log_src, log_tgt, log_tgt_line, *extra)

    line, lines, pads = (1, total_rows), (8, total_rows), (wide, LANES)
    side, columns = (1, wide), (lines, pads, pads, pads)
    sums, *kept_rows = call(first_kernel, sums, (), (line, block, lines, side), columns)
    sums, *kept_columns = call(
        second_kernel, sums, kept_rows, (line, block, side, line), (*columns, side, lines)
    )
    for iteration in range(ITERS - 3):
        (sums,) = call(
            later_kernel, sums, (*kept_rows, *kept_columns), (line,), (*columns, side, lines)
        )
    pads, side = (cols, LANES), (1, cols)
    log_coupling, row_potential, col_potential = call(
        functools.partial(last_kernel, merged), sums, kept_columns,
        ((rows, cols), (1, rows), side), (lines, pads, pads, pads, side, line),
    )
    return log_coupling, row_potential.reshape(-1), col_potential.reshape(-1)


def solution(mesh):
    in_specs = (P("src", "tgt"), P(None, "src"), P(None, "tgt"), P("src"), P("tgt"))
    out_specs = (P("src", "tgt"), P("src"), P("tgt"))
    return jax.shard_map(shards, mesh=mesh, in_specs=in_specs, out_specs=out_specs, check_vma=False)
```

```python
import functools
import math

import jax
import jax.numpy as jnp
from jax import lax
from jax.experimental import pallas as pl
from jax.experimental.pallas import tpu as pltpu
from jax.sharding import PartitionSpec as P

ITERS = 4

eps_reg = 0.5
marg_power = 1.0 / (1.0 + eps_reg)
tiny_eps = 1e-06

LANES = 128
DEPTH = 64
LN2 = math.log(2.0)
SCORES_BYTES = 1 << 24
LIFT = 54.0
SPAN = 145.0
VMEM = pl.BlockSpec(memory_space=pltpu.VMEM)


def params(mib):
    return pltpu.CompilerParams(vmem_limit_bytes=mib << 20)


def tree(values, combine):
    values = list(values)
    while len(values) > 1:
        paired = [combine(values[i], values[i + 1]) for i in range(0, len(values) - 1, 2)]
        values = paired + ([values[-1]] if len(values) % 2 else [])
    return values[0]


def pieces(value):
    high = value.astype(jnp.bfloat16)
    rest = value - high.astype(jnp.float32)
    middle = rest.astype(jnp.bfloat16)
    low = (rest - middle.astype(jnp.float32)).astype(jnp.bfloat16)
    return high, middle, low


def padded(value):
    return jnp.concatenate(
        [value, jnp.zeros((DEPTH - value.shape[0], value.shape[1]), value.dtype)], axis=0
    )


def front_kernel(*refs):
    sources, (half_ref, whole_ref, moment_ref), local, sems = refs[:5], refs[5:8], refs[8:13], refs[13]
    copies = [pltpu.make_async_copy(a, b, sems.at[i]) for i, (a, b) in enumerate(zip(sources, local))]
    for copy in copies:
        copy.start()
    coupling_ref, src_ref, tgt_ref, src_mass_ref, tgt_mass_ref = local
    pcs = src_ref.shape[0]
    half = half_ref.shape[1]
    odd = lax.rem(lax.axis_index("tgt"), 2)
    for copy in copies[1:]:
        copy.wait()
    src = src_ref[...].astype(jnp.float32)
    tgt = tgt_ref[...].astype(jnp.float32)
    below = jnp.zeros((half_ref.shape[0] - pcs - 1, 2 * half), jnp.float32)
    joined = jnp.concatenate([src, jnp.log2(src_mass_ref[...]), below], axis=0)
    half_ref[...] = jnp.where(odd == 0, joined[:, :half], joined[:, half:])
    below = jnp.zeros((half_ref.shape[0] - pcs - 1, tgt.shape[1]), jnp.float32)
    whole_ref[...] = jnp.concatenate([tgt, jnp.log2(tgt_mass_ref[...]), below], axis=0)
    src = padded(src).astype(jnp.bfloat16)
    tgt = padded(tgt).astype(jnp.bfloat16)
    twice = jnp.concatenate([src, src], axis=0)
    copies[0].wait()
    panel = jnp.dot(twice, coupling_ref[...], preferred_element_type=jnp.float32)
    moment = sum(
        lax.dot_general(tgt, part, (((1,), (1,)), ((), ())), preferred_element_type=jnp.float32)
        for part in pieces(panel)
    )
    lane = lax.broadcasted_iota(jnp.int32, (DEPTH // 2, LANES), 1)
    moment = jnp.where(lane < DEPTH, moment[: DEPTH // 2], moment[DEPTH // 2 :])
    for i in range(4):
        moment_ref[:, i * LANES : (i + 1) * LANES] = moment[i * 8 : i * 8 + 8]


def prepare_kernel(pcs, blocks, merged, near_ref, far_ref, *refs):
    tgt_refs, (src_ref, turned_ref, log_src_ref, log_tgt_ref, line_ref) = refs[:merged], refs[merged:]
    packed_rows = near_ref.shape[0] // blocks
    half = near_ref.shape[1]
    width = tgt_refs[0].shape[1]
    z = lax.axis_index("src")
    t = lax.axis_index("tgt")
    odd = lax.rem(t, 2)
    total_rows = 2 * half * blocks
    total_cols = width * lax.axis_size("tgt")
    for b in range(blocks):
        place = jnp.bitwise_xor(z, b)
        for ref, side in ((near_ref, odd), (far_ref, 1 - odd)):
            block = ref[pl.ds(b * packed_rows, packed_rows), :]
            lanes = pl.ds(pl.multiple_of((place * 2 + side) * half, half), half)
            log_src_ref[:, lanes] = marg_power * (block[pcs : pcs + 1] + math.log2(total_cols))
            block = padded(block).astype(jnp.bfloat16)
            for copy in range(4):
                src_ref[pl.ds(copy * DEPTH, DEPTH), lanes] = block
    mine = lax.rem(lax.div(t, 2), merged)
    for b in range(merged):
        base = pl.multiple_of(jnp.bitwise_xor(mine, b) * width, width)
        block = padded(tgt_refs[b][:packed_rows, :])
        line_ref[:, pl.ds(base, width)] = marg_power * (block[pcs : pcs + 1] + math.log2(total_rows))
        turned = jnp.concatenate([block, block], axis=0).T
        log_tgt_ref[pl.ds(base, width), :] = jnp.broadcast_to(
            marg_power * (turned[:, pcs : pcs + 1] + math.log2(total_rows)), (width, LANES)
        )
        turned_ref[pl.ds(base, width), :] = turned.astype(jnp.bfloat16)


def start_kernel(pcs, entries, turned_ref, *refs):
    moment_refs, weights = refs[:-1], refs[-1]
    packed = tree([ref[...] for ref in moment_refs], jnp.add) * entries ** (-0.5)
    spread = jnp.sqrt(jnp.sum(packed * packed) * (1.0 / (pcs * pcs)) + tiny_eps)
    packed = packed / spread * (2.0 / (eps_reg * pcs) / LN2)
    packed = jnp.concatenate([packed[:, i * LANES : (i + 1) * LANES] for i in range(4)], axis=0)
    turned = pltpu.roll(packed, DEPTH, axis=1)
    left = lax.broadcasted_iota(jnp.int32, packed.shape, 1) < DEPTH
    normed = jnp.concatenate(
        [jnp.where(left, packed, turned), jnp.where(left, turned, packed)], axis=0
    )
    high, middle, low = pieces(normed)
    upper = jnp.concatenate([high, middle], axis=0)
    lower = jnp.concatenate([low, jnp.zeros_like(low)], axis=0)

    width = min(512, turned_ref.shape[0])
    first = lax.broadcasted_iota(jnp.int32, (width, LANES), 1) < DEPTH
    for base in range(0, turned_ref.shape[0], width):
        at = pl.ds(base, width)
        weighted = sum(
            jnp.dot(turned_ref[at, :], part, preferred_element_type=jnp.float32)
            for part in (upper, lower)
        )
        high, middle, low = pieces(weighted)
        weights[at, :LANES] = jnp.where(first, high, middle)
        weights[at, LANES:] = jnp.where(first, low, jnp.zeros_like(low))


def down(highest, summed):
    top = jnp.max(highest, axis=0, keepdims=True)
    return top + jnp.log2(jnp.sum(summed * jnp.exp2(highest - top), axis=0, keepdims=True))


def logsum(one, other):
    top = jnp.maximum(one, other)
    return top + jnp.log2(jnp.exp2(one - top) + jnp.exp2(other - top))


def row_values(log_src_ref, sums_ref, more_ref):
    return log_src_ref[...] - marg_power * logsum(sums_ref[...], more_ref[...])


def lane_tiles(ref):
    return [pl.ds(j, LANES) for j in range(0, ref.shape[1], LANES)]


def halves(low):
    low = pl.multiple_of(low, 16)
    return pl.ds(low, 16), [pl.ds(low, 8), pl.ds(pl.multiple_of(low + 8, 8), 8)]


def running(highest, summed, terms):
    fresh = jnp.maximum(highest, tree(terms, jnp.maximum))
    total = tree([jnp.exp2(term - fresh) for term in terms], jnp.add)
    return fresh, summed * jnp.exp2(highest - fresh) + total


def columns_running(scores_ref, rows_ref, top_ref, sum_ref, base, count):
    tiles = lane_tiles(scores_ref)
    span = min(16, len(tiles))

    def scan(i, carry):
        for u in range(4):
            low = pl.multiple_of((i * 4 + u) * 8, 8)
            at = pl.ds(pl.multiple_of(base + low, 8), 8)
            state = None
            for start in range(0, len(tiles), span):
                terms = [scores_ref[at, lanes] + rows_ref[:, lanes] for lanes in tiles[start : start + span]]
                if state is None:
                    highest = tree(terms, jnp.maximum)
                    state = highest, tree([jnp.exp2(term - highest) for term in terms], jnp.add)
                else:
                    state = running(*state, terms)
            top_ref[pl.ds(low, 8), :], sum_ref[pl.ds(low, 8), :] = state
        return carry

    lax.fori_loop(0, count // 32, scan, 0)


def rows_running(scores_ref, out_ref):
    count, total = scores_ref.shape
    beside, deep = 8, 16
    unset = (jnp.full((8, LANES), -jnp.inf, jnp.float32), jnp.zeros((8, LANES), jnp.float32))
    for start in range(0, total, beside * LANES):
        tiles = [pl.ds(start + j * LANES, LANES) for j in range(beside)]

        def step(i, carry, tiles=tiles):
            ats = [pl.ds(pl.multiple_of((i * deep + g) * 8, 8), 8) for g in range(deep)]
            return tuple(
                running(*state, [scores_ref[at, lanes] for at in ats])
                for state, lanes in zip(carry, tiles)
            )

        carry = lax.fori_loop(0, count // (8 * deep), step, (unset,) * beside)
        for lanes, state in zip(tiles, carry):
            out_ref[:, lanes] = down(*state)


def columns_exp(scores_ref, rows_ref, top_ref, sum_ref, rounded_ref, count, keep_ref):
    tiles = lane_tiles(scores_ref)

    def highest(i, carry):
        places = [pl.ds(pl.multiple_of(i * 64 + g * 8, 8), 8) for g in range(8)]
        tops = [None] * 8
        for lanes in tiles:
            row = rows_ref[:, lanes]
            for g, place in enumerate(places):
                term = scores_ref[place, lanes] + row
                tops[g] = term if tops[g] is None else jnp.maximum(tops[g], term)
        for place, top in zip(places, tops):
            top_ref[place, :] = top - LIFT
        return carry

    def total(i, carry):
        pairs = [halves(i * 64 + g * 16) for g in range(4)]
        places = [place for _, pair in pairs for place in pair]
        tops = [top_ref[place, :] for place in places]
        sums = [jnp.zeros((8, LANES), jnp.float32)] * 8
        rounded = [jnp.zeros((8, LANES), jnp.float32)] * 8
        for lanes in tiles:
            row = rows_ref[:, lanes]
            for g, (at, sources) in enumerate(pairs):
                parts = [
                    jnp.exp2(scores_ref[source, lanes] + row - tops[2 * g + h])
                    for h, source in enumerate(sources)
                ]
                kept = jnp.concatenate(parts, axis=0).astype(keep_ref.dtype)
                keep_ref[at, lanes] = kept
                kept = kept.astype(jnp.float32)
                for h in range(2):
                    sums[2 * g + h] = sums[2 * g + h] + parts[h]
                    rounded[2 * g + h] = rounded[2 * g + h] + kept[8 * h : 8 * h + 8]
        for place, value, other in zip(places, sums, rounded):
            sum_ref[place, :] = value
            rounded_ref[place, :] = other
        return carry

    lax.fori_loop(0, count // 64, highest, 0)
    tops = top_ref[...]
    top_ref[...] = jnp.broadcast_to(jnp.max(tops, axis=1, keepdims=True), tops.shape)
    lax.fori_loop(0, count // 64, total, 0)


def split_rows(line):
    row = lax.broadcasted_iota(jnp.int32, (16, line.shape[1]), 0)
    high, middle, low = (part.astype(jnp.float32) for part in pieces(line))
    spread = jnp.where(row == 0, high, jnp.where(row == 1, middle, jnp.where(row == 2, low, 0.0)))
    return spread.astype(jnp.bfloat16)


def split_rows(line):
    row = lax.broadcasted_iota(jnp.int32, (16, line.shape[1]), 0)
    high, middle, low = (part.astype(jnp.float32) for part in pieces(line))
    spread = jnp.where(row == 0, high, jnp.where(row == 1, middle, jnp.where(row == 2, low, 0.0)))
    return spread.astype(jnp.bfloat16)


def columns_product(keep_ref, kept_top_ref, factor, shift, log_tgt_line_ref, line_ref, base, count):
    factors = split_rows(factor)
    part = min(count, 512)
    for low in range(0, count, part):
        at = pl.ds(pl.multiple_of(base + low, part), part)
        sums = lax.dot_general(
            factors, keep_ref[at, :], (((1,), (1,)), ((), ())), preferred_element_type=jnp.float32
        )
        logs = kept_top_ref[:, at] + (shift - LIFT) + jnp.log2(jnp.sum(sums, axis=0, keepdims=True))
        line_ref[:, pl.ds(low, part)] = log_tgt_line_ref[:, at] - marg_power * logs


def columns_finish(top_ref, sum_ref, log_tgt_ref, cols_ref, base, count):
    part = min(count, 2048)
    for low in range(0, count, part):
        here = pl.ds(low, part)
        tops = top_ref[here, :]
        top = jnp.max(tops, axis=1, keepdims=True)
        total = jnp.sum(sum_ref[here, :] * jnp.exp2(tops - top), axis=1, keepdims=True)
        at = pl.ds(pl.multiple_of(base + low, part), part)
        cols_ref[here, :] = log_tgt_ref[at, :] - marg_power * (top + jnp.log2(total))


BESIDE, DEEP = 8, 4


def over_tiles(count, width, body, first, done):
    for start in range(0, width, BESIDE * LANES):
        tiles = [pl.ds(start + j * LANES, LANES) for j in range(BESIDE)]

        def step(i, carry, tiles=tiles):
            carry = list(carry)
            body([halves((i * DEEP + g) * 16) for g in range(DEEP)], tiles, carry)
            return tuple(carry)

        state = lax.fori_loop(0, count // (16 * DEEP), step, tuple(first for _ in tiles))
        for lanes, value in zip(tiles, state):
            done(lanes, value)


def rows_highest(scores_ref, cols_ref, top_ref):
    def body(pairs, tiles, carry):
        for _, places in pairs:
            for place in places:
                if cols_ref is not None:
                    potential = cols_ref[place, :]
                for j, lanes in enumerate(tiles):
                    term = scores_ref[place, lanes]
                    if cols_ref is not None:
                        term = term + potential
                    carry[j] = jnp.maximum(carry[j], term)

    def done(lanes, value):
        top_ref[:, lanes] = jnp.broadcast_to(jnp.max(value, axis=0, keepdims=True), value.shape) - LIFT

    over_tiles(*scores_ref.shape, body, jnp.full((8, LANES), -jnp.inf, jnp.float32), done)


def rows_exp(scores_ref, cols_ref, top_ref, out_ref, keep_ref, level_ref):
    def body(pairs, tiles, carry):
        tops = [top_ref[:, lanes] for lanes in tiles]
        for at, places in pairs:
            potentials = [cols_ref[place, :] for place in places]
            for j, lanes in enumerate(tiles):
                terms = [scores_ref[place, lanes] + c for place, c in zip(places, potentials)]
                parts = [jnp.exp2(term - tops[j]) for term in terms]
                summed, rounded = carry[j]
                if keep_ref is not None:
                    kept = jnp.concatenate(parts, axis=0).astype(keep_ref.dtype)
                    keep_ref[at, lanes] = kept
                    kept = kept.astype(jnp.float32)
                    rounded = rounded + (kept[:8] + kept[8:])
                carry[j] = summed + (parts[0] + parts[1]), rounded

    def done(lanes, value):
        exact = down(top_ref[:, lanes], value[0])
        out_ref[:, lanes] = exact
        if keep_ref is not None:
            level = top_ref[:, lanes] + (exact - down(top_ref[:, lanes], value[1]))
            level_ref[:, lanes] = level

    zero = jnp.zeros((8, LANES), jnp.float32)
    over_tiles(*scores_ref.shape, body, (zero, zero), done)


def rows_product(keep_ref, kept_top_ref, factor, shift, out_ref):
    factors = split_rows(factor)
    chunk = 512
    for start in range(0, keep_ref.shape[1], chunk):
        lanes = pl.ds(start, chunk)
        sums = jnp.dot(factors, keep_ref[:, lanes], preferred_element_type=jnp.float32)
        out_ref[:, lanes] = (
            kept_top_ref[0:1, lanes] + (shift - LIFT) + jnp.log2(jnp.sum(sums, axis=0, keepdims=True))
        )


def columns_either(rows, shared, kept, line_ref, scratch, base, count):
    scores_ref, log_tgt_ref, log_tgt_line_ref = shared
    keep_ref, kept_top_ref, kept_rows_ref = kept
    rows_ref, cols_ref, top_ref, sum_ref = scratch
    change = rows - kept_rows_ref[...]
    shift = jnp.max(change)
    near = shift - jnp.min(change) <= SPAN

    @pl.when(near)
    def _():
        factor = jnp.exp2(change - (shift - LIFT))
        columns_product(keep_ref, kept_top_ref, factor, shift, log_tgt_line_ref, line_ref, base, count)

    @pl.when(jnp.logical_not(near))
    def _():
        rows_ref[...] = jnp.broadcast_to(rows, rows_ref.shape)
        columns_running(scores_ref, rows_ref, top_ref, sum_ref, base, count)
        columns_finish(top_ref, sum_ref, log_tgt_ref, cols_ref, base, count)
        line_ref[...] = cols_ref[...].T[0:1, :]


def rows_either(scores_ref, line_ref, kept, cols_ref, row_top_ref, out_ref):
    keep_ref, kept_top_ref, kept_line_ref = kept
    change = line_ref[...] - kept_line_ref[...]
    shift = jnp.max(change)
    near = shift - jnp.min(change) <= SPAN

    @pl.when(near)
    def _():
        rows_product(keep_ref, kept_top_ref, jnp.exp2(change - (shift - LIFT)), shift, out_ref)

    @pl.when(jnp.logical_not(near))
    def _():
        cols_ref[...] = jnp.broadcast_to(line_ref[...], (LANES, line_ref.shape[1])).T
        rows_highest(scores_ref, cols_ref, row_top_ref)
        rows_exp(scores_ref, cols_ref, row_top_ref, out_ref, None, None)


def first_kernel(scores_ref, sums_ref, more_ref, log_src_ref, log_tgt_ref, log_tgt_line_ref, *refs):
    out_ref, keep_ref, row_top_ref, line_ref = refs[:4]
    rows_ref, cols_ref, top_ref, sum_ref = refs[4:]
    rows_ref[...] = jnp.broadcast_to(row_values(log_src_ref, sums_ref, more_ref), rows_ref.shape)
    count = scores_ref.shape[0]
    columns_running(scores_ref, rows_ref, top_ref, sum_ref, 0, count)
    columns_finish(top_ref, sum_ref, log_tgt_ref, cols_ref, 0, count)
    line_ref[...] = cols_ref[...].T[0:1, :]
    rows_highest(scores_ref, cols_ref, row_top_ref)
    rows_exp(scores_ref, cols_ref, row_top_ref, out_ref, keep_ref, row_top_ref)


def second_kernel(scores_ref, sums_ref, more_ref, log_src_ref, log_tgt_ref, log_tgt_line_ref, *refs):
    kept, (out_ref, keep_ref, kept_top_ref, base_ref) = refs[:3], refs[3:7]
    rows_ref, cols_ref, top_ref, sum_ref, line_ref, row_top_ref, rounded_ref = refs[7:]
    base_ref[...] = row_values(log_src_ref, sums_ref, more_ref)
    rows_ref[...] = jnp.broadcast_to(base_ref[...], rows_ref.shape)
    count = scores_ref.shape[0]
    columns_exp(scores_ref, rows_ref, top_ref, sum_ref, rounded_ref, count, keep_ref)
    totals = jnp.log2(jnp.sum(sum_ref[...], axis=1, keepdims=True))
    level = top_ref[...] + (totals - jnp.log2(jnp.sum(rounded_ref[...], axis=1, keepdims=True)))
    kept_top_ref[...] = level.T[0:1, :]
    cols_ref[...] = log_tgt_ref[...] - marg_power * (top_ref[...] + totals)
    line_ref[...] = cols_ref[...].T[0:1, :]
    rows_either(scores_ref, line_ref, kept, cols_ref, row_top_ref, out_ref)


def later_kernel(scores_ref, sums_ref, more_ref, log_src_ref, log_tgt_ref, log_tgt_line_ref, *refs):
    kept, kept_columns, out_ref = refs[:3], refs[3:6], refs[6]
    scratch, line_ref, row_top_ref = refs[7:11], refs[11], refs[12]
    rows = row_values(log_src_ref, sums_ref, more_ref)
    shared = scores_ref, log_tgt_ref, log_tgt_line_ref
    columns_either(rows, shared, kept_columns, line_ref, scratch, 0, scores_ref.shape[0])
    rows_either(scores_ref, line_ref, kept, scratch[1], row_top_ref, out_ref)


def last_kernel(merged, scores_ref, sums_ref, more_ref, log_src_ref, log_tgt_ref, log_tgt_line_ref, *refs):
    kept_columns, (out_ref, row_ref, col_ref) = refs[:3], refs[3:6]
    scratch, line_ref, values_ref = refs[6:10], refs[10], refs[11]
    own_rows, own_cols = out_ref.shape
    rows = row_values(log_src_ref, sums_ref, more_ref)
    values_ref[...] = rows
    base = pl.multiple_of(lax.rem(lax.div(lax.axis_index("tgt"), 2), merged) * own_cols, own_cols)
    lanes = pl.ds(pl.multiple_of(lax.axis_index("src") * own_rows, own_rows), own_rows)
    shared = scores_ref, log_tgt_ref, log_tgt_line_ref
    columns_either(rows, shared, kept_columns, line_ref, scratch, base, own_cols)
    row_ref[...] = values_ref[:, lanes] * LN2
    col_ref[...] = line_ref[...] * LN2
    block = scores_ref[pl.ds(base, own_cols), lanes] + values_ref[:, lanes]
    out_ref[...] = (block.T + line_ref[...]) * LN2


def swap(value, axis, offset):
    return lax.ppermute(value, axis, [(i, i ^ offset) for i in range(lax.axis_size(axis))])


def staged_parts(value, axis, low, width):
    size = lax.axis_size(axis)
    terms = [value]
    while low < size:
        span = min(width, size // low)
        value = tree(terms, jnp.add)
        terms = [value] + [swap(value, axis, low * j) for j in range(1, span)]
        low *= span
    return terms


def shards(coupling, src_pcs, tgt_pcs, src_mass, tgt_mass):
    f32 = jnp.float32
    pcs = src_pcs.shape[0]
    rows, cols = coupling.shape
    src_size, tgt_size = lax.axis_size("src"), lax.axis_size("tgt")
    total_rows, total_cols = rows * src_size, cols * tgt_size
    merged = 1
    while 2 * merged * 2 <= tgt_size and 2 * merged * cols * total_rows * 4 <= SCORES_BYTES:
        merged *= 2
    wide = merged * cols
    packed_rows = -(-(pcs + 1) // 8) * 8

    arguments = (coupling, src_pcs, tgt_pcs, src_mass.reshape(1, -1), tgt_mass.reshape(1, -1))
    half, whole, moment = pl.pallas_call(
        front_kernel,
        out_shape=(
            pltpu.VMEM((packed_rows, rows // 2), f32),
            pltpu.VMEM((packed_rows, cols), f32),
            pltpu.VMEM((8, 4 * LANES), f32),
        ),
        in_specs=[pl.BlockSpec(memory_space=pltpu.HBM)] * 5,
        out_specs=(VMEM,) * 3,
        scratch_shapes=[pltpu.VMEM(a.shape, a.dtype) for a in arguments]
        + [pltpu.SemaphoreType.DMA((5,))],
        compiler_params=params(8),
    )(*[pltpu.with_memory_space_constraint(a, pltpu.HBM) for a in arguments])

    moment = moment + swap(moment, "tgt", 1)
    half, whole, moment = lax.optimization_barrier((half, whole, moment))
    parts, targets = [moment], [whole]
    if merged > 1:
        message = jnp.concatenate([whole, moment], axis=0)
        targets += [swap(message, "tgt", 2 * b) for b in range(1, merged)]
        parts += [target[packed_rows:] for target in targets[1:]]
    sources = [half] + [swap(half, "src", b) for b in range(1, src_size)]
    parts, sources, targets = lax.optimization_barrier((parts, sources, targets))
    if 2 * merged < tgt_size:
        parts = staged_parts(tree(parts, jnp.add), "tgt", 2 * merged, 4)
    moments = staged_parts(tree(parts, jnp.add), "src", 1, 4)
    near = jnp.concatenate(sources, axis=0)
    far = swap(near, "tgt", 1)

    src_all, turned, log_src, log_tgt, log_tgt_line = pl.pallas_call(
        functools.partial(prepare_kernel, pcs, src_size, merged),
        out_shape=(
            jax.ShapeDtypeStruct((4 * DEPTH, total_rows), jnp.bfloat16),
            jax.ShapeDtypeStruct((wide, LANES), jnp.bfloat16),
            jax.ShapeDtypeStruct((1, total_rows), f32),
            jax.ShapeDtypeStruct((wide, LANES), f32),
            jax.ShapeDtypeStruct((1, wide), f32),
        ),
        in_specs=[VMEM] * (2 + merged),
        out_specs=(VMEM,) * 5,
        compiler_params=params(10),
    )(near, far, *targets)
    weights = pl.pallas_call(
        functools.partial(start_kernel, pcs, total_rows * total_cols),
        out_shape=jax.ShapeDtypeStruct((wide, 4 * DEPTH), jnp.bfloat16),
        in_specs=[VMEM] * (1 + len(moments)),
        out_specs=VMEM,
        compiler_params=params(10),
    )(turned, *moments)
    scores = jnp.dot(weights, src_all, preferred_element_type=f32)
    sums = pl.pallas_call(
        rows_running,
        out_shape=jax.ShapeDtypeStruct((1, total_rows), f32),
        in_specs=[VMEM],
        out_specs=VMEM,
        compiler_params=params(10),
    )(scores)

    def both(value):
        offset = 2 * merged
        while offset < tgt_size:
            value = logsum(value, swap(value, "tgt", offset))
            offset *= 2
        return value, swap(value, "tgt", 1)

    bf16, block = jnp.bfloat16, (wide, total_rows)

    def call(kernel, sums, extra, outs, scratch):
        return pl.pallas_call(
            kernel,
            out_shape=tuple(jax.ShapeDtypeStruct(shape, bf16 if shape == block else f32) for shape in outs),
            in_specs=[VMEM] * (6 + len(extra)),
            out_specs=(VMEM,) * len(outs),
            scratch_shapes=[pltpu.VMEM(shape, f32) for shape in scratch],
            compiler_params=params(10),
        )(scores, *both(sums), log_src, log_tgt, log_tgt_line, *extra)

    line, lines, pads = (1, total_rows), (8, total_rows), (wide, LANES)
    side, columns = (1, wide), (lines, pads, pads, pads)
    sums, *kept_rows = call(first_kernel, sums, (), (line, block, lines, side), columns)
    sums, *kept_columns = call(
        second_kernel, sums, kept_rows, (line, block, side, line), (*columns, side, lines, pads)
    )
    for iteration in range(ITERS - 3):
        (sums,) = call(
            later_kernel, sums, (*kept_rows, *kept_columns), (line,), (*columns, side, lines)
        )
    pads, side = (cols, LANES), (1, cols)
    log_coupling, row_potential, col_potential = call(
        functools.partial(last_kernel, merged), sums, kept_columns,
        ((rows, cols), (1, rows), side), (lines, pads, pads, pads, side, line),
    )
    return log_coupling, row_potential.reshape(-1), col_potential.reshape(-1)


def solution(mesh):
    in_specs = (P("src", "tgt"), P(None, "src"), P(None, "tgt"), P("src"), P("tgt"))
    out_specs = (P("src", "tgt"), P("src"), P("tgt"))
    return jax.shard_map(shards, mesh=mesh, in_specs=in_specs, out_specs=out_specs, check_vma=False)
```

```python
import functools
import math

import jax
import jax.numpy as jnp
from jax import lax
from jax.experimental import pallas as pl
from jax.experimental.pallas import tpu as pltpu
from jax.sharding import PartitionSpec as P

ITERS = 4

eps_reg = 0.5
marg_power = 1.0 / (1.0 + eps_reg)
tiny_eps = 1e-06

LANES = 128
DEPTH = 64
LN2 = math.log(2.0)
SCORES_BYTES = 1 << 24
LIFT = 54.0
FAINT = 2.0**-60
SAMPLE = 4
SPAN = 145.0
VMEM = pl.BlockSpec(memory_space=pltpu.VMEM)


def params(mib):
    return pltpu.CompilerParams(vmem_limit_bytes=mib << 20)


def tree(values, combine):
    values = list(values)
    while len(values) > 1:
        paired = [combine(values[i], values[i + 1]) for i in range(0, len(values) - 1, 2)]
        values = paired + ([values[-1]] if len(values) % 2 else [])
    return values[0]


def pieces(value):
    high = value.astype(jnp.bfloat16)
    rest = value - high.astype(jnp.float32)
    middle = rest.astype(jnp.bfloat16)
    low = (rest - middle.astype(jnp.float32)).astype(jnp.bfloat16)
    return high, middle, low


def padded(value):
    return jnp.concatenate(
        [value, jnp.zeros((DEPTH - value.shape[0], value.shape[1]), value.dtype)], axis=0
    )


def front_kernel(*refs):
    sources, (half_ref, whole_ref, moment_ref), local, sems = refs[:5], refs[5:8], refs[8:13], refs[13]
    copies = [pltpu.make_async_copy(a, b, sems.at[i]) for i, (a, b) in enumerate(zip(sources, local))]
    for copy in copies:
        copy.start()
    coupling_ref, src_ref, tgt_ref, src_mass_ref, tgt_mass_ref = local
    pcs = src_ref.shape[0]
    half = half_ref.shape[1]
    odd = lax.rem(lax.axis_index("tgt"), 2)
    for copy in copies[1:]:
        copy.wait()
    src = src_ref[...].astype(jnp.float32)
    tgt = tgt_ref[...].astype(jnp.float32)
    below = jnp.zeros((half_ref.shape[0] - pcs - 1, 2 * half), jnp.float32)
    joined = jnp.concatenate([src, jnp.log2(src_mass_ref[...]), below], axis=0)
    half_ref[...] = jnp.where(odd == 0, joined[:, :half], joined[:, half:])
    below = jnp.zeros((half_ref.shape[0] - pcs - 1, tgt.shape[1]), jnp.float32)
    whole_ref[...] = jnp.concatenate([tgt, jnp.log2(tgt_mass_ref[...]), below], axis=0)
    src = padded(src).astype(jnp.bfloat16)
    tgt = padded(tgt).astype(jnp.bfloat16)
    twice = jnp.concatenate([src, src], axis=0)
    copies[0].wait()
    panel = jnp.dot(twice, coupling_ref[...], preferred_element_type=jnp.float32)
    moment = sum(
        lax.dot_general(tgt, part, (((1,), (1,)), ((), ())), preferred_element_type=jnp.float32)
        for part in pieces(panel)
    )
    lane = lax.broadcasted_iota(jnp.int32, (DEPTH // 2, LANES), 1)
    moment = jnp.where(lane < DEPTH, moment[: DEPTH // 2], moment[DEPTH // 2 :])
    for i in range(4):
        moment_ref[:, i * LANES : (i + 1) * LANES] = moment[i * 8 : i * 8 + 8]


def prepare_kernel(pcs, blocks, merged, near_ref, far_ref, *refs):
    tgt_refs, (src_ref, turned_ref, log_src_ref, log_tgt_ref, line_ref) = refs[:merged], refs[merged:]
    packed_rows = near_ref.shape[0] // blocks
    half = near_ref.shape[1]
    width = tgt_refs[0].shape[1]
    z = lax.axis_index("src")
    t = lax.axis_index("tgt")
    odd = lax.rem(t, 2)
    total_rows = 2 * half * blocks
    total_cols = width * lax.axis_size("tgt")
    for b in range(blocks):
        place = jnp.bitwise_xor(z, b)
        for ref, side in ((near_ref, odd), (far_ref, 1 - odd)):
            block = ref[pl.ds(b * packed_rows, packed_rows), :]
            lanes = pl.ds(pl.multiple_of((place * 2 + side) * half, half), half)
            log_src_ref[:, lanes] = marg_power * (block[pcs : pcs + 1] + math.log2(total_cols))
            block = padded(block).astype(jnp.bfloat16)
            for copy in range(4):
                src_ref[pl.ds(copy * DEPTH, DEPTH), lanes] = block
    mine = lax.rem(lax.div(t, 2), merged)
    for b in range(merged):
        base = pl.multiple_of(jnp.bitwise_xor(mine, b) * width, width)
        block = padded(tgt_refs[b][:packed_rows, :])
        line_ref[:, pl.ds(base, width)] = marg_power * (block[pcs : pcs + 1] + math.log2(total_rows))
        turned = jnp.concatenate([block, block], axis=0).T
        log_tgt_ref[pl.ds(base, width), :] = jnp.broadcast_to(
            marg_power * (turned[:, pcs : pcs + 1] + math.log2(total_rows)), (width, LANES)
        )
        turned_ref[pl.ds(base, width), :] = turned.astype(jnp.bfloat16)


def start_kernel(pcs, entries, turned_ref, *refs):
    moment_refs, weights = refs[:-1], refs[-1]
    packed = tree([ref[...] for ref in moment_refs], jnp.add) * entries ** (-0.5)
    spread = jnp.sqrt(jnp.sum(packed * packed) * (1.0 / (pcs * pcs)) + tiny_eps)
    packed = packed / spread * (2.0 / (eps_reg * pcs) / LN2)
    packed = jnp.concatenate([packed[:, i * LANES : (i + 1) * LANES] for i in range(4)], axis=0)
    turned = pltpu.roll(packed, DEPTH, axis=1)
    left = lax.broadcasted_iota(jnp.int32, packed.shape, 1) < DEPTH
    normed = jnp.concatenate(
        [jnp.where(left, packed, turned), jnp.where(left, turned, packed)], axis=0
    )
    high, middle, low = pieces(normed)
    upper = jnp.concatenate([high, middle], axis=0)
    lower = jnp.concatenate([low, jnp.zeros_like(low)], axis=0)

    width = min(512, turned_ref.shape[0])
    first = lax.broadcasted_iota(jnp.int32, (width, LANES), 1) < DEPTH
    for base in range(0, turned_ref.shape[0], width):
        at = pl.ds(base, width)
        weighted = sum(
            jnp.dot(turned_ref[at, :], part, preferred_element_type=jnp.float32)
            for part in (upper, lower)
        )
        high, middle, low = pieces(weighted)
        weights[at, :LANES] = jnp.where(first, high, middle)
        weights[at, LANES:] = jnp.where(first, low, jnp.zeros_like(low))


def down(highest, summed):
    top = jnp.max(highest, axis=0, keepdims=True)
    return top + jnp.log2(jnp.sum(summed * jnp.exp2(highest - top), axis=0, keepdims=True))


def logsum(one, other):
    top = jnp.maximum(one, other)
    return top + jnp.log2(jnp.exp2(one - top) + jnp.exp2(other - top))


def row_values(log_src_ref, sums_ref, more_ref):
    return log_src_ref[...] - marg_power * logsum(sums_ref[...], more_ref[...])


def lane_tiles(ref):
    return [pl.ds(j, LANES) for j in range(0, ref.shape[1], LANES)]


def halves(low):
    low = pl.multiple_of(low, 16)
    return pl.ds(low, 16), [pl.ds(low, 8), pl.ds(pl.multiple_of(low + 8, 8), 8)]


def running(highest, summed, terms):
    fresh = jnp.maximum(highest, tree(terms, jnp.maximum))
    total = tree([jnp.exp2(term - fresh) for term in terms], jnp.add)
    return fresh, summed * jnp.exp2(highest - fresh) + total


def columns_running(scores_ref, rows_ref, top_ref, sum_ref, base, count):
    tiles = lane_tiles(scores_ref)
    span = min(16, len(tiles))

    def scan(i, carry):
        for u in range(4):
            low = pl.multiple_of((i * 4 + u) * 8, 8)
            at = pl.ds(pl.multiple_of(base + low, 8), 8)
            state = None
            for start in range(0, len(tiles), span):
                terms = [scores_ref[at, lanes] + rows_ref[:, lanes] for lanes in tiles[start : start + span]]
                if state is None:
                    highest = tree(terms, jnp.maximum)
                    state = highest, tree([jnp.exp2(term - highest) for term in terms], jnp.add)
                else:
                    state = running(*state, terms)
            top_ref[pl.ds(low, 8), :], sum_ref[pl.ds(low, 8), :] = state
        return carry

    lax.fori_loop(0, count // 32, scan, 0)


def rows_running(scores_ref, out_ref):
    count, total = scores_ref.shape
    beside, deep = 8, 16
    unset = (jnp.full((8, LANES), -jnp.inf, jnp.float32), jnp.zeros((8, LANES), jnp.float32))
    for start in range(0, total, beside * LANES):
        tiles = [pl.ds(start + j * LANES, LANES) for j in range(beside)]

        def step(i, carry, tiles=tiles):
            ats = [pl.ds(pl.multiple_of((i * deep + g) * 8, 8), 8) for g in range(deep)]
            return tuple(
                running(*state, [scores_ref[at, lanes] for at in ats])
                for state, lanes in zip(carry, tiles)
            )

        carry = lax.fori_loop(0, count // (8 * deep), step, (unset,) * beside)
        for lanes, state in zip(tiles, carry):
            out_ref[:, lanes] = down(*state)


def columns_exp(scores_ref, rows_ref, top_ref, sum_ref, exact_ref, rounded_ref, count, keep_ref):
    tiles = lane_tiles(scores_ref)

    def highest(i, carry):
        places = [pl.ds(pl.multiple_of(i * 64 + g * 8, 8), 8) for g in range(8)]
        tops = [None] * 8
        for lanes in tiles:
            row = rows_ref[:, lanes]
            for g, place in enumerate(places):
                term = scores_ref[place, lanes] + row
                tops[g] = term if tops[g] is None else jnp.maximum(tops[g], term)
        for place, top in zip(places, tops):
            top_ref[place, :] = top - LIFT
        return carry

    def total(i, carry):
        pairs = [halves(i * 64 + g * 16) for g in range(4)]
        places = [place for _, pair in pairs for place in pair]
        tops = [top_ref[place, :] for place in places]
        sums = [jnp.zeros((8, LANES), jnp.float32)] * 8
        exact = [jnp.zeros((8, LANES), jnp.float32)] * 8
        rounded = [jnp.zeros((8, LANES), jnp.float32)] * 8
        for j, lanes in enumerate(tiles):
            row = rows_ref[:, lanes]
            for g, (at, sources) in enumerate(pairs):
                parts = [
                    jnp.exp2(scores_ref[source, lanes] + row - tops[2 * g + h])
                    for h, source in enumerate(sources)
                ]
                kept = jnp.concatenate(parts, axis=0).astype(keep_ref.dtype)
                keep_ref[at, lanes] = kept
                for h in range(2):
                    sums[2 * g + h] = sums[2 * g + h] + parts[h]
                if j % SAMPLE == 0:
                    kept = kept.astype(jnp.float32)
                    for h in range(2):
                        exact[2 * g + h] = exact[2 * g + h] + parts[h]
                        rounded[2 * g + h] = rounded[2 * g + h] + kept[8 * h : 8 * h + 8]
        for place, value, before, after in zip(places, sums, exact, rounded):
            sum_ref[place, :] = value
            exact_ref[place, :] = before
            rounded_ref[place, :] = after
        return carry

    lax.fori_loop(0, count // 64, highest, 0)
    tops = top_ref[...]
    top_ref[...] = jnp.broadcast_to(jnp.max(tops, axis=1, keepdims=True), tops.shape)
    lax.fori_loop(0, count // 64, total, 0)


def split_rows(line):
    row = lax.broadcasted_iota(jnp.int32, (16, line.shape[1]), 0)
    high, middle, low = (part.astype(jnp.float32) for part in pieces(line))
    spread = jnp.where(row == 0, high, jnp.where(row == 1, middle, jnp.where(row == 2, low, 0.0)))
    return spread.astype(jnp.bfloat16)


def split_rows(line):
    row = lax.broadcasted_iota(jnp.int32, (16, line.shape[1]), 0)
    high, middle, low = (part.astype(jnp.float32) for part in pieces(line))
    spread = jnp.where(row == 0, high, jnp.where(row == 1, middle, jnp.where(row == 2, low, 0.0)))
    return spread.astype(jnp.bfloat16)


def columns_product(keep_ref, kept_top_ref, factor, shift, log_tgt_line_ref, line_ref, base, count):
    factors = split_rows(factor)
    part = min(count, 512)
    for low in range(0, count, part):
        at = pl.ds(pl.multiple_of(base + low, part), part)
        sums = lax.dot_general(
            factors, keep_ref[at, :], (((1,), (1,)), ((), ())), preferred_element_type=jnp.float32
        )
        logs = kept_top_ref[:, at] + (shift - LIFT) + jnp.log2(jnp.sum(sums, axis=0, keepdims=True))
        line_ref[:, pl.ds(low, part)] = log_tgt_line_ref[:, at] - marg_power * logs


def columns_finish(top_ref, sum_ref, log_tgt_ref, cols_ref, base, count):
    part = min(count, 2048)
    for low in range(0, count, part):
        here = pl.ds(low, part)
        tops = top_ref[here, :]
        top = jnp.max(tops, axis=1, keepdims=True)
        total = jnp.sum(sum_ref[here, :] * jnp.exp2(tops - top), axis=1, keepdims=True)
        at = pl.ds(pl.multiple_of(base + low, part), part)
        cols_ref[here, :] = log_tgt_ref[at, :] - marg_power * (top + jnp.log2(total))


BESIDE, DEEP = 8, 4


def over_tiles(count, width, body, first, done):
    for start in range(0, width, BESIDE * LANES):
        tiles = [pl.ds(start + j * LANES, LANES) for j in range(BESIDE)]

        def step(i, carry, tiles=tiles):
            carry = list(carry)
            body([halves((i * DEEP + g) * 16) for g in range(DEEP)], tiles, carry)
            return tuple(carry)

        state = lax.fori_loop(0, count // (16 * DEEP), step, tuple(first for _ in tiles))
        for lanes, value in zip(tiles, state):
            done(lanes, value)


def rows_highest(scores_ref, cols_ref, top_ref):
    def body(pairs, tiles, carry):
        for _, places in pairs:
            for place in places:
                if cols_ref is not None:
                    potential = cols_ref[place, :]
                for j, lanes in enumerate(tiles):
                    term = scores_ref[place, lanes]
                    if cols_ref is not None:
                        term = term + potential
                    carry[j] = jnp.maximum(carry[j], term)

    def done(lanes, value):
        top_ref[:, lanes] = jnp.broadcast_to(jnp.max(value, axis=0, keepdims=True), value.shape) - LIFT

    over_tiles(*scores_ref.shape, body, jnp.full((8, LANES), -jnp.inf, jnp.float32), done)


def rows_exp(scores_ref, cols_ref, top_ref, out_ref, keep_ref, level_ref):
    def body(pairs, tiles, carry):
        tops = [top_ref[:, lanes] for lanes in tiles]
        for g, (at, places) in enumerate(pairs):
            potentials = [cols_ref[place, :] for place in places]
            for j, lanes in enumerate(tiles):
                terms = [scores_ref[place, lanes] + c for place, c in zip(places, potentials)]
                parts = [jnp.exp2(term - tops[j]) for term in terms]
                summed, exact, rounded = carry[j]
                both = parts[0] + parts[1]
                if keep_ref is not None:
                    kept = jnp.concatenate(parts, axis=0).astype(keep_ref.dtype)
                    keep_ref[at, lanes] = kept
                    if g % SAMPLE == 0:
                        kept = kept.astype(jnp.float32)
                        exact, rounded = exact + both, rounded + (kept[:8] + kept[8:])
                carry[j] = summed + both, exact, rounded

    def done(lanes, value):
        out_ref[:, lanes] = down(top_ref[:, lanes], value[0])
        if keep_ref is not None:
            exact, rounded = (jnp.sum(part, axis=0, keepdims=True) + FAINT for part in value[1:])
            level_ref[:, lanes] = top_ref[:, lanes] + jnp.log2(exact / rounded)

    zero = jnp.zeros((8, LANES), jnp.float32)
    over_tiles(*scores_ref.shape, body, (zero, zero, zero), done)


def rows_product(keep_ref, kept_top_ref, factor, shift, out_ref):
    factors = split_rows(factor)
    chunk = 512
    for start in range(0, keep_ref.shape[1], chunk):
        lanes = pl.ds(start, chunk)
        sums = jnp.dot(factors, keep_ref[:, lanes], preferred_element_type=jnp.float32)
        out_ref[:, lanes] = (
            kept_top_ref[0:1, lanes] + (shift - LIFT) + jnp.log2(jnp.sum(sums, axis=0, keepdims=True))
        )


def columns_either(rows, shared, kept, line_ref, scratch, base, count):
    scores_ref, log_tgt_ref, log_tgt_line_ref = shared
    keep_ref, kept_top_ref, kept_rows_ref = kept
    rows_ref, cols_ref, top_ref, sum_ref = scratch
    change = rows - kept_rows_ref[...]
    shift = jnp.max(change)
    near = shift - jnp.min(change) <= SPAN

    @pl.when(near)
    def _():
        factor = jnp.exp2(change - (shift - LIFT))
        columns_product(keep_ref, kept_top_ref, factor, shift, log_tgt_line_ref, line_ref, base, count)

    @pl.when(jnp.logical_not(near))
    def _():
        rows_ref[...] = jnp.broadcast_to(rows, rows_ref.shape)
        columns_running(scores_ref, rows_ref, top_ref, sum_ref, base, count)
        columns_finish(top_ref, sum_ref, log_tgt_ref, cols_ref, base, count)
        line_ref[...] = cols_ref[...].T[0:1, :]


def rows_either(scores_ref, line_ref, kept, cols_ref, row_top_ref, out_ref):
    keep_ref, kept_top_ref, kept_line_ref = kept
    change = line_ref[...] - kept_line_ref[...]
    shift = jnp.max(change)
    near = shift - jnp.min(change) <= SPAN

    @pl.when(near)
    def _():
        rows_product(keep_ref, kept_top_ref, jnp.exp2(change - (shift - LIFT)), shift, out_ref)

    @pl.when(jnp.logical_not(near))
    def _():
        cols_ref[...] = jnp.broadcast_to(line_ref[...], (LANES, line_ref.shape[1])).T
        rows_highest(scores_ref, cols_ref, row_top_ref)
        rows_exp(scores_ref, cols_ref, row_top_ref, out_ref, None, None)


def first_kernel(scores_ref, sums_ref, more_ref, log_src_ref, log_tgt_ref, log_tgt_line_ref, *refs):
    out_ref, keep_ref, row_top_ref, line_ref = refs[:4]
    rows_ref, cols_ref, top_ref, sum_ref = refs[4:]
    rows_ref[...] = jnp.broadcast_to(row_values(log_src_ref, sums_ref, more_ref), rows_ref.shape)
    count = scores_ref.shape[0]
    columns_running(scores_ref, rows_ref, top_ref, sum_ref, 0, count)
    columns_finish(top_ref, sum_ref, log_tgt_ref, cols_ref, 0, count)
    line_ref[...] = cols_ref[...].T[0:1, :]
    rows_highest(scores_ref, cols_ref, row_top_ref)
    rows_exp(scores_ref, cols_ref, row_top_ref, out_ref, keep_ref, row_top_ref)


def second_kernel(scores_ref, sums_ref, more_ref, log_src_ref, log_tgt_ref, log_tgt_line_ref, *refs):
    kept, (out_ref, keep_ref, kept_top_ref, base_ref) = refs[:3], refs[3:7]
    rows_ref, cols_ref, top_ref, sum_ref, line_ref, row_top_ref, rounded_ref, exact_ref = refs[7:]
    base_ref[...] = row_values(log_src_ref, sums_ref, more_ref)
    rows_ref[...] = jnp.broadcast_to(base_ref[...], rows_ref.shape)
    count = scores_ref.shape[0]
    columns_exp(scores_ref, rows_ref, top_ref, sum_ref, exact_ref, rounded_ref, count, keep_ref)
    columns_finish(top_ref, sum_ref, log_tgt_ref, cols_ref, 0, count)
    exact = jnp.sum(exact_ref[...], axis=1, keepdims=True)
    rounded = jnp.sum(rounded_ref[...], axis=1, keepdims=True)
    level = top_ref[...] + jnp.log2((exact + FAINT) / (rounded + FAINT))
    kept_top_ref[...] = level.T[0:1, :]
    line_ref[...] = cols_ref[...].T[0:1, :]
    rows_either(scores_ref, line_ref, kept, cols_ref, row_top_ref, out_ref)


def later_kernel(scores_ref, sums_ref, more_ref, log_src_ref, log_tgt_ref, log_tgt_line_ref, *refs):
    kept, kept_columns, out_ref = refs[:3], refs[3:6], refs[6]
    scratch, line_ref, row_top_ref = refs[7:11], refs[11], refs[12]
    rows = row_values(log_src_ref, sums_ref, more_ref)
    shared = scores_ref, log_tgt_ref, log_tgt_line_ref
    columns_either(rows, shared, kept_columns, line_ref, scratch, 0, scores_ref.shape[0])
    rows_either(scores_ref, line_ref, kept, scratch[1], row_top_ref, out_ref)


def last_kernel(merged, scores_ref, sums_ref, more_ref, log_src_ref, log_tgt_ref, log_tgt_line_ref, *refs):
    kept_columns, (out_ref, row_ref, col_ref) = refs[:3], refs[3:6]
    scratch, line_ref, values_ref = refs[6:10], refs[10], refs[11]
    own_rows, own_cols = out_ref.shape
    rows = row_values(log_src_ref, sums_ref, more_ref)
    values_ref[...] = rows
    base = pl.multiple_of(lax.rem(lax.div(lax.axis_index("tgt"), 2), merged) * own_cols, own_cols)
    lanes = pl.ds(pl.multiple_of(lax.axis_index("src") * own_rows, own_rows), own_rows)
    shared = scores_ref, log_tgt_ref, log_tgt_line_ref
    columns_either(rows, shared, kept_columns, line_ref, scratch, base, own_cols)
    row_ref[...] = values_ref[:, lanes] * LN2
    col_ref[...] = line_ref[...] * LN2
    block = scores_ref[pl.ds(base, own_cols), lanes] + values_ref[:, lanes]
    out_ref[...] = (block.T + line_ref[...]) * LN2


def swap(value, axis, offset):
    return lax.ppermute(value, axis, [(i, i ^ offset) for i in range(lax.axis_size(axis))])


def staged_parts(value, axis, low, width):
    size = lax.axis_size(axis)
    terms = [value]
    while low < size:
        span = min(width, size // low)
        value = tree(terms, jnp.add)
        terms = [value] + [swap(value, axis, low * j) for j in range(1, span)]
        low *= span
    return terms


def shards(coupling, src_pcs, tgt_pcs, src_mass, tgt_mass):
    f32 = jnp.float32
    pcs = src_pcs.shape[0]
    rows, cols = coupling.shape
    src_size, tgt_size = lax.axis_size("src"), lax.axis_size("tgt")
    total_rows, total_cols = rows * src_size, cols * tgt_size
    merged = 1
    while 2 * merged * 2 <= tgt_size and 2 * merged * cols * total_rows * 4 <= SCORES_BYTES:
        merged *= 2
    wide = merged * cols
    packed_rows = -(-(pcs + 1) // 8) * 8

    arguments = (coupling, src_pcs, tgt_pcs, src_mass.reshape(1, -1), tgt_mass.reshape(1, -1))
    half, whole, moment = pl.pallas_call(
        front_kernel,
        out_shape=(
            pltpu.VMEM((packed_rows, rows // 2), f32),
            pltpu.VMEM((packed_rows, cols), f32),
            pltpu.VMEM((8, 4 * LANES), f32),
        ),
        in_specs=[pl.BlockSpec(memory_space=pltpu.HBM)] * 5,
        out_specs=(VMEM,) * 3,
        scratch_shapes=[pltpu.VMEM(a.shape, a.dtype) for a in arguments]
        + [pltpu.SemaphoreType.DMA((5,))],
        compiler_params=params(8),
    )(*[pltpu.with_memory_space_constraint(a, pltpu.HBM) for a in arguments])

    moment = moment + swap(moment, "tgt", 1)
    half, whole, moment = lax.optimization_barrier((half, whole, moment))
    parts, targets = [moment], [whole]
    if merged > 1:
        message = jnp.concatenate([whole, moment], axis=0)
        targets += [swap(message, "tgt", 2 * b) for b in range(1, merged)]
        parts += [target[packed_rows:] for target in targets[1:]]
    sources = [half] + [swap(half, "src", b) for b in range(1, src_size)]
    parts, sources, targets = lax.optimization_barrier((parts, sources, targets))
    if 2 * merged < tgt_size:
        parts = staged_parts(tree(parts, jnp.add), "tgt", 2 * merged, 4)
    moments = staged_parts(tree(parts, jnp.add), "src", 1, 4)
    near = jnp.concatenate(sources, axis=0)
    far = swap(near, "tgt", 1)

    src_all, turned, log_src, log_tgt, log_tgt_line = pl.pallas_call(
        functools.partial(prepare_kernel, pcs, src_size, merged),
        out_shape=(
            jax.ShapeDtypeStruct((4 * DEPTH, total_rows), jnp.bfloat16),
            jax.ShapeDtypeStruct((wide, LANES), jnp.bfloat16),
            jax.ShapeDtypeStruct((1, total_rows), f32),
            jax.ShapeDtypeStruct((wide, LANES), f32),
            jax.ShapeDtypeStruct((1, wide), f32),
        ),
        in_specs=[VMEM] * (2 + merged),
        out_specs=(VMEM,) * 5,
        compiler_params=params(10),
    )(near, far, *targets)
    weights = pl.pallas_call(
        functools.partial(start_kernel, pcs, total_rows * total_cols),
        out_shape=jax.ShapeDtypeStruct((wide, 4 * DEPTH), jnp.bfloat16),
        in_specs=[VMEM] * (1 + len(moments)),
        out_specs=VMEM,
        compiler_params=params(10),
    )(turned, *moments)
    scores = jnp.dot(weights, src_all, preferred_element_type=f32)
    sums = pl.pallas_call(
        rows_running,
        out_shape=jax.ShapeDtypeStruct((1, total_rows), f32),
        in_specs=[VMEM],
        out_specs=VMEM,
        compiler_params=params(10),
    )(scores)

    def both(value):
        offset = 2 * merged
        while offset < tgt_size:
            value = logsum(value, swap(value, "tgt", offset))
            offset *= 2
        return value, swap(value, "tgt", 1)

    bf16, block = jnp.bfloat16, (wide, total_rows)

    def call(kernel, sums, extra, outs, scratch):
        return pl.pallas_call(
            kernel,
            out_shape=tuple(jax.ShapeDtypeStruct(shape, bf16 if shape == block else f32) for shape in outs),
            in_specs=[VMEM] * (6 + len(extra)),
            out_specs=(VMEM,) * len(outs),
            scratch_shapes=[pltpu.VMEM(shape, f32) for shape in scratch],
            compiler_params=params(10),
        )(scores, *both(sums), log_src, log_tgt, log_tgt_line, *extra)

    line, lines, pads = (1, total_rows), (8, total_rows), (wide, LANES)
    side, columns = (1, wide), (lines, pads, pads, pads)
    sums, *kept_rows = call(first_kernel, sums, (), (line, block, lines, side), columns)
    sums, *kept_columns = call(
        second_kernel, sums, kept_rows, (line, block, side, line), (*columns, side, lines, pads, pads)
    )
    for iteration in range(ITERS - 3):
        (sums,) = call(
            later_kernel, sums, (*kept_rows, *kept_columns), (line,), (*columns, side, lines)
        )
    pads, side = (cols, LANES), (1, cols)
    log_coupling, row_potential, col_potential = call(
        functools.partial(last_kernel, merged), sums, kept_columns,
        ((rows, cols), (1, rows), side), (lines, pads, pads, pads, side, line),
    )
    return log_coupling, row_potential.reshape(-1), col_potential.reshape(-1)


def solution(mesh):
    in_specs = (P("src", "tgt"), P(None, "src"), P(None, "tgt"), P("src"), P("tgt"))
    out_specs = (P("src", "tgt"), P("src"), P("tgt"))
    return jax.shard_map(shards, mesh=mesh, in_specs=in_specs, out_specs=out_specs, check_vma=False)
```

```python
import functools
import math

import jax
import jax.numpy as jnp
from jax import lax
from jax.experimental import pallas as pl
from jax.experimental.pallas import tpu as pltpu
from jax.sharding import PartitionSpec as P

ITERS = 4

eps_reg = 0.5
marg_power = 1.0 / (1.0 + eps_reg)
tiny_eps = 1e-06

LANES = 128
DEPTH = 64
LN2 = math.log(2.0)
SCORES_BYTES = 1 << 24
LIFT = 54.0
SPAN = 145.0
VMEM = pl.BlockSpec(memory_space=pltpu.VMEM)


def params(mib):
    return pltpu.CompilerParams(vmem_limit_bytes=mib << 20)


def tree(values, combine):
    values = list(values)
    while len(values) > 1:
        paired = [combine(values[i], values[i + 1]) for i in range(0, len(values) - 1, 2)]
        values = paired + ([values[-1]] if len(values) % 2 else [])
    return values[0]


def pieces(value):
    high = value.astype(jnp.bfloat16)
    rest = value - high.astype(jnp.float32)
    middle = rest.astype(jnp.bfloat16)
    low = (rest - middle.astype(jnp.float32)).astype(jnp.bfloat16)
    return high, middle, low


def padded(value):
    return jnp.concatenate(
        [value, jnp.zeros((DEPTH - value.shape[0], value.shape[1]), value.dtype)], axis=0
    )


def front_kernel(*refs):
    sources, (half_ref, whole_ref, moment_ref), local, sems = refs[:5], refs[5:8], refs[8:13], refs[13]
    copies = [pltpu.make_async_copy(a, b, sems.at[i]) for i, (a, b) in enumerate(zip(sources, local))]
    for copy in copies:
        copy.start()
    coupling_ref, src_ref, tgt_ref, src_mass_ref, tgt_mass_ref = local
    pcs = src_ref.shape[0]
    half = half_ref.shape[1]
    odd = lax.rem(lax.axis_index("tgt"), 2)
    for copy in copies[1:]:
        copy.wait()
    src = src_ref[...].astype(jnp.float32)
    tgt = tgt_ref[...].astype(jnp.float32)
    below = jnp.zeros((half_ref.shape[0] - pcs - 1, 2 * half), jnp.float32)
    joined = jnp.concatenate([src, jnp.log2(src_mass_ref[...]), below], axis=0)
    half_ref[...] = jnp.where(odd == 0, joined[:, :half], joined[:, half:])
    below = jnp.zeros((half_ref.shape[0] - pcs - 1, tgt.shape[1]), jnp.float32)
    whole_ref[...] = jnp.concatenate([tgt, jnp.log2(tgt_mass_ref[...]), below], axis=0)
    src = padded(src).astype(jnp.bfloat16)
    tgt = padded(tgt).astype(jnp.bfloat16)
    twice = jnp.concatenate([src, src], axis=0)
    copies[0].wait()
    panel = jnp.dot(twice, coupling_ref[...], preferred_element_type=jnp.float32)
    moment = sum(
        lax.dot_general(tgt, part, (((1,), (1,)), ((), ())), preferred_element_type=jnp.float32)
        for part in pieces(panel)
    )
    lane = lax.broadcasted_iota(jnp.int32, (DEPTH // 2, LANES), 1)
    moment = jnp.where(lane < DEPTH, moment[: DEPTH // 2], moment[DEPTH // 2 :])
    for i in range(4):
        moment_ref[:, i * LANES : (i + 1) * LANES] = moment[i * 8 : i * 8 + 8]


def prepare_kernel(pcs, blocks, merged, near_ref, far_ref, *refs):
    tgt_refs, (src_ref, turned_ref, log_src_ref, log_tgt_ref, line_ref) = refs[:merged], refs[merged:]
    packed_rows = near_ref.shape[0] // blocks
    half = near_ref.shape[1]
    width = tgt_refs[0].shape[1]
    z = lax.axis_index("src")
    t = lax.axis_index("tgt")
    odd = lax.rem(t, 2)
    total_rows = 2 * half * blocks
    total_cols = width * lax.axis_size("tgt")
    for b in range(blocks):
        place = jnp.bitwise_xor(z, b)
        for ref, side in ((near_ref, odd), (far_ref, 1 - odd)):
            block = ref[pl.ds(b * packed_rows, packed_rows), :]
            lanes = pl.ds(pl.multiple_of((place * 2 + side) * half, half), half)
            log_src_ref[:, lanes] = marg_power * (block[pcs : pcs + 1] + math.log2(total_cols))
            block = padded(block).astype(jnp.bfloat16)
            for copy in range(4):
                src_ref[pl.ds(copy * DEPTH, DEPTH), lanes] = block
    mine = lax.rem(lax.div(t, 2), merged)
    for b in range(merged):
        base = pl.multiple_of(jnp.bitwise_xor(mine, b) * width, width)
        block = padded(tgt_refs[b][:packed_rows, :])
        line_ref[:, pl.ds(base, width)] = marg_power * (block[pcs : pcs + 1] + math.log2(total_rows))
        turned = jnp.concatenate([block, block], axis=0).T
        log_tgt_ref[pl.ds(base, width), :] = jnp.broadcast_to(
            marg_power * (turned[:, pcs : pcs + 1] + math.log2(total_rows)), (width, LANES)
        )
        turned_ref[pl.ds(base, width), :] = turned.astype(jnp.bfloat16)


def start_kernel(pcs, entries, turned_ref, *refs):
    moment_refs, weights = refs[:-1], refs[-1]
    packed = tree([ref[...] for ref in moment_refs], jnp.add) * entries ** (-0.5)
    spread = jnp.sqrt(jnp.sum(packed * packed) * (1.0 / (pcs * pcs)) + tiny_eps)
    packed = packed / spread * (2.0 / (eps_reg * pcs) / LN2)
    packed = jnp.concatenate([packed[:, i * LANES : (i + 1) * LANES] for i in range(4)], axis=0)
    turned = pltpu.roll(packed, DEPTH, axis=1)
    left = lax.broadcasted_iota(jnp.int32, packed.shape, 1) < DEPTH
    normed = jnp.concatenate(
        [jnp.where(left, packed, turned), jnp.where(left, turned, packed)], axis=0
    )
    high, middle, low = pieces(normed)
    upper = jnp.concatenate([high, middle], axis=0)
    lower = jnp.concatenate([low, jnp.zeros_like(low)], axis=0)

    width = min(512, turned_ref.shape[0])
    first = lax.broadcasted_iota(jnp.int32, (width, LANES), 1) < DEPTH
    for base in range(0, turned_ref.shape[0], width):
        at = pl.ds(base, width)
        weighted = sum(
            jnp.dot(turned_ref[at, :], part, preferred_element_type=jnp.float32)
            for part in (upper, lower)
        )
        high, middle, low = pieces(weighted)
        weights[at, :LANES] = jnp.where(first, high, middle)
        weights[at, LANES:] = jnp.where(first, low, jnp.zeros_like(low))


def down(highest, summed):
    top = jnp.max(highest, axis=0, keepdims=True)
    return top + jnp.log2(jnp.sum(summed * jnp.exp2(highest - top), axis=0, keepdims=True))


def logsum(one, other):
    top = jnp.maximum(one, other)
    return top + jnp.log2(jnp.exp2(one - top) + jnp.exp2(other - top))


def row_values(log_src_ref, sums_ref, more_ref):
    return log_src_ref[...] - marg_power * logsum(sums_ref[...], more_ref[...])


def lane_tiles(ref):
    return [pl.ds(j, LANES) for j in range(0, ref.shape[1], LANES)]


def halves(low):
    low = pl.multiple_of(low, 16)
    return pl.ds(low, 16), [pl.ds(low, 8), pl.ds(pl.multiple_of(low + 8, 8), 8)]


def running(highest, summed, terms):
    fresh = jnp.maximum(highest, tree(terms, jnp.maximum))
    total = tree([jnp.exp2(term - fresh) for term in terms], jnp.add)
    return fresh, summed * jnp.exp2(highest - fresh) + total


def columns_running(scores_ref, rows_ref, top_ref, sum_ref, base, count):
    tiles = lane_tiles(scores_ref)
    span = min(16, len(tiles))

    def scan(i, carry):
        for u in range(4):
            low = pl.multiple_of((i * 4 + u) * 8, 8)
            at = pl.ds(pl.multiple_of(base + low, 8), 8)
            state = None
            for start in range(0, len(tiles), span):
                terms = [scores_ref[at, lanes] + rows_ref[:, lanes] for lanes in tiles[start : start + span]]
                if state is None:
                    highest = tree(terms, jnp.maximum)
                    state = highest, tree([jnp.exp2(term - highest) for term in terms], jnp.add)
                else:
                    state = running(*state, terms)
            top_ref[pl.ds(low, 8), :], sum_ref[pl.ds(low, 8), :] = state
        return carry

    lax.fori_loop(0, count // 32, scan, 0)


def columns_exp(scores_ref, rows_ref, top_ref, sum_ref, base, count, keep_ref):
    tiles = lane_tiles(scores_ref)

    def highest(i, carry):
        places = [pl.ds(pl.multiple_of(i * 64 + g * 8, 8), 8) for g in range(8)]
        sources = [pl.ds(pl.multiple_of(base + i * 64 + g * 8, 8), 8) for g in range(8)]
        tops = [None] * 8
        for lanes in tiles:
            row = rows_ref[:, lanes]
            for g, source in enumerate(sources):
                term = scores_ref[source, lanes] + row
                tops[g] = term if tops[g] is None else jnp.maximum(tops[g], term)
        for place, top in zip(places, tops):
            top_ref[place, :] = top - LIFT
        return carry

    def total(i, carry):
        pairs = [halves(base + i * 64 + g * 16) for g in range(4)]
        places = [place for g in range(4) for place in halves(i * 64 + g * 16)[1]]
        tops = [top_ref[place, :] for place in places]
        sums = [jnp.zeros((8, LANES), jnp.float32)] * 8
        for lanes in tiles:
            row = rows_ref[:, lanes]
            for g, (at, sources) in enumerate(pairs):
                parts = []
                for h, source in enumerate(sources):
                    parts.append(jnp.exp2(scores_ref[source, lanes] + row - tops[2 * g + h]))
                    sums[2 * g + h] = sums[2 * g + h] + parts[h]
                if keep_ref is not None:
                    keep_ref[at, lanes] = jnp.concatenate(parts, axis=0).astype(keep_ref.dtype)
        for place, value in zip(places, sums):
            sum_ref[place, :] = value
        return carry

    lax.fori_loop(0, count // 64, highest, 0)
    if keep_ref is not None:
        tops = top_ref[pl.ds(0, count), :]
        top_ref[pl.ds(0, count), :] = jnp.broadcast_to(jnp.max(tops, axis=1, keepdims=True), tops.shape)
    lax.fori_loop(0, count // 64, total, 0)


def split_rows(line):
    row = lax.broadcasted_iota(jnp.int32, (16, line.shape[1]), 0)
    high, middle, low = (part.astype(jnp.float32) for part in pieces(line))
    spread = jnp.where(row == 0, high, jnp.where(row == 1, middle, jnp.where(row == 2, low, 0.0)))
    return spread.astype(jnp.bfloat16)


def split_rows(line):
    row = lax.broadcasted_iota(jnp.int32, (16, line.shape[1]), 0)
    high, middle, low = (part.astype(jnp.float32) for part in pieces(line))
    spread = jnp.where(row == 0, high, jnp.where(row == 1, middle, jnp.where(row == 2, low, 0.0)))
    return spread.astype(jnp.bfloat16)


def columns_product(keep_ref, kept_top_ref, factor, shift, log_tgt_line_ref, line_ref, base, count):
    factors = split_rows(factor)
    part = min(count, 512)
    for low in range(0, count, part):
        at = pl.ds(pl.multiple_of(base + low, part), part)
        sums = lax.dot_general(
            factors, keep_ref[at, :], (((1,), (1,)), ((), ())), preferred_element_type=jnp.float32
        )
        logs = kept_top_ref[:, at] + (shift - LIFT) + jnp.log2(jnp.sum(sums, axis=0, keepdims=True))
        line_ref[:, pl.ds(low, part)] = log_tgt_line_ref[:, at] - marg_power * logs


def columns_finish(top_ref, sum_ref, log_tgt_ref, cols_ref, base, count):
    part = min(count, 2048)
    for low in range(0, count, part):
        here = pl.ds(low, part)
        tops = top_ref[here, :]
        top = jnp.max(tops, axis=1, keepdims=True)
        total = jnp.sum(sum_ref[here, :] * jnp.exp2(tops - top), axis=1, keepdims=True)
        at = pl.ds(pl.multiple_of(base + low, part), part)
        cols_ref[here, :] = log_tgt_ref[at, :] - marg_power * (top + jnp.log2(total))


BESIDE, DEEP = 8, 4


def over_tiles(count, width, body, first, done):
    for start in range(0, width, BESIDE * LANES):
        tiles = [pl.ds(start + j * LANES, LANES) for j in range(BESIDE)]

        def step(i, carry, tiles=tiles):
            carry = list(carry)
            body([halves((i * DEEP + g) * 16) for g in range(DEEP)], tiles, carry)
            return tuple(carry)

        state = lax.fori_loop(0, count // (16 * DEEP), step, tuple(first for _ in tiles))
        for lanes, value in zip(tiles, state):
            done(lanes, value)


def rows_highest(scores_ref, cols_ref, top_ref):
    def body(pairs, tiles, carry):
        for _, places in pairs:
            for place in places:
                if cols_ref is not None:
                    potential = cols_ref[place, :]
                for j, lanes in enumerate(tiles):
                    term = scores_ref[place, lanes]
                    if cols_ref is not None:
                        term = term + potential
                    carry[j] = jnp.maximum(carry[j], term)

    def done(lanes, value):
        top_ref[:, lanes] = jnp.broadcast_to(jnp.max(value, axis=0, keepdims=True), value.shape) - LIFT

    over_tiles(*scores_ref.shape, body, jnp.full((8, LANES), -jnp.inf, jnp.float32), done)


def rows_exp(scores_ref, cols_ref, top_ref, out_ref, keep_ref):
    def body(pairs, tiles, carry):
        tops = [top_ref[:, lanes] for lanes in tiles]
        for at, places in pairs:
            if cols_ref is not None:
                potentials = [cols_ref[place, :] for place in places]
            for j, lanes in enumerate(tiles):
                terms = [scores_ref[place, lanes] for place in places]
                if cols_ref is not None:
                    terms = [term + potential for term, potential in zip(terms, potentials)]
                parts = [jnp.exp2(term - tops[j]) for term in terms]
                if keep_ref is not None:
                    keep_ref[at, lanes] = jnp.concatenate(parts, axis=0).astype(keep_ref.dtype)
                carry[j] = carry[j] + (parts[0] + parts[1])

    def done(lanes, value):
        out_ref[:, lanes] = down(top_ref[:, lanes], value)

    over_tiles(*scores_ref.shape, body, jnp.zeros((8, LANES), jnp.float32), done)


def rows_product(keep_ref, kept_top_ref, factor, shift, out_ref):
    factors = split_rows(factor)
    chunk = 512
    for start in range(0, keep_ref.shape[1], chunk):
        lanes = pl.ds(start, chunk)
        sums = jnp.dot(factors, keep_ref[:, lanes], preferred_element_type=jnp.float32)
        out_ref[:, lanes] = (
            kept_top_ref[0:1, lanes] + (shift - LIFT) + jnp.log2(jnp.sum(sums, axis=0, keepdims=True))
        )


def columns_either(rows, shared, kept, line_ref, scratch, base, count):
    scores_ref, log_tgt_ref, log_tgt_line_ref = shared
    keep_ref, kept_top_ref, kept_rows_ref = kept
    rows_ref, cols_ref, top_ref, sum_ref = scratch
    change = rows - kept_rows_ref[...]
    shift = jnp.max(change)
    near = shift - jnp.min(change) <= SPAN

    @pl.when(near)
    def _():
        factor = jnp.exp2(change - (shift - LIFT))
        columns_product(keep_ref, kept_top_ref, factor, shift, log_tgt_line_ref, line_ref, base, count)

    @pl.when(jnp.logical_not(near))
    def _():
        rows_ref[...] = jnp.broadcast_to(rows, rows_ref.shape)
        columns_running(scores_ref, rows_ref, top_ref, sum_ref, base, count)
        columns_finish(top_ref, sum_ref, log_tgt_ref, cols_ref, base, count)
        line_ref[...] = cols_ref[...].T[0:1, :]


def rows_either(scores_ref, line_ref, kept, cols_ref, row_top_ref, out_ref):
    keep_ref, kept_top_ref, kept_line_ref = kept
    change = line_ref[...] - kept_line_ref[...]
    shift = jnp.max(change)
    near = shift - jnp.min(change) <= SPAN

    @pl.when(near)
    def _():
        rows_product(keep_ref, kept_top_ref, jnp.exp2(change - (shift - LIFT)), shift, out_ref)

    @pl.when(jnp.logical_not(near))
    def _():
        cols_ref[...] = jnp.broadcast_to(line_ref[...], (LANES, line_ref.shape[1])).T
        rows_highest(scores_ref, cols_ref, row_top_ref)
        rows_exp(scores_ref, cols_ref, row_top_ref, out_ref, None)


def first_kernel(scores_ref, sums_ref, more_ref, log_src_ref, log_tgt_ref, log_tgt_line_ref, *refs):
    out_ref, keep_ref, row_top_ref, line_ref = refs[:4]
    rows_ref, cols_ref, top_ref, sum_ref = refs[4:]
    rows_ref[...] = jnp.broadcast_to(row_values(log_src_ref, sums_ref, more_ref), rows_ref.shape)
    count = scores_ref.shape[0]
    columns_running(scores_ref, rows_ref, top_ref, sum_ref, 0, count)
    columns_finish(top_ref, sum_ref, log_tgt_ref, cols_ref, 0, count)
    line_ref[...] = cols_ref[...].T[0:1, :]
    rows_highest(scores_ref, cols_ref, row_top_ref)
    rows_exp(scores_ref, cols_ref, row_top_ref, out_ref, keep_ref)


def second_kernel(scores_ref, sums_ref, more_ref, log_src_ref, log_tgt_ref, log_tgt_line_ref, *refs):
    kept, (out_ref, keep_ref, kept_top_ref, base_ref) = refs[:3], refs[3:7]
    rows_ref, cols_ref, top_ref, sum_ref, line_ref, row_top_ref = refs[7:]
    base_ref[...] = row_values(log_src_ref, sums_ref, more_ref)
    rows_ref[...] = jnp.broadcast_to(base_ref[...], rows_ref.shape)
    count = scores_ref.shape[0]
    columns_exp(scores_ref, rows_ref, top_ref, sum_ref, 0, count, keep_ref)
    columns_finish(top_ref, sum_ref, log_tgt_ref, cols_ref, 0, count)
    kept_top_ref[...] = top_ref[...].T[0:1, :]
    line_ref[...] = cols_ref[...].T[0:1, :]
    rows_either(scores_ref, line_ref, kept, cols_ref, row_top_ref, out_ref)


def later_kernel(scores_ref, sums_ref, more_ref, log_src_ref, log_tgt_ref, log_tgt_line_ref, *refs):
    kept, kept_columns, out_ref = refs[:3], refs[3:6], refs[6]
    scratch, line_ref, row_top_ref = refs[7:11], refs[11], refs[12]
    rows = row_values(log_src_ref, sums_ref, more_ref)
    shared = scores_ref, log_tgt_ref, log_tgt_line_ref
    columns_either(rows, shared, kept_columns, line_ref, scratch, 0, scores_ref.shape[0])
    rows_either(scores_ref, line_ref, kept, scratch[1], row_top_ref, out_ref)


def last_kernel(merged, scores_ref, sums_ref, more_ref, log_src_ref, log_tgt_ref, log_tgt_line_ref, *refs):
    kept_columns, (out_ref, row_ref, col_ref) = refs[:3], refs[3:6]
    scratch, line_ref, values_ref = refs[6:10], refs[10], refs[11]
    own_rows, own_cols = out_ref.shape
    rows = row_values(log_src_ref, sums_ref, more_ref)
    values_ref[...] = rows
    base = pl.multiple_of(lax.rem(lax.div(lax.axis_index("tgt"), 2), merged) * own_cols, own_cols)
    lanes = pl.ds(pl.multiple_of(lax.axis_index("src") * own_rows, own_rows), own_rows)
    shared = scores_ref, log_tgt_ref, log_tgt_line_ref
    columns_either(rows, shared, kept_columns, line_ref, scratch, base, own_cols)
    row_ref[...] = values_ref[:, lanes] * LN2
    col_ref[...] = line_ref[...] * LN2
    block = scores_ref[pl.ds(base, own_cols), lanes] + values_ref[:, lanes]
    out_ref[...] = (block.T + line_ref[...]) * LN2


def swap(value, axis, offset):
    return lax.ppermute(value, axis, [(i, i ^ offset) for i in range(lax.axis_size(axis))])


def staged_parts(value, axis, low, width):
    size = lax.axis_size(axis)
    terms = [value]
    while low < size:
        span = min(width, size // low)
        value = tree(terms, jnp.add)
        terms = [value] + [swap(value, axis, low * j) for j in range(1, span)]
        low *= span
    return terms


def shards(coupling, src_pcs, tgt_pcs, src_mass, tgt_mass):
    f32 = jnp.float32
    pcs = src_pcs.shape[0]
    rows, cols = coupling.shape
    src_size, tgt_size = lax.axis_size("src"), lax.axis_size("tgt")
    total_rows, total_cols = rows * src_size, cols * tgt_size
    merged = 1
    while 2 * merged * 2 <= tgt_size and 2 * merged * cols * total_rows * 4 <= SCORES_BYTES:
        merged *= 2
    wide = merged * cols
    packed_rows = -(-(pcs + 1) // 8) * 8

    arguments = (coupling, src_pcs, tgt_pcs, src_mass.reshape(1, -1), tgt_mass.reshape(1, -1))
    half, whole, moment = pl.pallas_call(
        front_kernel,
        out_shape=(
            pltpu.VMEM((packed_rows, rows // 2), f32),
            pltpu.VMEM((packed_rows, cols), f32),
            pltpu.VMEM((8, 4 * LANES), f32),
        ),
        in_specs=[pl.BlockSpec(memory_space=pltpu.HBM)] * 5,
        out_specs=(VMEM,) * 3,
        scratch_shapes=[pltpu.VMEM(a.shape, a.dtype) for a in arguments]
        + [pltpu.SemaphoreType.DMA((5,))],
        compiler_params=params(8),
    )(*[pltpu.with_memory_space_constraint(a, pltpu.HBM) for a in arguments])

    moment = moment + swap(moment, "tgt", 1)
    half, whole, moment = lax.optimization_barrier((half, whole, moment))
    parts, targets = [moment], [whole]
    if merged > 1:
        message = jnp.concatenate([whole, moment], axis=0)
        targets += [swap(message, "tgt", 2 * b) for b in range(1, merged)]
        parts += [target[packed_rows:] for target in targets[1:]]
    sources = [half] + [swap(half, "src", b) for b in range(1, src_size)]
    parts, sources, targets = lax.optimization_barrier((parts, sources, targets))
    if 2 * merged < tgt_size:
        parts = staged_parts(tree(parts, jnp.add), "tgt", 2 * merged, 4)
    moments = staged_parts(tree(parts, jnp.add), "src", 1, 4)
    near = jnp.concatenate(sources, axis=0)
    far = swap(near, "tgt", 1)

    src_all, turned, log_src, log_tgt, log_tgt_line = pl.pallas_call(
        functools.partial(prepare_kernel, pcs, src_size, merged),
        out_shape=(
            jax.ShapeDtypeStruct((4 * DEPTH, total_rows), jnp.bfloat16),
            jax.ShapeDtypeStruct((wide, LANES), jnp.bfloat16),
            jax.ShapeDtypeStruct((1, total_rows), f32),
            jax.ShapeDtypeStruct((wide, LANES), f32),
            jax.ShapeDtypeStruct((1, wide), f32),
        ),
        in_specs=[VMEM] * (2 + merged),
        out_specs=(VMEM,) * 5,
        compiler_params=params(10),
    )(near, far, *targets)
    weights = pl.pallas_call(
        functools.partial(start_kernel, pcs, total_rows * total_cols),
        out_shape=jax.ShapeDtypeStruct((wide, 4 * DEPTH), jnp.bfloat16),
        in_specs=[VMEM] * (1 + len(moments)),
        out_specs=VMEM,
        compiler_params=params(10),
    )(turned, *moments)
    scores = jnp.dot(weights, src_all, preferred_element_type=f32)
    highest = jnp.max(scores, axis=0, keepdims=True)
    sums = highest + jnp.log2(jnp.sum(jnp.exp2(scores - highest), axis=0, keepdims=True))

    def both(value):
        offset = 2 * merged
        while offset < tgt_size:
            value = logsum(value, swap(value, "tgt", offset))
            offset *= 2
        return value, swap(value, "tgt", 1)

    bf16, block = jnp.bfloat16, (wide, total_rows)

    def call(kernel, sums, extra, outs, scratch):
        return pl.pallas_call(
            kernel,
            out_shape=tuple(jax.ShapeDtypeStruct(shape, bf16 if shape == block else f32) for shape in outs),
            in_specs=[VMEM] * (6 + len(extra)),
            out_specs=(VMEM,) * len(outs),
            scratch_shapes=[pltpu.VMEM(shape, f32) for shape in scratch],
            compiler_params=params(10),
        )(scores, *both(sums), log_src, log_tgt, log_tgt_line, *extra)

    line, lines, pads = (1, total_rows), (8, total_rows), (wide, LANES)
    side, columns = (1, wide), (lines, pads, pads, pads)
    sums, *kept_rows = call(first_kernel, sums, (), (line, block, lines, side), columns)
    sums, *kept_columns = call(
        second_kernel, sums, kept_rows, (line, block, side, line), (*columns, side, lines)
    )
    for iteration in range(ITERS - 3):
        (sums,) = call(
            later_kernel, sums, (*kept_rows, *kept_columns), (line,), (*columns, side, lines)
        )
    pads, side = (cols, LANES), (1, cols)
    log_coupling, row_potential, col_potential = call(
        functools.partial(last_kernel, merged), sums, kept_columns,
        ((rows, cols), (1, rows), side), (lines, pads, pads, pads, side, line),
    )
    return log_coupling, row_potential.reshape(-1), col_potential.reshape(-1)


def solution(mesh):
    in_specs = (P("src", "tgt"), P(None, "src"), P(None, "tgt"), P("src"), P("tgt"))
    out_specs = (P("src", "tgt"), P("src"), P("tgt"))
    return jax.shard_map(shards, mesh=mesh, in_specs=in_specs, out_specs=out_specs, check_vma=False)
```

```python
import functools
import math

import jax
import jax.numpy as jnp
from jax import lax
from jax.experimental import pallas as pl
from jax.experimental.pallas import tpu as pltpu
from jax.sharding import PartitionSpec as P

ITERS = 4

eps_reg = 0.5
marg_power = 1.0 / (1.0 + eps_reg)
tiny_eps = 1e-06

LANES = 128
DEPTH = 64
LN2 = math.log(2.0)
SCORES_BYTES = 1 << 24
LIFT = 54.0
SPAN = 145.0
VMEM = pl.BlockSpec(memory_space=pltpu.VMEM)


def params(mib):
    return pltpu.CompilerParams(vmem_limit_bytes=mib << 20)


def tree(values, combine):
    values = list(values)
    while len(values) > 1:
        paired = [combine(values[i], values[i + 1]) for i in range(0, len(values) - 1, 2)]
        values = paired + ([values[-1]] if len(values) % 2 else [])
    return values[0]


def pieces(value):
    high = value.astype(jnp.bfloat16)
    rest = value - high.astype(jnp.float32)
    middle = rest.astype(jnp.bfloat16)
    low = (rest - middle.astype(jnp.float32)).astype(jnp.bfloat16)
    return high, middle, low


def padded(value):
    return jnp.concatenate(
        [value, jnp.zeros((DEPTH - value.shape[0], value.shape[1]), value.dtype)], axis=0
    )


def front_kernel(*refs):
    sources, (half_ref, whole_ref, moment_ref), local, sems = refs[:5], refs[5:8], refs[8:13], refs[13]
    copies = [pltpu.make_async_copy(a, b, sems.at[i]) for i, (a, b) in enumerate(zip(sources, local))]
    for copy in copies:
        copy.start()
    coupling_ref, src_ref, tgt_ref, src_mass_ref, tgt_mass_ref = local
    pcs = src_ref.shape[0]
    half = half_ref.shape[1]
    odd = lax.rem(lax.axis_index("tgt"), 2)
    for copy in copies[1:]:
        copy.wait()
    src = src_ref[...].astype(jnp.float32)
    tgt = tgt_ref[...].astype(jnp.float32)
    below = jnp.zeros((half_ref.shape[0] - pcs - 1, 2 * half), jnp.float32)
    joined = jnp.concatenate([src, jnp.log2(src_mass_ref[...]), below], axis=0)
    half_ref[...] = jnp.where(odd == 0, joined[:, :half], joined[:, half:])
    below = jnp.zeros((half_ref.shape[0] - pcs - 1, tgt.shape[1]), jnp.float32)
    whole_ref[...] = jnp.concatenate([tgt, jnp.log2(tgt_mass_ref[...]), below], axis=0)
    src = padded(src).astype(jnp.bfloat16)
    tgt = padded(tgt).astype(jnp.bfloat16)
    twice = jnp.concatenate([src, src], axis=0)
    copies[0].wait()
    panel = jnp.dot(twice, coupling_ref[...], preferred_element_type=jnp.float32)
    moment = sum(
        lax.dot_general(tgt, part, (((1,), (1,)), ((), ())), preferred_element_type=jnp.float32)
        for part in pieces(panel)
    )
    lane = lax.broadcasted_iota(jnp.int32, (DEPTH // 2, LANES), 1)
    moment = jnp.where(lane < DEPTH, moment[: DEPTH // 2], moment[DEPTH // 2 :])
    for i in range(4):
        moment_ref[:, i * LANES : (i + 1) * LANES] = moment[i * 8 : i * 8 + 8]


def prepare_kernel(pcs, blocks, merged, near_ref, far_ref, *refs):
    tgt_refs, (src_ref, turned_ref, log_src_ref, log_tgt_ref, line_ref) = refs[:merged], refs[merged:]
    packed_rows = near_ref.shape[0] // blocks
    half = near_ref.shape[1]
    width = tgt_refs[0].shape[1]
    z = lax.axis_index("src")
    t = lax.axis_index("tgt")
    odd = lax.rem(t, 2)
    total_rows = 2 * half * blocks
    total_cols = width * lax.axis_size("tgt")
    for b in range(blocks):
        place = jnp.bitwise_xor(z, b)
        for ref, side in ((near_ref, odd), (far_ref, 1 - odd)):
            block = ref[pl.ds(b * packed_rows, packed_rows), :]
            lanes = pl.ds(pl.multiple_of((place * 2 + side) * half, half), half)
            log_src_ref[:, lanes] = marg_power * (block[pcs : pcs + 1] + math.log2(total_cols))
            block = padded(block).astype(jnp.bfloat16)
            for copy in range(4):
                src_ref[pl.ds(copy * DEPTH, DEPTH), lanes] = block
    mine = lax.rem(lax.div(t, 2), merged)
    for b in range(merged):
        base = pl.multiple_of(jnp.bitwise_xor(mine, b) * width, width)
        block = padded(tgt_refs[b][:packed_rows, :])
        line_ref[:, pl.ds(base, width)] = marg_power * (block[pcs : pcs + 1] + math.log2(total_rows))
        turned = jnp.concatenate([block, block], axis=0).T
        log_tgt_ref[pl.ds(base, width), :] = jnp.broadcast_to(
            marg_power * (turned[:, pcs : pcs + 1] + math.log2(total_rows)), (width, LANES)
        )
        turned_ref[pl.ds(base, width), :] = turned.astype(jnp.bfloat16)


def start_kernel(pcs, entries, turned_ref, *refs):
    moment_refs, weights = refs[:-1], refs[-1]
    packed = tree([ref[...] for ref in moment_refs], jnp.add) * entries ** (-0.5)
    spread = jnp.sqrt(jnp.sum(packed * packed) * (1.0 / (pcs * pcs)) + tiny_eps)
    packed = packed / spread * (2.0 / (eps_reg * pcs) / LN2)
    packed = jnp.concatenate([packed[:, i * LANES : (i + 1) * LANES] for i in range(4)], axis=0)
    turned = pltpu.roll(packed, DEPTH, axis=1)
    left = lax.broadcasted_iota(jnp.int32, packed.shape, 1) < DEPTH
    normed = jnp.concatenate(
        [jnp.where(left, packed, turned), jnp.where(left, turned, packed)], axis=0
    )
    high, middle, low = pieces(normed)
    upper = jnp.concatenate([high, middle], axis=0)
    lower = jnp.concatenate([low, jnp.zeros_like(low)], axis=0)

    width = min(512, turned_ref.shape[0])
    first = lax.broadcasted_iota(jnp.int32, (width, LANES), 1) < DEPTH
    for base in range(0, turned_ref.shape[0], width):
        at = pl.ds(base, width)
        weighted = sum(
            jnp.dot(turned_ref[at, :], part, preferred_element_type=jnp.float32)
            for part in (upper, lower)
        )
        high, middle, low = pieces(weighted)
        weights[at, :LANES] = jnp.where(first, high, middle)
        weights[at, LANES:] = jnp.where(first, low, jnp.zeros_like(low))


def down(highest, summed):
    top = jnp.max(highest, axis=0, keepdims=True)
    return top + jnp.log2(jnp.sum(summed * jnp.exp2(highest - top), axis=0, keepdims=True))


def logsum(one, other):
    top = jnp.maximum(one, other)
    return top + jnp.log2(jnp.exp2(one - top) + jnp.exp2(other - top))


def row_values(log_src_ref, sums_ref, more_ref):
    return log_src_ref[...] - marg_power * logsum(sums_ref[...], more_ref[...])


def lane_tiles(ref):
    return [pl.ds(j, LANES) for j in range(0, ref.shape[1], LANES)]


def halves(low):
    low = pl.multiple_of(low, 16)
    return pl.ds(low, 16), [pl.ds(low, 8), pl.ds(pl.multiple_of(low + 8, 8), 8)]


def running(highest, summed, terms):
    fresh = jnp.maximum(highest, tree(terms, jnp.maximum))
    total = tree([jnp.exp2(term - fresh) for term in terms], jnp.add)
    return fresh, summed * jnp.exp2(highest - fresh) + total


def columns_running(scores_ref, rows_ref, top_ref, sum_ref, base, count):
    tiles = lane_tiles(scores_ref)
    span = min(16, len(tiles))

    def scan(i, carry):
        for u in range(4):
            low = pl.multiple_of((i * 4 + u) * 8, 8)
            at = pl.ds(pl.multiple_of(base + low, 8), 8)
            state = None
            for start in range(0, len(tiles), span):
                terms = [scores_ref[at, lanes] + rows_ref[:, lanes] for lanes in tiles[start : start + span]]
                if state is None:
                    highest = tree(terms, jnp.maximum)
                    state = highest, tree([jnp.exp2(term - highest) for term in terms], jnp.add)
                else:
                    state = running(*state, terms)
            top_ref[pl.ds(low, 8), :], sum_ref[pl.ds(low, 8), :] = state
        return carry

    lax.fori_loop(0, count // 32, scan, 0)


def rows_running(scores_ref, out_ref):
    count, total = scores_ref.shape
    beside, deep = 8, 16
    unset = (jnp.full((8, LANES), -jnp.inf, jnp.float32), jnp.zeros((8, LANES), jnp.float32))
    for start in range(0, total, beside * LANES):
        tiles = [pl.ds(start + j * LANES, LANES) for j in range(beside)]

        def step(i, carry, tiles=tiles):
            ats = [pl.ds(pl.multiple_of((i * deep + g) * 8, 8), 8) for g in range(deep)]
            return tuple(
                running(*state, [scores_ref[at, lanes] for at in ats])
                for state, lanes in zip(carry, tiles)
            )

        carry = lax.fori_loop(0, count // (8 * deep), step, (unset,) * beside)
        for lanes, state in zip(tiles, carry):
            out_ref[:, lanes] = down(*state)


def columns_exp(scores_ref, rows_ref, top_ref, sum_ref, base, count, keep_ref):
    tiles = lane_tiles(scores_ref)

    def highest(i, carry):
        places = [pl.ds(pl.multiple_of(i * 64 + g * 8, 8), 8) for g in range(8)]
        sources = [pl.ds(pl.multiple_of(base + i * 64 + g * 8, 8), 8) for g in range(8)]
        tops = [None] * 8
        for lanes in tiles:
            row = rows_ref[:, lanes]
            for g, source in enumerate(sources):
                term = scores_ref[source, lanes] + row
                tops[g] = term if tops[g] is None else jnp.maximum(tops[g], term)
        for place, top in zip(places, tops):
            top_ref[place, :] = top - LIFT
        return carry

    def total(i, carry):
        pairs = [halves(base + i * 64 + g * 16) for g in range(4)]
        places = [place for g in range(4) for place in halves(i * 64 + g * 16)[1]]
        tops = [top_ref[place, :] for place in places]
        sums = [jnp.zeros((8, LANES), jnp.float32)] * 8
        for lanes in tiles:
            row = rows_ref[:, lanes]
            for g, (at, sources) in enumerate(pairs):
                parts = []
                for h, source in enumerate(sources):
                    parts.append(jnp.exp2(scores_ref[source, lanes] + row - tops[2 * g + h]))
                    sums[2 * g + h] = sums[2 * g + h] + parts[h]
                if keep_ref is not None:
                    keep_ref[at, lanes] = jnp.concatenate(parts, axis=0).astype(keep_ref.dtype)
        for place, value in zip(places, sums):
            sum_ref[place, :] = value
        return carry

    lax.fori_loop(0, count // 64, highest, 0)
    if keep_ref is not None:
        tops = top_ref[pl.ds(0, count), :]
        top_ref[pl.ds(0, count), :] = jnp.broadcast_to(jnp.max(tops, axis=1, keepdims=True), tops.shape)
    lax.fori_loop(0, count // 64, total, 0)


def split_rows(line):
    row = lax.broadcasted_iota(jnp.int32, (16, line.shape[1]), 0)
    high, middle, low = (part.astype(jnp.float32) for part in pieces(line))
    spread = jnp.where(row == 0, high, jnp.where(row == 1, middle, jnp.where(row == 2, low, 0.0)))
    return spread.astype(jnp.bfloat16)


def split_rows(line):
    row = lax.broadcasted_iota(jnp.int32, (16, line.shape[1]), 0)
    high, middle, low = (part.astype(jnp.float32) for part in pieces(line))
    spread = jnp.where(row == 0, high, jnp.where(row == 1, middle, jnp.where(row == 2, low, 0.0)))
    return spread.astype(jnp.bfloat16)


def columns_product(keep_ref, kept_top_ref, factor, shift, log_tgt_line_ref, line_ref, base, count):
    factors = split_rows(factor)
    part = min(count, 512)
    for low in range(0, count, part):
        at = pl.ds(pl.multiple_of(base + low, part), part)
        sums = lax.dot_general(
            factors, keep_ref[at, :], (((1,), (1,)), ((), ())), preferred_element_type=jnp.float32
        )
        logs = kept_top_ref[:, at] + (shift - LIFT) + jnp.log2(jnp.sum(sums, axis=0, keepdims=True))
        line_ref[:, pl.ds(low, part)] = log_tgt_line_ref[:, at] - marg_power * logs


def columns_finish(top_ref, sum_ref, log_tgt_ref, cols_ref, base, count):
    part = min(count, 2048)
    for low in range(0, count, part):
        here = pl.ds(low, part)
        tops = top_ref[here, :]
        top = jnp.max(tops, axis=1, keepdims=True)
        total = jnp.sum(sum_ref[here, :] * jnp.exp2(tops - top), axis=1, keepdims=True)
        at = pl.ds(pl.multiple_of(base + low, part), part)
        cols_ref[here, :] = log_tgt_ref[at, :] - marg_power * (top + jnp.log2(total))


BESIDE, DEEP = 4, 8


def over_tiles(count, width, body, first, done):
    for start in range(0, width, BESIDE * LANES):
        tiles = [pl.ds(start + j * LANES, LANES) for j in range(BESIDE)]

        def step(i, carry, tiles=tiles):
            carry = list(carry)
            body([halves((i * DEEP + g) * 16) for g in range(DEEP)], tiles, carry)
            return tuple(carry)

        state = lax.fori_loop(0, count // (16 * DEEP), step, tuple(first for _ in tiles))
        for lanes, value in zip(tiles, state):
            done(lanes, value)


def rows_highest(scores_ref, cols_ref, top_ref):
    def body(pairs, tiles, carry):
        for _, places in pairs:
            for place in places:
                if cols_ref is not None:
                    potential = cols_ref[place, :]
                for j, lanes in enumerate(tiles):
                    term = scores_ref[place, lanes]
                    if cols_ref is not None:
                        term = term + potential
                    carry[j] = jnp.maximum(carry[j], term)

    def done(lanes, value):
        top_ref[:, lanes] = jnp.broadcast_to(jnp.max(value, axis=0, keepdims=True), value.shape) - LIFT

    over_tiles(*scores_ref.shape, body, jnp.full((8, LANES), -jnp.inf, jnp.float32), done)


def rows_exp(scores_ref, cols_ref, top_ref, out_ref, keep_ref):
    def body(pairs, tiles, carry):
        tops = [top_ref[:, lanes] for lanes in tiles]
        for at, places in pairs:
            if cols_ref is not None:
                potentials = [cols_ref[place, :] for place in places]
            for j, lanes in enumerate(tiles):
                terms = [scores_ref[place, lanes] for place in places]
                if cols_ref is not None:
                    terms = [term + potential for term, potential in zip(terms, potentials)]
                parts = [jnp.exp2(term - tops[j]) for term in terms]
                if keep_ref is not None:
                    keep_ref[at, lanes] = jnp.concatenate(parts, axis=0).astype(keep_ref.dtype)
                carry[j] = carry[j] + (parts[0] + parts[1])

    def done(lanes, value):
        out_ref[:, lanes] = down(top_ref[:, lanes], value)

    over_tiles(*scores_ref.shape, body, jnp.zeros((8, LANES), jnp.float32), done)


def rows_product(keep_ref, kept_top_ref, factor, shift, out_ref):
    factors = split_rows(factor)
    chunk = 512
    for start in range(0, keep_ref.shape[1], chunk):
        lanes = pl.ds(start, chunk)
        sums = jnp.dot(factors, keep_ref[:, lanes], preferred_element_type=jnp.float32)
        out_ref[:, lanes] = (
            kept_top_ref[0:1, lanes] + (shift - LIFT) + jnp.log2(jnp.sum(sums, axis=0, keepdims=True))
        )


def columns_either(rows, shared, kept, line_ref, scratch, base, count):
    scores_ref, log_tgt_ref, log_tgt_line_ref = shared
    keep_ref, kept_top_ref, kept_rows_ref = kept
    rows_ref, cols_ref, top_ref, sum_ref = scratch
    change = rows - kept_rows_ref[...]
    shift = jnp.max(change)
    near = shift - jnp.min(change) <= SPAN

    @pl.when(near)
    def _():
        factor = jnp.exp2(change - (shift - LIFT))
        columns_product(keep_ref, kept_top_ref, factor, shift, log_tgt_line_ref, line_ref, base, count)

    @pl.when(jnp.logical_not(near))
    def _():
        rows_ref[...] = jnp.broadcast_to(rows, rows_ref.shape)
        columns_running(scores_ref, rows_ref, top_ref, sum_ref, base, count)
        columns_finish(top_ref, sum_ref, log_tgt_ref, cols_ref, base, count)
        line_ref[...] = cols_ref[...].T[0:1, :]


def rows_either(scores_ref, line_ref, kept, cols_ref, row_top_ref, out_ref):
    keep_ref, kept_top_ref, kept_line_ref = kept
    change = line_ref[...] - kept_line_ref[...]
    shift = jnp.max(change)
    near = shift - jnp.min(change) <= SPAN

    @pl.when(near)
    def _():
        rows_product(keep_ref, kept_top_ref, jnp.exp2(change - (shift - LIFT)), shift, out_ref)

    @pl.when(jnp.logical_not(near))
    def _():
        cols_ref[...] = jnp.broadcast_to(line_ref[...], (LANES, line_ref.shape[1])).T
        rows_highest(scores_ref, cols_ref, row_top_ref)
        rows_exp(scores_ref, cols_ref, row_top_ref, out_ref, None)


def first_kernel(scores_ref, sums_ref, more_ref, log_src_ref, log_tgt_ref, log_tgt_line_ref, *refs):
    out_ref, keep_ref, row_top_ref, line_ref = refs[:4]
    rows_ref, cols_ref, top_ref, sum_ref = refs[4:]
    rows_ref[...] = jnp.broadcast_to(row_values(log_src_ref, sums_ref, more_ref), rows_ref.shape)
    count = scores_ref.shape[0]
    columns_running(scores_ref, rows_ref, top_ref, sum_ref, 0, count)
    columns_finish(top_ref, sum_ref, log_tgt_ref, cols_ref, 0, count)
    line_ref[...] = cols_ref[...].T[0:1, :]
    rows_highest(scores_ref, cols_ref, row_top_ref)
    rows_exp(scores_ref, cols_ref, row_top_ref, out_ref, keep_ref)


def second_kernel(scores_ref, sums_ref, more_ref, log_src_ref, log_tgt_ref, log_tgt_line_ref, *refs):
    kept, (out_ref, keep_ref, kept_top_ref, base_ref) = refs[:3], refs[3:7]
    rows_ref, cols_ref, top_ref, sum_ref, line_ref, row_top_ref = refs[7:]
    base_ref[...] = row_values(log_src_ref, sums_ref, more_ref)
    rows_ref[...] = jnp.broadcast_to(base_ref[...], rows_ref.shape)
    count = scores_ref.shape[0]
    columns_exp(scores_ref, rows_ref, top_ref, sum_ref, 0, count, keep_ref)
    columns_finish(top_ref, sum_ref, log_tgt_ref, cols_ref, 0, count)
    kept_top_ref[...] = top_ref[...].T[0:1, :]
    line_ref[...] = cols_ref[...].T[0:1, :]
    rows_either(scores_ref, line_ref, kept, cols_ref, row_top_ref, out_ref)


def later_kernel(scores_ref, sums_ref, more_ref, log_src_ref, log_tgt_ref, log_tgt_line_ref, *refs):
    kept, kept_columns, out_ref = refs[:3], refs[3:6], refs[6]
    scratch, line_ref, row_top_ref = refs[7:11], refs[11], refs[12]
    rows = row_values(log_src_ref, sums_ref, more_ref)
    shared = scores_ref, log_tgt_ref, log_tgt_line_ref
    columns_either(rows, shared, kept_columns, line_ref, scratch, 0, scores_ref.shape[0])
    rows_either(scores_ref, line_ref, kept, scratch[1], row_top_ref, out_ref)


def last_kernel(merged, scores_ref, sums_ref, more_ref, log_src_ref, log_tgt_ref, log_tgt_line_ref, *refs):
    kept_columns, (out_ref, row_ref, col_ref) = refs[:3], refs[3:6]
    scratch, line_ref, values_ref = refs[6:10], refs[10], refs[11]
    own_rows, own_cols = out_ref.shape
    rows = row_values(log_src_ref, sums_ref, more_ref)
    values_ref[...] = rows
    base = pl.multiple_of(lax.rem(lax.div(lax.axis_index("tgt"), 2), merged) * own_cols, own_cols)
    lanes = pl.ds(pl.multiple_of(lax.axis_index("src") * own_rows, own_rows), own_rows)
    shared = scores_ref, log_tgt_ref, log_tgt_line_ref
    columns_either(rows, shared, kept_columns, line_ref, scratch, base, own_cols)
    row_ref[...] = values_ref[:, lanes] * LN2
    col_ref[...] = line_ref[...] * LN2
    block = scores_ref[pl.ds(base, own_cols), lanes] + values_ref[:, lanes]
    out_ref[...] = (block.T + line_ref[...]) * LN2


def swap(value, axis, offset):
    return lax.ppermute(value, axis, [(i, i ^ offset) for i in range(lax.axis_size(axis))])


def staged_parts(value, axis, low, width):
    size = lax.axis_size(axis)
    terms = [value]
    while low < size:
        span = min(width, size // low)
        value = tree(terms, jnp.add)
        terms = [value] + [swap(value, axis, low * j) for j in range(1, span)]
        low *= span
    return terms


def shards(coupling, src_pcs, tgt_pcs, src_mass, tgt_mass):
    f32 = jnp.float32
    pcs = src_pcs.shape[0]
    rows, cols = coupling.shape
    src_size, tgt_size = lax.axis_size("src"), lax.axis_size("tgt")
    total_rows, total_cols = rows * src_size, cols * tgt_size
    merged = 1
    while 2 * merged * 2 <= tgt_size and 2 * merged * cols * total_rows * 4 <= SCORES_BYTES:
        merged *= 2
    wide = merged * cols
    packed_rows = -(-(pcs + 1) // 8) * 8

    arguments = (coupling, src_pcs, tgt_pcs, src_mass.reshape(1, -1), tgt_mass.reshape(1, -1))
    half, whole, moment = pl.pallas_call(
        front_kernel,
        out_shape=(
            pltpu.VMEM((packed_rows, rows // 2), f32),
            pltpu.VMEM((packed_rows, cols), f32),
            pltpu.VMEM((8, 4 * LANES), f32),
        ),
        in_specs=[pl.BlockSpec(memory_space=pltpu.HBM)] * 5,
        out_specs=(VMEM,) * 3,
        scratch_shapes=[pltpu.VMEM(a.shape, a.dtype) for a in arguments]
        + [pltpu.SemaphoreType.DMA((5,))],
        compiler_params=params(8),
    )(*[pltpu.with_memory_space_constraint(a, pltpu.HBM) for a in arguments])

    moment = moment + swap(moment, "tgt", 1)
    half, whole, moment = lax.optimization_barrier((half, whole, moment))
    parts, targets = [moment], [whole]
    if merged > 1:
        message = jnp.concatenate([whole, moment], axis=0)
        targets += [swap(message, "tgt", 2 * b) for b in range(1, merged)]
        parts += [target[packed_rows:] for target in targets[1:]]
    sources = [half] + [swap(half, "src", b) for b in range(1, src_size)]
    parts, sources, targets = lax.optimization_barrier((parts, sources, targets))
    if 2 * merged < tgt_size:
        parts = staged_parts(tree(parts, jnp.add), "tgt", 2 * merged, 4)
    moments = staged_parts(tree(parts, jnp.add), "src", 1, 4)
    near = jnp.concatenate(sources, axis=0)
    far = swap(near, "tgt", 1)

    src_all, turned, log_src, log_tgt, log_tgt_line = pl.pallas_call(
        functools.partial(prepare_kernel, pcs, src_size, merged),
        out_shape=(
            jax.ShapeDtypeStruct((4 * DEPTH, total_rows), jnp.bfloat16),
            jax.ShapeDtypeStruct((wide, LANES), jnp.bfloat16),
            jax.ShapeDtypeStruct((1, total_rows), f32),
            jax.ShapeDtypeStruct((wide, LANES), f32),
            jax.ShapeDtypeStruct((1, wide), f32),
        ),
        in_specs=[VMEM] * (2 + merged),
        out_specs=(VMEM,) * 5,
        compiler_params=params(10),
    )(near, far, *targets)
    weights = pl.pallas_call(
        functools.partial(start_kernel, pcs, total_rows * total_cols),
        out_shape=jax.ShapeDtypeStruct((wide, 4 * DEPTH), jnp.bfloat16),
        in_specs=[VMEM] * (1 + len(moments)),
        out_specs=VMEM,
        compiler_params=params(10),
    )(turned, *moments)
    scores = jnp.dot(weights, src_all, preferred_element_type=f32)
    sums = pl.pallas_call(
        rows_running,
        out_shape=jax.ShapeDtypeStruct((1, total_rows), f32),
        in_specs=[VMEM],
        out_specs=VMEM,
        compiler_params=params(10),
    )(scores)

    def both(value):
        offset = 2 * merged
        while offset < tgt_size:
            value = logsum(value, swap(value, "tgt", offset))
            offset *= 2
        return value, swap(value, "tgt", 1)

    bf16, block = jnp.bfloat16, (wide, total_rows)

    def call(kernel, sums, extra, outs, scratch):
        return pl.pallas_call(
            kernel,
            out_shape=tuple(jax.ShapeDtypeStruct(shape, bf16 if shape == block else f32) for shape in outs),
            in_specs=[VMEM] * (6 + len(extra)),
            out_specs=(VMEM,) * len(outs),
            scratch_shapes=[pltpu.VMEM(shape, f32) for shape in scratch],
            compiler_params=params(10),
        )(scores, *both(sums), log_src, log_tgt, log_tgt_line, *extra)

    line, lines, pads = (1, total_rows), (8, total_rows), (wide, LANES)
    side, columns = (1, wide), (lines, pads, pads, pads)
    sums, *kept_rows = call(first_kernel, sums, (), (line, block, lines, side), columns)
    sums, *kept_columns = call(
        second_kernel, sums, kept_rows, (line, block, side, line), (*columns, side, lines)
    )
    for iteration in range(ITERS - 3):
        (sums,) = call(
            later_kernel, sums, (*kept_rows, *kept_columns), (line,), (*columns, side, lines)
        )
    pads, side = (cols, LANES), (1, cols)
    log_coupling, row_potential, col_potential = call(
        functools.partial(last_kernel, merged), sums, kept_columns,
        ((rows, cols), (1, rows), side), (lines, pads, pads, pads, side, line),
    )
    return log_coupling, row_potential.reshape(-1), col_potential.reshape(-1)


def solution(mesh):
    in_specs = (P("src", "tgt"), P(None, "src"), P(None, "tgt"), P("src"), P("tgt"))
    out_specs = (P("src", "tgt"), P("src"), P("tgt"))
    return jax.shard_map(shards, mesh=mesh, in_specs=in_specs, out_specs=out_specs, check_vma=False)
```

```python
import functools
import math

import jax
import jax.numpy as jnp
from jax import lax
from jax.experimental import pallas as pl
from jax.experimental.pallas import tpu as pltpu
from jax.sharding import PartitionSpec as P

ITERS = 4

eps_reg = 0.5
marg_power = 1.0 / (1.0 + eps_reg)
tiny_eps = 1e-06

LANES = 128
DEPTH = 64
LN2 = math.log(2.0)
SCORES_BYTES = 1 << 24
LIFT = 54.0
SPAN = 145.0
VMEM = pl.BlockSpec(memory_space=pltpu.VMEM)


def params(mib):
    return pltpu.CompilerParams(vmem_limit_bytes=mib << 20)


def tree(values, combine):
    values = list(values)
    while len(values) > 1:
        paired = [combine(values[i], values[i + 1]) for i in range(0, len(values) - 1, 2)]
        values = paired + ([values[-1]] if len(values) % 2 else [])
    return values[0]


def pieces(value):
    high = value.astype(jnp.bfloat16)
    rest = value - high.astype(jnp.float32)
    middle = rest.astype(jnp.bfloat16)
    low = (rest - middle.astype(jnp.float32)).astype(jnp.bfloat16)
    return high, middle, low


def padded(value):
    return jnp.concatenate(
        [value, jnp.zeros((DEPTH - value.shape[0], value.shape[1]), value.dtype)], axis=0
    )


def front_kernel(*refs):
    sources, (half_ref, whole_ref, moment_ref), local, sems = refs[:5], refs[5:8], refs[8:13], refs[13]
    copies = [pltpu.make_async_copy(a, b, sems.at[i]) for i, (a, b) in enumerate(zip(sources, local))]
    for copy in copies:
        copy.start()
    coupling_ref, src_ref, tgt_ref, src_mass_ref, tgt_mass_ref = local
    pcs = src_ref.shape[0]
    half = half_ref.shape[1]
    odd = lax.rem(lax.axis_index("tgt"), 2)
    for copy in copies[1:]:
        copy.wait()
    src = src_ref[...].astype(jnp.float32)
    tgt = tgt_ref[...].astype(jnp.float32)
    below = jnp.zeros((half_ref.shape[0] - pcs - 1, 2 * half), jnp.float32)
    joined = jnp.concatenate([src, jnp.log2(src_mass_ref[...]), below], axis=0)
    half_ref[...] = jnp.where(odd == 0, joined[:, :half], joined[:, half:])
    below = jnp.zeros((half_ref.shape[0] - pcs - 1, tgt.shape[1]), jnp.float32)
    whole_ref[...] = jnp.concatenate([tgt, jnp.log2(tgt_mass_ref[...]), below], axis=0)
    src = padded(src).astype(jnp.bfloat16)
    tgt = padded(tgt).astype(jnp.bfloat16)
    twice = jnp.concatenate([src, src], axis=0)
    copies[0].wait()
    panel = jnp.dot(twice, coupling_ref[...], preferred_element_type=jnp.float32)
    moment = sum(
        lax.dot_general(tgt, part, (((1,), (1,)), ((), ())), preferred_element_type=jnp.float32)
        for part in pieces(panel)
    )
    lane = lax.broadcasted_iota(jnp.int32, (DEPTH // 2, LANES), 1)
    moment = jnp.where(lane < DEPTH, moment[: DEPTH // 2], moment[DEPTH // 2 :])
    for i in range(4):
        moment_ref[:, i * LANES : (i + 1) * LANES] = moment[i * 8 : i * 8 + 8]


def prepare_kernel(pcs, blocks, merged, near_ref, far_ref, *refs):
    tgt_refs, (src_ref, turned_ref, log_src_ref, log_tgt_ref, line_ref) = refs[:merged], refs[merged:]
    packed_rows = near_ref.shape[0] // blocks
    half = near_ref.shape[1]
    width = tgt_refs[0].shape[1]
    z = lax.axis_index("src")
    t = lax.axis_index("tgt")
    odd = lax.rem(t, 2)
    total_rows = 2 * half * blocks
    total_cols = width * lax.axis_size("tgt")
    for b in range(blocks):
        place = jnp.bitwise_xor(z, b)
        for ref, side in ((near_ref, odd), (far_ref, 1 - odd)):
            block = ref[pl.ds(b * packed_rows, packed_rows), :]
            lanes = pl.ds(pl.multiple_of((place * 2 + side) * half, half), half)
            log_src_ref[:, lanes] = marg_power * (block[pcs : pcs + 1] + math.log2(total_cols))
            block = padded(block).astype(jnp.bfloat16)
            for copy in range(4):
                src_ref[pl.ds(copy * DEPTH, DEPTH), lanes] = block
    mine = lax.rem(lax.div(t, 2), merged)
    for b in range(merged):
        base = pl.multiple_of(jnp.bitwise_xor(mine, b) * width, width)
        block = padded(tgt_refs[b][:packed_rows, :])
        line_ref[:, pl.ds(base, width)] = marg_power * (block[pcs : pcs + 1] + math.log2(total_rows))
        turned = jnp.concatenate([block, block], axis=0).T
        log_tgt_ref[pl.ds(base, width), :] = jnp.broadcast_to(
            marg_power * (turned[:, pcs : pcs + 1] + math.log2(total_rows)), (width, LANES)
        )
        turned_ref[pl.ds(base, width), :] = turned.astype(jnp.bfloat16)


def start_kernel(pcs, entries, turned_ref, *refs):
    moment_refs, weights = refs[:-1], refs[-1]
    packed = tree([ref[...] for ref in moment_refs], jnp.add) * entries ** (-0.5)
    spread = jnp.sqrt(jnp.sum(packed * packed) * (1.0 / (pcs * pcs)) + tiny_eps)
    packed = packed / spread * (2.0 / (eps_reg * pcs) / LN2)
    packed = jnp.concatenate([packed[:, i * LANES : (i + 1) * LANES] for i in range(4)], axis=0)
    turned = pltpu.roll(packed, DEPTH, axis=1)
    left = lax.broadcasted_iota(jnp.int32, packed.shape, 1) < DEPTH
    normed = jnp.concatenate(
        [jnp.where(left, packed, turned), jnp.where(left, turned, packed)], axis=0
    )
    high, middle, low = pieces(normed)
    upper = jnp.concatenate([high, middle], axis=0)
    lower = jnp.concatenate([low, jnp.zeros_like(low)], axis=0)

    width = min(512, turned_ref.shape[0])
    first = lax.broadcasted_iota(jnp.int32, (width, LANES), 1) < DEPTH
    for base in range(0, turned_ref.shape[0], width):
        at = pl.ds(base, width)
        weighted = sum(
            jnp.dot(turned_ref[at, :], part, preferred_element_type=jnp.float32)
            for part in (upper, lower)
        )
        high, middle, low = pieces(weighted)
        weights[at, :LANES] = jnp.where(first, high, middle)
        weights[at, LANES:] = jnp.where(first, low, jnp.zeros_like(low))


def down(highest, summed):
    top = jnp.max(highest, axis=0, keepdims=True)
    return top + jnp.log2(jnp.sum(summed * jnp.exp2(highest - top), axis=0, keepdims=True))


def logsum(one, other):
    top = jnp.maximum(one, other)
    return top + jnp.log2(jnp.exp2(one - top) + jnp.exp2(other - top))


def row_values(log_src_ref, sums_ref, more_ref):
    return log_src_ref[...] - marg_power * logsum(sums_ref[...], more_ref[...])


def lane_tiles(ref):
    return [pl.ds(j, LANES) for j in range(0, ref.shape[1], LANES)]


def halves(low):
    low = pl.multiple_of(low, 16)
    return pl.ds(low, 16), [pl.ds(low, 8), pl.ds(pl.multiple_of(low + 8, 8), 8)]


def running(highest, summed, terms):
    fresh = jnp.maximum(highest, tree(terms, jnp.maximum))
    total = tree([jnp.exp2(term - fresh) for term in terms], jnp.add)
    return fresh, summed * jnp.exp2(highest - fresh) + total


def columns_running(scores_ref, rows_ref, top_ref, sum_ref, base, count):
    tiles = lane_tiles(scores_ref)
    span = min(8, len(tiles))

    def scan(i, carry):
        for u in range(4):
            low = pl.multiple_of((i * 4 + u) * 8, 8)
            at = pl.ds(pl.multiple_of(base + low, 8), 8)
            state = None
            for start in range(0, len(tiles), span):
                terms = [scores_ref[at, lanes] + rows_ref[:, lanes] for lanes in tiles[start : start + span]]
                if state is None:
                    highest = tree(terms, jnp.maximum)
                    state = highest, tree([jnp.exp2(term - highest) for term in terms], jnp.add)
                else:
                    state = running(*state, terms)
            top_ref[pl.ds(low, 8), :], sum_ref[pl.ds(low, 8), :] = state
        return carry

    lax.fori_loop(0, count // 32, scan, 0)


def rows_running(scores_ref, out_ref):
    count, total = scores_ref.shape
    beside, deep = 8, 8
    unset = (jnp.full((8, LANES), -jnp.inf, jnp.float32), jnp.zeros((8, LANES), jnp.float32))
    for start in range(0, total, beside * LANES):
        tiles = [pl.ds(start + j * LANES, LANES) for j in range(beside)]

        def step(i, carry, tiles=tiles):
            ats = [pl.ds(pl.multiple_of((i * deep + g) * 8, 8), 8) for g in range(deep)]
            return tuple(
                running(*state, [scores_ref[at, lanes] for at in ats])
                for state, lanes in zip(carry, tiles)
            )

        carry = lax.fori_loop(0, count // (8 * deep), step, (unset,) * beside)
        for lanes, state in zip(tiles, carry):
            out_ref[:, lanes] = down(*state)


def columns_exp(scores_ref, rows_ref, top_ref, sum_ref, base, count, keep_ref):
    tiles = lane_tiles(scores_ref)

    def highest(i, carry):
        places = [pl.ds(pl.multiple_of(i * 64 + g * 8, 8), 8) for g in range(8)]
        sources = [pl.ds(pl.multiple_of(base + i * 64 + g * 8, 8), 8) for g in range(8)]
        tops = [None] * 8
        for lanes in tiles:
            row = rows_ref[:, lanes]
            for g, source in enumerate(sources):
                term = scores_ref[source, lanes] + row
                tops[g] = term if tops[g] is None else jnp.maximum(tops[g], term)
        for place, top in zip(places, tops):
            top_ref[place, :] = top - LIFT
        return carry

    def total(i, carry):
        pairs = [halves(base + i * 64 + g * 16) for g in range(4)]
        places = [place for g in range(4) for place in halves(i * 64 + g * 16)[1]]
        tops = [top_ref[place, :] for place in places]
        sums = [jnp.zeros((8, LANES), jnp.float32)] * 8
        for lanes in tiles:
            row = rows_ref[:, lanes]
            for g, (at, sources) in enumerate(pairs):
                parts = []
                for h, source in enumerate(sources):
                    parts.append(jnp.exp2(scores_ref[source, lanes] + row - tops[2 * g + h]))
                    sums[2 * g + h] = sums[2 * g + h] + parts[h]
                if keep_ref is not None:
                    keep_ref[at, lanes] = jnp.concatenate(parts, axis=0).astype(keep_ref.dtype)
        for place, value in zip(places, sums):
            sum_ref[place, :] = value
        return carry

    lax.fori_loop(0, count // 64, highest, 0)
    if keep_ref is not None:
        tops = top_ref[pl.ds(0, count), :]
        top_ref[pl.ds(0, count), :] = jnp.broadcast_to(jnp.max(tops, axis=1, keepdims=True), tops.shape)
    lax.fori_loop(0, count // 64, total, 0)


def split_rows(line):
    row = lax.broadcasted_iota(jnp.int32, (16, line.shape[1]), 0)
    high, middle, low = (part.astype(jnp.float32) for part in pieces(line))
    spread = jnp.where(row == 0, high, jnp.where(row == 1, middle, jnp.where(row == 2, low, 0.0)))
    return spread.astype(jnp.bfloat16)


def split_rows(line):
    row = lax.broadcasted_iota(jnp.int32, (16, line.shape[1]), 0)
    high, middle, low = (part.astype(jnp.float32) for part in pieces(line))
    spread = jnp.where(row == 0, high, jnp.where(row == 1, middle, jnp.where(row == 2, low, 0.0)))
    return spread.astype(jnp.bfloat16)


def columns_product(keep_ref, kept_top_ref, factor, shift, log_tgt_line_ref, line_ref, base, count):
    factors = split_rows(factor)
    part = min(count, 512)
    for low in range(0, count, part):
        at = pl.ds(pl.multiple_of(base + low, part), part)
        sums = lax.dot_general(
            factors, keep_ref[at, :], (((1,), (1,)), ((), ())), preferred_element_type=jnp.float32
        )
        logs = kept_top_ref[:, at] + (shift - LIFT) + jnp.log2(jnp.sum(sums, axis=0, keepdims=True))
        line_ref[:, pl.ds(low, part)] = log_tgt_line_ref[:, at] - marg_power * logs


def columns_finish(top_ref, sum_ref, log_tgt_ref, cols_ref, base, count):
    part = min(count, 2048)
    for low in range(0, count, part):
        here = pl.ds(low, part)
        tops = top_ref[here, :]
        top = jnp.max(tops, axis=1, keepdims=True)
        total = jnp.sum(sum_ref[here, :] * jnp.exp2(tops - top), axis=1, keepdims=True)
        at = pl.ds(pl.multiple_of(base + low, part), part)
        cols_ref[here, :] = log_tgt_ref[at, :] - marg_power * (top + jnp.log2(total))


BESIDE, DEEP = 8, 4


def over_tiles(count, width, body, first, done):
    for start in range(0, width, BESIDE * LANES):
        tiles = [pl.ds(start + j * LANES, LANES) for j in range(BESIDE)]

        def step(i, carry, tiles=tiles):
            carry = list(carry)
            body([halves((i * DEEP + g) * 16) for g in range(DEEP)], tiles, carry)
            return tuple(carry)

        state = lax.fori_loop(0, count // (16 * DEEP), step, tuple(first for _ in tiles))
        for lanes, value in zip(tiles, state):
            done(lanes, value)


def rows_highest(scores_ref, cols_ref, top_ref):
    def body(pairs, tiles, carry):
        for _, places in pairs:
            for place in places:
                if cols_ref is not None:
                    potential = cols_ref[place, :]
                for j, lanes in enumerate(tiles):
                    term = scores_ref[place, lanes]
                    if cols_ref is not None:
                        term = term + potential
                    carry[j] = jnp.maximum(carry[j], term)

    def done(lanes, value):
        top_ref[:, lanes] = jnp.broadcast_to(jnp.max(value, axis=0, keepdims=True), value.shape) - LIFT

    over_tiles(*scores_ref.shape, body, jnp.full((8, LANES), -jnp.inf, jnp.float32), done)


def rows_exp(scores_ref, cols_ref, top_ref, out_ref, keep_ref):
    def body(pairs, tiles, carry):
        tops = [top_ref[:, lanes] for lanes in tiles]
        for at, places in pairs:
            if cols_ref is not None:
                potentials = [cols_ref[place, :] for place in places]
            for j, lanes in enumerate(tiles):
                terms = [scores_ref[place, lanes] for place in places]
                if cols_ref is not None:
                    terms = [term + potential for term, potential in zip(terms, potentials)]
                parts = [jnp.exp2(term - tops[j]) for term in terms]
                if keep_ref is not None:
                    keep_ref[at, lanes] = jnp.concatenate(parts, axis=0).astype(keep_ref.dtype)
                carry[j] = carry[j] + (parts[0] + parts[1])

    def done(lanes, value):
        out_ref[:, lanes] = down(top_ref[:, lanes], value)

    over_tiles(*scores_ref.shape, body, jnp.zeros((8, LANES), jnp.float32), done)


def rows_product(keep_ref, kept_top_ref, factor, shift, out_ref):
    factors = split_rows(factor)
    chunk = 512
    for start in range(0, keep_ref.shape[1], chunk):
        lanes = pl.ds(start, chunk)
        sums = jnp.dot(factors, keep_ref[:, lanes], preferred_element_type=jnp.float32)
        out_ref[:, lanes] = (
            kept_top_ref[0:1, lanes] + (shift - LIFT) + jnp.log2(jnp.sum(sums, axis=0, keepdims=True))
        )


def columns_either(rows, shared, kept, line_ref, scratch, base, count):
    scores_ref, log_tgt_ref, log_tgt_line_ref = shared
    keep_ref, kept_top_ref, kept_rows_ref = kept
    rows_ref, cols_ref, top_ref, sum_ref = scratch
    change = rows - kept_rows_ref[...]
    shift = jnp.max(change)
    near = shift - jnp.min(change) <= SPAN

    @pl.when(near)
    def _():
        factor = jnp.exp2(change - (shift - LIFT))
        columns_product(keep_ref, kept_top_ref, factor, shift, log_tgt_line_ref, line_ref, base, count)

    @pl.when(jnp.logical_not(near))
    def _():
        rows_ref[...] = jnp.broadcast_to(rows, rows_ref.shape)
        columns_running(scores_ref, rows_ref, top_ref, sum_ref, base, count)
        columns_finish(top_ref, sum_ref, log_tgt_ref, cols_ref, base, count)
        line_ref[...] = cols_ref[...].T[0:1, :]


def rows_either(scores_ref, line_ref, kept, cols_ref, row_top_ref, out_ref):
    keep_ref, kept_top_ref, kept_line_ref = kept
    change = line_ref[...] - kept_line_ref[...]
    shift = jnp.max(change)
    near = shift - jnp.min(change) <= SPAN

    @pl.when(near)
    def _():
        rows_product(keep_ref, kept_top_ref, jnp.exp2(change - (shift - LIFT)), shift, out_ref)

    @pl.when(jnp.logical_not(near))
    def _():
        cols_ref[...] = jnp.broadcast_to(line_ref[...], (LANES, line_ref.shape[1])).T
        rows_highest(scores_ref, cols_ref, row_top_ref)
        rows_exp(scores_ref, cols_ref, row_top_ref, out_ref, None)


def first_kernel(scores_ref, sums_ref, more_ref, log_src_ref, log_tgt_ref, log_tgt_line_ref, *refs):
    out_ref, keep_ref, row_top_ref, line_ref = refs[:4]
    rows_ref, cols_ref, top_ref, sum_ref = refs[4:]
    rows_ref[...] = jnp.broadcast_to(row_values(log_src_ref, sums_ref, more_ref), rows_ref.shape)
    count = scores_ref.shape[0]
    columns_running(scores_ref, rows_ref, top_ref, sum_ref, 0, count)
    columns_finish(top_ref, sum_ref, log_tgt_ref, cols_ref, 0, count)
    line_ref[...] = cols_ref[...].T[0:1, :]
    rows_highest(scores_ref, cols_ref, row_top_ref)
    rows_exp(scores_ref, cols_ref, row_top_ref, out_ref, keep_ref)


def second_kernel(scores_ref, sums_ref, more_ref, log_src_ref, log_tgt_ref, log_tgt_line_ref, *refs):
    kept, (out_ref, keep_ref, kept_top_ref, base_ref) = refs[:3], refs[3:7]
    rows_ref, cols_ref, top_ref, sum_ref, line_ref, row_top_ref = refs[7:]
    base_ref[...] = row_values(log_src_ref, sums_ref, more_ref)
    rows_ref[...] = jnp.broadcast_to(base_ref[...], rows_ref.shape)
    count = scores_ref.shape[0]
    columns_exp(scores_ref, rows_ref, top_ref, sum_ref, 0, count, keep_ref)
    columns_finish(top_ref, sum_ref, log_tgt_ref, cols_ref, 0, count)
    kept_top_ref[...] = top_ref[...].T[0:1, :]
    line_ref[...] = cols_ref[...].T[0:1, :]
    rows_either(scores_ref, line_ref, kept, cols_ref, row_top_ref, out_ref)


def later_kernel(scores_ref, sums_ref, more_ref, log_src_ref, log_tgt_ref, log_tgt_line_ref, *refs):
    kept, kept_columns, out_ref = refs[:3], refs[3:6], refs[6]
    scratch, line_ref, row_top_ref = refs[7:11], refs[11], refs[12]
    rows = row_values(log_src_ref, sums_ref, more_ref)
    shared = scores_ref, log_tgt_ref, log_tgt_line_ref
    columns_either(rows, shared, kept_columns, line_ref, scratch, 0, scores_ref.shape[0])
    rows_either(scores_ref, line_ref, kept, scratch[1], row_top_ref, out_ref)


def last_kernel(merged, scores_ref, sums_ref, more_ref, log_src_ref, log_tgt_ref, log_tgt_line_ref, *refs):
    kept_columns, (out_ref, row_ref, col_ref) = refs[:3], refs[3:6]
    scratch, line_ref, values_ref = refs[6:10], refs[10], refs[11]
    own_rows, own_cols = out_ref.shape
    rows = row_values(log_src_ref, sums_ref, more_ref)
    values_ref[...] = rows
    base = pl.multiple_of(lax.rem(lax.div(lax.axis_index("tgt"), 2), merged) * own_cols, own_cols)
    lanes = pl.ds(pl.multiple_of(lax.axis_index("src") * own_rows, own_rows), own_rows)
    shared = scores_ref, log_tgt_ref, log_tgt_line_ref
    columns_either(rows, shared, kept_columns, line_ref, scratch, base, own_cols)
    row_ref[...] = values_ref[:, lanes] * LN2
    col_ref[...] = line_ref[...] * LN2
    block = scores_ref[pl.ds(base, own_cols), lanes] + values_ref[:, lanes]
    out_ref[...] = (block.T + line_ref[...]) * LN2


def swap(value, axis, offset):
    return lax.ppermute(value, axis, [(i, i ^ offset) for i in range(lax.axis_size(axis))])


def staged_parts(value, axis, low, width):
    size = lax.axis_size(axis)
    terms = [value]
    while low < size:
        span = min(width, size // low)
        value = tree(terms, jnp.add)
        terms = [value] + [swap(value, axis, low * j) for j in range(1, span)]
        low *= span
    return terms


def shards(coupling, src_pcs, tgt_pcs, src_mass, tgt_mass):
    f32 = jnp.float32
    pcs = src_pcs.shape[0]
    rows, cols = coupling.shape
    src_size, tgt_size = lax.axis_size("src"), lax.axis_size("tgt")
    total_rows, total_cols = rows * src_size, cols * tgt_size
    merged = 1
    while 2 * merged * 2 <= tgt_size and 2 * merged * cols * total_rows * 4 <= SCORES_BYTES:
        merged *= 2
    wide = merged * cols
    packed_rows = -(-(pcs + 1) // 8) * 8

    arguments = (coupling, src_pcs, tgt_pcs, src_mass.reshape(1, -1), tgt_mass.reshape(1, -1))
    half, whole, moment = pl.pallas_call(
        front_kernel,
        out_shape=(
            pltpu.VMEM((packed_rows, rows // 2), f32),
            pltpu.VMEM((packed_rows, cols), f32),
            pltpu.VMEM((8, 4 * LANES), f32),
        ),
        in_specs=[pl.BlockSpec(memory_space=pltpu.HBM)] * 5,
        out_specs=(VMEM,) * 3,
        scratch_shapes=[pltpu.VMEM(a.shape, a.dtype) for a in arguments]
        + [pltpu.SemaphoreType.DMA((5,))],
        compiler_params=params(8),
    )(*[pltpu.with_memory_space_constraint(a, pltpu.HBM) for a in arguments])

    moment = moment + swap(moment, "tgt", 1)
    half, whole, moment = lax.optimization_barrier((half, whole, moment))
    parts, targets = [moment], [whole]
    if merged > 1:
        message = jnp.concatenate([whole, moment], axis=0)
        targets += [swap(message, "tgt", 2 * b) for b in range(1, merged)]
        parts += [target[packed_rows:] for target in targets[1:]]
    sources = [half] + [swap(half, "src", b) for b in range(1, src_size)]
    parts, sources, targets = lax.optimization_barrier((parts, sources, targets))
    if 2 * merged < tgt_size:
        parts = staged_parts(tree(parts, jnp.add), "tgt", 2 * merged, 4)
    moments = staged_parts(tree(parts, jnp.add), "src", 1, 4)
    near = jnp.concatenate(sources, axis=0)
    far = swap(near, "tgt", 1)

    src_all, turned, log_src, log_tgt, log_tgt_line = pl.pallas_call(
        functools.partial(prepare_kernel, pcs, src_size, merged),
        out_shape=(
            jax.ShapeDtypeStruct((4 * DEPTH, total_rows), jnp.bfloat16),
            jax.ShapeDtypeStruct((wide, LANES), jnp.bfloat16),
            jax.ShapeDtypeStruct((1, total_rows), f32),
            jax.ShapeDtypeStruct((wide, LANES), f32),
            jax.ShapeDtypeStruct((1, wide), f32),
        ),
        in_specs=[VMEM] * (2 + merged),
        out_specs=(VMEM,) * 5,
        compiler_params=params(10),
    )(near, far, *targets)
    weights = pl.pallas_call(
        functools.partial(start_kernel, pcs, total_rows * total_cols),
        out_shape=jax.ShapeDtypeStruct((wide, 4 * DEPTH), jnp.bfloat16),
        in_specs=[VMEM] * (1 + len(moments)),
        out_specs=VMEM,
        compiler_params=params(10),
    )(turned, *moments)
    scores = jnp.dot(weights, src_all, preferred_element_type=f32)
    sums = pl.pallas_call(
        rows_running,
        out_shape=jax.ShapeDtypeStruct((1, total_rows), f32),
        in_specs=[VMEM],
        out_specs=VMEM,
        compiler_params=params(10),
    )(scores)

    def both(value):
        offset = 2 * merged
        while offset < tgt_size:
            value = logsum(value, swap(value, "tgt", offset))
            offset *= 2
        return value, swap(value, "tgt", 1)

    bf16, block = jnp.bfloat16, (wide, total_rows)

    def call(kernel, sums, extra, outs, scratch):
        return pl.pallas_call(
            kernel,
            out_shape=tuple(jax.ShapeDtypeStruct(shape, bf16 if shape == block else f32) for shape in outs),
            in_specs=[VMEM] * (6 + len(extra)),
            out_specs=(VMEM,) * len(outs),
            scratch_shapes=[pltpu.VMEM(shape, f32) for shape in scratch],
            compiler_params=params(10),
        )(scores, *both(sums), log_src, log_tgt, log_tgt_line, *extra)

    line, lines, pads = (1, total_rows), (8, total_rows), (wide, LANES)
    side, columns = (1, wide), (lines, pads, pads, pads)
    sums, *kept_rows = call(first_kernel, sums, (), (line, block, lines, side), columns)
    sums, *kept_columns = call(
        second_kernel, sums, kept_rows, (line, block, side, line), (*columns, side, lines)
    )
    for iteration in range(ITERS - 3):
        (sums,) = call(
            later_kernel, sums, (*kept_rows, *kept_columns), (line,), (*columns, side, lines)
        )
    pads, side = (cols, LANES), (1, cols)
    log_coupling, row_potential, col_potential = call(
        functools.partial(last_kernel, merged), sums, kept_columns,
        ((rows, cols), (1, rows), side), (lines, pads, pads, pads, side, line),
    )
    return log_coupling, row_potential.reshape(-1), col_potential.reshape(-1)


def solution(mesh):
    in_specs = (P("src", "tgt"), P(None, "src"), P(None, "tgt"), P("src"), P("tgt"))
    out_specs = (P("src", "tgt"), P("src"), P("tgt"))
    return jax.shard_map(shards, mesh=mesh, in_specs=in_specs, out_specs=out_specs, check_vma=False)
```
